32 devices in a mesh: pipe: 4 (over z), sp: 4 (over y, core), cfg: 2 (over x).
Axes of the slice: x: 2, y: 2, z: 4, core: 2. Of those that a mesh axis runs over, the one named last changes fastest.
Arguments:
- flight: bfloat16 [4, 2, 512, 5120], P('pipe', 'cfg', 'sp'), may hold values from -6 to 6
- modulation: float32 [4, 2, 3, 5120], P('pipe', 'cfg'), may hold values from -4 to 4
- project_in: bfloat16 [4, 3, 5120, 3072], P('pipe', None, None, ('sp', 'cfg')), may hold values from -0.078125 to 0.078125
- project_out: bfloat16 [4, 3072, 5120], P('pipe', ('sp', 'cfg')), may hold values from -0.5 to 0.5
- stale_cache: bfloat16 [4, 2, 1024, 2, 3072], P('pipe', 'cfg', 'sp'), may hold values from -4 to 4
- visible: int32 [4, 4, 6], P('pipe'), may hold values from 0 to 11, all different within a row
Outputs:
- advanced: bfloat16 [4, 2, 512, 5120], P('pipe', 'cfg', 'sp')
The draws below stay inside these ranges and needn't reach their ends.
Inputs may be any that keep to these rules, and one draw needn't show every extreme that they name: `visible`: 6 different tile numbers for each query tile; number j < 4 is tile j of the segment's own patch, number 4 + j is tile j of its stale context.
All inputs are finite; a program needn't handle non-finite values.
Results may differ from the reference program's by a relative error of at most 0.006.
Values may be sent and summed in bfloat16 or wider, within the bound.
No kernel may reach another device: no remote copies, remote signals or barrier semaphores. Data moves between devices by JAX's collectives and lax.ppermute only.
A program may use at most 128 MiB of HBM per device.

```python
import jax
import jax.numpy as jnp
from jax import lax

D = 5120
H = 24
HD = 128
TILE = 128
KB = 6
PATCH = 512
CTX = 1024
QT = 4
CT = 8
N_PIPE = 4


def shard_levels(stream_key, dims, shards, low, high):
    def one(position, parts):
        steps = jax.random.uniform(jax.random.fold_in(jax.random.fold_in(stream_key, 6), position), (parts,), jnp.float32, low / len(shards), high / len(shards))
        return jnp.repeat(jnp.exp(steps), dims[position] // parts).reshape((-1,) + (1,) * (len(dims) - position - 1))

    loudness = one(*shards[0])
    for cut in shards[1:]:
        loudness = loudness * one(*cut)
    return loudness


def distinct(key, rows, count, top, lift):
    sequence = jax.random.permutation(jax.random.fold_in(key, 1), count)
    favour = sequence
    for power in range(3):
        favour = favour * favour // count
    favour = favour * lift // count
    chance = jax.random.randint(jax.random.fold_in(key, 2), (rows, count), 0, 4096) + favour
    sure = jax.random.permutation(jax.random.fold_in(key, 3), rows)[jnp.arange(count) % rows]
    chance = jnp.where(jnp.arange(rows)[:, None] == sure[None, :], 1 << 14, chance)
    score = chance * count + jnp.arange(count)
    return lax.top_k(score.astype(jnp.int32), top)[1].astype(jnp.int32)


def normal_values(own_key, dims, width, limit, shards=(), held_as=jnp.bfloat16):
    gain = shard_levels(own_key, dims, shards, -0.22, 0.18) if shards else 1.0
    values = jax.random.normal(own_key, dims, jnp.float32) * width * gain
    return jnp.minimum(jnp.maximum(values, -limit), limit).astype(held_as)


def setup_inputs(seed: int = 0) -> dict:
    key_list = jax.random.split(jax.random.key(seed), 7)
    flight = normal_values(key_list[0], (N_PIPE, 2, PATCH, D), 1.0, 6.0, ((0, 4), (1, 2), (2, 4)))
    modulation = normal_values(key_list[1], (N_PIPE, 2, 3, D), 1.0, 4.0, ((0, 4), (1, 2)), jnp.float32)
    project_in = normal_values(key_list[2], (N_PIPE, 3, D, H * HD), D ** -0.5, 0.078125, ((0, 4), (3, 8)))
    project_out = normal_values(key_list[3], (N_PIPE, H * HD, D), HD ** -0.5, 0.5, ((0, 4), (1, 8)))
    stale_cache = normal_values(key_list[4], (N_PIPE, 2, CTX, 2, H * HD), 1.0, 4.0, ((0, 4), (1, 2), (2, 4)))
    visible = distinct(key_list[5], N_PIPE * QT, QT + CT, KB, 0).reshape((N_PIPE, QT, KB))
    return dict(flight=flight, modulation=modulation, project_in=project_in, project_out=project_out, stale_cache=stale_cache, visible=visible)


guidance_scale = 5.0

def layer_norm(values):
    centre = values - lax.optimization_barrier(jnp.mean(values, axis=-1, keepdims=True))
    spread = lax.optimization_barrier(jnp.mean(centre * centre, axis=-1, keepdims=True))
    return centre * lax.rsqrt(spread + 1e-06)

def head_norm(values):
    return values * lax.rsqrt(lax.optimization_barrier(jnp.mean(values * values, axis=-1, keepdims=True)) + 1e-06)

def attend(queries, fresh_keys, fresh_values, context):
    head_count = queries.shape[1]
    keys_pool = jnp.concatenate([fresh_keys, context[:, 0]], axis=0).reshape(QT + CT, TILE, head_count, HD)
    values_pool = jnp.concatenate([fresh_values, context[:, 1]], axis=0).reshape(QT + CT, TILE, head_count, HD)
    return (keys_pool, values_pool)

def segment_layer(inputs):
    flight, modulation, project_in, project_out, stale_cache, visible = inputs
    results = []
    for branch in range(2):
        current = flight[branch].astype(jnp.float32)
        modulate = modulation[branch]
        modulated = (layer_norm(current) * (1.0 + modulate[1]) + modulate[0]).astype(jnp.bfloat16)
        projected = [jnp.dot(modulated, project_in[index], preferred_element_type=jnp.float32) for index in range(3)]
        queries = head_norm(projected[0].reshape(PATCH, H, HD)).astype(jnp.bfloat16)
        keys_fresh = head_norm(projected[1].reshape(PATCH, H, HD)).astype(jnp.bfloat16)
        values_fresh = projected[2].reshape(PATCH, H, HD).astype(jnp.bfloat16)
        context = stale_cache[branch].reshape(CTX, 2, H, HD)
        keys_pool, values_pool = attend(queries, keys_fresh, values_fresh, context)
        key_tiles = jnp.take(keys_pool, visible, axis=0).reshape(QT, KB * TILE, H, HD)
        value_tiles = jnp.take(values_pool, visible, axis=0).reshape(QT, KB * TILE, H, HD)
        query_tiles = queries.reshape(QT, TILE, H, HD)
        scores = jnp.einsum('qthd,qkhd->qhtk', query_tiles.astype(jnp.float32), key_tiles.astype(jnp.float32)) * HD ** (-0.5)
        exponent = jnp.exp(scores)
        probabilities = (exponent / lax.optimization_barrier(jnp.sum(exponent, axis=-1, keepdims=True))).astype(jnp.bfloat16)
        attended = jnp.einsum('qhtk,qkhd->qthd', probabilities.astype(jnp.float32), value_tiles.astype(jnp.float32))
        attended = attended.astype(jnp.bfloat16).reshape(PATCH, H * HD)
        mixed_sum = jnp.dot(attended, project_out, preferred_element_type=jnp.float32)
        results.append((current + modulate[2] * mixed_sum).astype(jnp.bfloat16))
    return jnp.stack(results)

def reference(flight, modulation, project_in, project_out, stale_cache, visible):
    layer_out = lax.map(segment_layer, (flight, modulation, project_in, project_out, stale_cache, visible))
    final_segment = layer_out[N_PIPE - 1].astype(jnp.float32)
    guided = (final_segment[0] + guidance_scale * (final_segment[1] - final_segment[0])).astype(jnp.bfloat16)
    first_segment = jnp.stack([guided, guided])[None]
    return jnp.concatenate([first_segment, layer_out[:N_PIPE - 1]], axis=0)
```

```python
import functools

import jax
import jax.numpy as jnp
from jax import lax
from jax.experimental import pallas as pl
from jax.experimental.pallas import tpu as pltpu
from jax.sharding import PartitionSpec as P

HD = 128
TILE = 128
MIB = 2**20
COLUMN_CHUNKS = 2

guidance_scale = 5.0


def from_behind(x, axis, by):
    count = lax.axis_size(axis)
    return lax.ppermute(x, axis, [(i, (i + by) % count) for i in range(count)])


def from_partner(value, axis, mask):
    pairs = [(source, source ^ mask) for source in range(lax.axis_size(axis))]
    return lax.ppermute(value, axis, pairs)


def norm_kernel(rows_ref, modulation_ref, out_ref):
    step = 16

    def body(index, carry):
        rows = pl.ds(pl.multiple_of(index * step, step), step)
        values = rows_ref[rows, :].astype(jnp.float32)
        centre = values - jnp.mean(values, axis=-1, keepdims=True)
        spread = jnp.mean(centre * centre, axis=-1, keepdims=True)
        normed = centre * lax.rsqrt(spread + 1e-06)
        out_ref[rows, :] = (
            normed * (1.0 + modulation_ref[1:2, :]) + modulation_ref[0:1, :]
        ).astype(jnp.bfloat16)
        return carry

    lax.fori_loop(0, rows_ref.shape[0] // step, body, 0)


def modulated_norm(rows, modulation):
    return pl.pallas_call(
        norm_kernel,
        out_shape=jax.ShapeDtypeStruct(rows.shape, jnp.bfloat16),
        name="modulated_norm",
        cost_estimate=pl.CostEstimate(
            flops=10 * rows.size, bytes_accessed=4 * rows.size, transcendentals=0
        ),
        compiler_params=pltpu.CompilerParams(vmem_limit_bytes=16 * MIB),
    )(rows, modulation)


def project_kernel(rows_ref, weights_ref, out_ref, total_ref):
    step = pl.program_id(0)
    weights = jnp.concatenate([weights_ref[0], weights_ref[1], weights_ref[2]], axis=1)
    product = jnp.dot(rows_ref[...], weights, preferred_element_type=jnp.float32)

    @pl.when(step == 0)
    def _():
        total_ref[...] = product

    @pl.when(step > 0)
    def _():
        total_ref[...] += product

    @pl.when(step == pl.num_programs(0) - 1)
    def _():
        width = weights_ref.shape[2]
        for head in range(2 * width // HD):
            columns = slice(head * HD, (head + 1) * HD)
            values = total_ref[:, columns]
            scale = lax.rsqrt(jnp.mean(values * values, axis=-1, keepdims=True) + 1e-06)
            out_ref[:, columns] = (values * scale).astype(jnp.bfloat16)
        out_ref[:, 2 * width :] = total_ref[:, 2 * width :].astype(jnp.bfloat16)


def project(rows, weights):
    count, depth = rows.shape
    width = weights.shape[2]
    block = 1024
    return pl.pallas_call(
        project_kernel,
        grid=(depth // block,),
        in_specs=[
            pl.BlockSpec((count, block), lambda k: (0, k)),
            pl.BlockSpec((3, block, width), lambda k: (0, k, 0)),
        ],
        out_specs=pl.BlockSpec((count, 3 * width), lambda k: (0, 0)),
        out_shape=jax.ShapeDtypeStruct((count, 3 * width), jnp.bfloat16),
        scratch_shapes=[pltpu.VMEM((count, 3 * width), jnp.float32)],
        name="project_heads",
        cost_estimate=pl.CostEstimate(
            flops=2 * count * depth * 3 * width,
            bytes_accessed=2 * (rows.size + weights.size),
            transcendentals=0,
        ),
        compiler_params=pltpu.CompilerParams(vmem_limit_bytes=40 * MIB),
    )(rows, weights)


def attend_kernel(
    visible_ref, heads_ref, context_ref, out_ref, queries, pool, query_sem, fresh_sem, stale_sem
):
    fresh_rows = heads_ref.shape[0]
    width = out_ref.shape[1]
    copies = (
        pltpu.make_async_copy(heads_ref.at[:, pl.ds(0, width)], queries, query_sem),
        pltpu.make_async_copy(
            heads_ref.at[:, pl.ds(width, 2 * width)], pool.at[pl.ds(0, fresh_rows)], fresh_sem
        ),
        pltpu.make_async_copy(
            context_ref, pool.at[pl.ds(fresh_rows, context_ref.shape[0])], stale_sem
        ),
    )
    for copy in copies:
        copy.start()
    for copy in copies:
        copy.wait()
    tiles_seen = visible_ref.shape[1]
    tiles_fresh = visible_ref.shape[0]

    def body(index, carry):
        tile, branch = index // 2, index % 2
        rows = pl.ds(pl.multiple_of(index * TILE, TILE), TILE)
        starts = []
        for seen in range(tiles_seen):
            number = visible_ref[tile, seen]
            older = number - tiles_fresh
            fresh = (number * 2 + branch) * TILE
            stale = fresh_rows + ((older // 2) * 2 + branch) * 2 * TILE + (older % 2) * TILE
            starts.append(pl.multiple_of(jnp.where(older < 0, fresh, stale), TILE))
        for head in range(width // HD):
            columns = slice(head * HD, (head + 1) * HD)
            value_columns = slice(width + head * HD, width + (head + 1) * HD)
            keys = jnp.concatenate([pool[pl.ds(s, TILE), columns] for s in starts], axis=0)
            values = jnp.concatenate([pool[pl.ds(s, TILE), value_columns] for s in starts], axis=0)
            scores = lax.dot_general(
                queries[rows, columns],
                keys,
                (((1,), (1,)), ((), ())),
                preferred_element_type=jnp.float32,
            )
            exponent = jnp.exp(scores * HD ** (-0.5))
            total = jnp.sum(exponent, axis=-1, keepdims=True)
            probabilities = (exponent / total).astype(jnp.bfloat16)
            mixed = jnp.dot(probabilities, values, preferred_element_type=jnp.float32)
            out_ref[rows, columns] = mixed.astype(jnp.bfloat16)
        return carry

    lax.fori_loop(0, fresh_rows // TILE, body, 0)


def attend(heads, context, visible):
    count = heads.shape[0]
    width = heads.shape[1] // 3
    return pl.pallas_call(
        attend_kernel,
        in_specs=[
            pl.BlockSpec(memory_space=pltpu.SMEM),
            pl.BlockSpec(memory_space=pl.ANY),
            pl.BlockSpec(memory_space=pl.ANY),
        ],
        out_shape=jax.ShapeDtypeStruct((count, width), jnp.bfloat16),
        scratch_shapes=[
            pltpu.VMEM((count, width), jnp.bfloat16),
            pltpu.VMEM((count + context.shape[0], 2 * width), jnp.bfloat16),
            pltpu.SemaphoreType.DMA,
            pltpu.SemaphoreType.DMA,
            pltpu.SemaphoreType.DMA,
        ],
        name="attend",
        cost_estimate=pl.CostEstimate(
            flops=4 * count * visible.shape[1] * TILE * width,
            bytes_accessed=2 * (heads.size + context.size),
            transcendentals=count * visible.shape[1] * TILE * width // HD,
        ),
        compiler_params=pltpu.CompilerParams(vmem_limit_bytes=32 * MIB),
    )(visible, heads, context)


def pick(values, index, axis):
    return lax.dynamic_index_in_dim(values, index, axis, keepdims=False)


def per_device(flight, modulation, project_in, project_out, stale_cache, visible):
    current = flight[0, 0]
    modulate = modulation[0, 0]
    token_rows, features = current.shape
    devices = lax.axis_size("sp") * lax.axis_size("cfg")
    branch = lax.axis_index("cfg")
    high, low = lax.axis_index("sp") // 2, lax.axis_index("sp") % 2

    modulated = modulated_norm(current, modulate)
    gathered = lax.all_gather(modulated, ("sp", "cfg"), axis=0, tiled=True)

    context_rows = stale_cache.shape[2]
    width = project_in.shape[3]
    packed = stale_cache[0, 0].reshape(context_rows, 2, devices, width)
    packed = packed.transpose(2, 0, 1, 3).reshape(devices, context_rows, 2 * width)
    context = lax.all_to_all(packed, ("sp", "cfg"), split_axis=0, concat_axis=0, tiled=True)
    context = context.reshape(devices * context_rows, 2 * width)

    heads = project(gathered, project_in[0])
    attended = attend(heads, context, visible[0])

    blocks = attended.reshape(2, 2, 2, token_rows, width)
    rows_sent = pick(blocks, 1 - low, 1).reshape(4 * token_rows, width)
    rows_kept = pick(blocks, low, 1).reshape(4 * token_rows, width)
    chunk = features // COLUMN_CHUNKS
    half = chunk // 2
    results = []
    for start in range(0, features, chunk):
        weights = project_out[0, :, start : start + chunk]
        sent = jnp.dot(rows_sent, weights, preferred_element_type=jnp.float32)
        received = from_partner(sent.astype(jnp.bfloat16), "sp", 1)
        kept = jnp.dot(rows_kept, weights, preferred_element_type=jnp.float32)
        kept = (kept + received.astype(jnp.float32)).reshape(2, 2, token_rows, chunk)

        first, second = kept[..., :half], kept[..., half:]
        first_in = from_partner(pick(first, 1 - branch, 1).astype(jnp.bfloat16), "cfg", 1)
        second_in = from_partner(pick(second, 1 - high, 0).astype(jnp.bfloat16), "sp", 2)
        first = pick(first, branch, 1) + first_in.astype(jnp.float32)
        second = pick(second, high, 0) + second_in.astype(jnp.float32)
        first_in = from_partner(pick(first, 1 - high, 0).astype(jnp.bfloat16), "sp", 2)
        second_in = from_partner(pick(second, 1 - branch, 0).astype(jnp.bfloat16), "cfg", 1)
        first = pick(first, high, 0) + first_in.astype(jnp.float32)
        second = pick(second, branch, 0) + second_in.astype(jnp.float32)
        mixed_sum = jnp.concatenate([first, second], axis=1)

        columns = slice(start, start + chunk)
        layer_out = (
            current[:, columns].astype(jnp.float32) + modulate[2, columns] * mixed_sum
        ).astype(jnp.bfloat16)
        arrived = from_behind(layer_out, "pipe", 1)
        partner = from_partner(arrived, "cfg", 1)
        cond_rows = jnp.where(branch == 1, arrived, partner).astype(jnp.float32)
        uncond_rows = jnp.where(branch == 1, partner, arrived).astype(jnp.float32)
        guided = (uncond_rows + guidance_scale * (cond_rows - uncond_rows)).astype(jnp.bfloat16)
        results.append(jnp.where(lax.axis_index("pipe") == 0, guided, arrived))
    return jnp.concatenate(results, axis=1)[None, None]


def solution(mesh):
    placed = (
        P("pipe", "cfg", "sp", None),
        P("pipe", "cfg", None, None),
        P("pipe", None, None, ("sp", "cfg")),
        P("pipe", ("sp", "cfg"), None),
        P("pipe", "cfg", "sp", None, None),
        P("pipe", None, None),
    )
    return jax.shard_map(
        per_device,
        mesh=mesh,
        in_specs=placed,
        out_specs=P("pipe", "cfg", "sp", None),
        check_vma=False,
    )
```

```python
import functools

import jax
import jax.numpy as jnp
from jax import lax
from jax.experimental import pallas as pl
from jax.experimental.pallas import tpu as pltpu
from jax.sharding import PartitionSpec as P

HD = 128
TILE = 128
MIB = 2**20
COLUMN_CHUNKS = 2

guidance_scale = 5.0


def from_behind(x, axis, by):
    count = lax.axis_size(axis)
    return lax.ppermute(x, axis, [(i, (i + by) % count) for i in range(count)])


def from_partner(value, axis, mask):
    pairs = [(source, source ^ mask) for source in range(lax.axis_size(axis))]
    return lax.ppermute(value, axis, pairs)


def norm_kernel(rows_ref, modulation_ref, out_ref):
    step = 16

    def body(index, carry):
        rows = pl.ds(pl.multiple_of(index * step, step), step)
        values = rows_ref[rows, :].astype(jnp.float32)
        centre = values - jnp.mean(values, axis=-1, keepdims=True)
        spread = jnp.mean(centre * centre, axis=-1, keepdims=True)
        normed = centre * lax.rsqrt(spread + 1e-06)
        out_ref[rows, :] = (
            normed * (1.0 + modulation_ref[1:2, :]) + modulation_ref[0:1, :]
        ).astype(jnp.bfloat16)
        return carry

    lax.fori_loop(0, rows_ref.shape[0] // step, body, 0)


def modulated_norm(rows, modulation):
    return pl.pallas_call(
        norm_kernel,
        out_shape=jax.ShapeDtypeStruct(rows.shape, jnp.bfloat16),
        name="modulated_norm",
        cost_estimate=pl.CostEstimate(
            flops=10 * rows.size, bytes_accessed=4 * rows.size, transcendentals=0
        ),
        compiler_params=pltpu.CompilerParams(vmem_limit_bytes=16 * MIB),
    )(rows, modulation)


def gate_kernel(value_ref, *refs):
    pass


def after(value, earlier):
    return pl.pallas_call(
        gate_kernel,
        in_specs=[pl.BlockSpec(memory_space=pl.ANY)] * (1 + len(earlier)),
        out_specs=pl.BlockSpec(memory_space=pl.ANY),
        out_shape=jax.ShapeDtypeStruct(value.shape, value.dtype),
        input_output_aliases={0: 0},
        name="after",
    )(value, *earlier)


def project_kernel(*refs):
    (*whole_refs, near_first, near_second, far_first, far_second, weights_ref, out_ref, total_ref) = refs
    step, steps = pl.program_id(0), pl.num_programs(0)
    weights = jnp.concatenate([weights_ref[0], weights_ref[1], weights_ref[2]], axis=1)
    early = step < steps // 2
    blocks = [ref[...] for ref in whole_refs]
    blocks.insert(3, jnp.where(early, near_first[...], near_second[...]))
    blocks.append(jnp.where(early, far_first[...], far_second[...]))
    rows = jnp.concatenate(blocks, axis=0)
    product = jnp.dot(rows, weights, preferred_element_type=jnp.float32)

    @pl.when(step == 0)
    def _():
        total_ref[...] = product

    @pl.when(step > 0)
    def _():
        total_ref[...] += product

    @pl.when(step == steps - 1)
    def _():
        width = weights_ref.shape[2]
        for head in range(2 * width // HD):
            columns = slice(head * HD, (head + 1) * HD)
            values = total_ref[:, columns]
            scale = lax.rsqrt(jnp.mean(values * values, axis=-1, keepdims=True) + 1e-06)
            out_ref[:, columns] = (values * scale).astype(jnp.bfloat16)
        out_ref[:, 2 * width :] = total_ref[:, 2 * width :].astype(jnp.bfloat16)


def project(near, far, weights):
    rows, depth = near[0].shape
    width = weights.shape[2]
    steps = 4
    block = depth // steps
    count = 8 * rows
    whole = pl.BlockSpec((rows, block), lambda k: (0, k))
    first = pl.BlockSpec((rows, block), lambda k: (0, jnp.minimum(k, steps // 2 - 1)))
    second = pl.BlockSpec((rows, block), lambda k: (0, jnp.maximum(k - steps // 2, 0)))
    return pl.pallas_call(
        project_kernel,
        grid=(steps,),
        in_specs=[whole] * 6
        + [first, second] * 2
        + [pl.BlockSpec((3, block, width), lambda k: (0, k, 0))],
        out_specs=pl.BlockSpec((count, 3 * width), lambda k: (0, 0)),
        out_shape=jax.ShapeDtypeStruct((count, 3 * width), jnp.bfloat16),
        scratch_shapes=[pltpu.VMEM((count, 3 * width), jnp.float32)],
        name="project_heads",
        cost_estimate=pl.CostEstimate(
            flops=2 * count * depth * 3 * width,
            bytes_accessed=2 * (count * depth + weights.size),
            transcendentals=0,
        ),
        compiler_params=pltpu.CompilerParams(vmem_limit_bytes=48 * MIB),
    )(*near[:3], *far[:3], *near[3:], *far[3:], weights)


def attend_kernel(
    visible_ref, heads_ref, context_ref, out_ref, queries, pool, query_sem, fresh_sem, stale_sem
):
    fresh_rows = heads_ref.shape[0]
    width = out_ref.shape[1]
    copies = (
        pltpu.make_async_copy(heads_ref.at[:, pl.ds(0, width)], queries, query_sem),
        pltpu.make_async_copy(
            heads_ref.at[:, pl.ds(width, 2 * width)], pool.at[pl.ds(0, fresh_rows)], fresh_sem
        ),
        pltpu.make_async_copy(
            context_ref, pool.at[pl.ds(fresh_rows, context_ref.shape[0])], stale_sem
        ),
    )
    for copy in copies:
        copy.start()
    for copy in copies:
        copy.wait()
    tiles_seen = visible_ref.shape[1]
    tiles_fresh = visible_ref.shape[0]

    mine_high, mine_low = lax.axis_index("sp") // 2, lax.axis_index("sp") % 2
    mine_branch = lax.axis_index("cfg")

    def body(index, carry):
        high, low = mine_high ^ ((index // 2) % 2), mine_low ^ (index // 4)
        tile, branch = high * 2 + low, mine_branch ^ (index % 2)
        rows = pl.ds(pl.multiple_of(index * TILE, TILE), TILE)
        starts = []
        for seen in range(tiles_seen):
            number = visible_ref[tile, seen]
            older = number - tiles_fresh
            fresh = (mine_low ^ (number % 2)) * 4 + (mine_high ^ ((number // 2) % 2)) * 2
            fresh = (fresh + index % 2) * TILE
            stale = fresh_rows + ((older // 2) * 2 + branch) * 2 * TILE + (older % 2) * TILE
            starts.append(pl.multiple_of(jnp.where(older < 0, fresh, stale), TILE))
        for head in range(width // HD):
            columns = slice(head * HD, (head + 1) * HD)
            value_columns = slice(width + head * HD, width + (head + 1) * HD)
            keys = jnp.concatenate([pool[pl.ds(s, TILE), columns] for s in starts], axis=0)
            values = jnp.concatenate([pool[pl.ds(s, TILE), value_columns] for s in starts], axis=0)
            scores = lax.dot_general(
                queries[rows, columns],
                keys,
                (((1,), (1,)), ((), ())),
                preferred_element_type=jnp.float32,
            )
            exponent = jnp.exp(scores * HD ** (-0.5))
            total = jnp.sum(exponent, axis=-1, keepdims=True)
            probabilities = (exponent / total).astype(jnp.bfloat16)
            mixed = jnp.dot(probabilities, values, preferred_element_type=jnp.float32)
            out_ref[rows, columns] = mixed.astype(jnp.bfloat16)
        return carry

    lax.fori_loop(0, fresh_rows // TILE, body, 0)


def attend(heads, context, visible):
    count = heads.shape[0]
    width = heads.shape[1] // 3
    return pl.pallas_call(
        attend_kernel,
        in_specs=[
            pl.BlockSpec(memory_space=pltpu.SMEM),
            pl.BlockSpec(memory_space=pl.ANY),
            pl.BlockSpec(memory_space=pl.ANY),
        ],
        out_shape=jax.ShapeDtypeStruct((count, width), jnp.bfloat16),
        scratch_shapes=[
            pltpu.VMEM((count, width), jnp.bfloat16),
            pltpu.VMEM((count + context.shape[0], 2 * width), jnp.bfloat16),
            pltpu.SemaphoreType.DMA,
            pltpu.SemaphoreType.DMA,
            pltpu.SemaphoreType.DMA,
        ],
        name="attend",
        cost_estimate=pl.CostEstimate(
            flops=4 * count * visible.shape[1] * TILE * width,
            bytes_accessed=2 * (heads.size + context.size),
            transcendentals=count * visible.shape[1] * TILE * width // HD,
        ),
        compiler_params=pltpu.CompilerParams(vmem_limit_bytes=32 * MIB),
    )(visible, heads, context)


def per_device(flight, modulation, project_in, project_out, stale_cache, visible):
    current = flight[0, 0]
    modulate = modulation[0, 0]
    token_rows, features = current.shape
    devices = lax.axis_size("sp") * lax.axis_size("cfg")
    branch = lax.axis_index("cfg")

    own = modulated_norm(current, modulate)
    across = from_partner(own, "cfg", 1)
    along = from_partner(own, "sp", 2)
    own_core = from_partner(own, "sp", 1)
    middle = features // 2
    first = from_partner(across[:, :middle], "sp", 2)
    second = from_partner(along[:, middle:], "cfg", 1)
    across_core = from_partner(across, "sp", 1)
    along_core = from_partner(along, "sp", 1)
    first_core = from_partner(first, "sp", 1)
    second_core = from_partner(second, "sp", 1)

    context_rows = stale_cache.shape[2]
    width = project_in.shape[3]
    packed = stale_cache[0, 0].reshape(context_rows, 2, devices, width)
    packed = packed.transpose(2, 0, 1, 3).reshape(devices, context_rows, 2 * width)
    packed = after(packed, (across, along))
    context = lax.all_to_all(packed, ("sp", "cfg"), split_axis=0, concat_axis=0, tiled=True)
    context = context.reshape(devices * context_rows, 2 * width)

    heads = project(
        (own, across, along, first, second),
        (own_core, across_core, along_core, first_core, second_core),
        project_in[0],
    )
    attended = attend(heads, context, visible[0])

    rows_kept, rows_sent = attended[: 4 * token_rows], attended[4 * token_rows :]
    chunk = features // COLUMN_CHUNKS
    half = chunk // 2
    results = []
    current_columns = current
    for start in range(0, features, chunk):
        weights = project_out[0, :, start : start + chunk]
        sent = jnp.dot(rows_sent, weights, preferred_element_type=jnp.float32)
        received = from_partner(sent.astype(jnp.bfloat16), "sp", 1)
        kept = jnp.dot(rows_kept, weights, preferred_element_type=jnp.float32)
        kept = (kept + received.astype(jnp.float32)).reshape(2, 2, token_rows, chunk)

        first, second = kept[..., :half], kept[..., half:]
        first_in = from_partner(first[:, 1].astype(jnp.bfloat16), "cfg", 1)
        second_in = from_partner(second[1].astype(jnp.bfloat16), "sp", 2)
        first = first[:, 0] + first_in.astype(jnp.float32)
        second = second[0] + second_in.astype(jnp.float32)
        first_in = from_partner(first[1].astype(jnp.bfloat16), "sp", 2)
        second_in = from_partner(second[1].astype(jnp.bfloat16), "cfg", 1)
        first = first[0] + first_in.astype(jnp.float32)
        second = second[0] + second_in.astype(jnp.float32)
        mixed_sum = jnp.concatenate([first, second], axis=1)

        columns = slice(start, start + chunk)
        layer_out = (
            current_columns[:, columns].astype(jnp.float32) + modulate[2, columns] * mixed_sum
        ).astype(jnp.bfloat16)
        current_columns, layer_out = lax.optimization_barrier((current_columns, layer_out))
        arrived = from_behind(layer_out, "pipe", 1)
        partner = from_partner(arrived, "cfg", 1)
        cond_rows = jnp.where(branch == 1, arrived, partner).astype(jnp.float32)
        uncond_rows = jnp.where(branch == 1, partner, arrived).astype(jnp.float32)
        guided = (uncond_rows + guidance_scale * (cond_rows - uncond_rows)).astype(jnp.bfloat16)
        results.append(jnp.where(lax.axis_index("pipe") == 0, guided, arrived))
    return jnp.concatenate(results, axis=1)[None, None]


def solution(mesh):
    placed = (
        P("pipe", "cfg", "sp", None),
        P("pipe", "cfg", None, None),
        P("pipe", None, None, ("sp", "cfg")),
        P("pipe", ("sp", "cfg"), None),
        P("pipe", "cfg", "sp", None, None),
        P("pipe", None, None),
    )
    return jax.shard_map(
        per_device,
        mesh=mesh,
        in_specs=placed,
        out_specs=P("pipe", "cfg", "sp", None),
        check_vma=False,
    )
```

```python
import jax
import jax.numpy as jnp
from jax import lax
from jax.experimental import pallas as pl
from jax.experimental.pallas import tpu as pltpu
from jax.sharding import PartitionSpec as P

HD = 128
TILE = 128
MIB = 2**20
COLUMN_CHUNKS = 4

guidance_scale = 5.0


def from_behind(x, axis, by):
    count = lax.axis_size(axis)
    return lax.ppermute(x, axis, [(i, (i + by) % count) for i in range(count)])


def from_partner(value, axis, mask):
    pairs = [(source, source ^ mask) for source in range(lax.axis_size(axis))]
    return lax.ppermute(value, axis, pairs)


def norm_kernel(rows_ref, modulation_ref, out_ref):
    step = 16

    def body(index, carry):
        rows = pl.ds(pl.multiple_of(index * step, step), step)
        values = rows_ref[rows, :].astype(jnp.float32)
        centre = values - jnp.mean(values, axis=-1, keepdims=True)
        spread = jnp.mean(centre * centre, axis=-1, keepdims=True)
        normed = centre * lax.rsqrt(spread + 1e-06)
        out_ref[rows, :] = (
            normed * (1.0 + modulation_ref[1:2, :]) + modulation_ref[0:1, :]
        ).astype(jnp.bfloat16)
        return carry

    lax.fori_loop(0, rows_ref.shape[0] // step, body, 0)


def modulated_norm(rows, modulation):
    return pl.pallas_call(
        norm_kernel,
        out_shape=jax.ShapeDtypeStruct(rows.shape, jnp.bfloat16),
        name="modulated_norm",
        cost_estimate=pl.CostEstimate(
            flops=10 * rows.size, bytes_accessed=4 * rows.size, transcendentals=0
        ),
        compiler_params=pltpu.CompilerParams(vmem_limit_bytes=16 * MIB),
    )(rows, modulation)


def gate_kernel(value_ref, *refs):
    pass


def after(value, earlier):
    return pl.pallas_call(
        gate_kernel,
        in_specs=[pl.BlockSpec(memory_space=pl.ANY)] * (1 + len(earlier)),
        out_specs=pl.BlockSpec(memory_space=pl.ANY),
        out_shape=jax.ShapeDtypeStruct(value.shape, value.dtype),
        input_output_aliases={0: 0},
        name="after",
    )(value, *earlier)


def project_kernel(*refs):
    (*whole_refs, near_first, near_second, far_first, far_second, weights_ref, out_ref, total_ref) = refs
    step, steps = pl.program_id(0), pl.num_programs(0)
    weights = jnp.concatenate([weights_ref[0], weights_ref[1], weights_ref[2]], axis=1)
    early = step < steps // 2
    blocks = [ref[...] for ref in whole_refs]
    blocks.insert(3, jnp.where(early, near_first[...], near_second[...]))
    blocks.append(jnp.where(early, far_first[...], far_second[...]))
    rows = jnp.concatenate(blocks, axis=0)
    product = jnp.dot(rows, weights, preferred_element_type=jnp.float32)

    @pl.when(step == 0)
    def _():
        total_ref[...] = product

    @pl.when(step > 0)
    def _():
        total_ref[...] += product

    @pl.when(step == steps - 1)
    def _():
        width = weights_ref.shape[2]
        for head in range(2 * width // HD):
            columns = slice(head * HD, (head + 1) * HD)
            values = total_ref[:, columns]
            scale = lax.rsqrt(jnp.mean(values * values, axis=-1, keepdims=True) + 1e-06)
            out_ref[:, columns] = (values * scale).astype(jnp.bfloat16)
        out_ref[:, 2 * width :] = total_ref[:, 2 * width :].astype(jnp.bfloat16)


def project(near, far, weights):
    rows, depth = near[0].shape
    width = weights.shape[2]
    steps = 4
    block = depth // steps
    count = 8 * rows
    whole = pl.BlockSpec((rows, block), lambda k: (0, k))
    first = pl.BlockSpec((rows, block), lambda k: (0, jnp.minimum(k, steps // 2 - 1)))
    second = pl.BlockSpec((rows, block), lambda k: (0, jnp.maximum(k - steps // 2, 0)))
    return pl.pallas_call(
        project_kernel,
        grid=(steps,),
        in_specs=[whole] * 6
        + [first, second] * 2
        + [pl.BlockSpec((3, block, width), lambda k: (0, k, 0))],
        out_specs=pl.BlockSpec((count, 3 * width), lambda k: (0, 0)),
        out_shape=jax.ShapeDtypeStruct((count, 3 * width), jnp.bfloat16),
        scratch_shapes=[pltpu.VMEM((count, 3 * width), jnp.float32)],
        name="project_heads",
        cost_estimate=pl.CostEstimate(
            flops=2 * count * depth * 3 * width,
            bytes_accessed=2 * (count * depth + weights.size),
            transcendentals=0,
        ),
        compiler_params=pltpu.CompilerParams(vmem_limit_bytes=48 * MIB),
    )(*near[:3], *far[:3], *near[3:], *far[3:], weights)


def attend_kernel(visible_ref, heads_ref, context_ref, out_ref):
    width = out_ref.shape[1]
    tiles_seen = visible_ref.shape[1]
    tiles_fresh = visible_ref.shape[0]
    mine_high, mine_low = lax.axis_index("sp") // 2, lax.axis_index("sp") % 2
    mine_branch = lax.axis_index("cfg")

    def body(index, carry):
        high, low = mine_high ^ ((index // 2) % 2), mine_low ^ (index // 4)
        tile, branch = high * 2 + low, mine_branch ^ (index % 2)
        rows = pl.ds(pl.multiple_of(index * TILE, TILE), TILE)
        places = []
        for seen in range(tiles_seen):
            number = visible_ref[tile, seen]
            older = jnp.maximum(number - tiles_fresh, 0)
            fresh = (mine_low ^ (number % 2)) * 4 + (mine_high ^ ((number // 2) % 2)) * 2
            fresh = (fresh + index % 2) * TILE
            stale = ((older // 2) * 2 + branch) * 2 * TILE + (older % 2) * TILE
            places.append(
                (
                    number < tiles_fresh,
                    pl.ds(pl.multiple_of(fresh, TILE), TILE),
                    pl.ds(pl.multiple_of(stale, TILE), TILE),
                )
            )

        def tiles(kind, head):
            fresh_columns = slice(kind * width + head * HD, kind * width + (head + 1) * HD)
            start = (kind - 1) * width + head * HD
            return jnp.concatenate(
                [
                    jnp.where(
                        is_fresh, heads_ref[fresh, fresh_columns], context_ref[stale, start : start + HD]
                    )
                    for is_fresh, fresh, stale in places
                ],
                axis=0,
            )

        for head in range(width // HD):
            columns = slice(head * HD, (head + 1) * HD)
            scores = lax.dot_general(
                heads_ref[rows, columns],
                tiles(1, head),
                (((1,), (1,)), ((), ())),
                preferred_element_type=jnp.float32,
            )
            exponent = jnp.exp(scores * HD ** (-0.5))
            total = jnp.sum(exponent, axis=-1, keepdims=True)
            mixed = jnp.dot(
                exponent.astype(jnp.bfloat16), tiles(2, head), preferred_element_type=jnp.float32
            )
            out_ref[rows, columns] = (mixed / total).astype(jnp.bfloat16)
        return carry

    lax.fori_loop(0, heads_ref.shape[0] // TILE, body, 0)


def attend(heads, context, visible):
    count = heads.shape[0]
    width = heads.shape[1] // 3
    return pl.pallas_call(
        attend_kernel,
        in_specs=[
            pl.BlockSpec(memory_space=pltpu.SMEM),
            pl.BlockSpec(memory_space=pltpu.VMEM),
            pl.BlockSpec(memory_space=pltpu.VMEM),
        ],
        out_shape=jax.ShapeDtypeStruct((count, width), jnp.bfloat16),
        name="attend",
        cost_estimate=pl.CostEstimate(
            flops=4 * count * visible.shape[1] * TILE * width,
            bytes_accessed=2 * (heads.size + context.size),
            transcendentals=count * visible.shape[1] * TILE * width // HD,
        ),
        compiler_params=pltpu.CompilerParams(vmem_limit_bytes=32 * MIB),
    )(visible, heads, context)


def per_device(flight, modulation, project_in, project_out, stale_cache, visible):
    current = flight[0, 0]
    modulate = modulation[0, 0]
    token_rows, features = current.shape
    devices = lax.axis_size("sp") * lax.axis_size("cfg")
    wide = current.astype(jnp.float32)

    gate = modulate[2]
    other_gate = from_partner(gate, "cfg", 1)
    last = lax.axis_index("pipe") == lax.axis_size("pipe") - 1
    conditional = lax.axis_index("cfg") == 1
    weight = jnp.where(conditional, guidance_scale, 1.0 - guidance_scale)
    other_weight = jnp.where(conditional, 1.0 - guidance_scale, guidance_scale)
    own_sent = jnp.where(last, weight, 0.0)
    other_sent = jnp.where(last, other_weight, 1.0)
    own_kept = jnp.where(last, weight, 1.0)
    other_kept = jnp.where(last, other_weight, 0.0)

    own = modulated_norm(current, modulate)
    across = from_partner(own, "cfg", 1)
    along = from_partner(own, "sp", 2)
    own_core = from_partner(own, "sp", 1)
    middle = features // 2
    first = from_partner(across[:, :middle], "sp", 2)
    second = from_partner(along[:, middle:], "cfg", 1)
    across_core = from_partner(across, "sp", 1)
    along_core = from_partner(along, "sp", 1)
    first_core = from_partner(first, "sp", 1)
    second_core = from_partner(second, "sp", 1)

    context_rows = stale_cache.shape[2]
    width = project_in.shape[3]
    packed = stale_cache[0, 0].reshape(context_rows, 2, devices, width)
    packed = packed.transpose(2, 0, 1, 3).reshape(devices, context_rows, 2 * width)
    packed = after(packed, (first, second))
    context = lax.all_to_all(packed, ("sp", "cfg"), split_axis=0, concat_axis=0, tiled=True)
    context = context.reshape(devices * context_rows, 2 * width)

    heads = project(
        (own, across, along, first, second),
        (own_core, across_core, along_core, first_core, second_core),
        project_in[0],
    )
    attended = attend(heads, context, visible[0])

    rows_kept, rows_sent = attended[: 4 * token_rows], attended[4 * token_rows :]
    chunk = features // COLUMN_CHUNKS
    half = chunk // 2
    results = []
    previous = None
    for start in range(0, features, chunk):
        weights = project_out[0, :, start : start + chunk]
        sent = jnp.dot(rows_sent, weights, preferred_element_type=jnp.float32)
        received = from_partner(sent.astype(jnp.bfloat16), "sp", 1)
        kept = jnp.dot(rows_kept, weights, preferred_element_type=jnp.float32)
        kept = (kept + received.astype(jnp.float32)).reshape(2, 2, token_rows, chunk)

        columns = slice(start, start + half)
        own, other = kept[:, 0, :, :half] * gate[columns], kept[:, 1, :, :half] * other_gate[columns]
        mine = jnp.stack([wide[:, columns], jnp.zeros_like(wide[:, columns])])
        first_out = (own_sent * (own + mine) + other_sent * other).astype(jnp.bfloat16)
        first = own_kept * (own + mine) + other_kept * other
        second_out = kept[1, :, :, half:].astype(jnp.bfloat16)
        second = kept[0, :, :, half:]
        if previous is not None:
            first_out = after(first_out, previous)
            second_out = after(second_out, previous)
        first_in = from_partner(first_out, "cfg", 1)
        second_in = from_partner(second_out, "sp", 2)
        previous = (first_in, second_in)

        first = first + first_in.astype(jnp.float32)
        first_in = from_partner(first[1].astype(jnp.bfloat16), "sp", 2)
        columns = slice(start + half, start + chunk)
        second = second + second_in.astype(jnp.float32)
        own, other = second[0] * gate[columns], second[1] * other_gate[columns]
        mine = wide[:, columns]
        second_out = (own_sent * (own + mine) + other_sent * other).astype(jnp.bfloat16)
        second_in = from_partner(second_out, "cfg", 1)
        second = own_kept * (own + mine) + other_kept * other

        first = first[0] + first_in.astype(jnp.float32)
        second = second + second_in.astype(jnp.float32)
        summed = jnp.concatenate([first, second], axis=1).astype(jnp.bfloat16)
        results.append(from_behind(summed, "pipe", 1))
    return jnp.concatenate(results, axis=1)[None, None]


def solution(mesh):
    placed = (
        P("pipe", "cfg", "sp", None),
        P("pipe", "cfg", None, None),
        P("pipe", None, None, ("sp", "cfg")),
        P("pipe", ("sp", "cfg"), None),
        P("pipe", "cfg", "sp", None, None),
        P("pipe", None, None),
    )
    return jax.shard_map(
        per_device,
        mesh=mesh,
        in_specs=placed,
        out_specs=P("pipe", "cfg", "sp", None),
        check_vma=False,
    )
```

```python
import functools

import jax
import jax.numpy as jnp
from jax import lax
from jax.experimental import pallas as pl
from jax.experimental.pallas import tpu as pltpu
from jax.sharding import PartitionSpec as P

HD = 128
TILE = 128
MIB = 2**20
COLUMN_CHUNKS = 5

guidance_scale = 5.0
SHORT = pl.CostEstimate(flops=1, bytes_accessed=1, transcendentals=0)


def from_behind(x, axis, by):
    count = lax.axis_size(axis)
    return lax.ppermute(x, axis, [(i, (i + by) % count) for i in range(count)])


def from_partner(value, axis, mask):
    pairs = [(source, source ^ mask) for source in range(lax.axis_size(axis))]
    return lax.ppermute(value, axis, pairs)


def norm_kernel(rows_ref, modulation_ref, out_ref):
    step = 16

    def body(index, carry):
        rows = pl.ds(pl.multiple_of(index * step, step), step)
        values = rows_ref[rows, :].astype(jnp.float32)
        centre = values - jnp.mean(values, axis=-1, keepdims=True)
        spread = jnp.mean(centre * centre, axis=-1, keepdims=True)
        normed = centre * lax.rsqrt(spread + 1e-06)
        out_ref[rows, :] = (
            normed * (1.0 + modulation_ref[1:2, :]) + modulation_ref[0:1, :]
        ).astype(jnp.bfloat16)
        return carry

    lax.fori_loop(0, rows_ref.shape[0] // step, body, 0)


def modulated_norm(rows, modulation):
    return pl.pallas_call(
        norm_kernel,
        out_shape=jax.ShapeDtypeStruct(rows.shape, jnp.bfloat16),
        name="modulated_norm",
        cost_estimate=pl.CostEstimate(
            flops=10 * rows.size, bytes_accessed=4 * rows.size, transcendentals=0
        ),
        compiler_params=pltpu.CompilerParams(vmem_limit_bytes=16 * MIB),
    )(rows, modulation)


def gate_kernel(value_ref, *refs):
    pass


def after(value, earlier):
    return pl.pallas_call(
        gate_kernel,
        in_specs=[pl.BlockSpec(memory_space=pl.ANY)] * (1 + len(earlier)),
        out_specs=pl.BlockSpec(memory_space=pl.ANY),
        out_shape=jax.ShapeDtypeStruct(value.shape, value.dtype),
        input_output_aliases={0: 0},
        name="after",
        cost_estimate=SHORT,
    )(value, *earlier)


def project_kernel(*refs):
    *whole_refs, near_first, near_second, far_first, far_second, weights_ref = refs[:11]
    out_ref, total_ref = refs[-2:]
    step, steps = pl.program_id(0), pl.num_programs(0)
    weights = jnp.concatenate([weights_ref[0], weights_ref[1], weights_ref[2]], axis=1)
    early = step < steps // 2
    blocks = [ref[...] for ref in whole_refs]
    blocks.insert(3, jnp.where(early, near_first[...], near_second[...]))
    blocks.append(jnp.where(early, far_first[...], far_second[...]))
    rows = jnp.concatenate(blocks, axis=0)
    product = jnp.dot(rows, weights, preferred_element_type=jnp.float32)

    @pl.when(step == 0)
    def _():
        total_ref[...] = product

    @pl.when(step > 0)
    def _():
        total_ref[...] += product

    @pl.when(step == steps - 1)
    def _():
        width = weights_ref.shape[2]
        for head in range(2 * width // HD):
            columns = slice(head * HD, (head + 1) * HD)
            values = total_ref[:, columns]
            scale = lax.rsqrt(jnp.mean(values * values, axis=-1, keepdims=True) + 1e-06)
            out_ref[:, columns] = (values * scale).astype(jnp.bfloat16)
        out_ref[:, 2 * width :] = total_ref[:, 2 * width :].astype(jnp.bfloat16)


def project(near, far, weights, earlier):
    rows, depth = near[0].shape
    width = weights.shape[2]
    steps = 4
    block = depth // steps
    count = 8 * rows
    whole = pl.BlockSpec((rows, block), lambda k: (0, k))
    first = pl.BlockSpec((rows, block), lambda k: (0, jnp.minimum(k, steps // 2 - 1)))
    second = pl.BlockSpec((rows, block), lambda k: (0, jnp.maximum(k - steps // 2, 0)))
    return pl.pallas_call(
        project_kernel,
        grid=(steps,),
        in_specs=[whole] * 6
        + [first, second] * 2
        + [pl.BlockSpec((3, block, width), lambda k: (0, k, 0))]
        + [pl.BlockSpec(memory_space=pl.ANY)],
        out_specs=pl.BlockSpec((count, 3 * width), lambda k: (0, 0)),
        out_shape=jax.ShapeDtypeStruct((count, 3 * width), jnp.bfloat16),
        scratch_shapes=[pltpu.VMEM((count, 3 * width), jnp.float32)],
        name="project_heads",
        cost_estimate=pl.CostEstimate(
            flops=2 * count * depth * 3 * width,
            bytes_accessed=2 * (count * depth + weights.size),
            transcendentals=0,
        ),
        compiler_params=pltpu.CompilerParams(vmem_limit_bytes=36 * MIB),
    )(*near[:3], *far[:3], *near[3:], *far[3:], weights, earlier)


def attend_kernel(visible_ref, heads_ref, context_ref, out_ref):
    width = out_ref.shape[1]
    tiles_seen = visible_ref.shape[1]
    tiles_fresh = visible_ref.shape[0]
    mine_high, mine_low = lax.axis_index("sp") // 2, lax.axis_index("sp") % 2
    mine_branch = lax.axis_index("cfg")

    def body(index, carry):
        high, low = mine_high ^ ((index // 2) % 2), mine_low ^ (index // 4)
        tile, branch = high * 2 + low, mine_branch ^ (index % 2)
        rows = pl.ds(pl.multiple_of(index * TILE, TILE), TILE)
        places = []
        for seen in range(tiles_seen):
            number = visible_ref[tile, seen]
            older = jnp.maximum(number - tiles_fresh, 0)
            fresh = (mine_low ^ (number % 2)) * 4 + (mine_high ^ ((number // 2) % 2)) * 2
            fresh = (fresh + index % 2) * TILE
            stale = ((older // 2) * 2 + branch) * 2 * TILE + (older % 2) * TILE
            places.append(
                (
                    number < tiles_fresh,
                    pl.ds(pl.multiple_of(fresh, TILE), TILE),
                    pl.ds(pl.multiple_of(stale, TILE), TILE),
                )
            )

        def tiles(kind, head):
            fresh_columns = slice(kind * width + head * HD, kind * width + (head + 1) * HD)
            start = (kind - 1) * width + head * HD
            return jnp.concatenate(
                [
                    jnp.where(
                        is_fresh, heads_ref[fresh, fresh_columns], context_ref[stale, start : start + HD]
                    )
                    for is_fresh, fresh, stale in places
                ],
                axis=0,
            )

        for head in range(width // HD):
            columns = slice(head * HD, (head + 1) * HD)
            scores = lax.dot_general(
                heads_ref[rows, columns],
                tiles(1, head),
                (((1,), (1,)), ((), ())),
                preferred_element_type=jnp.float32,
            )
            exponent = jnp.exp(scores * HD ** (-0.5))
            total = jnp.sum(exponent, axis=-1, keepdims=True)
            mixed = jnp.dot(
                exponent.astype(jnp.bfloat16), tiles(2, head), preferred_element_type=jnp.float32
            )
            out_ref[rows, columns] = (mixed / total).astype(jnp.bfloat16)
        return carry

    lax.fori_loop(0, heads_ref.shape[0] // TILE, body, 0)


def attend(heads, context, visible):
    count = heads.shape[0]
    width = heads.shape[1] // 3
    return pl.pallas_call(
        attend_kernel,
        in_specs=[
            pl.BlockSpec(memory_space=pltpu.SMEM),
            pl.BlockSpec(memory_space=pltpu.VMEM),
            pl.BlockSpec(memory_space=pltpu.VMEM),
        ],
        out_shape=jax.ShapeDtypeStruct((count, width), jnp.bfloat16),
        name="attend",
        cost_estimate=pl.CostEstimate(
            flops=4 * count * visible.shape[1] * TILE * width,
            bytes_accessed=2 * (heads.size + context.size),
            transcendentals=count * visible.shape[1] * TILE * width // HD,
        ),
        compiler_params=pltpu.CompilerParams(vmem_limit_bytes=32 * MIB),
    )(visible, heads, context)


def half_kernel(rows_ref, *refs, start):
    out_ref = refs[-1]
    out_ref[...] = rows_ref[:, start : start + out_ref.shape[1]]


def half_of(rows, start, earlier):
    return pl.pallas_call(
        functools.partial(half_kernel, start=start),
        in_specs=[pl.BlockSpec(memory_space=pltpu.VMEM), pl.BlockSpec(memory_space=pl.ANY)],
        out_shape=jax.ShapeDtypeStruct((rows.shape[0], rows.shape[1] // 2), rows.dtype),
        name="half_of",
        cost_estimate=SHORT,
        compiler_params=pltpu.CompilerParams(vmem_limit_bytes=8 * MIB),
    )(rows, earlier)


def sent_kernel(attended_ref, weights_ref, *out_refs, chunk):
    rows = attended_ref[attended_ref.shape[0] // 2 :, :]
    start = 0
    for out_ref in out_refs:
        for index in range(out_ref.shape[0]):
            out_ref[index] = jnp.dot(
                rows, weights_ref[:, start : start + chunk], preferred_element_type=jnp.float32
            ).astype(jnp.bfloat16)
            start += chunk


def sent_products(attended, weights, chunk):
    rows, count = attended.shape[0] // 2, weights.shape[1] // chunk
    return pl.pallas_call(
        functools.partial(sent_kernel, chunk=chunk),
        out_shape=[
            jax.ShapeDtypeStruct((pieces, rows, chunk), jnp.bfloat16) for pieces in (1, count - 1)
        ],
        in_specs=[pl.BlockSpec(memory_space=pltpu.VMEM)] * 2,
        name="sent_products",
        cost_estimate=SHORT,
        compiler_params=pltpu.CompilerParams(vmem_limit_bytes=20 * MIB),
    )(attended, weights)


def combined(own, other, mine, gates_ref, columns):
    conditional = lax.axis_index("cfg") == 1
    last = lax.axis_index("pipe") == lax.axis_size("pipe") - 1
    weight = jnp.where(conditional, guidance_scale, 1.0 - guidance_scale).astype(jnp.float32)
    other_weight = jnp.where(conditional, 1.0 - guidance_scale, guidance_scale).astype(jnp.float32)
    own = own * gates_ref[0:1, columns]
    other = other * gates_ref[1:2, columns]
    if mine is not None:
        own = own + mine
    guided = weight * own + other_weight * other
    return jnp.where(last, guided, other), jnp.where(last, guided, own)


def begin(index, start, refs, across_out, along_out, first_kept, second_kept):
    attended_ref, weights_ref, received_ref, rows_ref, gates_ref = refs
    tokens, half = rows_ref.shape[0], first_kept.shape[2]
    attended = attended_ref[: 4 * tokens, :]
    columns = slice(start, start + half)
    product = jnp.dot(attended, weights_ref[:, columns], preferred_element_type=jnp.float32)
    product = product + received_ref[index, :, :half].astype(jnp.float32)
    for tile in range(2):
        own = product[2 * tile * tokens : (2 * tile + 1) * tokens]
        other = product[(2 * tile + 1) * tokens : (2 * tile + 2) * tokens]
        mine = rows_ref[:, columns].astype(jnp.float32) if tile == 0 else None
        sent, kept = combined(own, other, mine, gates_ref, columns)
        across_out[tile] = sent.astype(jnp.bfloat16)
        first_kept[tile] = kept
    columns = slice(start + half, start + 2 * half)
    product = jnp.dot(attended, weights_ref[:, columns], preferred_element_type=jnp.float32)
    product = product + received_ref[index, :, half:].astype(jnp.float32)
    for branch in range(2):
        second_kept[branch] = product[branch * tokens : (branch + 1) * tokens]
        along_out[branch] = product[(branch + 2) * tokens : (branch + 3) * tokens].astype(
            jnp.bfloat16
        )


def stage_kernel(*refs, parts, start, next_start, piece, fresh, middle, final):
    named = dict(zip(parts, refs))
    if fresh:
        begin(
            piece,
            next_start,
            [named[name] for name in ("attended", "weights", "received", "rows", "gates")],
            named["across_out"],
            named["along_out"],
            named["first_kept_out"],
            named["second_kept_out"],
        )
    if middle:
        across, along = named["across"], named["along"]
        first_kept, second_kept = named["first_kept"], named["second_kept"]
        half = first_kept.shape[2]
        place = 2 if fresh else 0
        named["along_out"][place] = (first_kept[1] + across[1].astype(jnp.float32)).astype(
            jnp.bfloat16
        )
        named["first_left_out"][...] = first_kept[0] + across[0].astype(jnp.float32)
        columns = slice(start + half, start + 2 * half)
        sent, kept = combined(
            second_kept[0] + along[0].astype(jnp.float32),
            second_kept[1] + along[1].astype(jnp.float32),
            named["rows"][:, columns].astype(jnp.float32),
            named["gates"],
            columns,
        )
        named["across_out"][place] = sent.astype(jnp.bfloat16)
        named["second_left_out"][...] = kept
    if final:
        across, along = named["across"], named["along"]
        first_left, second_left = named["first_left"], named["second_left"]
        half = first_left.shape[1]
        place = 2 if middle else 0
        named["done_out"][:, :half] = (
            first_left[...] + along[place].astype(jnp.float32)
        ).astype(jnp.bfloat16)
        named["done_out"][:, half:] = (
            second_left[...] + across[place].astype(jnp.float32)
        ).astype(jnp.bfloat16)


def stage(operands, earlier, chunk, start, next_start, piece, fresh, middle, final):
    tokens, half = operands["rows"].shape[0], chunk // 2
    outs = {}
    if fresh or middle:
        pieces = 2 * fresh + middle
        outs["across_out"] = jax.ShapeDtypeStruct((pieces, tokens, half), jnp.bfloat16)
        outs["along_out"] = outs["across_out"]
    if fresh:
        outs["first_kept_out"] = jax.ShapeDtypeStruct((2, tokens, half), jnp.float32)
        outs["second_kept_out"] = outs["first_kept_out"]
    if middle:
        outs["first_left_out"] = jax.ShapeDtypeStruct((tokens, half), jnp.float32)
        outs["second_left_out"] = outs["first_left_out"]
    if final:
        outs["done_out"] = jax.ShapeDtypeStruct((tokens, chunk), jnp.bfloat16)
    parts = list(operands) + ["earlier"] * len(earlier) + list(outs)
    results = pl.pallas_call(
        functools.partial(
            stage_kernel,
            parts=parts,
            start=start,
            next_start=next_start,
            piece=piece,
            fresh=fresh,
            middle=middle,
            final=final,
        ),
        in_specs=[pl.BlockSpec(memory_space=pltpu.VMEM)] * len(operands)
        + [pl.BlockSpec(memory_space=pl.ANY)] * len(earlier),
        out_shape=list(outs.values()),
        name="sum_stage",
        cost_estimate=SHORT,
        compiler_params=pltpu.CompilerParams(vmem_limit_bytes=24 * MIB),
    )(*operands.values(), *earlier)
    return dict(zip(outs, results))


def place_kernel(part_ref, *refs, start):
    out_ref, semaphore = refs[-2:]
    copy = pltpu.make_async_copy(
        part_ref, out_ref.at[:, pl.ds(start, part_ref.shape[1])], semaphore
    )
    copy.start()
    copy.wait()


def place(part, whole, columns, start, earlier):
    held = () if whole is None else (whole,)
    return pl.pallas_call(
        functools.partial(place_kernel, start=start),
        in_specs=[pl.BlockSpec(memory_space=pl.ANY)] * (1 + len(held) + len(earlier)),
        out_specs=pl.BlockSpec(memory_space=pl.ANY),
        out_shape=jax.ShapeDtypeStruct((part.shape[0], columns), part.dtype),
        scratch_shapes=[pltpu.SemaphoreType.DMA],
        input_output_aliases={1: 0} if held else {},
        name="place",
        cost_estimate=SHORT,
    )(part, *held, *earlier)


def per_device(flight, modulation, project_in, project_out, stale_cache, visible):
    current = flight[0, 0]
    modulate = modulation[0, 0]
    token_rows, features = current.shape
    devices = lax.axis_size("sp") * lax.axis_size("cfg")

    context_rows = stale_cache.shape[2]
    width = project_in.shape[3]
    packed = stale_cache[0, 0].reshape(context_rows, 2, devices, width)
    packed = packed.transpose(2, 0, 1, 3).reshape(devices, context_rows, 2 * width)

    own = modulated_norm(current, modulate)
    across = from_partner(own, "cfg", 1)
    along = from_partner(own, "sp", 2)
    own_core = from_partner(own, "sp", 1)
    middle = features // 2
    first = from_partner(half_of(across, 0, packed), "sp", 2)
    second = from_partner(half_of(along, middle, packed), "cfg", 1)
    across_core = from_partner(across, "sp", 1)
    along_core = from_partner(along, "sp", 1)
    first_core = from_partner(first, "sp", 1)
    second_core = from_partner(second, "sp", 1)
    gate = modulate[2:3]
    gates = jnp.concatenate([gate, from_partner(gate, "cfg", 1)], axis=0)

    packed = after(packed, (first, second))
    context = lax.all_to_all(packed, ("sp", "cfg"), split_axis=0, concat_axis=0, tiled=True)
    context = context.reshape(devices * context_rows, 2 * width)

    heads = project(
        (own, across, along, first, second),
        (own_core, across_core, along_core, first_core, second_core),
        project_in[0],
        gates,
    )
    attended = attend(heads, context, visible[0])

    weights = project_out[0]
    count = COLUMN_CHUNKS
    chunk = features // count
    received = [from_partner(part, "sp", 1) for part in sent_products(attended, weights, chunk)]
    kept, left, flights, result, arrivals, earlier = {}, {}, {}, [], [], []
    for index in range(-2, count + 2):
        fresh, middle, final = index + 2 < count, 0 <= index < count, index >= 2
        operands = {"rows": current, "gates": gates}
        if fresh:
            operands["attended"], operands["weights"] = attended, weights
            operands["received"] = received[min(index + 2, 1)]
        if index >= 0:
            operands["across"], operands["along"] = flights.pop(index)
        if middle:
            operands["first_kept"], operands["second_kept"] = kept.pop(index)
        if final:
            operands["first_left"], operands["second_left"] = left.pop(index - 2)
        outs = stage(
            operands,
            earlier,
            chunk,
            max(index, 0) * chunk,
            (index + 2) * chunk,
            max(index + 1, 0),
            fresh,
            middle,
            final,
        )
        if "across_out" in outs:
            flights[index + 2] = (
                from_partner(outs["across_out"], "cfg", 1),
                from_partner(outs["along_out"], "sp", 2),
            )
        if fresh:
            kept[index + 2] = (outs["first_kept_out"], outs["second_kept_out"])
        if middle:
            left[index] = (outs["first_left_out"], outs["second_left_out"])
        if final:
            arrived = from_behind(outs["done_out"], "pipe", 1)
            whole = result[-1] if result else None
            result.append(place(arrived, whole, features, (index - 2) * chunk, []))
            arrivals.append(arrived)
        earlier = [list(outs.values())[-1]] + (arrivals[-2:-1] if 3 <= index < count else [])
    return result[-1][None, None]


def solution(mesh):
    placed = (
        P("pipe", "cfg", "sp", None),
        P("pipe", "cfg", None, None),
        P("pipe", None, None, ("sp", "cfg")),
        P("pipe", ("sp", "cfg"), None),
        P("pipe", "cfg", "sp", None, None),
        P("pipe", None, None),
    )
    return jax.shard_map(
        per_device,
        mesh=mesh,
        in_specs=placed,
        out_specs=P("pipe", "cfg", "sp", None),
        check_vma=False,
    )
```

```python
import functools

import jax
import jax.numpy as jnp
from jax import lax
from jax.experimental import pallas as pl
from jax.experimental.pallas import tpu as pltpu
from jax.sharding import PartitionSpec as P

HD = 128
TILE = 128
MIB = 2**20
COLUMN_CHUNKS = 5

guidance_scale = 5.0
SHORT = pl.CostEstimate(flops=1, bytes_accessed=1, transcendentals=0)


def from_behind(x, axis, by):
    count = lax.axis_size(axis)
    return lax.ppermute(x, axis, [(i, (i + by) % count) for i in range(count)])


def from_partner(value, axis, mask):
    pairs = [(source, source ^ mask) for source in range(lax.axis_size(axis))]
    return lax.ppermute(value, axis, pairs)


def norm_kernel(rows_ref, modulation_ref, out_ref):
    step = 16

    def body(index, carry):
        rows = pl.ds(pl.multiple_of(index * step, step), step)
        values = rows_ref[rows, :].astype(jnp.float32)
        centre = values - jnp.mean(values, axis=-1, keepdims=True)
        spread = jnp.mean(centre * centre, axis=-1, keepdims=True)
        normed = centre * lax.rsqrt(spread + 1e-06)
        out_ref[rows, :] = (
            normed * (1.0 + modulation_ref[1:2, :]) + modulation_ref[0:1, :]
        ).astype(jnp.bfloat16)
        return carry

    lax.fori_loop(0, rows_ref.shape[0] // step, body, 0)


def modulated_norm(rows, modulation):
    return pl.pallas_call(
        norm_kernel,
        out_shape=jax.ShapeDtypeStruct(rows.shape, jnp.bfloat16),
        name="modulated_norm",
        cost_estimate=pl.CostEstimate(
            flops=10 * rows.size, bytes_accessed=4 * rows.size, transcendentals=0
        ),
        compiler_params=pltpu.CompilerParams(vmem_limit_bytes=16 * MIB),
    )(rows, modulation)


def gate_kernel(value_ref, *refs):
    pass


def after(value, earlier):
    return pl.pallas_call(
        gate_kernel,
        in_specs=[pl.BlockSpec(memory_space=pl.ANY)] * (1 + len(earlier)),
        out_specs=pl.BlockSpec(memory_space=pl.ANY),
        out_shape=jax.ShapeDtypeStruct(value.shape, value.dtype),
        input_output_aliases={0: 0},
        name="after",
        cost_estimate=SHORT,
    )(value, *earlier)


def project_kernel(*refs, halves):
    weights_ref, out_ref, total_ref = refs[sum(halves)], refs[-2], refs[-1]
    step, steps = pl.program_id(0), pl.num_programs(0)
    weights = jnp.concatenate([weights_ref[0], weights_ref[1], weights_ref[2]], axis=1)
    early = step < steps // 2
    blocks, place = [], 0
    for count in halves:
        if count == 1:
            blocks.append(refs[place][...])
        else:
            blocks.append(jnp.where(early, refs[place][...], refs[place + 1][...]))
        place += count
    rows = jnp.concatenate(blocks, axis=0)
    product = jnp.dot(rows, weights, preferred_element_type=jnp.float32)

    @pl.when(step == 0)
    def _():
        total_ref[...] = product

    @pl.when(step > 0)
    def _():
        total_ref[...] += product

    @pl.when(step == steps - 1)
    def _():
        width = weights_ref.shape[2]
        for head in range(2 * width // HD):
            columns = slice(head * HD, (head + 1) * HD)
            values = total_ref[:, columns]
            scale = lax.rsqrt(jnp.mean(values * values, axis=-1, keepdims=True) + 1e-06)
            out_ref[:, columns] = (values * scale).astype(jnp.bfloat16)
        out_ref[:, 2 * width :] = total_ref[:, 2 * width :].astype(jnp.bfloat16)


def project(blocks, weights, earlier):
    _, depth, width = weights.shape
    rows = blocks[0][0].shape[0]
    steps = 4
    block = depth // steps
    count = len(blocks) * rows
    whole = pl.BlockSpec((rows, block), lambda k: (0, k))
    first = pl.BlockSpec((rows, block), lambda k: (0, jnp.minimum(k, steps // 2 - 1)))
    second = pl.BlockSpec((rows, block), lambda k: (0, jnp.maximum(k - steps // 2, 0)))
    specs = [spec for parts in blocks for spec in ([whole] if len(parts) == 1 else [first, second])]
    return pl.pallas_call(
        functools.partial(project_kernel, halves=[len(parts) for parts in blocks]),
        grid=(steps,),
        in_specs=specs
        + [pl.BlockSpec((3, block, width), lambda k: (0, k, 0))]
        + [pl.BlockSpec(memory_space=pl.ANY)] * len(earlier),
        out_specs=pl.BlockSpec((count, 3 * width), lambda k: (0, 0)),
        out_shape=jax.ShapeDtypeStruct((count, 3 * width), jnp.bfloat16),
        scratch_shapes=[pltpu.VMEM((count, 3 * width), jnp.float32)],
        name="project_heads",
        cost_estimate=pl.CostEstimate(
            flops=2 * count * depth * 3 * width,
            bytes_accessed=2 * (count * depth + weights.size),
            transcendentals=0,
        ),
        compiler_params=pltpu.CompilerParams(vmem_limit_bytes=30 * MIB),
    )(*[part for parts in blocks for part in parts], weights, *earlier)


def attend_kernel(visible_ref, heads_ref, context_ref, *refs, first_block):
    out_ref = refs[-1]
    width = out_ref.shape[1]
    tiles_seen = visible_ref.shape[1]
    tiles_fresh = visible_ref.shape[0]
    mine_high, mine_low = lax.axis_index("sp") // 2, lax.axis_index("sp") % 2
    mine_branch = lax.axis_index("cfg")

    def body(step, carry):
        index = first_block + step
        high, low = mine_high ^ ((index // 2) % 2), mine_low ^ (index // 4)
        tile, branch = high * 2 + low, mine_branch ^ (index % 2)
        rows = pl.ds(pl.multiple_of(index * TILE, TILE), TILE)
        out_rows = pl.ds(pl.multiple_of(step * TILE, TILE), TILE)
        places = []
        for seen in range(tiles_seen):
            number = visible_ref[tile, seen]
            older = jnp.maximum(number - tiles_fresh, 0)
            fresh = (mine_low ^ (number % 2)) * 4 + (mine_high ^ ((number // 2) % 2)) * 2
            fresh = (fresh + index % 2) * TILE
            stale = ((older // 2) * 2 + branch) * 2 * TILE + (older % 2) * TILE
            places.append(
                (
                    number < tiles_fresh,
                    pl.ds(pl.multiple_of(fresh, TILE), TILE),
                    pl.ds(pl.multiple_of(stale, TILE), TILE),
                )
            )

        def tiles(kind, head):
            fresh_columns = slice(kind * width + head * HD, kind * width + (head + 1) * HD)
            start = (kind - 1) * width + head * HD
            return jnp.concatenate(
                [
                    jnp.where(
                        is_fresh, heads_ref[fresh, fresh_columns], context_ref[stale, start : start + HD]
                    )
                    for is_fresh, fresh, stale in places
                ],
                axis=0,
            )

        for head in range(width // HD):
            columns = slice(head * HD, (head + 1) * HD)
            scores = lax.dot_general(
                heads_ref[rows, columns],
                tiles(1, head),
                (((1,), (1,)), ((), ())),
                preferred_element_type=jnp.float32,
            )
            exponent = jnp.exp(scores * HD ** (-0.5))
            total = jnp.sum(exponent, axis=-1, keepdims=True)
            mixed = jnp.dot(
                exponent.astype(jnp.bfloat16), tiles(2, head), preferred_element_type=jnp.float32
            )
            out_ref[out_rows, columns] = (mixed / total).astype(jnp.bfloat16)
        return carry

    lax.fori_loop(0, out_ref.shape[0] // TILE, body, 0)


def attend(heads, context, visible, first_block, earlier):
    count = heads.shape[0] // 2
    width = heads.shape[1] // 3
    return pl.pallas_call(
        functools.partial(attend_kernel, first_block=first_block),
        in_specs=[
            pl.BlockSpec(memory_space=pltpu.SMEM),
            pl.BlockSpec(memory_space=pltpu.VMEM),
            pl.BlockSpec(memory_space=pltpu.VMEM),
        ]
        + [pl.BlockSpec(memory_space=pl.ANY)] * len(earlier),
        out_shape=jax.ShapeDtypeStruct((count, width), jnp.bfloat16),
        name="attend",
        cost_estimate=pl.CostEstimate(
            flops=4 * count * visible.shape[1] * TILE * width,
            bytes_accessed=2 * (heads.size + context.size),
            transcendentals=count * visible.shape[1] * TILE * width // HD,
        ),
        compiler_params=pltpu.CompilerParams(vmem_limit_bytes=32 * MIB),
    )(visible, heads, context, *earlier)


def half_kernel(rows_ref, *refs, start):
    out_ref = refs[-1]
    out_ref[...] = rows_ref[:, start : start + out_ref.shape[1]]


def half_of(rows, start, earlier):
    return pl.pallas_call(
        functools.partial(half_kernel, start=start),
        in_specs=[pl.BlockSpec(memory_space=pltpu.VMEM)]
        + [pl.BlockSpec(memory_space=pl.ANY)] * len(earlier),
        out_shape=jax.ShapeDtypeStruct((rows.shape[0], rows.shape[1] // 2), rows.dtype),
        name="half_of",
        cost_estimate=SHORT,
        compiler_params=pltpu.CompilerParams(vmem_limit_bytes=8 * MIB),
    )(rows, *earlier)


def combined(own, other, mine, gates_ref, columns):
    conditional = lax.axis_index("cfg") == 1
    last = lax.axis_index("pipe") == lax.axis_size("pipe") - 1
    weight = jnp.where(conditional, guidance_scale, 1.0 - guidance_scale).astype(jnp.float32)
    other_weight = jnp.where(conditional, 1.0 - guidance_scale, guidance_scale).astype(jnp.float32)
    own = own * gates_ref[0:1, columns]
    other = other * gates_ref[1:2, columns]
    if mine is not None:
        own = own + mine
    guided = weight * own + other_weight * other
    return jnp.where(last, guided, other), jnp.where(last, guided, own)


def begin(start, refs, across_out, along_out, first_kept, second_kept):
    attended_ref, core_attended_ref, weights_ref, core_weights_ref, rows_ref, gates_ref = refs
    tokens, half = rows_ref.shape[0], first_kept.shape[2]
    attended = jnp.concatenate([attended_ref[...], core_attended_ref[...]], axis=1)

    def product_of(columns):
        weights = jnp.concatenate([weights_ref[:, columns], core_weights_ref[:, columns]], axis=0)
        return jnp.dot(attended, weights, preferred_element_type=jnp.float32)

    columns = slice(start, start + half)
    product = product_of(columns)
    for tile in range(2):
        own = product[2 * tile * tokens : (2 * tile + 1) * tokens]
        other = product[(2 * tile + 1) * tokens : (2 * tile + 2) * tokens]
        mine = rows_ref[:, columns].astype(jnp.float32) if tile == 0 else None
        sent, kept = combined(own, other, mine, gates_ref, columns)
        across_out[tile] = sent.astype(jnp.bfloat16)
        first_kept[tile] = kept
    columns = slice(start + half, start + 2 * half)
    product = product_of(columns)
    for branch in range(2):
        second_kept[branch] = product[branch * tokens : (branch + 1) * tokens]
        along_out[branch] = product[(branch + 2) * tokens : (branch + 3) * tokens].astype(
            jnp.bfloat16
        )


def stage_kernel(*refs, parts, start, next_start, fresh, middle, final):
    named = dict(zip(parts, refs))
    if fresh:
        begin(
            next_start,
            [
                named[name]
                for name in (
                    "attended", "core_attended", "weights", "core_weights", "rows", "gates"
                )
            ],
            named["across_out"],
            named["along_out"],
            named["first_kept_out"],
            named["second_kept_out"],
        )
    if middle:
        across, along = named["across"], named["along"]
        first_kept, second_kept = named["first_kept"], named["second_kept"]
        half = first_kept.shape[2]
        place = 2 if fresh else 0
        named["along_out"][place] = (first_kept[1] + across[1].astype(jnp.float32)).astype(
            jnp.bfloat16
        )
        named["first_left_out"][...] = first_kept[0] + across[0].astype(jnp.float32)
        columns = slice(start + half, start + 2 * half)
        sent, kept = combined(
            second_kept[0] + along[0].astype(jnp.float32),
            second_kept[1] + along[1].astype(jnp.float32),
            named["rows"][:, columns].astype(jnp.float32),
            named["gates"],
            columns,
        )
        named["across_out"][place] = sent.astype(jnp.bfloat16)
        named["second_left_out"][...] = kept
    if final:
        across, along = named["across"], named["along"]
        first_left, second_left = named["first_left"], named["second_left"]
        half = first_left.shape[1]
        place = 2 if middle else 0
        named["done_out"][:, :half] = (
            first_left[...] + along[place].astype(jnp.float32)
        ).astype(jnp.bfloat16)
        named["done_out"][:, half:] = (
            second_left[...] + across[place].astype(jnp.float32)
        ).astype(jnp.bfloat16)


def stage(operands, earlier, chunk, start, next_start, fresh, middle, final):
    tokens, half = operands["rows"].shape[0], chunk // 2
    outs = {}
    if fresh or middle:
        pieces = 2 * fresh + middle
        outs["across_out"] = jax.ShapeDtypeStruct((pieces, tokens, half), jnp.bfloat16)
        outs["along_out"] = outs["across_out"]
    if fresh:
        outs["first_kept_out"] = jax.ShapeDtypeStruct((2, tokens, half), jnp.float32)
        outs["second_kept_out"] = outs["first_kept_out"]
    if middle:
        outs["first_left_out"] = jax.ShapeDtypeStruct((tokens, half), jnp.float32)
        outs["second_left_out"] = outs["first_left_out"]
    if final:
        outs["done_out"] = jax.ShapeDtypeStruct((tokens, chunk), jnp.bfloat16)
    parts = list(operands) + ["earlier"] * len(earlier) + list(outs)
    results = pl.pallas_call(
        functools.partial(
            stage_kernel,
            parts=parts,
            start=start,
            next_start=next_start,
            fresh=fresh,
            middle=middle,
            final=final,
        ),
        in_specs=[pl.BlockSpec(memory_space=pltpu.VMEM)] * len(operands)
        + [pl.BlockSpec(memory_space=pl.ANY)] * len(earlier),
        out_shape=list(outs.values()),
        name="sum_stage",
        cost_estimate=SHORT,
        compiler_params=pltpu.CompilerParams(vmem_limit_bytes=24 * MIB),
    )(*operands.values(), *earlier)
    return dict(zip(outs, results))


def per_device(flight, modulation, project_in, project_out, stale_cache, visible):
    current = flight[0, 0]
    modulate = modulation[0, 0]
    token_rows, features = current.shape
    devices = lax.axis_size("sp") * lax.axis_size("cfg")

    context_rows = stale_cache.shape[2]
    width = project_in.shape[3]
    packed = stale_cache[0, 0].reshape(context_rows, 2, devices, width)
    packed = packed.transpose(2, 0, 1, 3).reshape(devices, context_rows, 2 * width)

    own = modulated_norm(current, modulate)
    across = from_partner(own, "cfg", 1)
    along = from_partner(own, "sp", 2)
    own_core = from_partner(own, "sp", 1)
    middle = features // 2
    gate = modulate[2:3]
    other_gate = from_partner(gate, "cfg", 1)
    across, along = after(across, (packed,)), after(along, (packed, other_gate))
    first = from_partner(half_of(across, 0, ()), "sp", 2)
    second = from_partner(half_of(along, middle, ()), "cfg", 1)
    gates = jnp.concatenate([gate, other_gate], axis=0)
    core_weights = from_partner(project_out[0], "sp", 1)
    near = [(own,), (across,), (along,), (first, second)]
    far = [(own_core,)] + [
        tuple(from_partner(part, "sp", 1) for part in parts) for parts in near[1:]
    ]

    packed = after(packed, far[2])
    context = lax.all_to_all(packed, ("sp", "cfg"), split_axis=0, concat_axis=0, tiled=True)
    context = context.reshape(devices * context_rows, 2 * width)

    heads = project(near + far, project_in[0], (core_weights,))
    for_core = attend(heads, context, visible[0], 4, ())
    core_attended = from_partner(for_core, "sp", 1)
    attended = attend(heads, context, visible[0], 0, (for_core,))

    weights = project_out[0]
    count = COLUMN_CHUNKS
    chunk = features // count
    kept, left, flights, arrivals, earlier = {}, {}, {}, [], []
    for index in range(-2, count + 2):
        fresh, middle, final = index + 2 < count, 0 <= index < count, index >= 2
        operands = {"rows": current, "gates": gates}
        if fresh:
            operands["attended"], operands["core_attended"] = attended, core_attended
            operands["weights"], operands["core_weights"] = weights, core_weights
        if index >= 0:
            operands["across"], operands["along"] = flights.pop(index)
        if middle:
            operands["first_kept"], operands["second_kept"] = kept.pop(index)
        if final:
            operands["first_left"], operands["second_left"] = left.pop(index - 2)
        outs = stage(
            operands,
            earlier,
            chunk,
            max(index, 0) * chunk,
            (index + 2) * chunk,
            fresh,
            middle,
            final,
        )
        if "across_out" in outs:
            flights[index + 2] = (
                from_partner(outs["across_out"], "cfg", 1),
                from_partner(outs["along_out"], "sp", 2),
            )
        if fresh:
            kept[index + 2] = (outs["first_kept_out"], outs["second_kept_out"])
        if middle:
            left[index] = (outs["first_left_out"], outs["second_left_out"])
        if final:
            arrivals.append(from_behind(outs["done_out"], "pipe", 1))
        earlier = [list(outs.values())[-1]] + (arrivals[-2:-1] if 3 <= index < count else [])
    return jnp.concatenate(arrivals, axis=1)[None, None]


def solution(mesh):
    placed = (
        P("pipe", "cfg", "sp", None),
        P("pipe", "cfg", None, None),
        P("pipe", None, None, ("sp", "cfg")),
        P("pipe", ("sp", "cfg"), None),
        P("pipe", "cfg", "sp", None, None),
        P("pipe", None, None),
    )
    return jax.shard_map(
        per_device,
        mesh=mesh,
        in_specs=placed,
        out_specs=P("pipe", "cfg", "sp", None),
        check_vma=False,
    )
```

```python
import functools

import jax
import jax.numpy as jnp
from jax import lax
from jax.experimental import pallas as pl
from jax.experimental.pallas import tpu as pltpu
from jax.sharding import PartitionSpec as P

HD = 128
TILE = 128
MIB = 2**20
COLUMN_CHUNKS = 5

guidance_scale = 5.0
SHORT = pl.CostEstimate(flops=1, bytes_accessed=1, transcendentals=0)


def from_behind(x, axis, by):
    count = lax.axis_size(axis)
    return lax.ppermute(x, axis, [(i, (i + by) % count) for i in range(count)])


def from_partner(value, axis, mask):
    pairs = [(source, source ^ mask) for source in range(lax.axis_size(axis))]
    return lax.ppermute(value, axis, pairs)


def norm_kernel(rows_ref, modulation_ref, out_ref):
    step = 16

    def body(index, carry):
        rows = pl.ds(pl.multiple_of(index * step, step), step)
        values = rows_ref[rows, :].astype(jnp.float32)
        centre = values - jnp.mean(values, axis=-1, keepdims=True)
        spread = jnp.mean(centre * centre, axis=-1, keepdims=True)
        normed = centre * lax.rsqrt(spread + 1e-06)
        out_ref[rows, :] = (
            normed * (1.0 + modulation_ref[1:2, :]) + modulation_ref[0:1, :]
        ).astype(jnp.bfloat16)
        return carry

    lax.fori_loop(0, rows_ref.shape[0] // step, body, 0)


def modulated_norm(rows, modulation):
    return pl.pallas_call(
        norm_kernel,
        out_shape=jax.ShapeDtypeStruct(rows.shape, jnp.bfloat16),
        name="modulated_norm",
        cost_estimate=pl.CostEstimate(
            flops=10 * rows.size, bytes_accessed=4 * rows.size, transcendentals=0
        ),
        compiler_params=pltpu.CompilerParams(vmem_limit_bytes=16 * MIB),
    )(rows, modulation)


def gate_kernel(value_ref, *refs):
    pass


def after(value, earlier):
    return pl.pallas_call(
        gate_kernel,
        in_specs=[pl.BlockSpec(memory_space=pl.ANY)] * (1 + len(earlier)),
        out_specs=pl.BlockSpec(memory_space=pl.ANY),
        out_shape=jax.ShapeDtypeStruct(value.shape, value.dtype),
        input_output_aliases={0: 0},
        name="after",
        cost_estimate=SHORT,
    )(value, *earlier)


def project_kernel(*refs, halves):
    weights_ref, out_ref, total_ref = refs[sum(halves)], refs[-2], refs[-1]
    step, steps = pl.program_id(0), pl.num_programs(0)
    weights = jnp.concatenate([weights_ref[0], weights_ref[1], weights_ref[2]], axis=1)
    early, block = step < steps // 2, weights.shape[0]
    columns = pl.ds(pl.multiple_of(step * block, block), block)
    half_columns = pl.ds(pl.multiple_of(step % (steps // 2) * block, block), block)
    blocks, place = [], 0
    for count in halves:
        if count == 1:
            blocks.append(refs[place][:, columns])
        else:
            parts = refs[place][:, half_columns], refs[place + 1][:, half_columns]
            blocks.append(jnp.where(early, *parts))
        place += count
    rows = jnp.concatenate(blocks, axis=0)
    product = jnp.dot(rows, weights, preferred_element_type=jnp.float32)

    @pl.when(step == 0)
    def _():
        total_ref[...] = product

    @pl.when(step > 0)
    def _():
        total_ref[...] += product

    @pl.when(step == steps - 1)
    def _():
        width = weights_ref.shape[2]
        for head in range(2 * width // HD):
            columns = slice(head * HD, (head + 1) * HD)
            values = total_ref[:, columns]
            scale = lax.rsqrt(jnp.mean(values * values, axis=-1, keepdims=True) + 1e-06)
            out_ref[:, columns] = (values * scale).astype(jnp.bfloat16)
        out_ref[:, 2 * width :] = total_ref[:, 2 * width :].astype(jnp.bfloat16)


def project(blocks, weights, earlier):
    _, depth, width = weights.shape
    rows = blocks[0][0].shape[0]
    steps = 4
    block = depth // steps
    count = len(blocks) * rows
    return pl.pallas_call(
        functools.partial(project_kernel, halves=[len(parts) for parts in blocks]),
        grid=(steps,),
        in_specs=[pl.BlockSpec(memory_space=pltpu.VMEM)] * sum(len(parts) for parts in blocks)
        + [pl.BlockSpec((3, block, width), lambda k: (0, k, 0))]
        + [pl.BlockSpec(memory_space=pl.ANY)] * len(earlier),
        out_specs=pl.BlockSpec((count, 3 * width), lambda k: (0, 0)),
        out_shape=jax.ShapeDtypeStruct((count, 3 * width), jnp.bfloat16),
        scratch_shapes=[pltpu.VMEM((count, 3 * width), jnp.float32)],
        name="project_heads",
        cost_estimate=pl.CostEstimate(
            flops=2 * count * depth * 3 * width,
            bytes_accessed=2 * (count * depth + weights.size),
            transcendentals=0,
        ),
        compiler_params=pltpu.CompilerParams(vmem_limit_bytes=26 * MIB),
    )(*[part for parts in blocks for part in parts], weights, *earlier)


def attend_kernel(visible_ref, heads_ref, context_ref, *refs, first_block):
    out_ref = refs[-1]
    width = out_ref.shape[1]
    tiles_seen = visible_ref.shape[1]
    tiles_fresh = visible_ref.shape[0]
    mine_high, mine_low = lax.axis_index("sp") // 2, lax.axis_index("sp") % 2
    mine_branch = lax.axis_index("cfg")

    def body(step, carry):
        index = first_block + step
        high, low = mine_high ^ ((index // 2) % 2), mine_low ^ (index // 4)
        tile, branch = high * 2 + low, mine_branch ^ (index % 2)
        rows = pl.ds(pl.multiple_of(index * TILE, TILE), TILE)
        out_rows = pl.ds(pl.multiple_of(step * TILE, TILE), TILE)
        places = []
        for seen in range(tiles_seen):
            number = visible_ref[tile, seen]
            older = jnp.maximum(number - tiles_fresh, 0)
            fresh = (mine_low ^ (number % 2)) * 4 + (mine_high ^ ((number // 2) % 2)) * 2
            fresh = (fresh + index % 2) * TILE
            stale = ((older // 2) * 2 + branch) * 2 * TILE + (older % 2) * TILE
            places.append(
                (
                    number < tiles_fresh,
                    pl.ds(pl.multiple_of(fresh, TILE), TILE),
                    pl.ds(pl.multiple_of(stale, TILE), TILE),
                )
            )

        def tiles(kind, head):
            fresh_columns = slice(kind * width + head * HD, kind * width + (head + 1) * HD)
            start = (kind - 1) * width + head * HD
            return jnp.concatenate(
                [
                    jnp.where(
                        is_fresh, heads_ref[fresh, fresh_columns], context_ref[stale, start : start + HD]
                    )
                    for is_fresh, fresh, stale in places
                ],
                axis=0,
            )

        for head in range(width // HD):
            columns = slice(head * HD, (head + 1) * HD)
            scores = lax.dot_general(
                heads_ref[rows, columns],
                tiles(1, head),
                (((1,), (1,)), ((), ())),
                preferred_element_type=jnp.float32,
            )
            exponent = jnp.exp(scores * HD ** (-0.5))
            total = jnp.sum(exponent, axis=-1, keepdims=True)
            mixed = jnp.dot(
                exponent.astype(jnp.bfloat16), tiles(2, head), preferred_element_type=jnp.float32
            )
            out_ref[out_rows, columns] = (mixed / total).astype(jnp.bfloat16)
        return carry

    lax.fori_loop(0, out_ref.shape[0] // TILE, body, 0)


def attend(heads, context, visible, first_block, earlier):
    count = heads.shape[0] // 2
    width = heads.shape[1] // 3
    return pl.pallas_call(
        functools.partial(attend_kernel, first_block=first_block),
        in_specs=[
            pl.BlockSpec(memory_space=pltpu.SMEM),
            pl.BlockSpec(memory_space=pltpu.VMEM),
            pl.BlockSpec(memory_space=pltpu.VMEM),
        ]
        + [pl.BlockSpec(memory_space=pl.ANY)] * len(earlier),
        out_shape=jax.ShapeDtypeStruct((count, width), jnp.bfloat16),
        name="attend",
        cost_estimate=pl.CostEstimate(
            flops=4 * count * visible.shape[1] * TILE * width,
            bytes_accessed=2 * (heads.size + context.size),
            transcendentals=count * visible.shape[1] * TILE * width // HD,
        ),
        compiler_params=pltpu.CompilerParams(vmem_limit_bytes=16 * MIB),
    )(visible, heads, context, *earlier)


def half_kernel(rows_ref, *refs, start):
    out_ref = refs[-1]
    out_ref[...] = rows_ref[:, start : start + out_ref.shape[1]]


def half_of(rows, start, earlier):
    return pl.pallas_call(
        functools.partial(half_kernel, start=start),
        in_specs=[pl.BlockSpec(memory_space=pltpu.VMEM)]
        + [pl.BlockSpec(memory_space=pl.ANY)] * len(earlier),
        out_shape=jax.ShapeDtypeStruct((rows.shape[0], rows.shape[1] // 2), rows.dtype),
        name="half_of",
        cost_estimate=SHORT,
        compiler_params=pltpu.CompilerParams(vmem_limit_bytes=8 * MIB),
    )(rows, *earlier)


def combined(own, other, mine, gates_ref, columns):
    conditional = lax.axis_index("cfg") == 1
    last = lax.axis_index("pipe") == lax.axis_size("pipe") - 1
    weight = jnp.where(conditional, guidance_scale, 1.0 - guidance_scale).astype(jnp.float32)
    other_weight = jnp.where(conditional, 1.0 - guidance_scale, guidance_scale).astype(jnp.float32)
    own = own * gates_ref[0:1, columns]
    other = other * gates_ref[1:2, columns]
    if mine is not None:
        own = own + mine
    guided = weight * own + other_weight * other
    return jnp.where(last, guided, other), jnp.where(last, guided, own)


def begin(start, refs, across_out, along_out, first_kept, second_kept):
    attended_ref, core_attended_ref, weights_ref, core_weights_ref, rows_ref, gates_ref = refs
    tokens, half = rows_ref.shape[0], first_kept.shape[2]

    def product_of(columns):
        near = jnp.dot(
            attended_ref[...], weights_ref[:, columns], preferred_element_type=jnp.float32
        )
        return near + jnp.dot(
            core_attended_ref[...], core_weights_ref[:, columns], preferred_element_type=jnp.float32
        )

    columns = slice(start, start + half)
    product = product_of(columns)
    for tile in range(2):
        own = product[2 * tile * tokens : (2 * tile + 1) * tokens]
        other = product[(2 * tile + 1) * tokens : (2 * tile + 2) * tokens]
        mine = rows_ref[:, columns].astype(jnp.float32) if tile == 0 else None
        sent, kept = combined(own, other, mine, gates_ref, columns)
        across_out[tile] = sent.astype(jnp.bfloat16)
        first_kept[tile] = kept
    columns = slice(start + half, start + 2 * half)
    product = product_of(columns)
    for branch in range(2):
        second_kept[branch] = product[branch * tokens : (branch + 1) * tokens]
        along_out[branch] = product[(branch + 2) * tokens : (branch + 3) * tokens].astype(
            jnp.bfloat16
        )


def stage_kernel(*refs, parts, start, next_start, fresh, middle, final):
    named = dict(zip(parts, refs))
    if fresh:
        begin(
            next_start,
            [
                named[name]
                for name in (
                    "attended", "core_attended", "weights", "core_weights", "rows", "gates"
                )
            ],
            named["across_out"],
            named["along_out"],
            named["first_kept_out"],
            named["second_kept_out"],
        )
    if middle:
        across, along = named["across"], named["along"]
        first_kept, second_kept = named["first_kept"], named["second_kept"]
        half = first_kept.shape[2]
        place = 2 if fresh else 0
        named["along_out"][place] = (first_kept[1] + across[1].astype(jnp.float32)).astype(
            jnp.bfloat16
        )
        named["first_left_out"][...] = first_kept[0] + across[0].astype(jnp.float32)
        columns = slice(start + half, start + 2 * half)
        sent, kept = combined(
            second_kept[0] + along[0].astype(jnp.float32),
            second_kept[1] + along[1].astype(jnp.float32),
            named["rows"][:, columns].astype(jnp.float32),
            named["gates"],
            columns,
        )
        named["across_out"][place] = sent.astype(jnp.bfloat16)
        named["second_left_out"][...] = kept
    if final:
        across, along = named["across"], named["along"]
        first_left, second_left = named["first_left"], named["second_left"]
        half = first_left.shape[1]
        place = 2 if middle else 0
        named["done_out"][:, :half] = (
            first_left[...] + along[place].astype(jnp.float32)
        ).astype(jnp.bfloat16)
        named["done_out"][:, half:] = (
            second_left[...] + across[place].astype(jnp.float32)
        ).astype(jnp.bfloat16)


def stage(operands, earlier, chunk, start, next_start, fresh, middle, final):
    tokens, half = operands["rows"].shape[0], chunk // 2
    outs = {}
    if fresh or middle:
        pieces = 2 * fresh + middle
        outs["across_out"] = jax.ShapeDtypeStruct((pieces, tokens, half), jnp.bfloat16)
        outs["along_out"] = outs["across_out"]
    if fresh:
        outs["first_kept_out"] = jax.ShapeDtypeStruct((2, tokens, half), jnp.float32)
        outs["second_kept_out"] = outs["first_kept_out"]
    if middle:
        outs["first_left_out"] = jax.ShapeDtypeStruct((tokens, half), jnp.float32)
        outs["second_left_out"] = outs["first_left_out"]
    if final:
        outs["done_out"] = jax.ShapeDtypeStruct((tokens, chunk), jnp.bfloat16)
    parts = list(operands) + ["earlier"] * len(earlier) + list(outs)
    results = pl.pallas_call(
        functools.partial(
            stage_kernel,
            parts=parts,
            start=start,
            next_start=next_start,
            fresh=fresh,
            middle=middle,
            final=final,
        ),
        in_specs=[pl.BlockSpec(memory_space=pltpu.VMEM)] * len(operands)
        + [pl.BlockSpec(memory_space=pl.ANY)] * len(earlier),
        out_shape=list(outs.values()),
        name="sum_stage",
        cost_estimate=SHORT,
        compiler_params=pltpu.CompilerParams(vmem_limit_bytes=16 * MIB),
    )(*operands.values(), *earlier)
    return dict(zip(outs, results))


def per_device(flight, modulation, project_in, project_out, stale_cache, visible):
    current = flight[0, 0]
    modulate = modulation[0, 0]
    token_rows, features = current.shape
    devices = lax.axis_size("sp") * lax.axis_size("cfg")

    context_rows = stale_cache.shape[2]
    width = project_in.shape[3]
    packed = stale_cache[0, 0].reshape(context_rows, 2, devices, width)
    packed = packed.transpose(2, 0, 1, 3).reshape(devices, context_rows, 2 * width)

    own = modulated_norm(current, modulate)
    across = from_partner(own, "cfg", 1)
    along = from_partner(own, "sp", 2)
    own_core = from_partner(own, "sp", 1)
    middle = features // 2
    gate = modulate[2:3]
    other_gate = from_partner(gate, "cfg", 1)
    halves = half_of(across, 0, (packed,)), half_of(along, middle, (packed,))
    first = from_partner(halves[0], "sp", 2)
    second = from_partner(halves[1], "cfg", 1)
    gates = jnp.concatenate([gate, other_gate], axis=0)
    core_weights = from_partner(project_out[0], "sp", 1)
    near = [(own,), (across,), (along,), (first, second)]
    far = [(own_core,)] + [
        tuple(from_partner(part, "sp", 1) for part in parts) for parts in near[1:]
    ]

    packed = after(packed, (first, second, other_gate))
    context = lax.all_to_all(packed, ("sp", "cfg"), split_axis=0, concat_axis=0, tiled=True)
    context = context.reshape(devices * context_rows, 2 * width)

    heads = project(near + far, project_in[0], (core_weights,))
    for_core = attend(heads, context, visible[0], 4, ())
    core_attended = from_partner(for_core, "sp", 1)
    attended = attend(heads, context, visible[0], 0, (for_core,))

    weights = project_out[0]
    count = COLUMN_CHUNKS
    chunk = features // count
    kept, left, flights, arrivals, earlier = {}, {}, {}, [], []
    for index in range(-2, count + 2):
        fresh, middle, final = index + 2 < count, 0 <= index < count, index >= 2
        operands = {"rows": current, "gates": gates}
        if fresh:
            operands["attended"], operands["core_attended"] = attended, core_attended
            operands["weights"], operands["core_weights"] = weights, core_weights
        if index >= 0:
            operands["across"], operands["along"] = flights.pop(index)
        if middle:
            operands["first_kept"], operands["second_kept"] = kept.pop(index)
        if final:
            operands["first_left"], operands["second_left"] = left.pop(index - 2)
        outs = stage(
            operands,
            earlier,
            chunk,
            max(index, 0) * chunk,
            (index + 2) * chunk,
            fresh,
            middle,
            final,
        )
        if "across_out" in outs:
            flights[index + 2] = (
                from_partner(outs["across_out"], "cfg", 1),
                from_partner(outs["along_out"], "sp", 2),
            )
        if fresh:
            kept[index + 2] = (outs["first_kept_out"], outs["second_kept_out"])
        if middle:
            left[index] = (outs["first_left_out"], outs["second_left_out"])
        if final:
            arrivals.append(from_behind(outs["done_out"], "pipe", 1))
        earlier = [list(outs.values())[-1]] + (arrivals[-2:-1] if 3 <= index < count else [])
    return jnp.concatenate(arrivals, axis=1)[None, None]


def solution(mesh):
    placed = (
        P("pipe", "cfg", "sp", None),
        P("pipe", "cfg", None, None),
        P("pipe", None, None, ("sp", "cfg")),
        P("pipe", ("sp", "cfg"), None),
        P("pipe", "cfg", "sp", None, None),
        P("pipe", None, None),
    )
    return jax.shard_map(
        per_device,
        mesh=mesh,
        in_specs=placed,
        out_specs=P("pipe", "cfg", "sp", None),
        check_vma=False,
    )
```

```python
import functools

import jax
import jax.numpy as jnp
from jax import lax
from jax.experimental import pallas as pl
from jax.experimental.pallas import tpu as pltpu
from jax.sharding import PartitionSpec as P

HD = 128
TILE = 128
MIB = 2**20
COLUMN_CHUNKS = 5

guidance_scale = 5.0
SHORT = pl.CostEstimate(flops=1, bytes_accessed=1, transcendentals=0)


def from_behind(x, axis, by):
    count = lax.axis_size(axis)
    return lax.ppermute(x, axis, [(i, (i + by) % count) for i in range(count)])


def from_partner(value, axis, mask):
    pairs = [(source, source ^ mask) for source in range(lax.axis_size(axis))]
    return lax.ppermute(value, axis, pairs)


def norm_kernel(rows_ref, modulation_ref, out_ref):
    step = 16

    def body(index, carry):
        rows = pl.ds(pl.multiple_of(index * step, step), step)
        values = rows_ref[rows, :].astype(jnp.float32)
        centre = values - jnp.mean(values, axis=-1, keepdims=True)
        spread = jnp.mean(centre * centre, axis=-1, keepdims=True)
        normed = centre * lax.rsqrt(spread + 1e-06)
        out_ref[rows, :] = (
            normed * (1.0 + modulation_ref[1:2, :]) + modulation_ref[0:1, :]
        ).astype(jnp.bfloat16)
        return carry

    lax.fori_loop(0, rows_ref.shape[0] // step, body, 0)


def modulated_norm(rows, modulation):
    return pl.pallas_call(
        norm_kernel,
        out_shape=jax.ShapeDtypeStruct(rows.shape, jnp.bfloat16),
        name="modulated_norm",
        cost_estimate=pl.CostEstimate(
            flops=10 * rows.size, bytes_accessed=4 * rows.size, transcendentals=0
        ),
        compiler_params=pltpu.CompilerParams(vmem_limit_bytes=16 * MIB),
    )(rows, modulation)


def gate_kernel(value_ref, *refs):
    pass


def after(value, earlier):
    return pl.pallas_call(
        gate_kernel,
        in_specs=[pl.BlockSpec(memory_space=pl.ANY)] * (1 + len(earlier)),
        out_specs=pl.BlockSpec(memory_space=pl.ANY),
        out_shape=jax.ShapeDtypeStruct(value.shape, value.dtype),
        input_output_aliases={0: 0},
        name="after",
        cost_estimate=SHORT,
        compiler_params=pltpu.CompilerParams(vmem_limit_bytes=MIB),
    )(value, *earlier)


def project_kernel(*refs, halves, carried):
    weights_ref, out_ref, total_ref = refs[sum(halves)], refs[-2], refs[-1]
    step, steps = pl.program_id(0), pl.num_programs(0)
    weights = jnp.concatenate([weights_ref[0], weights_ref[1], weights_ref[2]], axis=1)
    early, block = step < steps // 2, weights.shape[0]
    columns = pl.ds(pl.multiple_of(step * block, block), block)
    half_columns = pl.ds(pl.multiple_of(step % (steps // 2) * block, block), block)
    blocks, place = [], 0
    for count in halves:
        if count == 1:
            blocks.append(refs[place][:, columns])
        else:
            parts = refs[place][:, half_columns], refs[place + 1][:, half_columns]
            blocks.append(jnp.where(early, *parts))
        place += count
    rows = jnp.concatenate(blocks, axis=0)
    product = jnp.dot(rows, weights, preferred_element_type=jnp.float32)

    @pl.when(step == 0)
    def _():
        total_ref[...] = product

    @pl.when(step > 0)
    def _():
        total_ref[...] += product

    @pl.when(step == steps - 1)
    def _():
        width = weights_ref.shape[2]
        if carried:
            out_ref[:carried, :] = refs[sum(halves) + 1][...]
        for head in range(2 * width // HD):
            columns = slice(head * HD, (head + 1) * HD)
            values = total_ref[:, columns]
            scale = lax.rsqrt(jnp.mean(values * values, axis=-1, keepdims=True) + 1e-06)
            out_ref[carried:, columns] = (values * scale).astype(jnp.bfloat16)
        out_ref[carried:, 2 * width :] = total_ref[:, 2 * width :].astype(jnp.bfloat16)


def project(blocks, weights, held, earlier):
    _, depth, width = weights.shape
    rows = blocks[0][0].shape[0]
    steps = 4
    block = depth // steps
    count = len(blocks) * rows
    carried = sum(array.shape[0] for array in held)
    return pl.pallas_call(
        functools.partial(
            project_kernel, halves=[len(parts) for parts in blocks], carried=carried
        ),
        grid=(steps,),
        in_specs=[pl.BlockSpec(memory_space=pltpu.VMEM)] * sum(len(parts) for parts in blocks)
        + [pl.BlockSpec((3, block, width), lambda k: (0, k, 0))]
        + [pl.BlockSpec(memory_space=pltpu.VMEM)] * len(held)
        + [pl.BlockSpec(memory_space=pl.ANY)] * len(earlier),
        out_specs=pl.BlockSpec((carried + count, 3 * width), lambda k: (0, 0)),
        out_shape=jax.ShapeDtypeStruct((carried + count, 3 * width), jnp.bfloat16),
        scratch_shapes=[pltpu.VMEM((count, 3 * width), jnp.float32)],
        name="project_heads",
        cost_estimate=pl.CostEstimate(
            flops=2 * count * depth * 3 * width,
            bytes_accessed=2 * (count * depth + weights.size),
            transcendentals=0,
        ),
        compiler_params=pltpu.CompilerParams(vmem_limit_bytes=44 * MIB),
    )(*[part for parts in blocks for part in parts], weights, *held, *earlier)


def place_of(core, across):
    return jnp.where(across == 3, 6 + core, 3 * core + across)


def attend_blocks(visible_ref, heads_ref, context_ref, out_ref, first_block, first_head):
    width = heads_ref.shape[1] // 3
    held = context_ref.shape[1] // 2
    tiles_seen = visible_ref.shape[1]
    tiles_fresh = visible_ref.shape[0]
    mine_high, mine_low = lax.axis_index("sp") // 2, lax.axis_index("sp") % 2
    mine_branch = lax.axis_index("cfg")

    def body(step, carry):
        index = first_block + step
        high, low = mine_high ^ ((index // 2) % 2), mine_low ^ (index // 4)
        tile, branch = high * 2 + low, mine_branch ^ (index % 2)
        place = place_of(index // 4, index % 4)
        rows = pl.ds(pl.multiple_of(place * TILE, TILE), TILE)
        out_rows = pl.ds(pl.multiple_of(step * TILE, TILE), TILE)
        places = []
        for seen in range(tiles_seen):
            number = visible_ref[tile, seen]
            older = jnp.maximum(number - tiles_fresh, 0)
            across = (mine_high ^ ((number // 2) % 2)) * 2 + index % 2
            fresh = place_of(mine_low ^ (number % 2), across) * TILE
            stale = ((older // 2) * 2 + branch) * 2 * TILE + (older % 2) * TILE
            places.append(
                (
                    number < tiles_fresh,
                    pl.ds(pl.multiple_of(fresh, TILE), TILE),
                    pl.ds(pl.multiple_of(stale, TILE), TILE),
                )
            )

        def tiles(kind, head):
            start = kind * width + (first_head + head) * HD
            held_start = (kind - 1) * held + head * HD
            return jnp.concatenate(
                [
                    jnp.where(
                        is_fresh,
                        heads_ref[fresh, start : start + HD],
                        context_ref[stale, held_start : held_start + HD],
                    )
                    for is_fresh, fresh, stale in places
                ],
                axis=0,
            )

        for head in range(held // HD):
            columns = slice((first_head + head) * HD, (first_head + head + 1) * HD)
            scores = lax.dot_general(
                heads_ref[rows, columns],
                tiles(1, head),
                (((1,), (1,)), ((), ())),
                preferred_element_type=jnp.float32,
            )
            exponent = jnp.exp(scores * HD ** (-0.5))
            total = jnp.sum(exponent, axis=-1, keepdims=True)
            mixed = jnp.dot(
                exponent.astype(jnp.bfloat16), tiles(2, head), preferred_element_type=jnp.float32
            )
            out_ref[out_rows, head * HD : (head + 1) * HD] = (mixed / total).astype(jnp.bfloat16)
        return carry

    lax.fori_loop(0, out_ref.shape[0] // TILE, body, 0)


def attend_cost(heads, context, visible, count):
    keys = visible.shape[1] * TILE
    return pl.CostEstimate(
        flops=2 * count * keys * context.shape[1],
        bytes_accessed=2 * (heads.size + context.size),
        transcendentals=count * keys * context.shape[1] // (2 * HD),
    )


def attend_first_kernel(visible_ref, heads_ref, context_ref, kept_ref, sent_ref):
    attend_blocks(visible_ref, heads_ref, context_ref, sent_ref, kept_ref.shape[0] // TILE, 0)
    attend_blocks(visible_ref, heads_ref, context_ref, kept_ref, 0, 0)


def attend_first(heads, context, visible):
    count, width = heads.shape[0], context.shape[1] // 2
    return pl.pallas_call(
        attend_first_kernel,
        in_specs=[pl.BlockSpec(memory_space=pltpu.SMEM)]
        + [pl.BlockSpec(memory_space=pltpu.VMEM)] * 2,
        out_shape=[jax.ShapeDtypeStruct((count // 2, width), jnp.bfloat16)] * 2,
        name="attend_first",
        cost_estimate=attend_cost(heads, context, visible, count),
        compiler_params=pltpu.CompilerParams(vmem_limit_bytes=12 * MIB),
    )(visible, heads, context)


def attend_last_kernel(visible_ref, heads_ref, context_ref, *refs, first_block, first_head):
    attend_blocks(visible_ref, heads_ref, context_ref, refs[-1], first_block, first_head)


def attend_last(heads, context, visible, first_block, first_head, earlier):
    count, width = heads.shape[0], context.shape[1] // 2
    return pl.pallas_call(
        functools.partial(
            attend_last_kernel, first_block=first_block, first_head=first_head
        ),
        in_specs=[pl.BlockSpec(memory_space=pltpu.SMEM)]
        + [pl.BlockSpec(memory_space=pltpu.VMEM)] * 2
        + [pl.BlockSpec(memory_space=pl.ANY)] * len(earlier),
        out_shape=jax.ShapeDtypeStruct((count // 2, width), jnp.bfloat16),
        name="attend_last",
        cost_estimate=attend_cost(heads, context, visible, count // 2),
        compiler_params=pltpu.CompilerParams(vmem_limit_bytes=12 * MIB),
    )(visible, heads, context, *earlier)


def half_kernel(rows_ref, *refs, start):
    half_ref, whole_ref = refs[-2:]
    half_ref[...] = rows_ref[:, start : start + half_ref.shape[1]]
    whole_ref[...] = rows_ref[...]


def half_of(rows, start, earlier):
    count, columns = rows.shape
    return pl.pallas_call(
        functools.partial(half_kernel, start=start),
        in_specs=[pl.BlockSpec(memory_space=pltpu.VMEM)]
        + [pl.BlockSpec(memory_space=pl.ANY)] * len(earlier),
        out_shape=[
            jax.ShapeDtypeStruct((count, width), rows.dtype) for width in (columns // 2, columns)
        ],
        name="half_of",
        cost_estimate=SHORT,
        compiler_params=pltpu.CompilerParams(vmem_limit_bytes=8 * MIB),
    )(rows, *earlier)


def combined(own, other, mine, gates_ref, columns):
    conditional = lax.axis_index("cfg") == 1
    last = lax.axis_index("pipe") == lax.axis_size("pipe") - 1
    weight = jnp.where(conditional, guidance_scale, 1.0 - guidance_scale).astype(jnp.float32)
    other_weight = jnp.where(conditional, 1.0 - guidance_scale, guidance_scale).astype(jnp.float32)
    own = own * gates_ref[0:1, columns]
    other = other * gates_ref[1:2, columns]
    if mine is not None:
        own = own + mine
    guided = weight * own + other_weight * other
    return jnp.where(last, guided, other), jnp.where(last, guided, own)


def begin(start, refs, across_out, along_out, first_kept, second_kept):
    *attended_refs, weights_ref, core_weights_ref, rows_ref, gates_ref = refs
    tokens, half = rows_ref.shape[0], first_kept.shape[2]
    attended = jnp.concatenate([ref[...] for ref in attended_refs], axis=1)

    def product_of(columns):
        weights = jnp.concatenate([weights_ref[:, columns], core_weights_ref[:, columns]], axis=0)
        return jnp.dot(attended, weights, preferred_element_type=jnp.float32)

    columns = slice(start, start + half)
    product = product_of(slice(0, half))
    for tile in range(2):
        own = product[2 * tile * tokens : (2 * tile + 1) * tokens]
        other = product[(2 * tile + 1) * tokens : (2 * tile + 2) * tokens]
        mine = rows_ref[:, columns].astype(jnp.float32) if tile == 0 else None
        sent, kept = combined(own, other, mine, gates_ref, columns)
        across_out[tile] = sent.astype(jnp.bfloat16)
        first_kept[tile] = kept
    product = product_of(slice(half, 2 * half))
    for branch in range(2):
        second_kept[branch] = product[branch * tokens : (branch + 1) * tokens]
        along_out[branch] = product[(branch + 2) * tokens : (branch + 3) * tokens].astype(
            jnp.bfloat16
        )


def stage_kernel(*refs, parts, start, next_start, fresh, middle, final):
    named = dict(zip(parts, refs))
    if fresh:
        begin(
            next_start,
            [
                named[name]
                for name in (
                    "near_first",
                    "near_last",
                    "far_first",
                    "far_last",
                    "weights",
                    "core_weights",
                    "rows",
                    "gates",
                )
            ],
            named["across_out"],
            named["along_out"],
            named["first_kept_out"],
            named["second_kept_out"],
        )
    if middle:
        across, along = named["across"], named["along"]
        first_kept, second_kept = named["first_kept"], named["second_kept"]
        half = first_kept.shape[2]
        place = 2 if fresh else 0
        named["along_out"][place] = (first_kept[1] + across[1].astype(jnp.float32)).astype(
            jnp.bfloat16
        )
        named["first_left_out"][...] = first_kept[0] + across[0].astype(jnp.float32)
        columns = slice(start + half, start + 2 * half)
        sent, kept = combined(
            second_kept[0] + along[0].astype(jnp.float32),
            second_kept[1] + along[1].astype(jnp.float32),
            named["rows"][:, columns].astype(jnp.float32),
            named["gates"],
            columns,
        )
        named["across_out"][place] = sent.astype(jnp.bfloat16)
        named["second_left_out"][...] = kept
    if final:
        across, along = named["across"], named["along"]
        first_left, second_left = named["first_left"], named["second_left"]
        half = first_left.shape[1]
        place = 2 if middle else 0
        named["done_out"][:, :half] = (
            first_left[...] + along[place].astype(jnp.float32)
        ).astype(jnp.bfloat16)
        named["done_out"][:, half:] = (
            second_left[...] + across[place].astype(jnp.float32)
        ).astype(jnp.bfloat16)


def stage(operands, earlier, chunk, start, next_start, fresh, middle, final):
    tokens, half = operands["rows"].shape[0], chunk // 2
    outs = {}
    if fresh or middle:
        pieces = 2 * fresh + middle
        outs["across_out"] = jax.ShapeDtypeStruct((pieces, tokens, half), jnp.bfloat16)
        outs["along_out"] = outs["across_out"]
    if fresh:
        outs["first_kept_out"] = jax.ShapeDtypeStruct((2, tokens, half), jnp.float32)
        outs["second_kept_out"] = outs["first_kept_out"]
    if middle:
        outs["first_left_out"] = jax.ShapeDtypeStruct((tokens, half), jnp.float32)
        outs["second_left_out"] = outs["first_left_out"]
    if final:
        outs["done_out"] = jax.ShapeDtypeStruct((tokens, chunk), jnp.bfloat16)
    parts = list(operands) + ["earlier"] * len(earlier) + list(outs)
    results = pl.pallas_call(
        functools.partial(
            stage_kernel,
            parts=parts,
            start=start,
            next_start=next_start,
            fresh=fresh,
            middle=middle,
            final=final,
        ),
        grid=(1,),
        in_specs=[
            pl.BlockSpec((array.shape[0], chunk), lambda step: (0, next_start // chunk))
            if name in ("weights", "core_weights")
            else pl.BlockSpec(memory_space=pltpu.VMEM)
            for name, array in operands.items()
        ]
        + [pl.BlockSpec(memory_space=pl.ANY)] * len(earlier),
        out_specs=[pl.BlockSpec(memory_space=pltpu.VMEM)] * len(outs),
        out_shape=list(outs.values()),
        name="sum_stage",
        cost_estimate=SHORT,
        compiler_params=pltpu.CompilerParams(vmem_limit_bytes=16 * MIB),
    )(*operands.values(), *earlier)
    return dict(zip(outs, results))


def per_device(flight, modulation, project_in, project_out, stale_cache, visible):
    current = flight[0, 0]
    modulate = modulation[0, 0]
    token_rows, features = current.shape
    devices = lax.axis_size("sp") * lax.axis_size("cfg")

    context_rows = stale_cache.shape[2]
    width = project_in.shape[3]
    split = (width // HD - 1) * HD
    by_device = stale_cache[0, 0].reshape(context_rows, 2, devices, width).transpose(2, 0, 1, 3)
    packed, packed_last = [
        part.reshape(devices, context_rows, -1)
        for part in (by_device[..., :split], by_device[..., split:])
    ]

    own = modulated_norm(current, modulate)
    across = from_partner(own, "cfg", 1)
    along = from_partner(own, "sp", 2)
    own_core = from_partner(own, "sp", 1)
    middle = features // 2
    first_half, across = half_of(across, 0, (packed,))
    second_half, along = half_of(along, middle, (packed,))
    first = from_partner(first_half, "sp", 2)
    second = from_partner(second_half, "cfg", 1)
    core_weights = from_partner(project_out[0], "sp", 1)
    near = [(own,), (across,), (along,), (first, second)]
    far = [(own_core,)] + [
        tuple(from_partner(part, "sp", 1) for part in parts) for parts in near[1:]
    ]

    def exchange(part):
        context = lax.all_to_all(part, ("sp", "cfg"), split_axis=0, concat_axis=0, tiled=True)
        return context.reshape(devices * context_rows, -1)

    context = exchange(packed)
    heads = project(near[:3] + far[:3], project_in[0], (), ())
    packed_last = after(packed_last, (context, heads))
    context_last = exchange(packed_last)
    heads = project([near[3], far[3]], project_in[0], (heads,), (packed_last,))
    near_first, for_core = attend_first(heads, context, visible[0])
    far_first = from_partner(for_core, "sp", 1)
    gate = modulate[2:3]
    gates = jnp.concatenate([gate, from_partner(after(gate, (for_core,)), "cfg", 1)], axis=0)
    for_core = attend_last(heads, context_last, visible[0], 4, split // HD, (near_first,))
    far_last = from_partner(for_core, "sp", 1)
    near_last = attend_last(heads, context_last, visible[0], 0, split // HD, (for_core,))
    attended = dict(
        near_first=near_first, near_last=near_last, far_first=far_first, far_last=far_last
    )

    count = COLUMN_CHUNKS
    chunk = features // count
    kept, left, flights, arrivals, earlier = {}, {}, {}, [], []
    for index in range(-2, count + 2):
        fresh, middle, final = index + 2 < count, 0 <= index < count, index >= 2
        operands = {"rows": current, "gates": gates}
        if fresh:
            operands.update(attended, weights=project_out[0], core_weights=core_weights)
        if index >= 0:
            operands["across"], operands["along"] = flights.pop(index)
        if middle:
            operands["first_kept"], operands["second_kept"] = kept.pop(index)
        if final:
            operands["first_left"], operands["second_left"] = left.pop(index - 2)
        outs = stage(
            operands,
            earlier,
            chunk,
            max(index, 0) * chunk,
            (index + 2) * chunk,
            fresh,
            middle,
            final,
        )
        if "across_out" in outs:
            flights[index + 2] = (
                from_partner(outs["across_out"], "cfg", 1),
                from_partner(outs["along_out"], "sp", 2),
            )
        if fresh:
            kept[index + 2] = (outs["first_kept_out"], outs["second_kept_out"])
        if middle:
            left[index] = (outs["first_left_out"], outs["second_left_out"])
        if final:
            arrivals.append(from_behind(outs["done_out"], "pipe", 1))
        earlier = [list(outs.values())[-1]] + (arrivals[-2:-1] if 3 <= index < count else [])
    return jnp.concatenate(arrivals, axis=1)[None, None]


def solution(mesh):
    placed = (
        P("pipe", "cfg", "sp", None),
        P("pipe", "cfg", None, None),
        P("pipe", None, None, ("sp", "cfg")),
        P("pipe", ("sp", "cfg"), None),
        P("pipe", "cfg", "sp", None, None),
        P("pipe", None, None),
    )
    return jax.shard_map(
        per_device,
        mesh=mesh,
        in_specs=placed,
        out_specs=P("pipe", "cfg", "sp", None),
        check_vma=False,
    )
```

```python
import functools

import jax
import jax.numpy as jnp
from jax import lax
from jax.experimental import pallas as pl
from jax.experimental.pallas import tpu as pltpu
from jax.sharding import PartitionSpec as P

HD = 128
TILE = 128
MIB = 2**20
COLUMN_CHUNKS = 5

guidance_scale = 5.0
SHORT = pl.CostEstimate(flops=1, bytes_accessed=1, transcendentals=0)


def from_behind(x, axis, by):
    count = lax.axis_size(axis)
    return lax.ppermute(x, axis, [(i, (i + by) % count) for i in range(count)])


def from_partner(value, axis, mask):
    pairs = [(source, source ^ mask) for source in range(lax.axis_size(axis))]
    return lax.ppermute(value, axis, pairs)


def norm_kernel(*refs):
    *parts, modulation_ref, out_ref = refs
    step = 16

    def body(index, carry):
        rows = pl.ds(pl.multiple_of(index * step, step), step)
        values = [part[rows, :].astype(jnp.float32) for part in parts]
        values = jnp.concatenate(values, axis=1) if len(values) > 1 else values[0]
        centre = values - jnp.mean(values, axis=-1, keepdims=True)
        spread = jnp.mean(centre * centre, axis=-1, keepdims=True)
        normed = centre * lax.rsqrt(spread + 1e-06)
        out_ref[rows, :] = (
            normed * (1.0 + modulation_ref[1:2, :]) + modulation_ref[0:1, :]
        ).astype(jnp.bfloat16)
        return carry

    lax.fori_loop(0, out_ref.shape[0] // step, body, 0)


def modulated_norm(parts, modulation):
    rows, features = parts[0].shape[0], modulation.shape[1]
    return pl.pallas_call(
        norm_kernel,
        in_specs=[pl.BlockSpec(memory_space=pltpu.VMEM)] * (len(parts) + 1),
        out_shape=jax.ShapeDtypeStruct((rows, features), jnp.bfloat16),
        name="modulated_norm",
        cost_estimate=SHORT,
        compiler_params=pltpu.CompilerParams(vmem_limit_bytes=8 * MIB),
    )(*parts, modulation)


def gate_kernel(value_ref, *refs):
    pass


def after(value, earlier):
    return pl.pallas_call(
        gate_kernel,
        in_specs=[pl.BlockSpec(memory_space=pl.ANY)] * (1 + len(earlier)),
        out_specs=pl.BlockSpec(memory_space=pl.ANY),
        out_shape=jax.ShapeDtypeStruct(value.shape, value.dtype),
        input_output_aliases={0: 0},
        name="after",
        cost_estimate=SHORT,
        compiler_params=pltpu.CompilerParams(vmem_limit_bytes=MIB),
    )(value, *earlier)


def project_kernel(*refs):
    *block_refs, weights_ref, out_ref, total_ref = refs
    step, steps = pl.program_id(0), pl.num_programs(0)
    weights = jnp.concatenate([weights_ref[0], weights_ref[1], weights_ref[2]], axis=1)
    block = weights.shape[0]
    columns = pl.ds(pl.multiple_of(step * block, block), block)
    rows = jnp.concatenate([ref[:, columns] for ref in block_refs], axis=0)
    product = jnp.dot(rows, weights, preferred_element_type=jnp.float32)

    @pl.when(step == 0)
    def _():
        total_ref[...] = product

    @pl.when(step > 0)
    def _():
        total_ref[...] += product

    @pl.when(step == steps - 1)
    def _():
        width = weights_ref.shape[2]
        for head in range(2 * width // HD):
            columns = slice(head * HD, (head + 1) * HD)
            values = total_ref[:, columns]
            scale = lax.rsqrt(jnp.mean(values * values, axis=-1, keepdims=True) + 1e-06)
            out_ref[:, columns] = (values * scale).astype(jnp.bfloat16)
        out_ref[:, 2 * width :] = total_ref[:, 2 * width :].astype(jnp.bfloat16)


def project(blocks, weights):
    _, depth, width = weights.shape
    steps = 4
    block = depth // steps
    count = sum(rows.shape[0] for rows in blocks)
    return pl.pallas_call(
        project_kernel,
        grid=(steps,),
        in_specs=[pl.BlockSpec(memory_space=pltpu.VMEM)] * len(blocks)
        + [pl.BlockSpec((3, block, width), lambda k: (0, k, 0))],
        out_specs=pl.BlockSpec((count, 3 * width), lambda k: (0, 0)),
        out_shape=jax.ShapeDtypeStruct((count, 3 * width), jnp.bfloat16),
        scratch_shapes=[pltpu.VMEM((count, 3 * width), jnp.float32)],
        name="project_heads",
        cost_estimate=pl.CostEstimate(
            flops=2 * count * depth * 3 * width,
            bytes_accessed=2 * (count * depth + weights.size),
            transcendentals=0,
        ),
        compiler_params=pltpu.CompilerParams(vmem_limit_bytes=40 * MIB),
    )(*blocks, weights)


def attend_kernel(visible_ref, heads_ref, context_ref, *refs, first_block):
    out_ref = refs[-1]
    width = heads_ref.shape[1] // 3
    tiles_seen = visible_ref.shape[1]
    tiles_fresh = visible_ref.shape[0]
    mine_high, mine_low = lax.axis_index("sp") // 2, lax.axis_index("sp") % 2
    mine_branch = lax.axis_index("cfg")

    def body(step, carry):
        index = first_block + step
        high, low = mine_high ^ ((index // 2) % 2), mine_low ^ (index // 4)
        tile, branch = high * 2 + low, mine_branch ^ (index % 2)
        rows = pl.ds(pl.multiple_of(index * TILE, TILE), TILE)
        out_rows = pl.ds(pl.multiple_of(step * TILE, TILE), TILE)
        places = []
        for seen in range(tiles_seen):
            number = visible_ref[tile, seen]
            older = jnp.maximum(number - tiles_fresh, 0)
            fresh = (mine_low ^ (number % 2)) * 4 + (mine_high ^ ((number // 2) % 2)) * 2
            fresh = (fresh + index % 2) * TILE
            stale = ((older // 2) * 2 + branch) * 2 * TILE + (older % 2) * TILE
            places.append(
                (
                    number < tiles_fresh,
                    pl.ds(pl.multiple_of(fresh, TILE), TILE),
                    pl.ds(pl.multiple_of(stale, TILE), TILE),
                )
            )

        def tiles(kind, head):
            start = kind * width + head * HD
            held_start = start - width
            return jnp.concatenate(
                [
                    jnp.where(
                        is_fresh,
                        heads_ref[fresh, start : start + HD],
                        context_ref[stale, held_start : held_start + HD],
                    )
                    for is_fresh, fresh, stale in places
                ],
                axis=0,
            )

        for head in range(width // HD):
            columns = slice(head * HD, (head + 1) * HD)
            scores = lax.dot_general(
                heads_ref[rows, columns],
                tiles(1, head),
                (((1,), (1,)), ((), ())),
                preferred_element_type=jnp.float32,
            )
            exponent = jnp.exp(scores * HD ** (-0.5))
            total = jnp.sum(exponent, axis=-1, keepdims=True)
            mixed = jnp.dot(
                exponent.astype(jnp.bfloat16), tiles(2, head), preferred_element_type=jnp.float32
            )
            out_ref[out_rows, columns] = (mixed / total).astype(jnp.bfloat16)
        return carry

    lax.fori_loop(0, out_ref.shape[0] // TILE, body, 0, unroll=2)


def attend(heads, context, visible, first_block, earlier):
    count, width = heads.shape[0] // 2, heads.shape[1] // 3
    return pl.pallas_call(
        functools.partial(attend_kernel, first_block=first_block),
        in_specs=[pl.BlockSpec(memory_space=pltpu.SMEM)]
        + [pl.BlockSpec(memory_space=pltpu.VMEM)] * 2
        + [pl.BlockSpec(memory_space=pl.ANY)] * len(earlier),
        out_shape=jax.ShapeDtypeStruct((count, width), jnp.bfloat16),
        name="attend",
        cost_estimate=SHORT,
        compiler_params=pltpu.CompilerParams(vmem_limit_bytes=12 * MIB),
    )(visible, heads, context, *earlier)


def half_kernel(rows_ref, *refs, start):
    half_ref = refs[-1]
    half_ref[...] = rows_ref[:, start : start + half_ref.shape[1]]


def half_of(rows, start, earlier):
    count, columns = rows.shape
    return pl.pallas_call(
        functools.partial(half_kernel, start=start),
        in_specs=[pl.BlockSpec(memory_space=pltpu.VMEM)]
        + [pl.BlockSpec(memory_space=pl.ANY)] * len(earlier),
        out_shape=jax.ShapeDtypeStruct((count, columns // 2), rows.dtype),
        name="half_of",
        cost_estimate=SHORT,
        compiler_params=pltpu.CompilerParams(vmem_limit_bytes=8 * MIB),
    )(rows, *earlier)


def combined(own, other, mine, gates_ref, columns):
    conditional = lax.axis_index("cfg") == 1
    last = lax.axis_index("pipe") == lax.axis_size("pipe") - 1
    weight = jnp.where(conditional, guidance_scale, 1.0 - guidance_scale).astype(jnp.float32)
    other_weight = jnp.where(conditional, 1.0 - guidance_scale, guidance_scale).astype(jnp.float32)
    own = own * gates_ref[0:1, columns]
    other = other * gates_ref[1:2, columns]
    if mine is not None:
        own = own + mine
    guided = weight * own + other_weight * other
    return jnp.where(last, guided, other), jnp.where(last, guided, own)


def begin(start, refs, across_out, along_out, first_kept, second_kept):
    *attended_refs, weights_ref, core_weights_ref, rows_ref, gates_ref = refs
    tokens, half = rows_ref.shape[0], first_kept.shape[2]
    attended = jnp.concatenate([ref[...] for ref in attended_refs], axis=1)

    def product_of(columns):
        weights = jnp.concatenate([weights_ref[:, columns], core_weights_ref[:, columns]], axis=0)
        return jnp.dot(attended, weights, preferred_element_type=jnp.float32)

    columns = slice(start, start + half)
    product = product_of(slice(0, half))
    for tile in range(2):
        own = product[2 * tile * tokens : (2 * tile + 1) * tokens]
        other = product[(2 * tile + 1) * tokens : (2 * tile + 2) * tokens]
        mine = rows_ref[:, columns].astype(jnp.float32) if tile == 0 else None
        sent, kept = combined(own, other, mine, gates_ref, columns)
        across_out[tile] = sent.astype(jnp.bfloat16)
        first_kept[tile] = kept
    product = product_of(slice(half, 2 * half))
    for branch in range(2):
        second_kept[branch] = product[branch * tokens : (branch + 1) * tokens]
        along_out[branch] = product[(branch + 2) * tokens : (branch + 3) * tokens].astype(
            jnp.bfloat16
        )


def stage_kernel(*refs, parts, start, next_start, fresh, middle, final):
    named = dict(zip(parts, refs))
    if fresh:
        begin(
            next_start,
            [
                named[name]
                for name in (
                    "attended", "core_attended", "weights", "core_weights", "rows", "gates"
                )
            ],
            named["across_out"],
            named["along_out"],
            named["first_kept_out"],
            named["second_kept_out"],
        )
    if middle:
        across, along = named["across"], named["along"]
        first_kept, second_kept = named["first_kept"], named["second_kept"]
        half = first_kept.shape[2]
        place = 2 if fresh else 0
        named["along_out"][place] = (first_kept[1] + across[1].astype(jnp.float32)).astype(
            jnp.bfloat16
        )
        named["first_left_out"][...] = first_kept[0] + across[0].astype(jnp.float32)
        columns = slice(start + half, start + 2 * half)
        sent, kept = combined(
            second_kept[0] + along[0].astype(jnp.float32),
            second_kept[1] + along[1].astype(jnp.float32),
            named["rows"][:, columns].astype(jnp.float32),
            named["gates"],
            columns,
        )
        named["across_out"][place] = sent.astype(jnp.bfloat16)
        named["second_left_out"][...] = kept
    if final:
        across, along = named["across"], named["along"]
        first_left, second_left = named["first_left"], named["second_left"]
        half = first_left.shape[1]
        place = 2 if middle else 0
        named["done_out"][:, :half] = (
            first_left[...] + along[place].astype(jnp.float32)
        ).astype(jnp.bfloat16)
        named["done_out"][:, half:] = (
            second_left[...] + across[place].astype(jnp.float32)
        ).astype(jnp.bfloat16)


def stage(operands, earlier, chunk, start, next_start, fresh, middle, final):
    tokens, half = operands["rows"].shape[0], chunk // 2
    outs = {}
    if fresh or middle:
        pieces = 2 * fresh + middle
        outs["across_out"] = jax.ShapeDtypeStruct((pieces, tokens, half), jnp.bfloat16)
        outs["along_out"] = outs["across_out"]
    if fresh:
        outs["first_kept_out"] = jax.ShapeDtypeStruct((2, tokens, half), jnp.float32)
        outs["second_kept_out"] = outs["first_kept_out"]
    if middle:
        outs["first_left_out"] = jax.ShapeDtypeStruct((tokens, half), jnp.float32)
        outs["second_left_out"] = outs["first_left_out"]
    if final:
        outs["done_out"] = jax.ShapeDtypeStruct((tokens, chunk), jnp.bfloat16)
    parts = list(operands) + ["earlier"] * len(earlier) + list(outs)
    results = pl.pallas_call(
        functools.partial(
            stage_kernel,
            parts=parts,
            start=start,
            next_start=next_start,
            fresh=fresh,
            middle=middle,
            final=final,
        ),
        grid=(1,),
        in_specs=[
            pl.BlockSpec((array.shape[0], chunk), lambda step: (0, next_start // chunk))
            if name in ("weights", "core_weights")
            else pl.BlockSpec(memory_space=pltpu.VMEM)
            for name, array in operands.items()
        ]
        + [pl.BlockSpec(memory_space=pl.ANY)] * len(earlier),
        out_specs=[pl.BlockSpec(memory_space=pltpu.VMEM)] * len(outs),
        out_shape=list(outs.values()),
        name="sum_stage",
        cost_estimate=SHORT,
        compiler_params=pltpu.CompilerParams(vmem_limit_bytes=16 * MIB),
    )(*operands.values(), *earlier)
    return dict(zip(outs, results))


def per_device(flight, modulation, project_in, project_out, stale_cache, visible):
    current = flight[0, 0]
    modulate = modulation[0, 0]
    token_rows, features = current.shape
    devices = lax.axis_size("sp") * lax.axis_size("cfg")

    context_rows = stale_cache.shape[2]
    width = project_in.shape[3]
    packed = stale_cache[0, 0].reshape(context_rows, 2, devices, width)
    packed = packed.transpose(2, 0, 1, 3).reshape(devices, context_rows, 2 * width)

    across = from_partner(current, "cfg", 1)
    along = from_partner(current, "sp", 2)
    other_modulate = from_partner(modulate, "cfg", 1)
    own = modulated_norm([current], modulate)
    middle = features // 2
    first = from_partner(half_of(across, 0, (packed, other_modulate)), "sp", 2)
    second = from_partner(half_of(along, middle, (packed, other_modulate)), "cfg", 1)
    core_weights = from_partner(project_out[0], "sp", 1)
    near = [
        own,
        modulated_norm([across], other_modulate),
        modulated_norm([along], modulate),
        modulated_norm([first, second], other_modulate),
    ]
    far = [from_partner(rows, "sp", 1) for rows in near]

    packed = after(packed, (first, second, near[0]))
    context = lax.all_to_all(packed, ("sp", "cfg"), split_axis=0, concat_axis=0, tiled=True)
    context = context.reshape(devices * context_rows, 2 * width)

    heads = project(near + far, project_in[0])
    gates = jnp.concatenate([modulate[2:3], other_modulate[2:3]], axis=0)
    for_core = attend(heads, context, visible[0], 4, ())
    core_attended = from_partner(for_core, "sp", 1)
    attended = attend(heads, context, visible[0], 0, (for_core, gates))

    count = COLUMN_CHUNKS
    chunk = features // count
    kept, left, flights, arrivals, earlier = {}, {}, {}, [], []
    for index in range(-2, count + 2):
        fresh, middle, final = index + 2 < count, 0 <= index < count, index >= 2
        operands = {"rows": current, "gates": gates}
        if fresh:
            operands.update(
                attended=attended,
                core_attended=core_attended,
                weights=project_out[0],
                core_weights=core_weights,
            )
        if index >= 0:
            operands["across"], operands["along"] = flights.pop(index)
        if middle:
            operands["first_kept"], operands["second_kept"] = kept.pop(index)
        if final:
            operands["first_left"], operands["second_left"] = left.pop(index - 2)
        outs = stage(
            operands,
            earlier,
            chunk,
            max(index, 0) * chunk,
            (index + 2) * chunk,
            fresh,
            middle,
            final,
        )
        if "across_out" in outs:
            flights[index + 2] = (
                from_partner(outs["across_out"], "cfg", 1),
                from_partner(outs["along_out"], "sp", 2),
            )
        if fresh:
            kept[index + 2] = (outs["first_kept_out"], outs["second_kept_out"])
        if middle:
            left[index] = (outs["first_left_out"], outs["second_left_out"])
        if final:
            arrivals.append(from_behind(outs["done_out"], "pipe", 1))
        earlier = [list(outs.values())[-1]] + (arrivals[-2:-1] if 3 <= index < count else [])
    return jnp.concatenate(arrivals, axis=1)[None, None]


def solution(mesh):
    placed = (
        P("pipe", "cfg", "sp", None),
        P("pipe", "cfg", None, None),
        P("pipe", None, None, ("sp", "cfg")),
        P("pipe", ("sp", "cfg"), None),
        P("pipe", "cfg", "sp", None, None),
        P("pipe", None, None),
    )
    return jax.shard_map(
        per_device,
        mesh=mesh,
        in_specs=placed,
        out_specs=P("pipe", "cfg", "sp", None),
        check_vma=False,
    )
```

```python
import functools

import jax
import jax.numpy as jnp
from jax import lax
from jax.experimental import pallas as pl
from jax.experimental.pallas import tpu as pltpu
from jax.sharding import PartitionSpec as P

HD = 128
TILE = 128
MIB = 2**20
CHUNK_SHARES = (4, 4, 4, 4, 2, 2)

guidance_scale = 5.0
SHORT = pl.CostEstimate(flops=1, bytes_accessed=1, transcendentals=0)


def from_behind(x, axis, by):
    count = lax.axis_size(axis)
    return lax.ppermute(x, axis, [(i, (i + by) % count) for i in range(count)])


def from_partner(value, axis, mask):
    pairs = [(source, source ^ mask) for source in range(lax.axis_size(axis))]
    return lax.ppermute(value, axis, pairs)


def norm_kernel(*refs):
    *parts, modulation_ref, out_ref = refs
    step = 16
    start = 0
    for part in parts:

        def body(index, carry, part=part, start=start):
            rows = pl.ds(pl.multiple_of(index * step, step), step)
            out_rows = pl.ds(pl.multiple_of(start + index * step, step), step)
            values = part[rows, :].astype(jnp.float32)
            centre = values - jnp.mean(values, axis=-1, keepdims=True)
            spread = jnp.mean(centre * centre, axis=-1, keepdims=True)
            normed = centre * lax.rsqrt(spread + 1e-06)
            out_ref[out_rows, :] = (
                normed * (1.0 + modulation_ref[1:2, :]) + modulation_ref[0:1, :]
            ).astype(jnp.bfloat16)
            return carry

        lax.fori_loop(0, part.shape[0] // step, body, 0)
        start += part.shape[0]


def modulated_norm(parts, modulation):
    rows, features = sum(part.shape[0] for part in parts), modulation.shape[1]
    return pl.pallas_call(
        norm_kernel,
        in_specs=[pl.BlockSpec(memory_space=pltpu.VMEM)] * (len(parts) + 1),
        out_shape=jax.ShapeDtypeStruct((rows, features), jnp.bfloat16),
        name="modulated_norm",
        cost_estimate=SHORT,
        compiler_params=pltpu.CompilerParams(vmem_limit_bytes=8 * MIB),
    )(*parts, modulation)


def gate_kernel(value_ref, *refs):
    pass


def after(value, earlier):
    return pl.pallas_call(
        gate_kernel,
        in_specs=[pl.BlockSpec(memory_space=pl.ANY)] * (1 + len(earlier)),
        out_specs=pl.BlockSpec(memory_space=pl.ANY),
        out_shape=jax.ShapeDtypeStruct(value.shape, value.dtype),
        input_output_aliases={0: 0},
        name="after",
        cost_estimate=SHORT,
        compiler_params=pltpu.CompilerParams(vmem_limit_bytes=MIB),
    )(value, *earlier)


def project_kernel(*refs):
    *block_refs, weights_ref, out_ref, total_ref = refs
    step, steps = pl.program_id(0), pl.num_programs(0)
    weights = jnp.concatenate([weights_ref[0], weights_ref[1], weights_ref[2]], axis=1)
    block = weights.shape[0]
    columns = pl.ds(pl.multiple_of(step * block, block), block)
    rows = jnp.concatenate([ref[:, columns] for ref in block_refs], axis=0)
    product = jnp.dot(rows, weights, preferred_element_type=jnp.float32)

    @pl.when(step == 0)
    def _():
        total_ref[...] = product

    @pl.when(step > 0)
    def _():
        total_ref[...] += product

    @pl.when(step == steps - 1)
    def _():
        width = weights_ref.shape[2]
        for head in range(2 * width // HD):
            columns = slice(head * HD, (head + 1) * HD)
            values = total_ref[:, columns]
            scale = lax.rsqrt(jnp.mean(values * values, axis=-1, keepdims=True) + 1e-06)
            out_ref[:, columns] = (values * scale).astype(jnp.bfloat16)
        out_ref[:, 2 * width :] = total_ref[:, 2 * width :].astype(jnp.bfloat16)


def project(blocks, weights):
    _, depth, width = weights.shape
    steps = 4
    block = depth // steps
    count = sum(rows.shape[0] for rows in blocks)
    return pl.pallas_call(
        project_kernel,
        grid=(steps,),
        in_specs=[pl.BlockSpec(memory_space=pltpu.VMEM)] * len(blocks)
        + [pl.BlockSpec((3, block, width), lambda k: (0, k, 0))],
        out_specs=pl.BlockSpec((count, 3 * width), lambda k: (0, 0)),
        out_shape=jax.ShapeDtypeStruct((count, 3 * width), jnp.bfloat16),
        scratch_shapes=[pltpu.VMEM((count, 3 * width), jnp.float32)],
        name="project_heads",
        cost_estimate=pl.CostEstimate(
            flops=2 * count * depth * 3 * width,
            bytes_accessed=2 * (count * depth + weights.size),
            transcendentals=0,
        ),
        compiler_params=pltpu.CompilerParams(vmem_limit_bytes=40 * MIB),
    )(*blocks, weights)


def attend_kernel(visible_ref, heads_ref, context_ref, *refs, first_block):
    out_ref = refs[-1]
    width = heads_ref.shape[1] // 3
    tiles_seen = visible_ref.shape[1]
    tiles_fresh = visible_ref.shape[0]
    mine_high, mine_low = lax.axis_index("sp") // 2, lax.axis_index("sp") % 2
    mine_branch = lax.axis_index("cfg")

    def body(step, carry):
        index = first_block + step
        high, low = mine_high ^ ((index // 2) % 2), mine_low ^ (index // 4)
        tile, branch = high * 2 + low, mine_branch ^ (index % 2)
        rows = pl.ds(pl.multiple_of(index * TILE, TILE), TILE)
        out_rows = pl.ds(pl.multiple_of(step * TILE, TILE), TILE)
        places = []
        for seen in range(tiles_seen):
            number = visible_ref[tile, seen]
            older = jnp.maximum(number - tiles_fresh, 0)
            fresh = (mine_low ^ (number % 2)) * 4 + (mine_high ^ ((number // 2) % 2)) * 2
            fresh = (fresh + index % 2) * TILE
            stale = ((older // 2) * 2 + branch) * 2 * TILE + (older % 2) * TILE
            places.append(
                (
                    number < tiles_fresh,
                    pl.ds(pl.multiple_of(fresh, TILE), TILE),
                    pl.ds(pl.multiple_of(stale, TILE), TILE),
                )
            )

        def tiles(kind, head):
            start = kind * width + head * HD
            held_start = start - width
            return jnp.concatenate(
                [
                    jnp.where(
                        is_fresh,
                        heads_ref[fresh, start : start + HD],
                        context_ref[stale, held_start : held_start + HD],
                    )
                    for is_fresh, fresh, stale in places
                ],
                axis=0,
            )

        for head in range(width // HD):
            columns = slice(head * HD, (head + 1) * HD)
            scores = lax.dot_general(
                heads_ref[rows, columns],
                tiles(1, head),
                (((1,), (1,)), ((), ())),
                preferred_element_type=jnp.float32,
            )
            exponent = jnp.exp(scores * HD ** (-0.5))
            total = jnp.sum(exponent, axis=-1, keepdims=True)
            mixed = jnp.dot(
                exponent.astype(jnp.bfloat16), tiles(2, head), preferred_element_type=jnp.float32
            )
            out_ref[out_rows, columns] = (mixed / total).astype(jnp.bfloat16)
        return carry

    lax.fori_loop(0, out_ref.shape[0] // TILE, body, 0)


def attend(heads, context, visible, first_block, earlier):
    count, width = heads.shape[0] // 2, heads.shape[1] // 3
    return pl.pallas_call(
        functools.partial(attend_kernel, first_block=first_block),
        in_specs=[pl.BlockSpec(memory_space=pltpu.SMEM)]
        + [pl.BlockSpec(memory_space=pltpu.VMEM)] * 2
        + [pl.BlockSpec(memory_space=pl.ANY)] * len(earlier),
        out_shape=jax.ShapeDtypeStruct((count, width), jnp.bfloat16),
        name="attend",
        cost_estimate=SHORT,
        compiler_params=pltpu.CompilerParams(vmem_limit_bytes=12 * MIB),
    )(visible, heads, context, *earlier)


def combined(own, other, mine, gates_ref, columns):
    conditional = lax.axis_index("cfg") == 1
    last = lax.axis_index("pipe") == lax.axis_size("pipe") - 1
    weight = jnp.where(conditional, guidance_scale, 1.0 - guidance_scale).astype(jnp.float32)
    other_weight = jnp.where(conditional, 1.0 - guidance_scale, guidance_scale).astype(jnp.float32)
    own = own * gates_ref[0:1, columns]
    other = other * gates_ref[1:2, columns]
    if mine is not None:
        own = own + mine
    guided = weight * own + other_weight * other
    return jnp.where(last, guided, other), jnp.where(last, guided, own)


def begin(start, refs, across_out, along_out, first_kept, second_kept):
    *attended_refs, weights_ref, core_weights_ref, rows_ref, gates_ref = refs
    tokens, half = rows_ref.shape[0], first_kept.shape[2]
    attended = jnp.concatenate([ref[...] for ref in attended_refs], axis=1)

    def product_of(columns):
        weights = jnp.concatenate([weights_ref[:, columns], core_weights_ref[:, columns]], axis=0)
        return jnp.dot(attended, weights, preferred_element_type=jnp.float32)

    columns = slice(start, start + half)
    product = product_of(slice(0, half))
    for tile in range(2):
        sent_columns = slice(tile * half, (tile + 1) * half)
        own = product[2 * tile * tokens : (2 * tile + 1) * tokens]
        other = product[(2 * tile + 1) * tokens : (2 * tile + 2) * tokens]
        mine = rows_ref[:, columns].astype(jnp.float32) if tile == 0 else None
        sent, kept = combined(own, other, mine, gates_ref, columns)
        across_out[:, sent_columns] = sent.astype(jnp.bfloat16)
        first_kept[tile] = kept
    product = product_of(slice(half, 2 * half))
    for branch in range(2):
        sent_columns = slice(branch * half, (branch + 1) * half)
        second_kept[branch] = product[branch * tokens : (branch + 1) * tokens]
        along_out[:, sent_columns] = product[(branch + 2) * tokens : (branch + 3) * tokens].astype(
            jnp.bfloat16
        )


def stage_kernel(*refs, parts, start, next_start, fresh, middle, final):
    named = dict(zip(parts, refs))
    if fresh:
        begin(
            next_start,
            [
                named[name]
                for name in (
                    "attended", "core_attended", "weights", "core_weights", "rows", "gates"
                )
            ],
            named["across_out"],
            named["along_out"],
            named["first_kept_out"],
            named["second_kept_out"],
        )
    if middle:
        across, along = named["across"], named["along"]
        first_kept, second_kept = named["first_kept"], named["second_kept"]
        half = first_kept.shape[2]
        sent_columns = slice(named["across_out"].shape[1] - half, named["across_out"].shape[1])
        named["along_out"][:, sent_columns] = (
            first_kept[1] + across[:, half : 2 * half].astype(jnp.float32)
        ).astype(jnp.bfloat16)
        named["first_left_out"][...] = first_kept[0] + across[:, :half].astype(jnp.float32)
        columns = slice(start + half, start + 2 * half)
        sent, kept = combined(
            second_kept[0] + along[:, :half].astype(jnp.float32),
            second_kept[1] + along[:, half : 2 * half].astype(jnp.float32),
            named["rows"][:, columns].astype(jnp.float32),
            named["gates"],
            columns,
        )
        named["across_out"][:, sent_columns] = sent.astype(jnp.bfloat16)
        named["second_left_out"][...] = kept
    if final:
        across, along = named["across"], named["along"]
        first_left, second_left = named["first_left"], named["second_left"]
        half = first_left.shape[1]
        columns = slice(across.shape[1] - half, across.shape[1])
        named["done_out"][:, :half] = (
            first_left[...] + along[:, columns].astype(jnp.float32)
        ).astype(jnp.bfloat16)
        named["done_out"][:, half:] = (
            second_left[...] + across[:, columns].astype(jnp.float32)
        ).astype(jnp.bfloat16)


def stage(operands, earlier, chunks, index, fresh, middle, final):
    tokens = operands["rows"].shape[0]
    next_start, next_chunk = chunks[index + 2] if fresh else (0, 0)
    start, chunk = chunks[index] if middle else (0, 0)
    outs = {}
    if fresh or middle:
        columns = next_chunk + chunk // 2
        outs["across_out"] = jax.ShapeDtypeStruct((tokens, columns), jnp.bfloat16)
        outs["along_out"] = outs["across_out"]
    if fresh:
        outs["first_kept_out"] = jax.ShapeDtypeStruct((2, tokens, next_chunk // 2), jnp.float32)
        outs["second_kept_out"] = outs["first_kept_out"]
    if middle:
        outs["first_left_out"] = jax.ShapeDtypeStruct((tokens, chunk // 2), jnp.float32)
        outs["second_left_out"] = outs["first_left_out"]
    if final:
        outs["done_out"] = jax.ShapeDtypeStruct((tokens, chunks[index - 2][1]), jnp.bfloat16)
    parts = list(operands) + ["earlier"] * len(earlier) + list(outs)
    results = pl.pallas_call(
        functools.partial(
            stage_kernel,
            parts=parts,
            start=start,
            next_start=next_start,
            fresh=fresh,
            middle=middle,
            final=final,
        ),
        grid=(1,),
        in_specs=[
            pl.BlockSpec((array.shape[0], next_chunk), lambda step: (0, next_start // next_chunk))
            if name in ("weights", "core_weights")
            else pl.BlockSpec(memory_space=pltpu.VMEM)
            for name, array in operands.items()
        ]
        + [pl.BlockSpec(memory_space=pl.ANY)] * len(earlier),
        out_specs=[pl.BlockSpec(memory_space=pltpu.VMEM)] * len(outs),
        out_shape=list(outs.values()),
        name="sum_stage",
        cost_estimate=SHORT,
        compiler_params=pltpu.CompilerParams(vmem_limit_bytes=16 * MIB),
    )(*operands.values(), *earlier)
    return dict(zip(outs, results))


def per_device(flight, modulation, project_in, project_out, stale_cache, visible):
    current = flight[0, 0]
    modulate = modulation[0, 0]
    token_rows, features = current.shape
    devices = lax.axis_size("sp") * lax.axis_size("cfg")

    context_rows = stale_cache.shape[2]
    width = project_in.shape[3]
    packed = stale_cache[0, 0].reshape(context_rows, 2, devices, width)
    packed = packed.transpose(2, 0, 1, 3).reshape(devices, context_rows, 2 * width)

    upper, lower = current[: token_rows // 2], current[token_rows // 2 :]
    across_upper, along_lower = from_partner(upper, "cfg", 1), from_partner(lower, "sp", 2)
    across_lower, along_upper = from_partner(lower, "cfg", 1), from_partner(upper, "sp", 2)
    other_modulate = from_partner(modulate, "cfg", 1)
    first, second = from_partner(across_upper, "sp", 2), from_partner(along_lower, "cfg", 1)
    core_weights = from_partner(project_out[0], "sp", 1)
    near = [
        modulated_norm([current], modulate),
        modulated_norm([across_upper, across_lower], other_modulate),
        modulated_norm([along_upper, along_lower], modulate),
        modulated_norm([first, second], other_modulate),
    ]
    far = [from_partner(rows, "sp", 1) for rows in near]

    packed = after(packed, (across_lower, along_upper, other_modulate))
    context = lax.all_to_all(packed, ("sp", "cfg"), split_axis=0, concat_axis=0, tiled=True)
    context = context.reshape(devices * context_rows, 2 * width)

    heads = project(near + far, project_in[0])
    gates = jnp.concatenate([modulate[2:3], other_modulate[2:3]], axis=0)
    for_core = attend(heads, context, visible[0], 4, ())
    core_attended = from_partner(for_core, "sp", 1)
    attended = attend(heads, context, visible[0], 0, (for_core, gates))

    count = len(CHUNK_SHARES)
    unit = features // sum(CHUNK_SHARES)
    chunks = [
        (sum(CHUNK_SHARES[:index]) * unit, share * unit) for index, share in enumerate(CHUNK_SHARES)
    ]
    kept, left, flights, arrivals, earlier = {}, {}, {}, [], []
    for index in range(-2, count + 2):
        fresh, middle, final = index + 2 < count, 0 <= index < count, index >= 2
        operands = {"rows": current, "gates": gates}
        if fresh:
            operands.update(
                attended=attended,
                core_attended=core_attended,
                weights=project_out[0],
                core_weights=core_weights,
            )
        if index >= 0:
            operands["across"], operands["along"] = flights.pop(index)
        if middle:
            operands["first_kept"], operands["second_kept"] = kept.pop(index)
        if final:
            operands["first_left"], operands["second_left"] = left.pop(index - 2)
        outs = stage(
            operands,
            earlier,
            chunks,
            index,
            fresh,
            middle,
            final,
        )
        if "across_out" in outs:
            flights[index + 2] = (
                from_partner(outs["across_out"], "cfg", 1),
                from_partner(outs["along_out"], "sp", 2),
            )
        if fresh:
            kept[index + 2] = (outs["first_kept_out"], outs["second_kept_out"])
        if middle:
            left[index] = (outs["first_left_out"], outs["second_left_out"])
        if final:
            arrivals.append(from_behind(outs["done_out"], "pipe", 1))
        earlier = [list(outs.values())[-1]] + (arrivals[-2:-1] if 3 <= index < count else [])
    return jnp.concatenate(arrivals, axis=1)[None, None]


def solution(mesh):
    placed = (
        P("pipe", "cfg", "sp", None),
        P("pipe", "cfg", None, None),
        P("pipe", None, None, ("sp", "cfg")),
        P("pipe", ("sp", "cfg"), None),
        P("pipe", "cfg", "sp", None, None),
        P("pipe", None, None),
    )
    return jax.shard_map(
        per_device,
        mesh=mesh,
        in_specs=placed,
        out_specs=P("pipe", "cfg", "sp", None),
        check_vma=False,
    )
```

```python
import functools

import jax
import jax.numpy as jnp
from jax import lax
from jax.experimental import pallas as pl
from jax.experimental.pallas import tpu as pltpu
from jax.sharding import PartitionSpec as P

HD = 128
TILE = 128
MIB = 2**20
CHUNK_SHARES = (4, 4, 4, 4, 2, 2)

guidance_scale = 5.0
SHORT = pl.CostEstimate(flops=1, bytes_accessed=1, transcendentals=0)


def from_behind(x, axis, by):
    count = lax.axis_size(axis)
    return lax.ppermute(x, axis, [(i, (i + by) % count) for i in range(count)])


def from_partner(value, axis, mask):
    pairs = [(source, source ^ mask) for source in range(lax.axis_size(axis))]
    return lax.ppermute(value, axis, pairs)


def norm_kernel(*refs):
    *parts, modulation_ref, out_ref = refs
    step = 16
    start = 0
    for part in parts:

        def body(index, carry, part=part, start=start):
            rows = pl.ds(pl.multiple_of(index * step, step), step)
            out_rows = pl.ds(pl.multiple_of(start + index * step, step), step)
            values = part[rows, :].astype(jnp.float32)
            centre = values - jnp.mean(values, axis=-1, keepdims=True)
            spread = jnp.mean(centre * centre, axis=-1, keepdims=True)
            normed = centre * lax.rsqrt(spread + 1e-06)
            out_ref[out_rows, :] = (
                normed * (1.0 + modulation_ref[1:2, :]) + modulation_ref[0:1, :]
            ).astype(jnp.bfloat16)
            return carry

        lax.fori_loop(0, part.shape[0] // step, body, 0)
        start += part.shape[0]


def modulated_norm(parts, modulation):
    rows, features = sum(part.shape[0] for part in parts), modulation.shape[1]
    return pl.pallas_call(
        norm_kernel,
        in_specs=[pl.BlockSpec(memory_space=pltpu.VMEM)] * (len(parts) + 1),
        out_shape=jax.ShapeDtypeStruct((rows, features), jnp.bfloat16),
        name="modulated_norm",
        cost_estimate=SHORT,
        compiler_params=pltpu.CompilerParams(vmem_limit_bytes=8 * MIB),
    )(*parts, modulation)


def gate_kernel(value_ref, *refs):
    pass


def after(value, earlier):
    return pl.pallas_call(
        gate_kernel,
        in_specs=[pl.BlockSpec(memory_space=pl.ANY)] * (1 + len(earlier)),
        out_specs=pl.BlockSpec(memory_space=pl.ANY),
        out_shape=jax.ShapeDtypeStruct(value.shape, value.dtype),
        input_output_aliases={0: 0},
        name="after",
        cost_estimate=SHORT,
        compiler_params=pltpu.CompilerParams(vmem_limit_bytes=MIB),
    )(value, *earlier)


def project_kernel(*refs, blocks):
    block_refs, (weights_ref, out_ref, total_ref, heads_ref, sems) = refs[:blocks], refs[blocks:]
    step, steps = pl.program_id(0), pl.num_programs(0)
    weights = jnp.concatenate([weights_ref[0], weights_ref[1], weights_ref[2]], axis=1)
    block = weights.shape[0]
    columns = pl.ds(pl.multiple_of(step * block, block), block)
    rows = jnp.concatenate([ref[:, columns] for ref in block_refs], axis=0)
    product = jnp.dot(rows, weights, preferred_element_type=jnp.float32)

    @pl.when(step == 0)
    def _():
        total_ref[...] = product

    @pl.when(step > 0)
    def _():
        total_ref[...] += product

    @pl.when(step == steps - 1)
    def _():
        heads = heads_ref.shape[0]
        copies = []
        for head in range(heads):
            values = total_ref[:, head * HD : (head + 1) * HD]
            if head < 2 * heads // 3:
                square = jnp.mean(values * values, axis=-1, keepdims=True)
                values = values * lax.rsqrt(square + 1e-06)
            heads_ref[head] = values.astype(jnp.bfloat16)
            copies.append(
                pltpu.make_async_copy(heads_ref.at[head], out_ref.at[head], sems.at[head])
            )
            copies[-1].start()
        for copy in copies:
            copy.wait()


def project(blocks, weights):
    _, depth, width = weights.shape
    steps = 4
    block = depth // steps
    count = sum(rows.shape[0] for rows in blocks)
    heads = 3 * width // HD
    return pl.pallas_call(
        functools.partial(project_kernel, blocks=len(blocks)),
        grid=(steps,),
        in_specs=[pl.BlockSpec(memory_space=pltpu.VMEM)] * len(blocks)
        + [pl.BlockSpec((3, block, width), lambda k: (0, k, 0))],
        out_specs=pl.BlockSpec(memory_space=pltpu.HBM),
        out_shape=jax.ShapeDtypeStruct((heads, count, HD), jnp.bfloat16),
        scratch_shapes=[
            pltpu.VMEM((count, 3 * width), jnp.float32),
            pltpu.VMEM((heads, count, HD), jnp.bfloat16),
            pltpu.SemaphoreType.DMA((heads,)),
        ],
        name="project_heads",
        cost_estimate=pl.CostEstimate(
            flops=2 * count * depth * 3 * width,
            bytes_accessed=2 * (count * depth + weights.size),
            transcendentals=0,
        ),
        compiler_params=pltpu.CompilerParams(vmem_limit_bytes=42 * MIB),
    )(*blocks, weights)


def attend_head(visible_ref, heads_ref, context_ref, out_ref, first_block, head):
    heads = heads_ref.shape[0] // 3
    tiles_seen = visible_ref.shape[1]
    tiles_fresh = visible_ref.shape[0]
    mine_high, mine_low = lax.axis_index("sp") // 2, lax.axis_index("sp") % 2
    mine_branch = lax.axis_index("cfg")

    def body(step, carry):
        index = first_block + step
        high, low = mine_high ^ ((index // 2) % 2), mine_low ^ (index // 4)
        tile, branch = high * 2 + low, mine_branch ^ (index % 2)
        rows = pl.ds(pl.multiple_of(index * TILE, TILE), TILE)
        out_rows = pl.ds(pl.multiple_of(step * TILE, TILE), TILE)
        places = []
        for seen in range(tiles_seen):
            number = visible_ref[tile, seen]
            older = jnp.maximum(number - tiles_fresh, 0)
            fresh = (mine_low ^ (number % 2)) * 4 + (mine_high ^ ((number // 2) % 2)) * 2
            fresh = (fresh + index % 2) * TILE
            stale = ((older // 2) * 2 + branch) * 2 * TILE + (older % 2) * TILE
            places.append(
                (
                    number < tiles_fresh,
                    pl.ds(pl.multiple_of(fresh, TILE), TILE),
                    pl.ds(pl.multiple_of(stale, TILE), TILE),
                )
            )

        def tiles(kind):
            start = ((kind - 1) * heads + head) * HD
            return jnp.concatenate(
                [
                    jnp.where(
                        is_fresh,
                        heads_ref[kind * heads + head, fresh, :],
                        context_ref[stale, start : start + HD],
                    )
                    for is_fresh, fresh, stale in places
                ],
                axis=0,
            )

        scores = lax.dot_general(
            heads_ref[head, rows, :],
            tiles(1),
            (((1,), (1,)), ((), ())),
            preferred_element_type=jnp.float32,
        )
        exponent = jnp.exp(scores * HD ** (-0.5))
        total = jnp.sum(exponent, axis=-1, keepdims=True)
        mixed = jnp.dot(
            exponent.astype(jnp.bfloat16), tiles(2), preferred_element_type=jnp.float32
        )
        out_ref[out_rows, head * HD : (head + 1) * HD] = (mixed / total).astype(jnp.bfloat16)
        return carry

    lax.fori_loop(0, out_ref.shape[0] // TILE, body, 0, unroll=2)


def attend_kernel(visible_ref, heads_in, context_in, *refs, first_block):
    out_ref, heads_ref, context_ref, sems = refs[-4:]
    heads = heads_ref.shape[0] // 3
    copies = []
    for head in range(heads):
        of_head = []
        for kind in range(3):
            place = kind * heads + head
            of_head.append(
                pltpu.make_async_copy(heads_in.at[place], heads_ref.at[place], sems.at[head, kind])
            )
        for kind in range(2):
            columns = pl.ds((kind * heads + head) * HD, HD)
            of_head.append(
                pltpu.make_async_copy(
                    context_in.at[:, columns], context_ref.at[:, columns], sems.at[head, 3 + kind]
                )
            )
        for copy in of_head:
            copy.start()
        copies.append(of_head)
    for head in range(heads):
        for copy in copies[head]:
            copy.wait()
        attend_head(visible_ref, heads_ref, context_ref, out_ref, first_block, head)


def attend(heads, context, visible, first_block, earlier):
    count = heads.shape[1] // 2
    return pl.pallas_call(
        functools.partial(attend_kernel, first_block=first_block),
        in_specs=[
            pl.BlockSpec(memory_space=pltpu.SMEM),
            pl.BlockSpec(memory_space=pltpu.HBM),
            pl.BlockSpec(memory_space=pl.ANY),
        ]
        + [pl.BlockSpec(memory_space=pl.ANY)] * len(earlier),
        out_specs=pl.BlockSpec(memory_space=pltpu.VMEM),
        out_shape=jax.ShapeDtypeStruct((count, heads.shape[0] // 3 * HD), jnp.bfloat16),
        scratch_shapes=[
            pltpu.VMEM(heads.shape, heads.dtype),
            pltpu.VMEM(context.shape, context.dtype),
            pltpu.SemaphoreType.DMA((heads.shape[0] // 3, 5)),
        ],
        name="attend",
        cost_estimate=SHORT,
        compiler_params=pltpu.CompilerParams(vmem_limit_bytes=53 * MIB),
    )(visible, heads, context, *earlier)


def combined(own, other, mine, gates_ref, columns):
    conditional = lax.axis_index("cfg") == 1
    last = lax.axis_index("pipe") == lax.axis_size("pipe") - 1
    weight = jnp.where(conditional, guidance_scale, 1.0 - guidance_scale).astype(jnp.float32)
    other_weight = jnp.where(conditional, 1.0 - guidance_scale, guidance_scale).astype(jnp.float32)
    own = own * gates_ref[0:1, columns]
    other = other * gates_ref[1:2, columns]
    if mine is not None:
        own = own + mine
    guided = weight * own + other_weight * other
    return jnp.where(last, guided, other), jnp.where(last, guided, own)


def begin(start, refs, across_out, along_out, first_kept, second_kept):
    attended_ref, core_attended_ref, *weights_refs, rows_ref, gates_ref = refs
    tokens, half = rows_ref.shape[0], first_kept.shape[2]
    attended = jnp.concatenate([attended_ref[...], core_attended_ref[...]], axis=1)

    def product_of(columns):
        weights = jnp.concatenate([ref[:, columns] for ref in weights_refs], axis=0)
        return jnp.dot(attended, weights, preferred_element_type=jnp.float32)

    columns = slice(start, start + half)
    product = product_of(slice(0, half))
    for tile in range(2):
        sent_columns = slice(tile * half, (tile + 1) * half)
        own = product[2 * tile * tokens : (2 * tile + 1) * tokens]
        other = product[(2 * tile + 1) * tokens : (2 * tile + 2) * tokens]
        mine = rows_ref[:, columns].astype(jnp.float32) if tile == 0 else None
        sent, kept = combined(own, other, mine, gates_ref, columns)
        across_out[:, sent_columns] = sent.astype(jnp.bfloat16)
        first_kept[tile] = kept
    product = product_of(slice(half, 2 * half))
    for branch in range(2):
        sent_columns = slice(branch * half, (branch + 1) * half)
        second_kept[branch] = product[branch * tokens : (branch + 1) * tokens]
        along_out[:, sent_columns] = product[(branch + 2) * tokens : (branch + 3) * tokens].astype(
            jnp.bfloat16
        )


def stage_kernel(*refs, parts, start, next_start, fresh, middle, final):
    named = dict(zip(parts, refs))
    if fresh:
        begin(
            next_start,
            [
                named[name]
                for name in (
                    "attended", "core_attended", "weights", "core_weights", "rows", "gates"
                )
            ],
            named["across_out"],
            named["along_out"],
            named["first_kept_out"],
            named["second_kept_out"],
        )
    if middle:
        across, along = named["across"], named["along"]
        first_kept, second_kept = named["first_kept"], named["second_kept"]
        half = first_kept.shape[2]
        sent_columns = slice(named["across_out"].shape[1] - half, named["across_out"].shape[1])
        named["along_out"][:, sent_columns] = (
            first_kept[1] + across[:, half : 2 * half].astype(jnp.float32)
        ).astype(jnp.bfloat16)
        named["first_left_out"][...] = first_kept[0] + across[:, :half].astype(jnp.float32)
        columns = slice(start + half, start + 2 * half)
        sent, kept = combined(
            second_kept[0] + along[:, :half].astype(jnp.float32),
            second_kept[1] + along[:, half : 2 * half].astype(jnp.float32),
            named["rows"][:, columns].astype(jnp.float32),
            named["gates"],
            columns,
        )
        named["across_out"][:, sent_columns] = sent.astype(jnp.bfloat16)
        named["second_left_out"][...] = kept
    if final:
        across, along = named["across"], named["along"]
        first_left, second_left = named["first_left"], named["second_left"]
        half = first_left.shape[1]
        columns = slice(across.shape[1] - half, across.shape[1])
        named["done_out"][:, :half] = (
            first_left[...] + along[:, columns].astype(jnp.float32)
        ).astype(jnp.bfloat16)
        named["done_out"][:, half:] = (
            second_left[...] + across[:, columns].astype(jnp.float32)
        ).astype(jnp.bfloat16)


def stage(operands, earlier, chunks, index, fresh, middle, final):
    tokens = operands["rows"].shape[0]
    next_start, next_chunk = chunks[index + 2] if fresh else (0, 0)
    start, chunk = chunks[index] if middle else (0, 0)
    outs = {}
    if fresh or middle:
        columns = next_chunk + chunk // 2
        outs["across_out"] = jax.ShapeDtypeStruct((tokens, columns), jnp.bfloat16)
        outs["along_out"] = outs["across_out"]
    if fresh:
        outs["first_kept_out"] = jax.ShapeDtypeStruct((2, tokens, next_chunk // 2), jnp.float32)
        outs["second_kept_out"] = outs["first_kept_out"]
    if middle:
        outs["first_left_out"] = jax.ShapeDtypeStruct((tokens, chunk // 2), jnp.float32)
        outs["second_left_out"] = outs["first_left_out"]
    if final:
        outs["done_out"] = jax.ShapeDtypeStruct((tokens, chunks[index - 2][1]), jnp.bfloat16)
    parts = list(operands) + ["earlier"] * len(earlier) + list(outs)
    results = pl.pallas_call(
        functools.partial(
            stage_kernel,
            parts=parts,
            start=start,
            next_start=next_start,
            fresh=fresh,
            middle=middle,
            final=final,
        ),
        grid=(1,),
        in_specs=[
            pl.BlockSpec((array.shape[0], next_chunk), lambda step: (0, next_start // next_chunk))
            if name in ("weights", "core_weights")
            else pl.BlockSpec(memory_space=pltpu.VMEM)
            for name, array in operands.items()
        ]
        + [pl.BlockSpec(memory_space=pl.ANY)] * len(earlier),
        out_specs=[pl.BlockSpec(memory_space=pltpu.VMEM)] * len(outs),
        out_shape=list(outs.values()),
        name="sum_stage",
        cost_estimate=SHORT,
        compiler_params=pltpu.CompilerParams(vmem_limit_bytes=16 * MIB),
    )(*operands.values(), *earlier)
    return dict(zip(outs, results))


def per_device(flight, modulation, project_in, project_out, stale_cache, visible):
    current = flight[0, 0]
    modulate = modulation[0, 0]
    token_rows, features = current.shape
    devices = lax.axis_size("sp") * lax.axis_size("cfg")

    context_rows = stale_cache.shape[2]
    width = project_in.shape[3]
    packed = stale_cache[0, 0].reshape(context_rows, 2, devices, width)
    packed = packed.transpose(2, 0, 1, 3).reshape(devices, context_rows, 2 * width)

    upper, lower = current[: token_rows // 2], current[token_rows // 2 :]
    across_upper, along_lower = from_partner(upper, "cfg", 1), from_partner(lower, "sp", 2)
    across_lower, along_upper = from_partner(lower, "cfg", 1), from_partner(upper, "sp", 2)
    other_modulate = from_partner(modulate, "cfg", 1)
    first, second = from_partner(across_upper, "sp", 2), from_partner(along_lower, "cfg", 1)
    core_weights = from_partner(project_out[0], "sp", 1)
    near = [
        modulated_norm([current], modulate),
        modulated_norm([across_upper, across_lower], other_modulate),
        modulated_norm([along_upper, along_lower], modulate),
        modulated_norm([first, second], other_modulate),
    ]
    far = [from_partner(rows, "sp", 1) for rows in near]

    packed = after(packed, (across_lower, along_upper, other_modulate))
    context = lax.all_to_all(packed, ("sp", "cfg"), split_axis=0, concat_axis=0, tiled=True)
    context = context.reshape(devices * context_rows, 2 * width)

    heads = project(near + far, project_in[0])
    gates = jnp.concatenate([modulate[2:3], other_modulate[2:3]], axis=0)
    count = len(CHUNK_SHARES)
    unit = features // sum(CHUNK_SHARES)
    chunks = [
        (sum(CHUNK_SHARES[:index]) * unit, share * unit) for index, share in enumerate(CHUNK_SHARES)
    ]
    for_core = attend(heads, context, visible[0], heads.shape[1] // TILE // 2, ())
    core_attended = from_partner(for_core, "sp", 1)
    attended = attend(heads, context, visible[0], 0, (for_core, gates))

    kept, left, flights, arrivals, earlier = {}, {}, {}, [], []
    for index in range(-2, count + 2):
        fresh, middle, final = index + 2 < count, 0 <= index < count, index >= 2
        operands = {"rows": current, "gates": gates}
        if fresh:
            operands.update(
                attended=attended,
                core_attended=core_attended,
                weights=project_out[0],
                core_weights=core_weights,
            )
        if index >= 0:
            operands["across"], operands["along"] = flights.pop(index)
        if middle:
            operands["first_kept"], operands["second_kept"] = kept.pop(index)
        if final:
            operands["first_left"], operands["second_left"] = left.pop(index - 2)
        outs = stage(
            operands,
            earlier,
            chunks,
            index,
            fresh,
            middle,
            final,
        )
        if "across_out" in outs:
            flights[index + 2] = (
                from_partner(outs["across_out"], "cfg", 1),
                from_partner(outs["along_out"], "sp", 2),
            )
        if fresh:
            kept[index + 2] = (outs["first_kept_out"], outs["second_kept_out"])
        if middle:
            left[index] = (outs["first_left_out"], outs["second_left_out"])
        if final:
            arrivals.append(from_behind(outs["done_out"], "pipe", 1))
        earlier = [list(outs.values())[-1]] + (arrivals[-2:-1] if 3 <= index < count else [])
    return jnp.concatenate(arrivals, axis=1)[None, None]


def solution(mesh):
    placed = (
        P("pipe", "cfg", "sp", None),
        P("pipe", "cfg", None, None),
        P("pipe", None, None, ("sp", "cfg")),
        P("pipe", ("sp", "cfg"), None),
        P("pipe", "cfg", "sp", None, None),
        P("pipe", None, None),
    )
    return jax.shard_map(
        per_device,
        mesh=mesh,
        in_specs=placed,
        out_specs=P("pipe", "cfg", "sp", None),
        check_vma=False,
    )
```

```python
import functools

import jax
import jax.numpy as jnp
from jax import lax
from jax.experimental import pallas as pl
from jax.experimental.pallas import tpu as pltpu
from jax.sharding import PartitionSpec as P

HD = 128
TILE = 128
MIB = 2**20
SPARE = 39
CHUNK_SHARES = (4, 4, 4, 4, 2, 2)

guidance_scale = 5.0
SHORT = pl.CostEstimate(flops=1, bytes_accessed=1, transcendentals=0)


def from_behind(x, axis, by):
    count = lax.axis_size(axis)
    return lax.ppermute(x, axis, [(i, (i + by) % count) for i in range(count)])


def from_partner(value, axis, mask):
    pairs = [(source, source ^ mask) for source in range(lax.axis_size(axis))]
    return lax.ppermute(value, axis, pairs)


def norm_kernel(*refs):
    *parts, modulation_ref, out_ref = refs
    step = 16
    start = 0
    for part in parts:

        def body(index, carry, part=part, start=start):
            rows = pl.ds(pl.multiple_of(index * step, step), step)
            out_rows = pl.ds(pl.multiple_of(start + index * step, step), step)
            values = part[rows, :].astype(jnp.float32)
            centre = values - jnp.mean(values, axis=-1, keepdims=True)
            spread = jnp.mean(centre * centre, axis=-1, keepdims=True)
            normed = centre * lax.rsqrt(spread + 1e-06)
            out_ref[out_rows, :] = (
                normed * (1.0 + modulation_ref[1:2, :]) + modulation_ref[0:1, :]
            ).astype(jnp.bfloat16)
            return carry

        lax.fori_loop(0, part.shape[0] // step, body, 0, unroll=2)
        start += part.shape[0]


def modulated_norm(parts, modulation):
    rows, features = sum(part.shape[0] for part in parts), modulation.shape[1]
    return pl.pallas_call(
        norm_kernel,
        in_specs=[pl.BlockSpec(memory_space=pltpu.VMEM)] * (len(parts) + 1),
        out_shape=jax.ShapeDtypeStruct((rows, features), jnp.bfloat16),
        name="modulated_norm",
        cost_estimate=SHORT,
        compiler_params=pltpu.CompilerParams(vmem_limit_bytes=8 * MIB),
    )(*parts, modulation)


def gate_kernel(value_ref, *refs):
    pass


def after(value, earlier):
    return pl.pallas_call(
        gate_kernel,
        in_specs=[pl.BlockSpec(memory_space=pl.ANY)] * (1 + len(earlier)),
        out_specs=pl.BlockSpec(memory_space=pl.ANY),
        out_shape=jax.ShapeDtypeStruct(value.shape, value.dtype),
        input_output_aliases={0: 0},
        name="after",
        cost_estimate=SHORT,
        compiler_params=pltpu.CompilerParams(vmem_limit_bytes=MIB),
    )(value, *earlier)


def project_kernel(*refs, blocks):
    block_refs, (weights_ref, out_ref, total_ref, heads_ref, sems) = refs[:blocks], refs[blocks:]
    step, steps = pl.program_id(0), pl.num_programs(0)
    weights = jnp.concatenate([weights_ref[0], weights_ref[1], weights_ref[2]], axis=1)
    block = weights.shape[0]
    columns = pl.ds(pl.multiple_of(step * block, block), block)
    rows = jnp.concatenate([ref[:, columns] for ref in block_refs], axis=0)
    product = jnp.dot(rows, weights, preferred_element_type=jnp.float32)

    @pl.when(step == 0)
    def _():
        total_ref[...] = product

    @pl.when((step > 0) & (step < steps - 1))
    def _():
        total_ref[...] += product

    @pl.when(step == steps - 1)
    def _():
        heads = heads_ref.shape[0]
        copies = []
        for head in range(heads):
            columns = slice(head * HD, (head + 1) * HD)
            values = total_ref[:, columns] + product[:, columns]
            if head < 2 * heads // 3:
                square = jnp.mean(values * values, axis=-1, keepdims=True)
                values = values * lax.rsqrt(square + 1e-06)
            heads_ref[head] = values.astype(jnp.bfloat16)
            copies.append(
                pltpu.make_async_copy(heads_ref.at[head], out_ref.at[head], sems.at[head])
            )
            copies[-1].start()
        for copy in copies:
            copy.wait()


def project(blocks, weights):
    _, depth, width = weights.shape
    steps = 2
    block = depth // steps
    count = sum(rows.shape[0] for rows in blocks)
    heads = 3 * width // HD
    return pl.pallas_call(
        functools.partial(project_kernel, blocks=len(blocks)),
        grid=(steps,),
        in_specs=[pl.BlockSpec(memory_space=pltpu.VMEM)] * len(blocks)
        + [pl.BlockSpec((3, block, width), lambda k: (0, k, 0))],
        out_specs=pl.BlockSpec(memory_space=pltpu.HBM),
        out_shape=jax.ShapeDtypeStruct((heads + SPARE, count, HD), jnp.bfloat16),
        scratch_shapes=[
            pltpu.VMEM((count, 3 * width), jnp.float32),
            pltpu.VMEM((heads, count, HD), jnp.bfloat16),
            pltpu.SemaphoreType.DMA((heads,)),
        ],
        name="project_heads",
        cost_estimate=pl.CostEstimate(
            flops=2 * count * depth * 3 * width,
            bytes_accessed=2 * (count * depth + weights.size),
            transcendentals=0,
        ),
        compiler_params=pltpu.CompilerParams(vmem_limit_bytes=42 * MIB),
    )(*blocks, weights)


def attend_blocks(visible_ref, heads_ref, context_ref, out_ref, first_block):
    heads = heads_ref.shape[0] // 3
    tiles_seen = visible_ref.shape[1]
    tiles_fresh = visible_ref.shape[0]
    mine_high, mine_low = lax.axis_index("sp") // 2, lax.axis_index("sp") % 2
    mine_branch = lax.axis_index("cfg")

    def body(step, carry):
        index = first_block + step
        high, low = mine_high ^ ((index // 2) % 2), mine_low ^ (index // 4)
        tile, branch = high * 2 + low, mine_branch ^ (index % 2)
        rows = pl.ds(pl.multiple_of(index * TILE, TILE), TILE)
        out_rows = pl.ds(pl.multiple_of(step * TILE, TILE), TILE)
        places = []
        for seen in range(tiles_seen):
            number = visible_ref[tile, seen]
            older = jnp.maximum(number - tiles_fresh, 0)
            fresh = (mine_low ^ (number % 2)) * 4 + (mine_high ^ ((number // 2) % 2)) * 2
            fresh = (fresh + index % 2) * TILE
            stale = ((older // 2) * 2 + branch) * 2 * TILE + (older % 2) * TILE
            places.append(
                (
                    number < tiles_fresh,
                    pl.ds(pl.multiple_of(fresh, TILE), TILE),
                    pl.ds(pl.multiple_of(stale, TILE), TILE),
                )
            )

        def tiles(kind, head):
            start = ((kind - 1) * heads + head) * HD
            return jnp.concatenate(
                [
                    jnp.where(
                        is_fresh,
                        heads_ref[kind * heads + head, fresh, :],
                        context_ref[stale, start : start + HD],
                    )
                    for is_fresh, fresh, stale in places
                ],
                axis=0,
            )

        for head in range(heads):
            scores = lax.dot_general(
                heads_ref[head, rows, :],
                tiles(1, head),
                (((1,), (1,)), ((), ())),
                preferred_element_type=jnp.float32,
            )
            exponent = jnp.exp(scores * HD ** (-0.5))
            total = jnp.sum(exponent, axis=-1, keepdims=True)
            mixed = jnp.dot(
                exponent.astype(jnp.bfloat16), tiles(2, head), preferred_element_type=jnp.float32
            )
            out_ref[out_rows, head * HD : (head + 1) * HD] = (mixed / total).astype(jnp.bfloat16)
        return carry

    lax.fori_loop(0, out_ref.shape[0] // TILE, body, 0, unroll=2)


def attend_first_kernel(
    visible_ref, heads_in, context_in, out_ref, heads_ref, context_ref, heads_sem, context_sem
):
    copies = (
        pltpu.make_async_copy(
            heads_in.at[pl.ds(0, heads_ref.shape[0])], heads_ref, heads_sem
        ),
        pltpu.make_async_copy(context_in, context_ref, context_sem),
    )
    for copy in copies:
        copy.start()
    for copy in copies:
        copy.wait()
    attend_blocks(visible_ref, heads_ref, context_ref, out_ref, out_ref.shape[0] // TILE)


def attend_first(heads, context, visible):
    number, count = heads.shape[0] - SPARE, heads.shape[1] // 2
    return pl.pallas_call(
        attend_first_kernel,
        in_specs=[
            pl.BlockSpec(memory_space=pltpu.SMEM),
            pl.BlockSpec(memory_space=pltpu.HBM),
            pl.BlockSpec(memory_space=pl.ANY),
        ],
        out_specs=[pl.BlockSpec(memory_space=pltpu.VMEM)] * 3,
        out_shape=[
            jax.ShapeDtypeStruct((count, number // 3 * HD), jnp.bfloat16),
            jax.ShapeDtypeStruct((number,) + heads.shape[1:], heads.dtype),
            jax.ShapeDtypeStruct(context.shape, context.dtype),
        ],
        scratch_shapes=[pltpu.SemaphoreType.DMA, pltpu.SemaphoreType.DMA],
        name="attend_first",
        cost_estimate=SHORT,
        compiler_params=pltpu.CompilerParams(vmem_limit_bytes=44 * MIB),
    )(visible, heads, context)


def attend_second_kernel(visible_ref, heads_ref, context_ref, *refs):
    attend_blocks(visible_ref, heads_ref, context_ref, refs[-1], 0)


def attend_second(heads, context, visible, earlier):
    count = heads.shape[1] // 2
    return pl.pallas_call(
        attend_second_kernel,
        in_specs=[pl.BlockSpec(memory_space=pltpu.SMEM)]
        + [pl.BlockSpec(memory_space=pltpu.VMEM)] * 2
        + [pl.BlockSpec(memory_space=pl.ANY)] * len(earlier),
        out_specs=pl.BlockSpec(memory_space=pltpu.VMEM),
        out_shape=jax.ShapeDtypeStruct((count, heads.shape[0] // 3 * HD), jnp.bfloat16),
        name="attend_second",
        cost_estimate=SHORT,
        compiler_params=pltpu.CompilerParams(vmem_limit_bytes=12 * MIB),
    )(visible, heads, context, *earlier)


def combined(own, other, mine, gates_ref, columns):
    conditional = lax.axis_index("cfg") == 1
    last = lax.axis_index("pipe") == lax.axis_size("pipe") - 1
    weight = jnp.where(conditional, guidance_scale, 1.0 - guidance_scale).astype(jnp.float32)
    other_weight = jnp.where(conditional, 1.0 - guidance_scale, guidance_scale).astype(jnp.float32)
    own = own * gates_ref[0:1, columns]
    other = other * gates_ref[1:2, columns]
    if mine is not None:
        own = own + mine
    guided = weight * own + other_weight * other
    return jnp.where(last, guided, other), jnp.where(last, guided, own)


def begin(start, refs, across_out, along_out, first_kept, second_kept):
    attended_ref, core_attended_ref, *weights_refs, rows_ref, gates_ref = refs
    tokens, half = rows_ref.shape[0], first_kept.shape[2]
    attended = jnp.concatenate([attended_ref[...], core_attended_ref[...]], axis=1)

    def product_of(columns):
        weights = jnp.concatenate([ref[:, columns] for ref in weights_refs], axis=0)
        return jnp.dot(attended, weights, preferred_element_type=jnp.float32)

    columns = slice(start, start + half)
    product = product_of(slice(0, half))
    for tile in range(2):
        sent_columns = slice(tile * half, (tile + 1) * half)
        own = product[2 * tile * tokens : (2 * tile + 1) * tokens]
        other = product[(2 * tile + 1) * tokens : (2 * tile + 2) * tokens]
        mine = rows_ref[:, columns].astype(jnp.float32) if tile == 0 else None
        sent, kept = combined(own, other, mine, gates_ref, columns)
        across_out[:, sent_columns] = sent.astype(jnp.bfloat16)
        first_kept[tile] = kept
    product = product_of(slice(half, 2 * half))
    for branch in range(2):
        sent_columns = slice(branch * half, (branch + 1) * half)
        second_kept[branch] = product[branch * tokens : (branch + 1) * tokens]
        along_out[:, sent_columns] = product[(branch + 2) * tokens : (branch + 3) * tokens].astype(
            jnp.bfloat16
        )


def stage_kernel(*refs, parts, start, next_start, fresh, middle, final):
    named = dict(zip(parts, refs))
    if fresh:
        begin(
            next_start,
            [
                named[name]
                for name in (
                    "attended", "core_attended", "weights", "core_weights", "rows", "gates"
                )
            ],
            named["across_out"],
            named["along_out"],
            named["first_kept_out"],
            named["second_kept_out"],
        )
    if middle:
        across, along = named["across"], named["along"]
        first_kept, second_kept = named["first_kept"], named["second_kept"]
        half = first_kept.shape[2]
        sent_columns = slice(named["across_out"].shape[1] - half, named["across_out"].shape[1])
        named["along_out"][:, sent_columns] = (
            first_kept[1] + across[:, half : 2 * half].astype(jnp.float32)
        ).astype(jnp.bfloat16)
        named["first_left_out"][...] = first_kept[0] + across[:, :half].astype(jnp.float32)
        columns = slice(start + half, start + 2 * half)
        sent, kept = combined(
            second_kept[0] + along[:, :half].astype(jnp.float32),
            second_kept[1] + along[:, half : 2 * half].astype(jnp.float32),
            named["rows"][:, columns].astype(jnp.float32),
            named["gates"],
            columns,
        )
        named["across_out"][:, sent_columns] = sent.astype(jnp.bfloat16)
        named["second_left_out"][...] = kept
    if final:
        across, along = named["across"], named["along"]
        first_left, second_left = named["first_left"], named["second_left"]
        half = first_left.shape[1]
        columns = slice(across.shape[1] - half, across.shape[1])
        named["done_out"][:, :half] = (
            first_left[...] + along[:, columns].astype(jnp.float32)
        ).astype(jnp.bfloat16)
        named["done_out"][:, half:] = (
            second_left[...] + across[:, columns].astype(jnp.float32)
        ).astype(jnp.bfloat16)


def stage(operands, earlier, chunks, index, fresh, middle, final):
    tokens = operands["rows"].shape[0]
    next_start, next_chunk = chunks[index + 2] if fresh else (0, 0)
    start, chunk = chunks[index] if middle else (0, 0)
    outs = {}
    if fresh or middle:
        columns = next_chunk + chunk // 2
        outs["across_out"] = jax.ShapeDtypeStruct((tokens, columns), jnp.bfloat16)
        outs["along_out"] = outs["across_out"]
    if fresh:
        outs["first_kept_out"] = jax.ShapeDtypeStruct((2, tokens, next_chunk // 2), jnp.float32)
        outs["second_kept_out"] = outs["first_kept_out"]
    if middle:
        outs["first_left_out"] = jax.ShapeDtypeStruct((tokens, chunk // 2), jnp.float32)
        outs["second_left_out"] = outs["first_left_out"]
    if final:
        outs["done_out"] = jax.ShapeDtypeStruct((tokens, chunks[index - 2][1]), jnp.bfloat16)
    parts = list(operands) + ["earlier"] * len(earlier) + list(outs)
    results = pl.pallas_call(
        functools.partial(
            stage_kernel,
            parts=parts,
            start=start,
            next_start=next_start,
            fresh=fresh,
            middle=middle,
            final=final,
        ),
        grid=(1,),
        in_specs=[
            pl.BlockSpec((array.shape[0], next_chunk), lambda step: (0, next_start // next_chunk))
            if name in ("weights", "core_weights")
            else pl.BlockSpec(memory_space=pltpu.VMEM)
            for name, array in operands.items()
        ]
        + [pl.BlockSpec(memory_space=pl.ANY)] * len(earlier),
        out_specs=[pl.BlockSpec(memory_space=pltpu.VMEM)] * len(outs),
        out_shape=list(outs.values()),
        name="sum_stage",
        cost_estimate=SHORT,
        compiler_params=pltpu.CompilerParams(vmem_limit_bytes=16 * MIB),
    )(*operands.values(), *earlier)
    return dict(zip(outs, results))


def per_device(flight, modulation, project_in, project_out, stale_cache, visible):
    current = flight[0, 0]
    modulate = modulation[0, 0]
    token_rows, features = current.shape
    devices = lax.axis_size("sp") * lax.axis_size("cfg")

    context_rows = stale_cache.shape[2]
    width = project_in.shape[3]
    packed = stale_cache[0, 0].reshape(context_rows, 2, devices, width)
    packed = packed.transpose(2, 0, 1, 3).reshape(devices, context_rows, 2 * width)

    upper, lower = current[: token_rows // 2], current[token_rows // 2 :]
    across_upper, along_lower = from_partner(upper, "cfg", 1), from_partner(lower, "sp", 2)
    across_lower, along_upper = from_partner(lower, "cfg", 1), from_partner(upper, "sp", 2)
    other_modulate = from_partner(modulate, "cfg", 1)
    first, second = from_partner(across_upper, "sp", 2), from_partner(along_lower, "cfg", 1)
    core_weights = from_partner(project_out[0], "sp", 1)
    near = [
        modulated_norm([current], modulate),
        modulated_norm([across_upper, across_lower], other_modulate),
        modulated_norm([along_upper, along_lower], modulate),
        modulated_norm([first, second], other_modulate),
    ]
    far = [from_partner(rows, "sp", 1) for rows in near]

    packed = after(packed, (across_lower, along_upper, other_modulate))
    context = lax.all_to_all(packed, ("sp", "cfg"), split_axis=0, concat_axis=0, tiled=True)
    context = context.reshape(devices * context_rows, 2 * width)

    heads = project(near + far, project_in[0])
    gates = jnp.concatenate([modulate[2:3], other_modulate[2:3]], axis=0)
    count = len(CHUNK_SHARES)
    unit = features // sum(CHUNK_SHARES)
    chunks = [
        (sum(CHUNK_SHARES[:index]) * unit, share * unit) for index, share in enumerate(CHUNK_SHARES)
    ]
    for_core, heads, context = attend_first(heads, context, visible[0])
    core_attended = from_partner(for_core, "sp", 1)
    attended = attend_second(heads, context, visible[0], (for_core, gates))

    kept, left, flights, arrivals, earlier = {}, {}, {}, [], []
    for index in range(-2, count + 2):
        fresh, middle, final = index + 2 < count, 0 <= index < count, index >= 2
        operands = {"rows": current, "gates": gates}
        if fresh:
            operands.update(
                attended=attended,
                core_attended=core_attended,
                weights=project_out[0],
                core_weights=core_weights,
            )
        if index >= 0:
            operands["across"], operands["along"] = flights.pop(index)
        if middle:
            operands["first_kept"], operands["second_kept"] = kept.pop(index)
        if final:
            operands["first_left"], operands["second_left"] = left.pop(index - 2)
        outs = stage(
            operands,
            earlier,
            chunks,
            index,
            fresh,
            middle,
            final,
        )
        if "across_out" in outs:
            flights[index + 2] = (
                from_partner(outs["across_out"], "cfg", 1),
                from_partner(outs["along_out"], "sp", 2),
            )
        if fresh:
            kept[index + 2] = (outs["first_kept_out"], outs["second_kept_out"])
        if middle:
            left[index] = (outs["first_left_out"], outs["second_left_out"])
        if final:
            arrivals.append(from_behind(outs["done_out"], "pipe", 1))
        earlier = [list(outs.values())[-1]] + (arrivals[-2:-1] if 3 <= index < count else [])
    return jnp.concatenate(arrivals, axis=1)[None, None]


def solution(mesh):
    placed = (
        P("pipe", "cfg", "sp", None),
        P("pipe", "cfg", None, None),
        P("pipe", None, None, ("sp", "cfg")),
        P("pipe", ("sp", "cfg"), None),
        P("pipe", "cfg", "sp", None, None),
        P("pipe", None, None),
    )
    return jax.shard_map(
        per_device,
        mesh=mesh,
        in_specs=placed,
        out_specs=P("pipe", "cfg", "sp", None),
        check_vma=False,
    )
```

```python
import functools

import jax
import jax.numpy as jnp
from jax import lax
from jax.experimental import pallas as pl
from jax.experimental.pallas import tpu as pltpu
from jax.sharding import PartitionSpec as P

HD = 128
TILE = 128
MIB = 2**20
SPARE = 39
CHUNK_SHARES = (4, 4, 4, 4, 2, 2)

guidance_scale = 5.0
SHORT = pl.CostEstimate(flops=1, bytes_accessed=1, transcendentals=0)


def from_behind(x, axis, by):
    count = lax.axis_size(axis)
    return lax.ppermute(x, axis, [(i, (i + by) % count) for i in range(count)])


def from_partner(value, axis, mask):
    pairs = [(source, source ^ mask) for source in range(lax.axis_size(axis))]
    return lax.ppermute(value, axis, pairs)


def norm_kernel(*refs):
    *parts, modulation_ref, out_ref = refs
    step = 16
    start = 0
    for part in parts:

        def body(index, carry, part=part, start=start):
            rows = pl.ds(pl.multiple_of(index * step, step), step)
            out_rows = pl.ds(pl.multiple_of(start + index * step, step), step)
            values = part[rows, :].astype(jnp.float32)
            centre = values - jnp.mean(values, axis=-1, keepdims=True)
            spread = jnp.mean(centre * centre, axis=-1, keepdims=True)
            normed = centre * lax.rsqrt(spread + 1e-06)
            out_ref[out_rows, :] = (
                normed * (1.0 + modulation_ref[1:2, :]) + modulation_ref[0:1, :]
            ).astype(jnp.bfloat16)
            return carry

        lax.fori_loop(0, part.shape[0] // step, body, 0, unroll=2)
        start += part.shape[0]


def modulated_norm(parts, modulation):
    rows, features = sum(part.shape[0] for part in parts), modulation.shape[1]
    return pl.pallas_call(
        norm_kernel,
        in_specs=[pl.BlockSpec(memory_space=pltpu.VMEM)] * (len(parts) + 1),
        out_shape=jax.ShapeDtypeStruct((rows, features), jnp.bfloat16),
        name="modulated_norm",
        cost_estimate=SHORT,
        compiler_params=pltpu.CompilerParams(vmem_limit_bytes=8 * MIB),
    )(*parts, modulation)


def gate_kernel(value_ref, *refs):
    pass


def after(value, earlier):
    return pl.pallas_call(
        gate_kernel,
        in_specs=[pl.BlockSpec(memory_space=pl.ANY)] * (1 + len(earlier)),
        out_specs=pl.BlockSpec(memory_space=pl.ANY),
        out_shape=jax.ShapeDtypeStruct(value.shape, value.dtype),
        input_output_aliases={0: 0},
        name="after",
        cost_estimate=SHORT,
        compiler_params=pltpu.CompilerParams(vmem_limit_bytes=MIB),
    )(value, *earlier)


def project_kernel(*refs, blocks):
    block_refs, (weights_ref, out_ref, total_ref, heads_ref, sems) = refs[:blocks], refs[blocks:]
    step, steps = pl.program_id(0), pl.num_programs(0)
    weights = jnp.concatenate([weights_ref[0], weights_ref[1], weights_ref[2]], axis=1)
    block = weights.shape[0]
    columns = pl.ds(pl.multiple_of(step * block, block), block)
    rows = jnp.concatenate([ref[:, columns] for ref in block_refs], axis=0)
    product = jnp.dot(rows, weights, preferred_element_type=jnp.float32)

    @pl.when(step == 0)
    def _():
        total_ref[...] = product

    @pl.when((step > 0) & (step < steps - 1))
    def _():
        total_ref[...] += product

    @pl.when(step == steps - 1)
    def _():
        heads = heads_ref.shape[0]
        copies = []
        for head in range(heads):
            columns = slice(head * HD, (head + 1) * HD)
            values = total_ref[:, columns] + product[:, columns]
            if head < 2 * heads // 3:
                square = jnp.mean(values * values, axis=-1, keepdims=True)
                values = values * lax.rsqrt(square + 1e-06)
            heads_ref[head] = values.astype(jnp.bfloat16)
            copies.append(
                pltpu.make_async_copy(heads_ref.at[head], out_ref.at[head], sems.at[head])
            )
            copies[-1].start()
        for copy in copies:
            copy.wait()


def project(blocks, weights):
    _, depth, width = weights.shape
    steps = 2
    block = depth // steps
    count = sum(rows.shape[0] for rows in blocks)
    heads = 3 * width // HD
    return pl.pallas_call(
        functools.partial(project_kernel, blocks=len(blocks)),
        grid=(steps,),
        in_specs=[pl.BlockSpec(memory_space=pltpu.VMEM)] * len(blocks)
        + [pl.BlockSpec((3, block, width), lambda k: (0, k, 0))],
        out_specs=pl.BlockSpec(memory_space=pltpu.HBM),
        out_shape=jax.ShapeDtypeStruct((heads + SPARE, count, HD), jnp.bfloat16),
        scratch_shapes=[
            pltpu.VMEM((count, 3 * width), jnp.float32),
            pltpu.VMEM((heads, count, HD), jnp.bfloat16),
            pltpu.SemaphoreType.DMA((heads,)),
        ],
        name="project_heads",
        cost_estimate=pl.CostEstimate(
            flops=2 * count * depth * 3 * width,
            bytes_accessed=2 * (count * depth + weights.size),
            transcendentals=0,
        ),
        compiler_params=pltpu.CompilerParams(vmem_limit_bytes=42 * MIB),
    )(*blocks, weights)


def attend_head(visible_ref, heads_ref, context_ref, out_ref, first_block, head):
    heads = heads_ref.shape[0] // 3
    tiles_seen = visible_ref.shape[1]
    tiles_fresh = visible_ref.shape[0]
    mine_high, mine_low = lax.axis_index("sp") // 2, lax.axis_index("sp") % 2
    mine_branch = lax.axis_index("cfg")

    def body(step, carry):
        index = first_block + step
        high, low = mine_high ^ ((index // 2) % 2), mine_low ^ (index // 4)
        tile, branch = high * 2 + low, mine_branch ^ (index % 2)
        rows = pl.ds(pl.multiple_of(index * TILE, TILE), TILE)
        out_rows = pl.ds(pl.multiple_of(step * TILE, TILE), TILE)
        places = []
        for seen in range(tiles_seen):
            number = visible_ref[tile, seen]
            older = jnp.maximum(number - tiles_fresh, 0)
            fresh = (mine_low ^ (number % 2)) * 4 + (mine_high ^ ((number // 2) % 2)) * 2
            fresh = (fresh + index % 2) * TILE
            stale = ((older // 2) * 2 + branch) * 2 * TILE + (older % 2) * TILE
            places.append(
                (
                    number < tiles_fresh,
                    pl.ds(pl.multiple_of(fresh, TILE), TILE),
                    pl.ds(pl.multiple_of(stale, TILE), TILE),
                )
            )

        def tiles(kind):
            start = ((kind - 1) * heads + head) * HD
            return jnp.concatenate(
                [
                    jnp.where(
                        is_fresh,
                        heads_ref[kind * heads + head, fresh, :],
                        context_ref[stale, start : start + HD],
                    )
                    for is_fresh, fresh, stale in places
                ],
                axis=0,
            )

        scores = lax.dot_general(
            heads_ref[head, rows, :],
            tiles(1),
            (((1,), (1,)), ((), ())),
            preferred_element_type=jnp.float32,
        )
        exponent = jnp.exp(scores * HD ** (-0.5))
        total = jnp.sum(exponent, axis=-1, keepdims=True)
        mixed = jnp.dot(
            exponent.astype(jnp.bfloat16), tiles(2), preferred_element_type=jnp.float32
        )
        out_ref[out_rows, head * HD : (head + 1) * HD] = (mixed / total).astype(jnp.bfloat16)
        return carry

    lax.fori_loop(0, out_ref.shape[0] // TILE, body, 0, unroll=True)


def attend_first_kernel(
    visible_ref, heads_in, context_in, out_ref, heads_ref, context_ref, sems
):
    heads = heads_ref.shape[0] // 3
    copies = []
    for head in range(heads):
        of_head = []
        for kind in range(3):
            place = kind * heads + head
            of_head.append(
                pltpu.make_async_copy(heads_in.at[place], heads_ref.at[place], sems.at[head, kind])
            )
        for kind in range(2):
            columns = pl.ds((kind * heads + head) * HD, HD)
            of_head.append(
                pltpu.make_async_copy(
                    context_in.at[:, columns], context_ref.at[:, columns], sems.at[head, 3 + kind]
                )
            )
        for copy in of_head:
            copy.start()
        copies.append(of_head)
    for head in range(heads):
        for copy in copies[head]:
            copy.wait()
        first_block = out_ref.shape[0] // TILE
        attend_head(visible_ref, heads_ref, context_ref, out_ref, first_block, head)


def attend_first(heads, context, visible):
    number, count = heads.shape[0] - SPARE, heads.shape[1] // 2
    return pl.pallas_call(
        attend_first_kernel,
        in_specs=[
            pl.BlockSpec(memory_space=pltpu.SMEM),
            pl.BlockSpec(memory_space=pltpu.HBM),
            pl.BlockSpec(memory_space=pl.ANY),
        ],
        out_specs=[pl.BlockSpec(memory_space=pltpu.VMEM)] * 3,
        out_shape=[
            jax.ShapeDtypeStruct((count, number // 3 * HD), jnp.bfloat16),
            jax.ShapeDtypeStruct((number,) + heads.shape[1:], heads.dtype),
            jax.ShapeDtypeStruct(context.shape, context.dtype),
        ],
        scratch_shapes=[pltpu.SemaphoreType.DMA((number // 3, 5))],
        name="attend_first",
        cost_estimate=SHORT,
        compiler_params=pltpu.CompilerParams(vmem_limit_bytes=44 * MIB),
    )(visible, heads, context)


def attend_second_kernel(visible_ref, heads_ref, context_ref, *refs):
    weights_ref, core_weights_ref = refs[:2]
    out_ref, both_ref, sems = refs[-3:]
    depth, columns = weights_ref.shape[0], pl.ds(0, both_ref.shape[1])
    copies = [
        pltpu.make_async_copy(
            ref.at[:, columns], both_ref.at[pl.ds(core * depth, depth)], sems.at[core]
        )
        for core, ref in enumerate((weights_ref, core_weights_ref))
    ]
    for copy in copies:
        copy.start()
    for head in range(heads_ref.shape[0] // 3):
        attend_head(visible_ref, heads_ref, context_ref, out_ref, 0, head)
    for copy in copies:
        copy.wait()


def attend_second(heads, context, visible, weights, core_weights, columns, earlier):
    count = heads.shape[1] // 2
    return pl.pallas_call(
        attend_second_kernel,
        in_specs=[pl.BlockSpec(memory_space=pltpu.SMEM)]
        + [pl.BlockSpec(memory_space=pltpu.VMEM)] * 2
        + [pl.BlockSpec(memory_space=pl.ANY)] * (2 + len(earlier)),
        out_specs=[pl.BlockSpec(memory_space=pltpu.VMEM)] * 2,
        out_shape=[
            jax.ShapeDtypeStruct((count, heads.shape[0] // 3 * HD), jnp.bfloat16),
            jax.ShapeDtypeStruct((2 * weights.shape[0], columns), weights.dtype),
        ],
        scratch_shapes=[pltpu.SemaphoreType.DMA((2,))],
        name="attend_second",
        cost_estimate=SHORT,
        compiler_params=pltpu.CompilerParams(vmem_limit_bytes=12 * MIB),
    )(visible, heads, context, weights, core_weights, *earlier)


def combined(own, other, mine, gates_ref, columns):
    conditional = lax.axis_index("cfg") == 1
    last = lax.axis_index("pipe") == lax.axis_size("pipe") - 1
    weight = jnp.where(conditional, guidance_scale, 1.0 - guidance_scale).astype(jnp.float32)
    other_weight = jnp.where(conditional, 1.0 - guidance_scale, guidance_scale).astype(jnp.float32)
    own = own * gates_ref[0:1, columns]
    other = other * gates_ref[1:2, columns]
    if mine is not None:
        own = own + mine
    guided = weight * own + other_weight * other
    return jnp.where(last, guided, other), jnp.where(last, guided, own)


def begin(start, refs, across_out, along_out, first_kept, second_kept):
    attended_ref, core_attended_ref, *weights_refs, rows_ref, gates_ref = refs
    tokens, half = rows_ref.shape[0], first_kept.shape[2]
    attended = jnp.concatenate([attended_ref[...], core_attended_ref[...]], axis=1)

    def product_of(columns):
        weights = jnp.concatenate([ref[:, columns] for ref in weights_refs], axis=0)
        return jnp.dot(attended, weights, preferred_element_type=jnp.float32)

    columns = slice(start, start + half)
    product = product_of(slice(0, half))
    for tile in range(2):
        sent_columns = slice(tile * half, (tile + 1) * half)
        own = product[2 * tile * tokens : (2 * tile + 1) * tokens]
        other = product[(2 * tile + 1) * tokens : (2 * tile + 2) * tokens]
        mine = rows_ref[:, columns].astype(jnp.float32) if tile == 0 else None
        sent, kept = combined(own, other, mine, gates_ref, columns)
        across_out[:, sent_columns] = sent.astype(jnp.bfloat16)
        first_kept[tile] = kept
    product = product_of(slice(half, 2 * half))
    for branch in range(2):
        sent_columns = slice(branch * half, (branch + 1) * half)
        second_kept[branch] = product[branch * tokens : (branch + 1) * tokens]
        along_out[:, sent_columns] = product[(branch + 2) * tokens : (branch + 3) * tokens].astype(
            jnp.bfloat16
        )


def stage_kernel(*refs, parts, start, next_start, fresh, middle, final):
    named = dict(zip(parts, refs))
    if fresh:
        begin(
            next_start,
            [
                named[name]
                for name in (
                    "attended", "core_attended", "weights", "core_weights", "both", "rows", "gates"
                )
                if name in named
            ],
            named["across_out"],
            named["along_out"],
            named["first_kept_out"],
            named["second_kept_out"],
        )
    if middle:
        across, along = named["across"], named["along"]
        first_kept, second_kept = named["first_kept"], named["second_kept"]
        half = first_kept.shape[2]
        sent_columns = slice(named["across_out"].shape[1] - half, named["across_out"].shape[1])
        named["along_out"][:, sent_columns] = (
            first_kept[1] + across[:, half : 2 * half].astype(jnp.float32)
        ).astype(jnp.bfloat16)
        named["first_left_out"][...] = first_kept[0] + across[:, :half].astype(jnp.float32)
        columns = slice(start + half, start + 2 * half)
        sent, kept = combined(
            second_kept[0] + along[:, :half].astype(jnp.float32),
            second_kept[1] + along[:, half : 2 * half].astype(jnp.float32),
            named["rows"][:, columns].astype(jnp.float32),
            named["gates"],
            columns,
        )
        named["across_out"][:, sent_columns] = sent.astype(jnp.bfloat16)
        named["second_left_out"][...] = kept
    if final:
        across, along = named["across"], named["along"]
        first_left, second_left = named["first_left"], named["second_left"]
        half = first_left.shape[1]
        columns = slice(across.shape[1] - half, across.shape[1])
        named["done_out"][:, :half] = (
            first_left[...] + along[:, columns].astype(jnp.float32)
        ).astype(jnp.bfloat16)
        named["done_out"][:, half:] = (
            second_left[...] + across[:, columns].astype(jnp.float32)
        ).astype(jnp.bfloat16)


def stage(operands, earlier, chunks, index, fresh, middle, final):
    tokens = operands["rows"].shape[0]
    next_start, next_chunk = chunks[index + 2] if fresh else (0, 0)
    start, chunk = chunks[index] if middle else (0, 0)
    outs = {}
    if fresh or middle:
        columns = next_chunk + chunk // 2
        outs["across_out"] = jax.ShapeDtypeStruct((tokens, columns), jnp.bfloat16)
        outs["along_out"] = outs["across_out"]
    if fresh:
        outs["first_kept_out"] = jax.ShapeDtypeStruct((2, tokens, next_chunk // 2), jnp.float32)
        outs["second_kept_out"] = outs["first_kept_out"]
    if middle:
        outs["first_left_out"] = jax.ShapeDtypeStruct((tokens, chunk // 2), jnp.float32)
        outs["second_left_out"] = outs["first_left_out"]
    if final:
        outs["done_out"] = jax.ShapeDtypeStruct((tokens, chunks[index - 2][1]), jnp.bfloat16)
    parts = list(operands) + ["earlier"] * len(earlier) + list(outs)
    results = pl.pallas_call(
        functools.partial(
            stage_kernel,
            parts=parts,
            start=start,
            next_start=next_start,
            fresh=fresh,
            middle=middle,
            final=final,
        ),
        grid=(1,),
        in_specs=[
            pl.BlockSpec((array.shape[0], next_chunk), lambda step: (0, next_start // next_chunk))
            if name in ("weights", "core_weights")
            else pl.BlockSpec(memory_space=pltpu.VMEM)
            for name, array in operands.items()
        ]
        + [pl.BlockSpec(memory_space=pl.ANY)] * len(earlier),
        out_specs=[pl.BlockSpec(memory_space=pltpu.VMEM)] * len(outs),
        out_shape=list(outs.values()),
        name="sum_stage",
        cost_estimate=SHORT,
        compiler_params=pltpu.CompilerParams(vmem_limit_bytes=16 * MIB),
    )(*operands.values(), *earlier)
    return dict(zip(outs, results))


def per_device(flight, modulation, project_in, project_out, stale_cache, visible):
    current = flight[0, 0]
    modulate = modulation[0, 0]
    token_rows, features = current.shape
    devices = lax.axis_size("sp") * lax.axis_size("cfg")

    context_rows = stale_cache.shape[2]
    width = project_in.shape[3]
    unpacked = stale_cache[0, 0].reshape(context_rows, 2, devices, width)
    packed = unpacked.transpose(2, 0, 1, 3).reshape(devices, context_rows, 2 * width)

    upper, lower = current[: token_rows // 2], current[token_rows // 2 :]
    across_upper, along_lower = from_partner(upper, "cfg", 1), from_partner(lower, "sp", 2)
    across_lower, along_upper = from_partner(lower, "cfg", 1), from_partner(upper, "sp", 2)
    other_modulate = from_partner(modulation, "cfg", 1)[0, 0]
    across_upper, along_lower = after(across_upper, (unpacked,)), after(along_lower, (unpacked,))
    first, second = from_partner(across_upper, "sp", 2), from_partner(along_lower, "cfg", 1)
    core_weights = from_partner(project_out[0], "sp", 1)
    near = [
        modulated_norm([current], modulate),
        modulated_norm([across_upper, across_lower], other_modulate),
        modulated_norm([along_upper, along_lower], modulate),
        modulated_norm([first, second], other_modulate),
    ]
    far = [from_partner(rows, "sp", 1) for rows in near]

    packed = after(packed, (across_lower, along_upper))
    context = lax.all_to_all(packed, ("sp", "cfg"), split_axis=0, concat_axis=0, tiled=True)
    context = context.reshape(devices * context_rows, 2 * width)

    heads = project(near + far, project_in[0])
    gates = jnp.concatenate([modulate[2:3], other_modulate[2:3]], axis=0)
    count = len(CHUNK_SHARES)
    unit = features // sum(CHUNK_SHARES)
    chunks = [
        (sum(CHUNK_SHARES[:index]) * unit, share * unit) for index, share in enumerate(CHUNK_SHARES)
    ]
    for_core, heads, context = attend_first(heads, context, visible[0])
    core_attended = from_partner(for_core, "sp", 1)
    attended, first_weights = attend_second(
        heads, context, visible[0], project_out[0], core_weights, chunks[0][1], (for_core, gates)
    )

    kept, left, flights, arrivals, earlier = {}, {}, {}, [], []
    for index in range(-2, count + 2):
        fresh, middle, final = index + 2 < count, 0 <= index < count, index >= 2
        operands = {"rows": current, "gates": gates}
        if fresh:
            operands.update(attended=attended, core_attended=core_attended)
            if index == -2:
                operands["both"] = first_weights
            else:
                operands.update(weights=project_out[0], core_weights=core_weights)
        if index >= 0:
            operands["across"], operands["along"] = flights.pop(index)
        if middle:
            operands["first_kept"], operands["second_kept"] = kept.pop(index)
        if final:
            operands["first_left"], operands["second_left"] = left.pop(index - 2)
        outs = stage(
            operands,
            earlier,
            chunks,
            index,
            fresh,
            middle,
            final,
        )
        if "across_out" in outs:
            flights[index + 2] = (
                from_partner(outs["across_out"], "cfg", 1),
                from_partner(outs["along_out"], "sp", 2),
            )
        if fresh:
            kept[index + 2] = (outs["first_kept_out"], outs["second_kept_out"])
        if middle:
            left[index] = (outs["first_left_out"], outs["second_left_out"])
        if final:
            arrivals.append(from_behind(outs["done_out"], "pipe", 1))
        earlier = [list(outs.values())[-1]] + (arrivals[-2:-1] if 3 <= index < count else [])
    return jnp.concatenate(arrivals, axis=1)[None, None]


def solution(mesh):
    placed = (
        P("pipe", "cfg", "sp", None),
        P("pipe", "cfg", None, None),
        P("pipe", None, None, ("sp", "cfg")),
        P("pipe", ("sp", "cfg"), None),
        P("pipe", "cfg", "sp", None, None),
        P("pipe", None, None),
    )
    return jax.shard_map(
        per_device,
        mesh=mesh,
        in_specs=placed,
        out_specs=P("pipe", "cfg", "sp", None),
        check_vma=False,
    )
```

```python
import functools

import jax
import jax.numpy as jnp
from jax import lax
from jax.experimental import pallas as pl
from jax.experimental.pallas import tpu as pltpu
from jax.sharding import PartitionSpec as P

HD = 128
TILE = 128
MIB = 2**20
SPARE = 39
LOG2E = 1.4426950408889634
CHUNK_SHARES = (4, 4, 4, 4, 2, 2)

guidance_scale = 5.0
SHORT = pl.CostEstimate(flops=1, bytes_accessed=1, transcendentals=0)


def from_behind(x, axis, by):
    count = lax.axis_size(axis)
    return lax.ppermute(x, axis, [(i, (i + by) % count) for i in range(count)])


def from_partner(value, axis, mask):
    pairs = [(source, source ^ mask) for source in range(lax.axis_size(axis))]
    return lax.ppermute(value, axis, pairs)


def norm_kernel(*refs):
    *parts, modulation_ref, out_ref = refs
    step = 16
    start = 0
    for part in parts:

        def body(index, carry, part=part, start=start):
            rows = pl.ds(pl.multiple_of(index * step, step), step)
            out_rows = pl.ds(pl.multiple_of(start + index * step, step), step)
            values = part[rows, :].astype(jnp.float32)
            centre = values - jnp.mean(values, axis=-1, keepdims=True)
            spread = jnp.mean(centre * centre, axis=-1, keepdims=True)
            normed = centre * lax.rsqrt(spread + 1e-06)
            out_ref[out_rows, :] = (
                normed * (1.0 + modulation_ref[1:2, :]) + modulation_ref[0:1, :]
            ).astype(jnp.bfloat16)
            return carry

        lax.fori_loop(0, part.shape[0] // step, body, 0, unroll=2)
        start += part.shape[0]


def modulated_norm(parts, modulation):
    rows, features = sum(part.shape[0] for part in parts), modulation.shape[1]
    return pl.pallas_call(
        norm_kernel,
        in_specs=[pl.BlockSpec(memory_space=pltpu.VMEM)] * (len(parts) + 1),
        out_shape=jax.ShapeDtypeStruct((rows, features), jnp.bfloat16),
        name="modulated_norm",
        cost_estimate=SHORT,
        compiler_params=pltpu.CompilerParams(vmem_limit_bytes=8 * MIB),
    )(*parts, modulation)


def gate_kernel(value_ref, *refs):
    pass


def after(value, earlier):
    return pl.pallas_call(
        gate_kernel,
        in_specs=[pl.BlockSpec(memory_space=pl.ANY)] * (1 + len(earlier)),
        out_specs=pl.BlockSpec(memory_space=pl.ANY),
        out_shape=jax.ShapeDtypeStruct(value.shape, value.dtype),
        input_output_aliases={0: 0},
        name="after",
        cost_estimate=SHORT,
        compiler_params=pltpu.CompilerParams(vmem_limit_bytes=MIB),
    )(value, *earlier)


def project_kernel(*refs, blocks):
    block_refs, (weights_ref, out_ref, total_ref, heads_ref, sems) = refs[:blocks], refs[blocks:]
    step, steps = pl.program_id(0), pl.num_programs(0)
    weights = jnp.concatenate([weights_ref[0], weights_ref[1], weights_ref[2]], axis=1)
    block = weights.shape[0]
    columns = pl.ds(pl.multiple_of(step * block, block), block)
    rows = jnp.concatenate([ref[:, columns] for ref in block_refs], axis=0)
    product = jnp.dot(rows, weights, preferred_element_type=jnp.float32)

    @pl.when(step == 0)
    def _():
        total_ref[...] = product

    @pl.when((step > 0) & (step < steps - 1))
    def _():
        total_ref[...] += product

    @pl.when(step == steps - 1)
    def _():
        heads = heads_ref.shape[0]
        copies = []
        for head in range(heads):
            columns = slice(head * HD, (head + 1) * HD)
            values = total_ref[:, columns] + product[:, columns]
            if head < 2 * heads // 3:
                square = jnp.mean(values * values, axis=-1, keepdims=True)
                values = values * lax.rsqrt(square + 1e-06)
            heads_ref[head] = values.astype(jnp.bfloat16)
            copies.append(
                pltpu.make_async_copy(heads_ref.at[head], out_ref.at[head], sems.at[head])
            )
            copies[-1].start()
        for copy in copies:
            copy.wait()


def project(blocks, weights):
    _, depth, width = weights.shape
    steps = 2
    block = depth // steps
    count = sum(rows.shape[0] for rows in blocks)
    heads = 3 * width // HD
    return pl.pallas_call(
        functools.partial(project_kernel, blocks=len(blocks)),
        grid=(steps,),
        in_specs=[pl.BlockSpec(memory_space=pltpu.VMEM)] * len(blocks)
        + [pl.BlockSpec((3, block, width), lambda k: (0, k, 0))],
        out_specs=pl.BlockSpec(memory_space=pltpu.HBM),
        out_shape=jax.ShapeDtypeStruct((heads + SPARE, count, HD), jnp.bfloat16),
        scratch_shapes=[
            pltpu.VMEM((count, 3 * width), jnp.float32),
            pltpu.VMEM((heads, count, HD), jnp.bfloat16),
            pltpu.SemaphoreType.DMA((heads,)),
        ],
        name="project_heads",
        cost_estimate=pl.CostEstimate(
            flops=2 * count * depth * 3 * width,
            bytes_accessed=2 * (count * depth + weights.size),
            transcendentals=0,
        ),
        compiler_params=pltpu.CompilerParams(vmem_limit_bytes=42 * MIB),
    )(*blocks, weights)


def attend_head(visible_ref, queries_ref, pool_ref, out_ref, first_block, head):
    heads, fresh_rows, _ = queries_ref.shape
    tiles_seen = visible_ref.shape[1]
    tiles_fresh = visible_ref.shape[0]
    mine_high, mine_low = lax.axis_index("sp") // 2, lax.axis_index("sp") % 2
    mine_branch = lax.axis_index("cfg")
    ones = jnp.ones((tiles_seen * TILE, HD), jnp.bfloat16)

    def body(step, carry):
        index = first_block + step
        high, low = mine_high ^ ((index // 2) % 2), mine_low ^ (index // 4)
        tile, branch = high * 2 + low, mine_branch ^ (index % 2)
        rows = pl.ds(pl.multiple_of(index * TILE, TILE), TILE)
        out_rows = pl.ds(pl.multiple_of(step * TILE, TILE), TILE)
        places = []
        for seen in range(tiles_seen):
            number = visible_ref[tile, seen]
            older = number - tiles_fresh
            fresh = (mine_low ^ (number % 2)) * 4 + (mine_high ^ ((number // 2) % 2)) * 2
            fresh = (fresh + index % 2) * TILE
            stale = fresh_rows + ((older // 2) * 2 + branch) * 2 * TILE + (older % 2) * TILE
            start = jnp.where(number < tiles_fresh, fresh, stale)
            places.append(pl.ds(pl.multiple_of(start, TILE), TILE))

        keys = jnp.concatenate([pool_ref[head, place, :] for place in places], axis=0)
        values = jnp.concatenate([pool_ref[heads + head, place, :] for place in places], axis=0)
        scores = lax.dot_general(
            queries_ref[head, rows, :],
            keys,
            (((1,), (1,)), ((), ())),
            preferred_element_type=jnp.float32,
        )
        exponent = jnp.exp2(scores * (HD ** (-0.5) * LOG2E)).astype(jnp.bfloat16)
        mixed = jnp.dot(
            exponent, jnp.concatenate([values, ones], axis=1), preferred_element_type=jnp.float32
        )
        out_ref[out_rows, head * HD : (head + 1) * HD] = (mixed[:, :HD] / mixed[:, HD:]).astype(
            jnp.bfloat16
        )
        return carry

    lax.fori_loop(0, out_ref.shape[0] // TILE, body, 0, unroll=True)


def attend_first_kernel(
    visible_ref, heads_in, context_in, out_ref, queries_ref, pool_ref, sems
):
    heads, fresh_rows, _ = queries_ref.shape
    fresh, stale = pl.ds(0, fresh_rows), pl.ds(fresh_rows, context_in.shape[0])
    copies = []
    for head in range(heads):
        pairs = [(heads_in.at[head], queries_ref.at[head])]
        for kind in range(2):
            place = kind * heads + head
            columns = pl.ds(place * HD, HD)
            pairs.append((heads_in.at[heads + place], pool_ref.at[place, fresh]))
            pairs.append((context_in.at[:, columns], pool_ref.at[place, stale]))
        of_head = [
            pltpu.make_async_copy(source, target, sems.at[head, number])
            for number, (source, target) in enumerate(pairs)
        ]
        for copy in of_head:
            copy.start()
        copies.append(of_head)
    for head in range(heads):
        for copy in copies[head]:
            copy.wait()
        first_block = out_ref.shape[0] // TILE
        attend_head(visible_ref, queries_ref, pool_ref, out_ref, first_block, head)


def attend_first(heads, context, visible):
    number, rows = (heads.shape[0] - SPARE) // 3, heads.shape[1]
    return pl.pallas_call(
        attend_first_kernel,
        in_specs=[
            pl.BlockSpec(memory_space=pltpu.SMEM),
            pl.BlockSpec(memory_space=pltpu.HBM),
            pl.BlockSpec(memory_space=pl.ANY),
        ],
        out_specs=[pl.BlockSpec(memory_space=pltpu.VMEM)] * 3,
        out_shape=[
            jax.ShapeDtypeStruct((rows // 2, number * HD), jnp.bfloat16),
            jax.ShapeDtypeStruct((number, rows, HD), heads.dtype),
            jax.ShapeDtypeStruct((2 * number, rows + context.shape[0], HD), heads.dtype),
        ],
        scratch_shapes=[pltpu.SemaphoreType.DMA((number, 5))],
        name="attend_first",
        cost_estimate=SHORT,
        compiler_params=pltpu.CompilerParams(vmem_limit_bytes=44 * MIB),
    )(visible, heads, context)


def attend_second_kernel(visible_ref, queries_ref, pool_ref, *refs):
    weights_ref, core_weights_ref = refs[:2]
    out_ref, both_ref, sems = refs[-3:]
    depth, columns = weights_ref.shape[0], pl.ds(0, both_ref.shape[1])
    copies = [
        pltpu.make_async_copy(
            ref.at[:, columns], both_ref.at[pl.ds(core * depth, depth)], sems.at[core]
        )
        for core, ref in enumerate((weights_ref, core_weights_ref))
    ]
    for copy in copies:
        copy.start()
    for head in range(queries_ref.shape[0]):
        attend_head(visible_ref, queries_ref, pool_ref, out_ref, 0, head)
    for copy in copies:
        copy.wait()


def attend_second(queries, pool, visible, weights, core_weights, columns, earlier):
    number, rows, _ = queries.shape
    return pl.pallas_call(
        attend_second_kernel,
        in_specs=[pl.BlockSpec(memory_space=pltpu.SMEM)]
        + [pl.BlockSpec(memory_space=pltpu.VMEM)] * 2
        + [pl.BlockSpec(memory_space=pl.ANY)] * (2 + len(earlier)),
        out_specs=[pl.BlockSpec(memory_space=pltpu.VMEM)] * 2,
        out_shape=[
            jax.ShapeDtypeStruct((rows // 2, number * HD), jnp.bfloat16),
            jax.ShapeDtypeStruct((2 * weights.shape[0], columns), weights.dtype),
        ],
        scratch_shapes=[pltpu.SemaphoreType.DMA((2,))],
        name="attend_second",
        cost_estimate=SHORT,
        compiler_params=pltpu.CompilerParams(vmem_limit_bytes=12 * MIB),
    )(visible, queries, pool, weights, core_weights, *earlier)


def combined(own, other, mine, gates_ref, columns):
    conditional = lax.axis_index("cfg") == 1
    last = lax.axis_index("pipe") == lax.axis_size("pipe") - 1
    weight = jnp.where(conditional, guidance_scale, 1.0 - guidance_scale).astype(jnp.float32)
    other_weight = jnp.where(conditional, 1.0 - guidance_scale, guidance_scale).astype(jnp.float32)
    own = own * gates_ref[0:1, columns]
    other = other * gates_ref[1:2, columns]
    if mine is not None:
        own = own + mine
    guided = weight * own + other_weight * other
    return jnp.where(last, guided, other), jnp.where(last, guided, own)


def begin(start, refs, across_out, along_out, first_kept, second_kept):
    attended_ref, core_attended_ref, *weights_refs, rows_ref, gates_ref = refs
    tokens, half = rows_ref.shape[0], first_kept.shape[2]
    attended = jnp.concatenate([attended_ref[...], core_attended_ref[...]], axis=1)

    def product_of(columns):
        weights = jnp.concatenate([ref[:, columns] for ref in weights_refs], axis=0)
        return jnp.dot(attended, weights, preferred_element_type=jnp.float32)

    columns = slice(start, start + half)
    product = product_of(slice(0, half))
    for tile in range(2):
        sent_columns = slice(tile * half, (tile + 1) * half)
        own = product[2 * tile * tokens : (2 * tile + 1) * tokens]
        other = product[(2 * tile + 1) * tokens : (2 * tile + 2) * tokens]
        mine = rows_ref[:, columns].astype(jnp.float32) if tile == 0 else None
        sent, kept = combined(own, other, mine, gates_ref, columns)
        across_out[:, sent_columns] = sent.astype(jnp.bfloat16)
        first_kept[tile] = kept
    product = product_of(slice(half, 2 * half))
    for branch in range(2):
        sent_columns = slice(branch * half, (branch + 1) * half)
        second_kept[branch] = product[branch * tokens : (branch + 1) * tokens]
        along_out[:, sent_columns] = product[(branch + 2) * tokens : (branch + 3) * tokens].astype(
            jnp.bfloat16
        )


def stage_kernel(*refs, parts, start, next_start, fresh, middle, final):
    named = dict(zip(parts, refs))
    if fresh:
        begin(
            next_start,
            [
                named[name]
                for name in (
                    "attended", "core_attended", "weights", "core_weights", "both", "rows", "gates"
                )
                if name in named
            ],
            named["across_out"],
            named["along_out"],
            named["first_kept_out"],
            named["second_kept_out"],
        )
    if middle:
        across, along = named["across"], named["along"]
        first_kept, second_kept = named["first_kept"], named["second_kept"]
        half = first_kept.shape[2]
        sent_columns = slice(named["across_out"].shape[1] - half, named["across_out"].shape[1])
        named["along_out"][:, sent_columns] = (
            first_kept[1] + across[:, half : 2 * half].astype(jnp.float32)
        ).astype(jnp.bfloat16)
        named["first_left_out"][...] = first_kept[0] + across[:, :half].astype(jnp.float32)
        columns = slice(start + half, start + 2 * half)
        sent, kept = combined(
            second_kept[0] + along[:, :half].astype(jnp.float32),
            second_kept[1] + along[:, half : 2 * half].astype(jnp.float32),
            named["rows"][:, columns].astype(jnp.float32),
            named["gates"],
            columns,
        )
        named["across_out"][:, sent_columns] = sent.astype(jnp.bfloat16)
        named["second_left_out"][...] = kept
    if final:
        across, along = named["across"], named["along"]
        first_left, second_left = named["first_left"], named["second_left"]
        half = first_left.shape[1]
        columns = slice(across.shape[1] - half, across.shape[1])
        named["done_out"][:, :half] = (
            first_left[...] + along[:, columns].astype(jnp.float32)
        ).astype(jnp.bfloat16)
        named["done_out"][:, half:] = (
            second_left[...] + across[:, columns].astype(jnp.float32)
        ).astype(jnp.bfloat16)


def stage(operands, earlier, chunks, index, fresh, middle, final):
    tokens = operands["rows"].shape[0]
    next_start, next_chunk = chunks[index + 2] if fresh else (0, 0)
    start, chunk = chunks[index] if middle else (0, 0)
    outs = {}
    if fresh or middle:
        columns = next_chunk + chunk // 2
        outs["across_out"] = jax.ShapeDtypeStruct((tokens, columns), jnp.bfloat16)
        outs["along_out"] = outs["across_out"]
    if fresh:
        outs["first_kept_out"] = jax.ShapeDtypeStruct((2, tokens, next_chunk // 2), jnp.float32)
        outs["second_kept_out"] = outs["first_kept_out"]
    if middle:
        outs["first_left_out"] = jax.ShapeDtypeStruct((tokens, chunk // 2), jnp.float32)
        outs["second_left_out"] = outs["first_left_out"]
    if final:
        outs["done_out"] = jax.ShapeDtypeStruct((tokens, chunks[index - 2][1]), jnp.bfloat16)
    parts = list(operands) + ["earlier"] * len(earlier) + list(outs)
    results = pl.pallas_call(
        functools.partial(
            stage_kernel,
            parts=parts,
            start=start,
            next_start=next_start,
            fresh=fresh,
            middle=middle,
            final=final,
        ),
        grid=(1,),
        in_specs=[
            pl.BlockSpec((array.shape[0], next_chunk), lambda step: (0, next_start // next_chunk))
            if name in ("weights", "core_weights")
            else pl.BlockSpec(memory_space=pltpu.VMEM)
            for name, array in operands.items()
        ]
        + [pl.BlockSpec(memory_space=pl.ANY)] * len(earlier),
        out_specs=[pl.BlockSpec(memory_space=pltpu.VMEM)] * len(outs),
        out_shape=list(outs.values()),
        name="sum_stage",
        cost_estimate=SHORT,
        compiler_params=pltpu.CompilerParams(vmem_limit_bytes=16 * MIB),
    )(*operands.values(), *earlier)
    return dict(zip(outs, results))


def per_device(flight, modulation, project_in, project_out, stale_cache, visible):
    current = flight[0, 0]
    modulate = modulation[0, 0]
    token_rows, features = current.shape
    devices = lax.axis_size("sp") * lax.axis_size("cfg")

    context_rows = stale_cache.shape[2]
    width = project_in.shape[3]
    unpacked = stale_cache[0, 0].reshape(context_rows, 2, devices, width)
    packed = unpacked.transpose(2, 0, 1, 3).reshape(devices, context_rows, 2 * width)

    upper, lower = current[: token_rows // 2], current[token_rows // 2 :]
    across_upper, along_lower = from_partner(upper, "cfg", 1), from_partner(lower, "sp", 2)
    across_lower, along_upper = from_partner(lower, "cfg", 1), from_partner(upper, "sp", 2)
    other_modulate = from_partner(modulation, "cfg", 1)[0, 0]
    across_upper, along_lower = after(across_upper, (unpacked,)), after(along_lower, (unpacked,))
    first, second = from_partner(across_upper, "sp", 2), from_partner(along_lower, "cfg", 1)
    core_weights = from_partner(project_out[0], "sp", 1)
    near = [
        modulated_norm([current], modulate),
        modulated_norm([across_upper, across_lower], other_modulate),
        modulated_norm([along_upper, along_lower], modulate),
        modulated_norm([first, second], other_modulate),
    ]
    far = [from_partner(rows, "sp", 1) for rows in near]

    packed = after(packed, (across_lower, along_upper))
    context = lax.all_to_all(packed, ("sp", "cfg"), split_axis=0, concat_axis=0, tiled=True)
    context = context.reshape(devices * context_rows, 2 * width)

    heads = project(near + far, project_in[0])
    gates = jnp.concatenate([modulate[2:3], other_modulate[2:3]], axis=0)
    count = len(CHUNK_SHARES)
    unit = features // sum(CHUNK_SHARES)
    chunks = [
        (sum(CHUNK_SHARES[:index]) * unit, share * unit) for index, share in enumerate(CHUNK_SHARES)
    ]
    for_core, queries, pool = attend_first(heads, context, visible[0])
    core_attended = from_partner(for_core, "sp", 1)
    attended, first_weights = attend_second(
        queries, pool, visible[0], project_out[0], core_weights, chunks[0][1], (for_core, gates)
    )

    kept, left, flights, arrivals, earlier = {}, {}, {}, [], []
    for index in range(-2, count + 2):
        fresh, middle, final = index + 2 < count, 0 <= index < count, index >= 2
        operands = {"rows": current, "gates": gates}
        if fresh:
            operands.update(attended=attended, core_attended=core_attended)
            if index == -2:
                operands["both"] = first_weights
            else:
                operands.update(weights=project_out[0], core_weights=core_weights)
        if index >= 0:
            operands["across"], operands["along"] = flights.pop(index)
        if middle:
            operands["first_kept"], operands["second_kept"] = kept.pop(index)
        if final:
            operands["first_left"], operands["second_left"] = left.pop(index - 2)
        outs = stage(
            operands,
            earlier,
            chunks,
            index,
            fresh,
            middle,
            final,
        )
        if "across_out" in outs:
            flights[index + 2] = (
                from_partner(outs["across_out"], "cfg", 1),
                from_partner(outs["along_out"], "sp", 2),
            )
        if fresh:
            kept[index + 2] = (outs["first_kept_out"], outs["second_kept_out"])
        if middle:
            left[index] = (outs["first_left_out"], outs["second_left_out"])
        if final:
            arrivals.append(from_behind(outs["done_out"], "pipe", 1))
        earlier = [list(outs.values())[-1]] + (arrivals[-2:-1] if 3 <= index < count else [])
    return jnp.concatenate(arrivals, axis=1)[None, None]


def solution(mesh):
    placed = (
        P("pipe", "cfg", "sp", None),
        P("pipe", "cfg", None, None),
        P("pipe", None, None, ("sp", "cfg")),
        P("pipe", ("sp", "cfg"), None),
        P("pipe", "cfg", "sp", None, None),
        P("pipe", None, None),
    )
    return jax.shard_map(
        per_device,
        mesh=mesh,
        in_specs=placed,
        out_specs=P("pipe", "cfg", "sp", None),
        check_vma=False,
    )
```

```python
import functools

import jax
import jax.numpy as jnp
from jax import lax
from jax.experimental import pallas as pl
from jax.experimental.pallas import tpu as pltpu
from jax.sharding import PartitionSpec as P

HD = 128
TILE = 128
MIB = 2**20
SPARE = 39
LOG2E = 1.4426950408889634
CHUNK_SHARES = (5, 5, 2, 3, 3, 2)

guidance_scale = 5.0
SHORT = pl.CostEstimate(flops=1, bytes_accessed=1, transcendentals=0)


def from_behind(x, axis, by):
    count = lax.axis_size(axis)
    return lax.ppermute(x, axis, [(i, (i + by) % count) for i in range(count)])


def from_partner(value, axis, mask):
    pairs = [(source, source ^ mask) for source in range(lax.axis_size(axis))]
    return lax.ppermute(value, axis, pairs)


def norm_kernel(*refs):
    *parts, modulation_ref, out_ref = refs
    step = 16
    start = 0
    for part in parts:

        def body(index, carry, part=part, start=start):
            rows = pl.ds(pl.multiple_of(index * step, step), step)
            out_rows = pl.ds(pl.multiple_of(start + index * step, step), step)
            values = part[rows, :].astype(jnp.float32)
            centre = values - jnp.mean(values, axis=-1, keepdims=True)
            spread = jnp.mean(centre * centre, axis=-1, keepdims=True)
            normed = centre * lax.rsqrt(spread + 1e-06)
            out_ref[out_rows, :] = (
                normed * (1.0 + modulation_ref[1:2, :]) + modulation_ref[0:1, :]
            ).astype(jnp.bfloat16)
            return carry

        lax.fori_loop(0, part.shape[0] // step, body, 0, unroll=2)
        start += part.shape[0]


def modulated_norm(parts, modulation):
    rows, features = sum(part.shape[0] for part in parts), modulation.shape[1]
    return pl.pallas_call(
        norm_kernel,
        in_specs=[pl.BlockSpec(memory_space=pltpu.VMEM)] * (len(parts) + 1),
        out_shape=jax.ShapeDtypeStruct((rows, features), jnp.bfloat16),
        name="modulated_norm",
        cost_estimate=SHORT,
        compiler_params=pltpu.CompilerParams(vmem_limit_bytes=8 * MIB),
    )(*parts, modulation)


def gate_kernel(value_ref, *refs):
    pass


def after(value, earlier):
    return pl.pallas_call(
        gate_kernel,
        in_specs=[pl.BlockSpec(memory_space=pl.ANY)] * (1 + len(earlier)),
        out_specs=pl.BlockSpec(memory_space=pl.ANY),
        out_shape=jax.ShapeDtypeStruct(value.shape, value.dtype),
        input_output_aliases={0: 0},
        name="after",
        cost_estimate=SHORT,
        compiler_params=pltpu.CompilerParams(vmem_limit_bytes=MIB),
    )(value, *earlier)


def project_kernel(*refs, blocks):
    block_refs, (weights_ref, out_ref, total_ref, heads_ref, sems) = refs[:blocks], refs[blocks:]
    step, steps = pl.program_id(0), pl.num_programs(0)
    weights = jnp.concatenate([weights_ref[0], weights_ref[1], weights_ref[2]], axis=1)
    block = weights.shape[0]
    columns = pl.ds(pl.multiple_of(step * block, block), block)
    rows = jnp.concatenate([ref[:, columns] for ref in block_refs], axis=0)
    product = jnp.dot(rows, weights, preferred_element_type=jnp.float32)

    @pl.when(step == 0)
    def _():
        total_ref[...] = product

    @pl.when((step > 0) & (step < steps - 1))
    def _():
        total_ref[...] += product

    @pl.when(step == steps - 1)
    def _():
        heads = heads_ref.shape[0]
        copies = []
        for head in range(heads):
            columns = slice(head * HD, (head + 1) * HD)
            values = total_ref[:, columns] + product[:, columns]
            if head < 2 * heads // 3:
                square = jnp.mean(values * values, axis=-1, keepdims=True)
                values = values * lax.rsqrt(square + 1e-06)
            heads_ref[head] = values.astype(jnp.bfloat16)
            copies.append(
                pltpu.make_async_copy(heads_ref.at[head], out_ref.at[head], sems.at[head])
            )
            copies[-1].start()
        for copy in copies:
            copy.wait()


def project(blocks, weights):
    _, depth, width = weights.shape
    steps = 2
    block = depth // steps
    count = sum(rows.shape[0] for rows in blocks)
    heads = 3 * width // HD
    return pl.pallas_call(
        functools.partial(project_kernel, blocks=len(blocks)),
        grid=(steps,),
        in_specs=[pl.BlockSpec(memory_space=pltpu.VMEM)] * len(blocks)
        + [pl.BlockSpec((3, block, width), lambda k: (0, k, 0))],
        out_specs=pl.BlockSpec(memory_space=pltpu.HBM),
        out_shape=jax.ShapeDtypeStruct((heads + SPARE, count, HD), jnp.bfloat16),
        scratch_shapes=[
            pltpu.VMEM((count, 3 * width), jnp.float32),
            pltpu.VMEM((heads, count, HD), jnp.bfloat16),
            pltpu.SemaphoreType.DMA((heads,)),
        ],
        name="project_heads",
        cost_estimate=pl.CostEstimate(
            flops=2 * count * depth * 3 * width,
            bytes_accessed=2 * (count * depth + weights.size),
            transcendentals=0,
        ),
        compiler_params=pltpu.CompilerParams(vmem_limit_bytes=42 * MIB),
    )(*blocks, weights)


def attend_head(visible_ref, queries_ref, pool_ref, out_ref, first_block, head):
    heads, fresh_rows, _ = queries_ref.shape
    tiles_seen = visible_ref.shape[1]
    tiles_fresh = visible_ref.shape[0]
    mine_high, mine_low = lax.axis_index("sp") // 2, lax.axis_index("sp") % 2
    mine_branch = lax.axis_index("cfg")
    ones = jnp.ones((tiles_seen * TILE, HD), jnp.bfloat16)

    def body(step, carry):
        index = first_block + step
        high, low = mine_high ^ ((index // 2) % 2), mine_low ^ (index // 4)
        tile, branch = high * 2 + low, mine_branch ^ (index % 2)
        rows = pl.ds(pl.multiple_of(index * TILE, TILE), TILE)
        out_rows = pl.ds(pl.multiple_of(step * TILE, TILE), TILE)
        places = []
        for seen in range(tiles_seen):
            number = visible_ref[tile, seen]
            older = number - tiles_fresh
            fresh = (mine_low ^ (number % 2)) * 4 + (mine_high ^ ((number // 2) % 2)) * 2
            fresh = (fresh + index % 2) * TILE
            stale = fresh_rows + ((older // 2) * 2 + branch) * 2 * TILE + (older % 2) * TILE
            start = jnp.where(number < tiles_fresh, fresh, stale)
            places.append(pl.ds(pl.multiple_of(start, TILE), TILE))

        keys = jnp.concatenate([pool_ref[head, place, :] for place in places], axis=0)
        values = jnp.concatenate([pool_ref[heads + head, place, :] for place in places], axis=0)
        scores = lax.dot_general(
            queries_ref[head, rows, :],
            keys,
            (((1,), (1,)), ((), ())),
            preferred_element_type=jnp.float32,
        )
        exponent = jnp.exp2(scores * (HD ** (-0.5) * LOG2E)).astype(jnp.bfloat16)
        mixed = jnp.dot(
            exponent, jnp.concatenate([values, ones], axis=1), preferred_element_type=jnp.float32
        )
        out_ref[out_rows, head * HD : (head + 1) * HD] = (mixed[:, :HD] / mixed[:, HD:]).astype(
            jnp.bfloat16
        )
        return carry

    lax.fori_loop(0, out_ref.shape[0] // TILE, body, 0, unroll=True)


def attend_first_kernel(
    visible_ref, heads_in, context_in, out_ref, queries_ref, pool_ref, sems
):
    heads, fresh_rows, _ = queries_ref.shape
    fresh, stale = pl.ds(0, fresh_rows), pl.ds(fresh_rows, context_in.shape[0])
    copies = []
    for head in range(heads):
        pairs = [(heads_in.at[head], queries_ref.at[head])]
        for kind in range(2):
            place = kind * heads + head
            columns = pl.ds(place * HD, HD)
            pairs.append((heads_in.at[heads + place], pool_ref.at[place, fresh]))
            pairs.append((context_in.at[:, columns], pool_ref.at[place, stale]))
        of_head = [
            pltpu.make_async_copy(source, target, sems.at[head, number])
            for number, (source, target) in enumerate(pairs)
        ]
        for copy in of_head:
            copy.start()
        copies.append(of_head)
    for head in range(heads):
        for copy in copies[head]:
            copy.wait()
        first_block = out_ref.shape[0] // TILE
        attend_head(visible_ref, queries_ref, pool_ref, out_ref, first_block, head)


def attend_first(heads, context, visible):
    number, rows = (heads.shape[0] - SPARE) // 3, heads.shape[1]
    return pl.pallas_call(
        attend_first_kernel,
        in_specs=[
            pl.BlockSpec(memory_space=pltpu.SMEM),
            pl.BlockSpec(memory_space=pltpu.HBM),
            pl.BlockSpec(memory_space=pl.ANY),
        ],
        out_specs=[pl.BlockSpec(memory_space=pltpu.VMEM)] * 3,
        out_shape=[
            jax.ShapeDtypeStruct((rows // 2, number * HD), jnp.bfloat16),
            jax.ShapeDtypeStruct((number, rows, HD), heads.dtype),
            jax.ShapeDtypeStruct((2 * number, rows + context.shape[0], HD), heads.dtype),
        ],
        scratch_shapes=[pltpu.SemaphoreType.DMA((number, 5))],
        name="attend_first",
        cost_estimate=SHORT,
        compiler_params=pltpu.CompilerParams(vmem_limit_bytes=44 * MIB),
    )(visible, heads, context)


def attend_second_kernel(visible_ref, queries_ref, pool_ref, *refs):
    weights_ref, core_weights_ref = refs[:2]
    out_ref, both_ref, sems = refs[-3:]
    depth, columns = weights_ref.shape[0], pl.ds(0, both_ref.shape[1])
    copies = [
        pltpu.make_async_copy(
            ref.at[:, columns], both_ref.at[pl.ds(core * depth, depth)], sems.at[core]
        )
        for core, ref in enumerate((weights_ref, core_weights_ref))
    ]
    for copy in copies:
        copy.start()
    for head in range(queries_ref.shape[0]):
        attend_head(visible_ref, queries_ref, pool_ref, out_ref, 0, head)
    for copy in copies:
        copy.wait()


def attend_second(queries, pool, visible, weights, core_weights, columns, earlier):
    number, rows, _ = queries.shape
    return pl.pallas_call(
        attend_second_kernel,
        in_specs=[pl.BlockSpec(memory_space=pltpu.SMEM)]
        + [pl.BlockSpec(memory_space=pltpu.VMEM)] * 2
        + [pl.BlockSpec(memory_space=pl.ANY)] * (2 + len(earlier)),
        out_specs=[pl.BlockSpec(memory_space=pltpu.VMEM)] * 2,
        out_shape=[
            jax.ShapeDtypeStruct((rows // 2, number * HD), jnp.bfloat16),
            jax.ShapeDtypeStruct((2 * weights.shape[0], columns), weights.dtype),
        ],
        scratch_shapes=[pltpu.SemaphoreType.DMA((2,))],
        name="attend_second",
        cost_estimate=SHORT,
        compiler_params=pltpu.CompilerParams(vmem_limit_bytes=12 * MIB),
    )(visible, queries, pool, weights, core_weights, *earlier)


def combined(own, other, mine, gates_ref, columns):
    conditional = lax.axis_index("cfg") == 1
    last = lax.axis_index("pipe") == lax.axis_size("pipe") - 1
    weight = jnp.where(conditional, guidance_scale, 1.0 - guidance_scale).astype(jnp.float32)
    other_weight = jnp.where(conditional, 1.0 - guidance_scale, guidance_scale).astype(jnp.float32)
    own = own * gates_ref[0:1, columns]
    other = other * gates_ref[1:2, columns]
    if mine is not None:
        own = own + mine
    guided = weight * own + other_weight * other
    return jnp.where(last, guided, other), jnp.where(last, guided, own)


def begin(start, refs, across_out, along_out, first_kept, second_kept):
    attended_ref, core_attended_ref, *weights_refs, rows_ref, gates_ref = refs
    tokens, half = rows_ref.shape[0], first_kept.shape[2]
    attended = jnp.concatenate([attended_ref[...], core_attended_ref[...]], axis=1)

    def product_of(columns):
        weights = jnp.concatenate([ref[:, columns] for ref in weights_refs], axis=0)
        return jnp.dot(attended, weights, preferred_element_type=jnp.float32)

    columns = slice(start, start + half)
    product = product_of(slice(0, half))
    for tile in range(2):
        sent_columns = slice(tile * half, (tile + 1) * half)
        own = product[2 * tile * tokens : (2 * tile + 1) * tokens]
        other = product[(2 * tile + 1) * tokens : (2 * tile + 2) * tokens]
        mine = rows_ref[:, columns].astype(jnp.float32) if tile == 0 else None
        sent, kept = combined(own, other, mine, gates_ref, columns)
        across_out[:, sent_columns] = sent.astype(jnp.bfloat16)
        first_kept[tile] = kept
    product = product_of(slice(half, 2 * half))
    for branch in range(2):
        sent_columns = slice(branch * half, (branch + 1) * half)
        second_kept[branch] = product[branch * tokens : (branch + 1) * tokens]
        along_out[:, sent_columns] = product[(branch + 2) * tokens : (branch + 3) * tokens].astype(
            jnp.bfloat16
        )


def stage_kernel(*refs, parts, start, next_start, fresh, middle, final):
    named = dict(zip(parts, refs))
    if fresh:
        begin(
            next_start,
            [
                named[name]
                for name in (
                    "attended", "core_attended", "weights", "core_weights", "both", "rows", "gates"
                )
                if name in named
            ],
            named["across_out"],
            named["along_out"],
            named["first_kept_out"],
            named["second_kept_out"],
        )
    if middle:
        across, along = named["across"], named["along"]
        first_kept, second_kept = named["first_kept"], named["second_kept"]
        half = first_kept.shape[2]
        sent_columns = slice(named["across_out"].shape[1] - half, named["across_out"].shape[1])
        named["along_out"][:, sent_columns] = (
            first_kept[1] + across[:, half : 2 * half].astype(jnp.float32)
        ).astype(jnp.bfloat16)
        named["first_left_out"][...] = first_kept[0] + across[:, :half].astype(jnp.float32)
        columns = slice(start + half, start + 2 * half)
        sent, kept = combined(
            second_kept[0] + along[:, :half].astype(jnp.float32),
            second_kept[1] + along[:, half : 2 * half].astype(jnp.float32),
            named["rows"][:, columns].astype(jnp.float32),
            named["gates"],
            columns,
        )
        named["across_out"][:, sent_columns] = sent.astype(jnp.bfloat16)
        named["second_left_out"][...] = kept
    if final:
        across, along = named["across"], named["along"]
        first_left, second_left = named["first_left"], named["second_left"]
        half = first_left.shape[1]
        columns = slice(across.shape[1] - half, across.shape[1])
        named["done_out"][:, :half] = (
            first_left[...] + along[:, columns].astype(jnp.float32)
        ).astype(jnp.bfloat16)
        named["done_out"][:, half:] = (
            second_left[...] + across[:, columns].astype(jnp.float32)
        ).astype(jnp.bfloat16)


def stage(operands, earlier, chunks, index, fresh, middle, final):
    tokens = operands["rows"].shape[0]
    next_start, next_chunk = chunks[index + 2] if fresh else (0, 0)
    start, chunk = chunks[index] if middle else (0, 0)
    outs = {}
    if fresh or middle:
        columns = next_chunk + chunk // 2
        outs["across_out"] = jax.ShapeDtypeStruct((tokens, columns), jnp.bfloat16)
        outs["along_out"] = outs["across_out"]
    if fresh:
        outs["first_kept_out"] = jax.ShapeDtypeStruct((2, tokens, next_chunk // 2), jnp.float32)
        outs["second_kept_out"] = outs["first_kept_out"]
    if middle:
        outs["first_left_out"] = jax.ShapeDtypeStruct((tokens, chunk // 2), jnp.float32)
        outs["second_left_out"] = outs["first_left_out"]
    if final:
        outs["done_out"] = jax.ShapeDtypeStruct((tokens, chunks[index - 2][1]), jnp.bfloat16)
    parts = list(operands) + ["earlier"] * len(earlier) + list(outs)
    results = pl.pallas_call(
        functools.partial(
            stage_kernel,
            parts=parts,
            start=start,
            next_start=next_start,
            fresh=fresh,
            middle=middle,
            final=final,
        ),
        grid=(1,),
        in_specs=[
            pl.BlockSpec((array.shape[0], next_chunk), lambda step: (0, next_start // next_chunk))
            if name in ("weights", "core_weights")
            else pl.BlockSpec(memory_space=pltpu.VMEM)
            for name, array in operands.items()
        ]
        + [pl.BlockSpec(memory_space=pl.ANY)] * len(earlier),
        out_specs=[pl.BlockSpec(memory_space=pltpu.VMEM)] * len(outs),
        out_shape=list(outs.values()),
        name="sum_stage",
        cost_estimate=SHORT,
        compiler_params=pltpu.CompilerParams(vmem_limit_bytes=16 * MIB),
    )(*operands.values(), *earlier)
    return dict(zip(outs, results))


def per_device(flight, modulation, project_in, project_out, stale_cache, visible):
    current = flight[0, 0]
    modulate = modulation[0, 0]
    token_rows, features = current.shape
    devices = lax.axis_size("sp") * lax.axis_size("cfg")

    context_rows = stale_cache.shape[2]
    width = project_in.shape[3]
    unpacked = stale_cache[0, 0].reshape(context_rows, 2, devices, width)
    packed = unpacked.transpose(2, 0, 1, 3).reshape(devices, context_rows, 2 * width)

    upper, lower = current[: token_rows // 2], current[token_rows // 2 :]
    across_upper, along_lower = from_partner(upper, "cfg", 1), from_partner(lower, "sp", 2)
    across_lower, along_upper = from_partner(lower, "cfg", 1), from_partner(upper, "sp", 2)
    other_modulate = from_partner(modulation, "cfg", 1)[0, 0]
    across_upper, along_lower = after(across_upper, (unpacked,)), after(along_lower, (unpacked,))
    first, second = from_partner(across_upper, "sp", 2), from_partner(along_lower, "cfg", 1)
    core_weights = from_partner(project_out[0], "sp", 1)
    near = [
        modulated_norm([current], modulate),
        modulated_norm([across_upper, across_lower], other_modulate),
        modulated_norm([along_upper, along_lower], modulate),
        modulated_norm([first, second], other_modulate),
    ]
    far = [from_partner(rows, "sp", 1) for rows in near]

    packed = after(packed, (across_lower, along_upper))
    context = lax.all_to_all(packed, ("sp", "cfg"), split_axis=0, concat_axis=0, tiled=True)
    context = context.reshape(devices * context_rows, 2 * width)

    heads = project(near + far, project_in[0])
    gates = jnp.concatenate([modulate[2:3], other_modulate[2:3]], axis=0)
    count = len(CHUNK_SHARES)
    unit = features // sum(CHUNK_SHARES)
    chunks = [
        (sum(CHUNK_SHARES[:index]) * unit, share * unit) for index, share in enumerate(CHUNK_SHARES)
    ]
    for_core, queries, pool = attend_first(heads, context, visible[0])
    core_attended = from_partner(for_core, "sp", 1)
    attended, first_weights = attend_second(
        queries, pool, visible[0], project_out[0], core_weights, chunks[0][1], (for_core, gates)
    )

    kept, left, flights, arrivals, earlier = {}, {}, {}, [], []
    for index in range(-2, count + 2):
        fresh, middle, final = index + 2 < count, 0 <= index < count, index >= 2
        operands = {"rows": current, "gates": gates}
        if fresh:
            operands.update(attended=attended, core_attended=core_attended)
            if index == -2:
                operands["both"] = first_weights
            else:
                operands.update(weights=project_out[0], core_weights=core_weights)
        if index >= 0:
            operands["across"], operands["along"] = flights.pop(index)
        if middle:
            operands["first_kept"], operands["second_kept"] = kept.pop(index)
        if final:
            operands["first_left"], operands["second_left"] = left.pop(index - 2)
        outs = stage(
            operands,
            earlier,
            chunks,
            index,
            fresh,
            middle,
            final,
        )
        if "across_out" in outs:
            flights[index + 2] = (
                from_partner(outs["across_out"], "cfg", 1),
                from_partner(outs["along_out"], "sp", 2),
            )
        if fresh:
            kept[index + 2] = (outs["first_kept_out"], outs["second_kept_out"])
        if middle:
            left[index] = (outs["first_left_out"], outs["second_left_out"])
        if final:
            arrivals.append(from_behind(outs["done_out"], "pipe", 1))
        earlier = [list(outs.values())[-1]] + (arrivals[-2:-1] if 3 <= index < count else [])
    return jnp.concatenate(arrivals, axis=1)[None, None]


def solution(mesh):
    placed = (
        P("pipe", "cfg", "sp", None),
        P("pipe", "cfg", None, None),
        P("pipe", None, None, ("sp", "cfg")),
        P("pipe", ("sp", "cfg"), None),
        P("pipe", "cfg", "sp", None, None),
        P("pipe", None, None),
    )
    return jax.shard_map(
        per_device,
        mesh=mesh,
        in_specs=placed,
        out_specs=P("pipe", "cfg", "sp", None),
        check_vma=False,
    )
```

```python
import functools

import jax
import jax.numpy as jnp
from jax import lax
from jax.experimental import pallas as pl
from jax.experimental.pallas import tpu as pltpu
from jax.sharding import PartitionSpec as P

HD = 128
TILE = 128
MIB = 2**20
SPARE = 39
LOG2E = 1.4426950408889634
CHUNK_SHARES = (5, 5, 2, 3, 3, 2)

guidance_scale = 5.0
SHORT = pl.CostEstimate(flops=1, bytes_accessed=1, transcendentals=0)


def from_behind(x, axis, by):
    count = lax.axis_size(axis)
    return lax.ppermute(x, axis, [(i, (i + by) % count) for i in range(count)])


def from_partner(value, axis, mask):
    pairs = [(source, source ^ mask) for source in range(lax.axis_size(axis))]
    return lax.ppermute(value, axis, pairs)


def norm_kernel(*refs):
    *parts, modulation_ref, out_ref = refs
    step = 16
    start = 0
    for part in parts:

        def body(index, carry, part=part, start=start):
            rows = pl.ds(pl.multiple_of(index * step, step), step)
            out_rows = pl.ds(pl.multiple_of(start + index * step, step), step)
            values = part[rows, :].astype(jnp.float32)
            centre = values - jnp.mean(values, axis=-1, keepdims=True)
            spread = jnp.mean(centre * centre, axis=-1, keepdims=True)
            normed = centre * lax.rsqrt(spread + 1e-06)
            out_ref[out_rows, :] = (
                normed * (1.0 + modulation_ref[1:2, :]) + modulation_ref[0:1, :]
            ).astype(jnp.bfloat16)
            return carry

        lax.fori_loop(0, part.shape[0] // step, body, 0, unroll=2)
        start += part.shape[0]


def modulated_norm(parts, modulation):
    rows, features = sum(part.shape[0] for part in parts), modulation.shape[1]
    return pl.pallas_call(
        norm_kernel,
        in_specs=[pl.BlockSpec(memory_space=pltpu.VMEM)] * (len(parts) + 1),
        out_shape=jax.ShapeDtypeStruct((rows, features), jnp.bfloat16),
        name="modulated_norm",
        cost_estimate=SHORT,
        compiler_params=pltpu.CompilerParams(vmem_limit_bytes=8 * MIB),
    )(*parts, modulation)


def gate_kernel(value_ref, *refs):
    pass


def after(value, earlier, limit=1):
    return pl.pallas_call(
        gate_kernel,
        in_specs=[pl.BlockSpec(memory_space=pl.ANY)] * (1 + len(earlier)),
        out_specs=pl.BlockSpec(memory_space=pl.ANY),
        out_shape=jax.ShapeDtypeStruct(value.shape, value.dtype),
        input_output_aliases={0: 0},
        name="after",
        cost_estimate=SHORT,
        compiler_params=pltpu.CompilerParams(vmem_limit_bytes=limit * MIB),
    )(value, *earlier)


def project_kernel(*refs, blocks):
    block_refs, (weights_ref, out_ref, total_ref, heads_ref, sems) = refs[:blocks], refs[blocks:]
    step, steps = pl.program_id(0), pl.num_programs(0)
    weights = jnp.concatenate([weights_ref[0], weights_ref[1], weights_ref[2]], axis=1)
    block = weights.shape[0]
    columns = pl.ds(pl.multiple_of(step * block, block), block)
    rows = jnp.concatenate([ref[:, columns] for ref in block_refs], axis=0)
    product = jnp.dot(rows, weights, preferred_element_type=jnp.float32)

    @pl.when(step == 0)
    def _():
        total_ref[...] = product

    @pl.when((step > 0) & (step < steps - 1))
    def _():
        total_ref[...] += product

    @pl.when(step == steps - 1)
    def _():
        heads = heads_ref.shape[0]
        copies = []
        for head in range(heads):
            columns = slice(head * HD, (head + 1) * HD)
            values = total_ref[:, columns] + product[:, columns]
            if head < 2 * heads // 3:
                square = jnp.mean(values * values, axis=-1, keepdims=True)
                values = values * lax.rsqrt(square + 1e-06)
            heads_ref[head] = values.astype(jnp.bfloat16)
            copies.append(
                pltpu.make_async_copy(heads_ref.at[head], out_ref.at[head], sems.at[head])
            )
            copies[-1].start()
        for copy in copies:
            copy.wait()


def project(blocks, weights):
    _, depth, width = weights.shape
    steps = 2
    block = depth // steps
    count = sum(rows.shape[0] for rows in blocks)
    heads = 3 * width // HD
    return pl.pallas_call(
        functools.partial(project_kernel, blocks=len(blocks)),
        grid=(steps,),
        in_specs=[pl.BlockSpec(memory_space=pltpu.VMEM)] * len(blocks)
        + [pl.BlockSpec((3, block, width), lambda k: (0, k, 0))],
        out_specs=pl.BlockSpec(memory_space=pltpu.HBM),
        out_shape=jax.ShapeDtypeStruct((heads + SPARE, count, HD), jnp.bfloat16),
        scratch_shapes=[
            pltpu.VMEM((count, 3 * width), jnp.float32),
            pltpu.VMEM((heads, count, HD), jnp.bfloat16),
            pltpu.SemaphoreType.DMA((heads,)),
        ],
        name="project_heads",
        cost_estimate=pl.CostEstimate(
            flops=2 * count * depth * 3 * width,
            bytes_accessed=2 * (count * depth + weights.size),
            transcendentals=0,
        ),
        compiler_params=pltpu.CompilerParams(vmem_limit_bytes=42 * MIB),
    )(*blocks, weights)


def attend_head(visible_ref, queries_ref, pool_ref, out_ref, first_block, head):
    heads, fresh_rows, _ = queries_ref.shape
    tiles_seen = visible_ref.shape[1]
    tiles_fresh = visible_ref.shape[0]
    mine_high, mine_low = lax.axis_index("sp") // 2, lax.axis_index("sp") % 2
    mine_branch = lax.axis_index("cfg")

    def body(step, carry):
        index = first_block + step
        high, low = mine_high ^ ((index // 2) % 2), mine_low ^ (index // 4)
        tile, branch = high * 2 + low, mine_branch ^ (index % 2)
        rows = pl.ds(pl.multiple_of(index * TILE, TILE), TILE)
        out_rows = pl.ds(pl.multiple_of(step * TILE, TILE), TILE)
        places = []
        for seen in range(tiles_seen):
            number = visible_ref[tile, seen]
            older = number - tiles_fresh
            fresh = (mine_low ^ (number % 2)) * 4 + (mine_high ^ ((number // 2) % 2)) * 2
            fresh = (fresh + index % 2) * TILE
            stale = fresh_rows + ((older // 2) * 2 + branch) * 2 * TILE + (older % 2) * TILE
            start = jnp.where(number < tiles_fresh, fresh, stale)
            places.append(pl.ds(pl.multiple_of(start, TILE), TILE))

        mixed = 0.0
        for pair in range(0, tiles_seen, 2):
            pair = places[pair : pair + 2]
            keys = jnp.concatenate([pool_ref[head, place, :] for place in pair], axis=0)
            values = jnp.concatenate([pool_ref[heads + head, place, :] for place in pair], axis=0)
            scores = lax.dot_general(
                queries_ref[head, rows, :],
                keys,
                (((1,), (1,)), ((), ())),
                preferred_element_type=jnp.float32,
            )
            exponent = jnp.exp2(scores * (HD ** (-0.5) * LOG2E)).astype(jnp.bfloat16)
            ones = jnp.ones(values.shape, jnp.bfloat16)
            mixed += jnp.dot(
                exponent,
                jnp.concatenate([values, ones], axis=1),
                preferred_element_type=jnp.float32,
            )
        out_ref[out_rows, head * HD : (head + 1) * HD] = (mixed[:, :HD] / mixed[:, HD:]).astype(
            jnp.bfloat16
        )
        return carry

    lax.fori_loop(0, out_ref.shape[0] // TILE, body, 0, unroll=True)


def attend_first_kernel(
    visible_ref, heads_in, context_in, out_ref, queries_ref, pool_ref, sems
):
    heads, fresh_rows, _ = queries_ref.shape
    fresh, stale = pl.ds(0, fresh_rows), pl.ds(fresh_rows, context_in.shape[0])
    copies = []
    for head in range(heads):
        pairs = [(heads_in.at[head], queries_ref.at[head])]
        for kind in range(2):
            place = kind * heads + head
            columns = pl.ds(place * HD, HD)
            pairs.append((heads_in.at[heads + place], pool_ref.at[place, fresh]))
            pairs.append((context_in.at[:, columns], pool_ref.at[place, stale]))
        of_head = [
            pltpu.make_async_copy(source, target, sems.at[head, number])
            for number, (source, target) in enumerate(pairs)
        ]
        for copy in of_head:
            copy.start()
        copies.append(of_head)
    for head in range(heads):
        for copy in copies[head]:
            copy.wait()
        first_block = out_ref.shape[0] // TILE
        attend_head(visible_ref, queries_ref, pool_ref, out_ref, first_block, head)


def attend_first(heads, context, visible):
    number, rows = (heads.shape[0] - SPARE) // 3, heads.shape[1]
    return pl.pallas_call(
        attend_first_kernel,
        in_specs=[
            pl.BlockSpec(memory_space=pltpu.SMEM),
            pl.BlockSpec(memory_space=pltpu.HBM),
            pl.BlockSpec(memory_space=pl.ANY),
        ],
        out_specs=[pl.BlockSpec(memory_space=pltpu.VMEM)] * 3,
        out_shape=[
            jax.ShapeDtypeStruct((rows // 2, number * HD), jnp.bfloat16),
            jax.ShapeDtypeStruct((number, rows, HD), heads.dtype),
            jax.ShapeDtypeStruct((2 * number, rows + context.shape[0], HD), heads.dtype),
        ],
        scratch_shapes=[pltpu.SemaphoreType.DMA((number, 5))],
        name="attend_first",
        cost_estimate=SHORT,
        compiler_params=pltpu.CompilerParams(vmem_limit_bytes=44 * MIB),
    )(visible, heads, context)


def attend_second_kernel(visible_ref, queries_ref, pool_ref, *refs):
    weights_ref, core_weights_ref = refs[:2]
    out_ref, both_ref, sems = refs[-3:]
    depth, columns = weights_ref.shape[0], pl.ds(0, both_ref.shape[1])
    copies = [
        pltpu.make_async_copy(
            ref.at[:, columns], both_ref.at[pl.ds(core * depth, depth)], sems.at[core]
        )
        for core, ref in enumerate((weights_ref, core_weights_ref))
    ]
    for copy in copies:
        copy.start()
    for head in range(queries_ref.shape[0]):
        attend_head(visible_ref, queries_ref, pool_ref, out_ref, 0, head)
    for copy in copies:
        copy.wait()


def attend_second(queries, pool, visible, weights, core_weights, columns, earlier):
    number, rows, _ = queries.shape
    return pl.pallas_call(
        attend_second_kernel,
        in_specs=[pl.BlockSpec(memory_space=pltpu.SMEM)]
        + [pl.BlockSpec(memory_space=pltpu.VMEM)] * 2
        + [pl.BlockSpec(memory_space=pl.ANY)] * (2 + len(earlier)),
        out_specs=[pl.BlockSpec(memory_space=pltpu.VMEM)] * 2,
        out_shape=[
            jax.ShapeDtypeStruct((rows // 2, number * HD), jnp.bfloat16),
            jax.ShapeDtypeStruct((2 * weights.shape[0], columns), weights.dtype),
        ],
        scratch_shapes=[pltpu.SemaphoreType.DMA((2,))],
        name="attend_second",
        cost_estimate=SHORT,
        compiler_params=pltpu.CompilerParams(vmem_limit_bytes=12 * MIB),
    )(visible, queries, pool, weights, core_weights, *earlier)


def combined(own, other, mine, gates_ref, columns):
    conditional = lax.axis_index("cfg") == 1
    last = lax.axis_index("pipe") == lax.axis_size("pipe") - 1
    weight = jnp.where(conditional, guidance_scale, 1.0 - guidance_scale).astype(jnp.float32)
    other_weight = jnp.where(conditional, 1.0 - guidance_scale, guidance_scale).astype(jnp.float32)
    own = own * gates_ref[0:1, columns]
    other = other * gates_ref[1:2, columns]
    if mine is not None:
        own = own + mine
    guided = weight * own + other_weight * other
    return jnp.where(last, guided, other), jnp.where(last, guided, own)


def begin(start, refs, across_out, along_out, first_kept, second_kept):
    attended_ref, core_attended_ref, *weights_refs, rows_ref, gates_ref = refs
    tokens, half = rows_ref.shape[0], first_kept.shape[2]
    attended = jnp.concatenate([attended_ref[...], core_attended_ref[...]], axis=1)

    def product_of(columns):
        weights = jnp.concatenate([ref[:, columns] for ref in weights_refs], axis=0)
        return jnp.dot(attended, weights, preferred_element_type=jnp.float32)

    columns = slice(start, start + half)
    product = product_of(slice(0, half))
    for tile in range(2):
        sent_columns = slice(tile * half, (tile + 1) * half)
        own = product[2 * tile * tokens : (2 * tile + 1) * tokens]
        other = product[(2 * tile + 1) * tokens : (2 * tile + 2) * tokens]
        mine = rows_ref[:, columns].astype(jnp.float32) if tile == 0 else None
        sent, kept = combined(own, other, mine, gates_ref, columns)
        across_out[:, sent_columns] = sent.astype(jnp.bfloat16)
        first_kept[tile] = kept
    product = product_of(slice(half, 2 * half))
    for branch in range(2):
        sent_columns = slice(branch * half, (branch + 1) * half)
        second_kept[branch] = product[branch * tokens : (branch + 1) * tokens]
        along_out[:, sent_columns] = product[(branch + 2) * tokens : (branch + 3) * tokens].astype(
            jnp.bfloat16
        )


def stage_kernel(*refs, parts, start, next_start, fresh, middle, final):
    named = dict(zip(parts, refs))
    if fresh:
        begin(
            next_start,
            [
                named[name]
                for name in (
                    "attended", "core_attended", "weights", "core_weights", "both", "rows", "gates"
                )
                if name in named
            ],
            named["across_out"],
            named["along_out"],
            named["first_kept_out"],
            named["second_kept_out"],
        )
    if middle:
        across, along = named["across"], named["along"]
        first_kept, second_kept = named["first_kept"], named["second_kept"]
        half = first_kept.shape[2]
        sent_columns = slice(named["across_out"].shape[1] - half, named["across_out"].shape[1])
        named["along_out"][:, sent_columns] = (
            first_kept[1] + across[:, half : 2 * half].astype(jnp.float32)
        ).astype(jnp.bfloat16)
        named["first_left_out"][...] = first_kept[0] + across[:, :half].astype(jnp.float32)
        columns = slice(start + half, start + 2 * half)
        sent, kept = combined(
            second_kept[0] + along[:, :half].astype(jnp.float32),
            second_kept[1] + along[:, half : 2 * half].astype(jnp.float32),
            named["rows"][:, columns].astype(jnp.float32),
            named["gates"],
            columns,
        )
        named["across_out"][:, sent_columns] = sent.astype(jnp.bfloat16)
        named["second_left_out"][...] = kept
    if final:
        across, along = named["across"], named["along"]
        first_left, second_left = named["first_left"], named["second_left"]
        half = first_left.shape[1]
        columns = slice(across.shape[1] - half, across.shape[1])
        named["done_out"][:, :half] = (
            first_left[...] + along[:, columns].astype(jnp.float32)
        ).astype(jnp.bfloat16)
        named["done_out"][:, half:] = (
            second_left[...] + across[:, columns].astype(jnp.float32)
        ).astype(jnp.bfloat16)


def stage(operands, earlier, chunks, index, fresh, middle, final):
    tokens = operands["rows"].shape[0]
    next_start, next_chunk = chunks[index + 2] if fresh else (0, 0)
    start, chunk = chunks[index] if middle else (0, 0)
    outs = {}
    if fresh or middle:
        columns = next_chunk + chunk // 2
        outs["across_out"] = jax.ShapeDtypeStruct((tokens, columns), jnp.bfloat16)
        outs["along_out"] = outs["across_out"]
    if fresh:
        outs["first_kept_out"] = jax.ShapeDtypeStruct((2, tokens, next_chunk // 2), jnp.float32)
        outs["second_kept_out"] = outs["first_kept_out"]
    if middle:
        outs["first_left_out"] = jax.ShapeDtypeStruct((tokens, chunk // 2), jnp.float32)
        outs["second_left_out"] = outs["first_left_out"]
    if final:
        outs["done_out"] = jax.ShapeDtypeStruct((tokens, chunks[index - 2][1]), jnp.bfloat16)
    parts = list(operands) + ["earlier"] * len(earlier) + list(outs)
    results = pl.pallas_call(
        functools.partial(
            stage_kernel,
            parts=parts,
            start=start,
            next_start=next_start,
            fresh=fresh,
            middle=middle,
            final=final,
        ),
        grid=(1,),
        in_specs=[
            pl.BlockSpec((array.shape[0], next_chunk), lambda step: (0, next_start // next_chunk))
            if name in ("weights", "core_weights")
            else pl.BlockSpec(memory_space=pltpu.VMEM)
            for name, array in operands.items()
        ]
        + [pl.BlockSpec(memory_space=pl.ANY)] * len(earlier),
        out_specs=[pl.BlockSpec(memory_space=pltpu.VMEM)] * len(outs),
        out_shape=list(outs.values()),
        name="sum_stage",
        cost_estimate=SHORT,
        compiler_params=pltpu.CompilerParams(vmem_limit_bytes=16 * MIB),
    )(*operands.values(), *earlier)
    return dict(zip(outs, results))


def per_device(flight, modulation, project_in, project_out, stale_cache, visible):
    current = flight[0, 0]
    modulate = modulation[0, 0]
    token_rows, features = current.shape
    devices = lax.axis_size("sp") * lax.axis_size("cfg")

    context_rows = stale_cache.shape[2]
    width = project_in.shape[3]
    unpacked = stale_cache[0, 0].reshape(context_rows, 2, devices, width)
    packed = unpacked.transpose(2, 0, 1, 3).reshape(devices, context_rows, 2 * width)

    upper, lower = current[: token_rows // 2], current[token_rows // 2 :]
    across_upper, along_lower = from_partner(upper, "cfg", 1), from_partner(lower, "sp", 2)
    across_lower, along_upper = from_partner(lower, "cfg", 1), from_partner(upper, "sp", 2)
    other_modulate = from_partner(modulation, "cfg", 1)[0, 0]
    across_upper, along_lower = after(across_upper, (unpacked,)), after(along_lower, (unpacked,))
    first, second = from_partner(across_upper, "sp", 2), from_partner(along_lower, "cfg", 1)
    core_weights = from_partner(project_out[0], "sp", 1)
    near = [
        modulated_norm([current], modulate),
        modulated_norm([across_upper, across_lower], other_modulate),
        modulated_norm([along_upper, along_lower], modulate),
        modulated_norm([first, second], other_modulate),
    ]
    far = [from_partner(rows, "sp", 1) for rows in near]

    packed = after(packed, (across_lower, along_upper), limit=60)
    context = lax.all_to_all(packed, ("sp", "cfg"), split_axis=0, concat_axis=0, tiled=True)
    context = context.reshape(devices * context_rows, 2 * width)

    heads = project(near + far, project_in[0])
    gates = jnp.concatenate([modulate[2:3], other_modulate[2:3]], axis=0)
    count = len(CHUNK_SHARES)
    unit = features // sum(CHUNK_SHARES)
    chunks = [
        (sum(CHUNK_SHARES[:index]) * unit, share * unit) for index, share in enumerate(CHUNK_SHARES)
    ]
    for_core, queries, pool = attend_first(heads, context, visible[0])
    core_attended = from_partner(for_core, "sp", 1)
    attended, first_weights = attend_second(
        queries, pool, visible[0], project_out[0], core_weights, chunks[0][1], (for_core, gates)
    )

    kept, left, flights, arrivals, earlier = {}, {}, {}, [], []
    for index in range(-2, count + 2):
        fresh, middle, final = index + 2 < count, 0 <= index < count, index >= 2
        operands = {"rows": current, "gates": gates}
        if fresh:
            operands.update(attended=attended, core_attended=core_attended)
            if index == -2:
                operands["both"] = first_weights
            else:
                operands.update(weights=project_out[0], core_weights=core_weights)
        if index >= 0:
            operands["across"], operands["along"] = flights.pop(index)
        if middle:
            operands["first_kept"], operands["second_kept"] = kept.pop(index)
        if final:
            operands["first_left"], operands["second_left"] = left.pop(index - 2)
        outs = stage(
            operands,
            earlier,
            chunks,
            index,
            fresh,
            middle,
            final,
        )
        if "across_out" in outs:
            flights[index + 2] = (
                from_partner(outs["across_out"], "cfg", 1),
                from_partner(outs["along_out"], "sp", 2),
            )
        if fresh:
            kept[index + 2] = (outs["first_kept_out"], outs["second_kept_out"])
        if middle:
            left[index] = (outs["first_left_out"], outs["second_left_out"])
        if final:
            arrivals.append(from_behind(outs["done_out"], "pipe", 1))
        earlier = [list(outs.values())[-1]] + (arrivals[-2:-1] if 3 <= index < count else [])
    return jnp.concatenate(arrivals, axis=1)[None, None]


def solution(mesh):
    placed = (
        P("pipe", "cfg", "sp", None),
        P("pipe", "cfg", None, None),
        P("pipe", None, None, ("sp", "cfg")),
        P("pipe", ("sp", "cfg"), None),
        P("pipe", "cfg", "sp", None, None),
        P("pipe", None, None),
    )
    return jax.shard_map(
        per_device,
        mesh=mesh,
        in_specs=placed,
        out_specs=P("pipe", "cfg", "sp", None),
        check_vma=False,
    )
```

```python
import functools

import jax
import jax.numpy as jnp
from jax import lax
from jax.experimental import pallas as pl
from jax.experimental.pallas import tpu as pltpu
from jax.sharding import PartitionSpec as P

HD = 128
TILE = 128
MIB = 2**20
SPARE = 39
LOG2E = 1.4426950408889634
CHUNK_SHARES = (5, 5, 2, 3, 3, 2)

guidance_scale = 5.0
SHORT = pl.CostEstimate(flops=1, bytes_accessed=1, transcendentals=0)


def from_behind(x, axis, by):
    count = lax.axis_size(axis)
    return lax.ppermute(x, axis, [(i, (i + by) % count) for i in range(count)])


def from_partner(value, axis, mask):
    pairs = [(source, source ^ mask) for source in range(lax.axis_size(axis))]
    return lax.ppermute(value, axis, pairs)


def norm_kernel(*refs):
    *parts, modulation_ref, out_ref = refs
    step = 16
    start = 0
    for part in parts:

        def body(index, carry, part=part, start=start):
            rows = pl.ds(pl.multiple_of(index * step, step), step)
            out_rows = pl.ds(pl.multiple_of(start + index * step, step), step)
            values = part[rows, :].astype(jnp.float32)
            centre = values - jnp.mean(values, axis=-1, keepdims=True)
            spread = jnp.mean(centre * centre, axis=-1, keepdims=True)
            normed = centre * lax.rsqrt(spread + 1e-06)
            out_ref[out_rows, :] = (
                normed * (1.0 + modulation_ref[1:2, :]) + modulation_ref[0:1, :]
            ).astype(jnp.bfloat16)
            return carry

        lax.fori_loop(0, part.shape[0] // step, body, 0, unroll=2)
        start += part.shape[0]


def modulated_norm(parts, modulation):
    rows, features = sum(part.shape[0] for part in parts), modulation.shape[1]
    return pl.pallas_call(
        norm_kernel,
        in_specs=[pl.BlockSpec(memory_space=pltpu.VMEM)] * (len(parts) + 1),
        out_shape=jax.ShapeDtypeStruct((rows, features), jnp.bfloat16),
        name="modulated_norm",
        cost_estimate=SHORT,
        compiler_params=pltpu.CompilerParams(vmem_limit_bytes=8 * MIB),
    )(*parts, modulation)


def gate_kernel(value_ref, *refs):
    pass


def after(value, earlier, limit=1):
    return pl.pallas_call(
        gate_kernel,
        in_specs=[pl.BlockSpec(memory_space=pl.ANY)] * (1 + len(earlier)),
        out_specs=pl.BlockSpec(memory_space=pl.ANY),
        out_shape=jax.ShapeDtypeStruct(value.shape, value.dtype),
        input_output_aliases={0: 0},
        name="after",
        cost_estimate=SHORT,
        compiler_params=pltpu.CompilerParams(vmem_limit_bytes=limit * MIB),
    )(value, *earlier)


def project_kernel(*refs, blocks):
    block_refs, (weights_ref, out_ref, total_ref, heads_ref, sems) = refs[:blocks], refs[blocks:]
    step, steps = pl.program_id(0), pl.num_programs(0)
    weights = jnp.concatenate([weights_ref[0], weights_ref[1], weights_ref[2]], axis=1)
    block = weights.shape[0]
    columns = pl.ds(pl.multiple_of(step * block, block), block)
    rows = jnp.concatenate([ref[:, columns] for ref in block_refs], axis=0)
    product = jnp.dot(rows, weights, preferred_element_type=jnp.float32)

    @pl.when(step == 0)
    def _():
        total_ref[...] = product

    @pl.when((step > 0) & (step < steps - 1))
    def _():
        total_ref[...] += product

    @pl.when(step == steps - 1)
    def _():
        heads = heads_ref.shape[0]
        copies = []
        for head in range(heads):
            columns = slice(head * HD, (head + 1) * HD)
            values = total_ref[:, columns] + product[:, columns]
            if head < 2 * heads // 3:
                square = jnp.mean(values * values, axis=-1, keepdims=True)
                values = values * lax.rsqrt(square + 1e-06)
            heads_ref[head] = values.astype(jnp.bfloat16)
            copies.append(
                pltpu.make_async_copy(heads_ref.at[head], out_ref.at[head], sems.at[head])
            )
            copies[-1].start()
        for copy in copies:
            copy.wait()


def project(blocks, weights):
    _, depth, width = weights.shape
    steps = 2
    block = depth // steps
    count = sum(rows.shape[0] for rows in blocks)
    heads = 3 * width // HD
    return pl.pallas_call(
        functools.partial(project_kernel, blocks=len(blocks)),
        grid=(steps,),
        in_specs=[pl.BlockSpec(memory_space=pltpu.VMEM)] * len(blocks)
        + [pl.BlockSpec((3, block, width), lambda k: (0, k, 0))],
        out_specs=pl.BlockSpec(memory_space=pltpu.HBM),
        out_shape=jax.ShapeDtypeStruct((heads + SPARE, count, HD), jnp.bfloat16),
        scratch_shapes=[
            pltpu.VMEM((count, 3 * width), jnp.float32),
            pltpu.VMEM((heads, count, HD), jnp.bfloat16),
            pltpu.SemaphoreType.DMA((heads,)),
        ],
        name="project_heads",
        cost_estimate=pl.CostEstimate(
            flops=2 * count * depth * 3 * width,
            bytes_accessed=2 * (count * depth + weights.size),
            transcendentals=0,
        ),
        compiler_params=pltpu.CompilerParams(vmem_limit_bytes=42 * MIB),
    )(*blocks, weights)


def attend_units(visible_ref, queries_ref, pool_ref, out_ref, first_block, before_head):
    heads, fresh_rows, _ = queries_ref.shape
    tiles_seen = visible_ref.shape[1]
    tiles_fresh = visible_ref.shape[0]
    mine_high, mine_low = lax.axis_index("sp") // 2, lax.axis_index("sp") % 2
    mine_branch = lax.axis_index("cfg")
    blocks = out_ref.shape[0] // TILE
    places = []
    for block in range(blocks):
        index = first_block + block
        high, low = mine_high ^ ((index // 2) % 2), mine_low ^ (index // 4)
        tile, branch = high * 2 + low, mine_branch ^ (index % 2)
        seen = []
        for number in range(tiles_seen):
            number = visible_ref[tile, number]
            older = number - tiles_fresh
            fresh = (mine_low ^ (number % 2)) * 4 + (mine_high ^ ((number // 2) % 2)) * 2
            fresh = (fresh + index % 2) * TILE
            stale = fresh_rows + ((older // 2) * 2 + branch) * 2 * TILE + (older % 2) * TILE
            start = jnp.where(number < tiles_fresh, fresh, stale)
            seen.append(pl.ds(pl.multiple_of(start, TILE), TILE))
        places.append(seen)

    def scores_of(head, block):
        rows = pl.ds((first_block + block) * TILE, TILE)
        keys = jnp.concatenate([pool_ref[head, place, :] for place in places[block]], axis=0)
        return lax.dot_general(
            queries_ref[head, rows, :],
            keys,
            (((1,), (1,)), ((), ())),
            preferred_element_type=jnp.float32,
        )

    def finish(head, block, scores):
        values = [pool_ref[heads + head, place, :] for place in places[block]]
        values = jnp.concatenate(values, axis=0)
        exponent = jnp.exp2(scores * (HD ** (-0.5) * LOG2E)).astype(jnp.bfloat16)
        ones = jnp.ones(values.shape, jnp.bfloat16)
        mixed = jnp.dot(
            exponent, jnp.concatenate([values, ones], axis=1), preferred_element_type=jnp.float32
        )
        out_ref[block * TILE : (block + 1) * TILE, head * HD : (head + 1) * HD] = (
            mixed[:, :HD] / mixed[:, HD:]
        ).astype(jnp.bfloat16)

    waiting = None
    for head in range(heads):
        before_head(head)
        for block in range(blocks):
            scores = scores_of(head, block)
            if waiting is not None:
                finish(*waiting)
            waiting = head, block, scores
    finish(*waiting)


def attend_first_kernel(
    visible_ref, heads_in, context_in, out_ref, queries_ref, pool_ref, sems
):
    heads, fresh_rows, _ = queries_ref.shape
    fresh, stale = pl.ds(0, fresh_rows), pl.ds(fresh_rows, context_in.shape[0])
    copies = []
    for head in range(heads):
        pairs = [(heads_in.at[head], queries_ref.at[head])]
        for kind in range(2):
            place = kind * heads + head
            columns = pl.ds(place * HD, HD)
            pairs.append((heads_in.at[heads + place], pool_ref.at[place, fresh]))
            pairs.append((context_in.at[:, columns], pool_ref.at[place, stale]))
        of_head = [
            pltpu.make_async_copy(source, target, sems.at[head, number])
            for number, (source, target) in enumerate(pairs)
        ]
        for copy in of_head:
            copy.start()
        copies.append(of_head)

    def before_head(head):
        for copy in copies[head]:
            copy.wait()

    first_block = out_ref.shape[0] // TILE
    attend_units(visible_ref, queries_ref, pool_ref, out_ref, first_block, before_head)


def attend_first(heads, context, visible):
    number, rows = (heads.shape[0] - SPARE) // 3, heads.shape[1]
    return pl.pallas_call(
        attend_first_kernel,
        in_specs=[
            pl.BlockSpec(memory_space=pltpu.SMEM),
            pl.BlockSpec(memory_space=pltpu.HBM),
            pl.BlockSpec(memory_space=pl.ANY),
        ],
        out_specs=[pl.BlockSpec(memory_space=pltpu.VMEM)] * 3,
        out_shape=[
            jax.ShapeDtypeStruct((rows // 2, number * HD), jnp.bfloat16),
            jax.ShapeDtypeStruct((number, rows, HD), heads.dtype),
            jax.ShapeDtypeStruct((2 * number, rows + context.shape[0], HD), heads.dtype),
        ],
        scratch_shapes=[pltpu.SemaphoreType.DMA((number, 5))],
        name="attend_first",
        cost_estimate=SHORT,
        compiler_params=pltpu.CompilerParams(vmem_limit_bytes=44 * MIB),
    )(visible, heads, context)


def attend_second_kernel(visible_ref, queries_ref, pool_ref, *refs):
    weights_ref, core_weights_ref = refs[:2]
    out_ref, both_ref, sems = refs[-3:]
    depth, columns = weights_ref.shape[0], pl.ds(0, both_ref.shape[1])
    copies = [
        pltpu.make_async_copy(
            ref.at[:, columns], both_ref.at[pl.ds(core * depth, depth)], sems.at[core]
        )
        for core, ref in enumerate((weights_ref, core_weights_ref))
    ]
    for copy in copies:
        copy.start()
    attend_units(visible_ref, queries_ref, pool_ref, out_ref, 0, lambda head: None)
    for copy in copies:
        copy.wait()


def attend_second(queries, pool, visible, weights, core_weights, columns, earlier):
    number, rows, _ = queries.shape
    return pl.pallas_call(
        attend_second_kernel,
        in_specs=[pl.BlockSpec(memory_space=pltpu.SMEM)]
        + [pl.BlockSpec(memory_space=pltpu.VMEM)] * 2
        + [pl.BlockSpec(memory_space=pl.ANY)] * (2 + len(earlier)),
        out_specs=[pl.BlockSpec(memory_space=pltpu.VMEM)] * 2,
        out_shape=[
            jax.ShapeDtypeStruct((rows // 2, number * HD), jnp.bfloat16),
            jax.ShapeDtypeStruct((2 * weights.shape[0], columns), weights.dtype),
        ],
        scratch_shapes=[pltpu.SemaphoreType.DMA((2,))],
        name="attend_second",
        cost_estimate=SHORT,
        compiler_params=pltpu.CompilerParams(vmem_limit_bytes=12 * MIB),
    )(visible, queries, pool, weights, core_weights, *earlier)


def combined(own, other, mine, gates_ref, columns):
    conditional = lax.axis_index("cfg") == 1
    last = lax.axis_index("pipe") == lax.axis_size("pipe") - 1
    weight = jnp.where(conditional, guidance_scale, 1.0 - guidance_scale).astype(jnp.float32)
    other_weight = jnp.where(conditional, 1.0 - guidance_scale, guidance_scale).astype(jnp.float32)
    own = own * gates_ref[0:1, columns]
    other = other * gates_ref[1:2, columns]
    if mine is not None:
        own = own + mine
    guided = weight * own + other_weight * other
    return jnp.where(last, guided, other), jnp.where(last, guided, own)


def begin(start, refs, across_out, along_out, first_kept, second_kept):
    attended_ref, core_attended_ref, *weights_refs, rows_ref, gates_ref = refs
    tokens, half = rows_ref.shape[0], first_kept.shape[2]
    attended = jnp.concatenate([attended_ref[...], core_attended_ref[...]], axis=1)

    def product_of(columns):
        weights = jnp.concatenate([ref[:, columns] for ref in weights_refs], axis=0)
        return jnp.dot(attended, weights, preferred_element_type=jnp.float32)

    columns = slice(start, start + half)
    product = product_of(slice(0, half))
    for tile in range(2):
        sent_columns = slice(tile * half, (tile + 1) * half)
        own = product[2 * tile * tokens : (2 * tile + 1) * tokens]
        other = product[(2 * tile + 1) * tokens : (2 * tile + 2) * tokens]
        mine = rows_ref[:, columns].astype(jnp.float32) if tile == 0 else None
        sent, kept = combined(own, other, mine, gates_ref, columns)
        across_out[:, sent_columns] = sent.astype(jnp.bfloat16)
        first_kept[tile] = kept
    product = product_of(slice(half, 2 * half))
    for branch in range(2):
        sent_columns = slice(branch * half, (branch + 1) * half)
        second_kept[branch] = product[branch * tokens : (branch + 1) * tokens]
        along_out[:, sent_columns] = product[(branch + 2) * tokens : (branch + 3) * tokens].astype(
            jnp.bfloat16
        )


def stage_kernel(*refs, parts, start, next_start, fresh, middle, final):
    named = dict(zip(parts, refs))
    if fresh:
        begin(
            next_start,
            [
                named[name]
                for name in (
                    "attended", "core_attended", "weights", "core_weights", "both", "rows", "gates"
                )
                if name in named
            ],
            named["across_out"],
            named["along_out"],
            named["first_kept_out"],
            named["second_kept_out"],
        )
    if middle:
        across, along = named["across"], named["along"]
        first_kept, second_kept = named["first_kept"], named["second_kept"]
        half = first_kept.shape[2]
        sent_columns = slice(named["across_out"].shape[1] - half, named["across_out"].shape[1])
        named["along_out"][:, sent_columns] = (
            first_kept[1] + across[:, half : 2 * half].astype(jnp.float32)
        ).astype(jnp.bfloat16)
        named["first_left_out"][...] = first_kept[0] + across[:, :half].astype(jnp.float32)
        columns = slice(start + half, start + 2 * half)
        sent, kept = combined(
            second_kept[0] + along[:, :half].astype(jnp.float32),
            second_kept[1] + along[:, half : 2 * half].astype(jnp.float32),
            named["rows"][:, columns].astype(jnp.float32),
            named["gates"],
            columns,
        )
        named["across_out"][:, sent_columns] = sent.astype(jnp.bfloat16)
        named["second_left_out"][...] = kept
    if final:
        across, along = named["across"], named["along"]
        first_left, second_left = named["first_left"], named["second_left"]
        half = first_left.shape[1]
        columns = slice(across.shape[1] - half, across.shape[1])
        named["done_out"][:, :half] = (
            first_left[...] + along[:, columns].astype(jnp.float32)
        ).astype(jnp.bfloat16)
        named["done_out"][:, half:] = (
            second_left[...] + across[:, columns].astype(jnp.float32)
        ).astype(jnp.bfloat16)


def stage(operands, earlier, chunks, index, fresh, middle, final):
    tokens = operands["rows"].shape[0]
    next_start, next_chunk = chunks[index + 2] if fresh else (0, 0)
    start, chunk = chunks[index] if middle else (0, 0)
    outs = {}
    if fresh or middle:
        columns = next_chunk + chunk // 2
        outs["across_out"] = jax.ShapeDtypeStruct((tokens, columns), jnp.bfloat16)
        outs["along_out"] = outs["across_out"]
    if fresh:
        outs["first_kept_out"] = jax.ShapeDtypeStruct((2, tokens, next_chunk // 2), jnp.float32)
        outs["second_kept_out"] = outs["first_kept_out"]
    if middle:
        outs["first_left_out"] = jax.ShapeDtypeStruct((tokens, chunk // 2), jnp.float32)
        outs["second_left_out"] = outs["first_left_out"]
    if final:
        outs["done_out"] = jax.ShapeDtypeStruct((tokens, chunks[index - 2][1]), jnp.bfloat16)
    parts = list(operands) + ["earlier"] * len(earlier) + list(outs)
    results = pl.pallas_call(
        functools.partial(
            stage_kernel,
            parts=parts,
            start=start,
            next_start=next_start,
            fresh=fresh,
            middle=middle,
            final=final,
        ),
        grid=(1,),
        in_specs=[
            pl.BlockSpec((array.shape[0], next_chunk), lambda step: (0, next_start // next_chunk))
            if name in ("weights", "core_weights")
            else pl.BlockSpec(memory_space=pltpu.VMEM)
            for name, array in operands.items()
        ]
        + [pl.BlockSpec(memory_space=pl.ANY)] * len(earlier),
        out_specs=[pl.BlockSpec(memory_space=pltpu.VMEM)] * len(outs),
        out_shape=list(outs.values()),
        name="sum_stage",
        cost_estimate=SHORT,
        compiler_params=pltpu.CompilerParams(vmem_limit_bytes=16 * MIB),
    )(*operands.values(), *earlier)
    return dict(zip(outs, results))


def per_device(flight, modulation, project_in, project_out, stale_cache, visible):
    current = flight[0, 0]
    modulate = modulation[0, 0]
    token_rows, features = current.shape
    devices = lax.axis_size("sp") * lax.axis_size("cfg")

    context_rows = stale_cache.shape[2]
    width = project_in.shape[3]
    unpacked = stale_cache[0, 0].reshape(context_rows, 2, devices, width)
    packed = unpacked.transpose(2, 0, 1, 3).reshape(devices, context_rows, 2 * width)

    upper, lower = current[: token_rows // 2], current[token_rows // 2 :]
    across_upper, along_lower = from_partner(upper, "cfg", 1), from_partner(lower, "sp", 2)
    across_lower, along_upper = from_partner(lower, "cfg", 1), from_partner(upper, "sp", 2)
    other_modulate = from_partner(modulation, "cfg", 1)[0, 0]
    across_upper, along_lower = after(across_upper, (unpacked,)), after(along_lower, (unpacked,))
    first, second = from_partner(across_upper, "sp", 2), from_partner(along_lower, "cfg", 1)
    core_weights = from_partner(project_out[0], "sp", 1)
    near = [
        modulated_norm([current], modulate),
        modulated_norm([across_upper, across_lower], other_modulate),
        modulated_norm([along_upper, along_lower], modulate),
        modulated_norm([first, second], other_modulate),
    ]
    far = [from_partner(rows, "sp", 1) for rows in near]

    packed = after(packed, (across_lower, along_upper), limit=60)
    context = lax.all_to_all(packed, ("sp", "cfg"), split_axis=0, concat_axis=0, tiled=True)
    context = context.reshape(devices * context_rows, 2 * width)

    heads = project(near + far, project_in[0])
    gates = jnp.concatenate([modulate[2:3], other_modulate[2:3]], axis=0)
    count = len(CHUNK_SHARES)
    unit = features // sum(CHUNK_SHARES)
    chunks = [
        (sum(CHUNK_SHARES[:index]) * unit, share * unit) for index, share in enumerate(CHUNK_SHARES)
    ]
    for_core, queries, pool = attend_first(heads, context, visible[0])
    core_attended = from_partner(for_core, "sp", 1)
    attended, first_weights = attend_second(
        queries, pool, visible[0], project_out[0], core_weights, chunks[0][1], (for_core, gates)
    )

    kept, left, flights, arrivals, earlier = {}, {}, {}, [], []
    for index in range(-2, count + 2):
        fresh, middle, final = index + 2 < count, 0 <= index < count, index >= 2
        operands = {"rows": current, "gates": gates}
        if fresh:
            operands.update(attended=attended, core_attended=core_attended)
            if index == -2:
                operands["both"] = first_weights
            else:
                operands.update(weights=project_out[0], core_weights=core_weights)
        if index >= 0:
            operands["across"], operands["along"] = flights.pop(index)
        if middle:
            operands["first_kept"], operands["second_kept"] = kept.pop(index)
        if final:
            operands["first_left"], operands["second_left"] = left.pop(index - 2)
        outs = stage(
            operands,
            earlier,
            chunks,
            index,
            fresh,
            middle,
            final,
        )
        if "across_out" in outs:
            flights[index + 2] = (
                from_partner(outs["across_out"], "cfg", 1),
                from_partner(outs["along_out"], "sp", 2),
            )
        if fresh:
            kept[index + 2] = (outs["first_kept_out"], outs["second_kept_out"])
        if middle:
            left[index] = (outs["first_left_out"], outs["second_left_out"])
        if final:
            arrivals.append(from_behind(outs["done_out"], "pipe", 1))
        earlier = [list(outs.values())[-1]] + (arrivals[-2:-1] if 3 <= index < count else [])
    return jnp.concatenate(arrivals, axis=1)[None, None]


def solution(mesh):
    placed = (
        P("pipe", "cfg", "sp", None),
        P("pipe", "cfg", None, None),
        P("pipe", None, None, ("sp", "cfg")),
        P("pipe", ("sp", "cfg"), None),
        P("pipe", "cfg", "sp", None, None),
        P("pipe", None, None),
    )
    return jax.shard_map(
        per_device,
        mesh=mesh,
        in_specs=placed,
        out_specs=P("pipe", "cfg", "sp", None),
        check_vma=False,
    )
```

```python
import functools

import jax
import jax.numpy as jnp
from jax import lax
from jax.experimental import pallas as pl
from jax.experimental.pallas import tpu as pltpu
from jax.sharding import PartitionSpec as P

HD = 128
TILE = 128
MIB = 2**20
SPARE = 39
LOG2E = 1.4426950408889634
CHUNK_SHARES = (5, 5, 2, 3, 3, 2)

guidance_scale = 5.0
SHORT = pl.CostEstimate(flops=1, bytes_accessed=1, transcendentals=0)


def from_behind(x, axis, by):
    count = lax.axis_size(axis)
    return lax.ppermute(x, axis, [(i, (i + by) % count) for i in range(count)])


def from_partner(value, axis, mask):
    pairs = [(source, source ^ mask) for source in range(lax.axis_size(axis))]
    return lax.ppermute(value, axis, pairs)


def norm_kernel(*refs):
    *parts, modulation_ref, out_ref = refs
    step = 16
    start = 0
    for part in parts:

        def body(index, carry, part=part, start=start):
            rows = pl.ds(pl.multiple_of(index * step, step), step)
            out_rows = pl.ds(pl.multiple_of(start + index * step, step), step)
            values = part[rows, :].astype(jnp.float32)
            centre = values - jnp.mean(values, axis=-1, keepdims=True)
            spread = jnp.mean(centre * centre, axis=-1, keepdims=True)
            normed = centre * lax.rsqrt(spread + 1e-06)
            out_ref[out_rows, :] = (
                normed * (1.0 + modulation_ref[1:2, :]) + modulation_ref[0:1, :]
            ).astype(jnp.bfloat16)
            return carry

        lax.fori_loop(0, part.shape[0] // step, body, 0, unroll=2)
        start += part.shape[0]


def modulated_norm(parts, modulation):
    rows, features = sum(part.shape[0] for part in parts), modulation.shape[1]
    return pl.pallas_call(
        norm_kernel,
        in_specs=[pl.BlockSpec(memory_space=pltpu.VMEM)] * (len(parts) + 1),
        out_shape=jax.ShapeDtypeStruct((rows, features), jnp.bfloat16),
        name="modulated_norm",
        cost_estimate=SHORT,
        compiler_params=pltpu.CompilerParams(vmem_limit_bytes=8 * MIB),
    )(*parts, modulation)


def gate_kernel(value_ref, *refs):
    pass


def after(value, earlier, limit=1):
    return pl.pallas_call(
        gate_kernel,
        in_specs=[pl.BlockSpec(memory_space=pl.ANY)] * (1 + len(earlier)),
        out_specs=pl.BlockSpec(memory_space=pl.ANY),
        out_shape=jax.ShapeDtypeStruct(value.shape, value.dtype),
        input_output_aliases={0: 0},
        name="after",
        cost_estimate=SHORT,
        compiler_params=pltpu.CompilerParams(vmem_limit_bytes=limit * MIB),
    )(value, *earlier)


def project_kernel(*refs, blocks):
    block_refs, (weights_ref, out_ref, total_ref, heads_ref, sems) = refs[:blocks], refs[blocks:]
    step, steps = pl.program_id(0), pl.num_programs(0)
    weights = jnp.concatenate([weights_ref[0], weights_ref[1], weights_ref[2]], axis=1)
    block = weights.shape[0]
    columns = pl.ds(pl.multiple_of(step * block, block), block)
    rows = jnp.concatenate([ref[:, columns] for ref in block_refs], axis=0)
    product = jnp.dot(rows, weights, preferred_element_type=jnp.float32)

    @pl.when(step == 0)
    def _():
        total_ref[...] = product

    @pl.when((step > 0) & (step < steps - 1))
    def _():
        total_ref[...] += product

    @pl.when(step == steps - 1)
    def _():
        heads = heads_ref.shape[0]
        copies = []
        for head in range(heads):
            columns = slice(head * HD, (head + 1) * HD)
            values = total_ref[:, columns] + product[:, columns]
            if head < 2 * heads // 3:
                square = jnp.mean(values * values, axis=-1, keepdims=True)
                values = values * lax.rsqrt(square + 1e-06)
            heads_ref[head] = values.astype(jnp.bfloat16)
            copies.append(
                pltpu.make_async_copy(heads_ref.at[head], out_ref.at[head], sems.at[head])
            )
            copies[-1].start()
        for copy in copies:
            copy.wait()


def project(blocks, weights):
    _, depth, width = weights.shape
    steps = 2
    block = depth // steps
    count = sum(rows.shape[0] for rows in blocks)
    heads = 3 * width // HD
    return pl.pallas_call(
        functools.partial(project_kernel, blocks=len(blocks)),
        grid=(steps,),
        in_specs=[pl.BlockSpec(memory_space=pltpu.VMEM)] * len(blocks)
        + [pl.BlockSpec((3, block, width), lambda k: (0, k, 0))],
        out_specs=pl.BlockSpec(memory_space=pltpu.HBM),
        out_shape=jax.ShapeDtypeStruct((heads + SPARE, count, HD), jnp.bfloat16),
        scratch_shapes=[
            pltpu.VMEM((count, 3 * width), jnp.float32),
            pltpu.VMEM((heads, count, HD), jnp.bfloat16),
            pltpu.SemaphoreType.DMA((heads,)),
        ],
        name="project_heads",
        cost_estimate=pl.CostEstimate(
            flops=2 * count * depth * 3 * width,
            bytes_accessed=2 * (count * depth + weights.size),
            transcendentals=0,
        ),
        compiler_params=pltpu.CompilerParams(vmem_limit_bytes=42 * MIB),
    )(*blocks, weights)


def attend_units(visible_ref, queries_ref, pool_ref, out_ref, first_block, before_head):
    heads, fresh_rows, _ = queries_ref.shape
    tiles_seen = visible_ref.shape[1]
    tiles_fresh = visible_ref.shape[0]
    mine_high, mine_low = lax.axis_index("sp") // 2, lax.axis_index("sp") % 2
    mine_branch = lax.axis_index("cfg")
    blocks = out_ref.shape[0] // TILE
    places = []
    for block in range(blocks):
        index = first_block + block
        high, low = mine_high ^ ((index // 2) % 2), mine_low ^ (index // 4)
        tile, branch = high * 2 + low, mine_branch ^ (index % 2)
        seen = []
        for number in range(tiles_seen):
            number = visible_ref[tile, number]
            older = number - tiles_fresh
            fresh = (mine_low ^ (number % 2)) * 4 + (mine_high ^ ((number // 2) % 2)) * 2
            fresh = (fresh + index % 2) * TILE
            stale = fresh_rows + ((older // 2) * 2 + branch) * 2 * TILE + (older % 2) * TILE
            start = jnp.where(number < tiles_fresh, fresh, stale)
            seen.append(pl.ds(pl.multiple_of(start, TILE), TILE))
        places.append(seen)

    def scores_of(head, block):
        rows = pl.ds((first_block + block) * TILE, TILE)
        keys = jnp.concatenate([pool_ref[head, place, :] for place in places[block]], axis=0)
        return lax.dot_general(
            queries_ref[head, rows, :],
            keys,
            (((1,), (1,)), ((), ())),
            preferred_element_type=jnp.float32,
        )

    def finish(head, block, scores):
        values = [pool_ref[heads + head, place, :] for place in places[block]]
        values = jnp.concatenate(values, axis=0)
        exponent = jnp.exp2(scores * (HD ** (-0.5) * LOG2E)).astype(jnp.bfloat16)
        ones = jnp.ones(values.shape, jnp.bfloat16)
        mixed = jnp.dot(
            exponent, jnp.concatenate([values, ones], axis=1), preferred_element_type=jnp.float32
        )
        out_ref[block * TILE : (block + 1) * TILE, head * HD : (head + 1) * HD] = (
            mixed[:, :HD] / mixed[:, HD:]
        ).astype(jnp.bfloat16)

    waiting = []
    for head in range(heads):
        before_head(head)
        for block in range(blocks):
            waiting.append((head, block, scores_of(head, block)))
            if len(waiting) > 2:
                finish(*waiting.pop(0))
    for unit in waiting:
        finish(*unit)


def attend_first_kernel(
    visible_ref, heads_in, context_in, out_ref, queries_ref, pool_ref, sems
):
    heads, fresh_rows, _ = queries_ref.shape
    fresh, stale = pl.ds(0, fresh_rows), pl.ds(fresh_rows, context_in.shape[0])
    copies = []
    for head in range(heads):
        pairs = [(heads_in.at[head], queries_ref.at[head])]
        for kind in range(2):
            place = kind * heads + head
            columns = pl.ds(place * HD, HD)
            pairs.append((heads_in.at[heads + place], pool_ref.at[place, fresh]))
            pairs.append((context_in.at[:, columns], pool_ref.at[place, stale]))
        of_head = [
            pltpu.make_async_copy(source, target, sems.at[head, number])
            for number, (source, target) in enumerate(pairs)
        ]
        for copy in of_head:
            copy.start()
        copies.append(of_head)

    def before_head(head):
        for copy in copies[head]:
            copy.wait()

    first_block = out_ref.shape[0] // TILE
    attend_units(visible_ref, queries_ref, pool_ref, out_ref, first_block, before_head)


def attend_first(heads, context, visible):
    number, rows = (heads.shape[0] - SPARE) // 3, heads.shape[1]
    return pl.pallas_call(
        attend_first_kernel,
        in_specs=[
            pl.BlockSpec(memory_space=pltpu.SMEM),
            pl.BlockSpec(memory_space=pltpu.HBM),
            pl.BlockSpec(memory_space=pl.ANY),
        ],
        out_specs=[pl.BlockSpec(memory_space=pltpu.VMEM)] * 3,
        out_shape=[
            jax.ShapeDtypeStruct((rows // 2, number * HD), jnp.bfloat16),
            jax.ShapeDtypeStruct((number, rows, HD), heads.dtype),
            jax.ShapeDtypeStruct((2 * number, rows + context.shape[0], HD), heads.dtype),
        ],
        scratch_shapes=[pltpu.SemaphoreType.DMA((number, 5))],
        name="attend_first",
        cost_estimate=SHORT,
        compiler_params=pltpu.CompilerParams(vmem_limit_bytes=44 * MIB),
    )(visible, heads, context)


def attend_second_kernel(visible_ref, queries_ref, pool_ref, *refs):
    weights_ref, core_weights_ref = refs[:2]
    out_ref, both_ref, sems = refs[-3:]
    depth, columns = weights_ref.shape[0], pl.ds(0, both_ref.shape[1])
    copies = [
        pltpu.make_async_copy(
            ref.at[:, columns], both_ref.at[pl.ds(core * depth, depth)], sems.at[core]
        )
        for core, ref in enumerate((weights_ref, core_weights_ref))
    ]
    for copy in copies:
        copy.start()
    attend_units(visible_ref, queries_ref, pool_ref, out_ref, 0, lambda head: None)
    for copy in copies:
        copy.wait()


def attend_second(queries, pool, visible, weights, core_weights, columns, earlier):
    number, rows, _ = queries.shape
    return pl.pallas_call(
        attend_second_kernel,
        in_specs=[pl.BlockSpec(memory_space=pltpu.SMEM)]
        + [pl.BlockSpec(memory_space=pltpu.VMEM)] * 2
        + [pl.BlockSpec(memory_space=pl.ANY)] * (2 + len(earlier)),
        out_specs=[pl.BlockSpec(memory_space=pltpu.VMEM)] * 2,
        out_shape=[
            jax.ShapeDtypeStruct((rows // 2, number * HD), jnp.bfloat16),
            jax.ShapeDtypeStruct((2 * weights.shape[0], columns), weights.dtype),
        ],
        scratch_shapes=[pltpu.SemaphoreType.DMA((2,))],
        name="attend_second",
        cost_estimate=SHORT,
        compiler_params=pltpu.CompilerParams(vmem_limit_bytes=12 * MIB),
    )(visible, queries, pool, weights, core_weights, *earlier)


def combined(own, other, mine, gates_ref, columns):
    conditional = lax.axis_index("cfg") == 1
    last = lax.axis_index("pipe") == lax.axis_size("pipe") - 1
    weight = jnp.where(conditional, guidance_scale, 1.0 - guidance_scale).astype(jnp.float32)
    other_weight = jnp.where(conditional, 1.0 - guidance_scale, guidance_scale).astype(jnp.float32)
    own = own * gates_ref[0:1, columns]
    other = other * gates_ref[1:2, columns]
    if mine is not None:
        own = own + mine
    guided = weight * own + other_weight * other
    return jnp.where(last, guided, other), jnp.where(last, guided, own)


def begin(start, refs, across_out, along_out, first_kept, second_kept):
    attended_ref, core_attended_ref, *weights_refs, rows_ref, gates_ref = refs
    tokens, half = rows_ref.shape[0], first_kept.shape[2]
    attended = jnp.concatenate([attended_ref[...], core_attended_ref[...]], axis=1)

    def product_of(columns):
        weights = jnp.concatenate([ref[:, columns] for ref in weights_refs], axis=0)
        return jnp.dot(attended, weights, preferred_element_type=jnp.float32)

    columns = slice(start, start + half)
    product = product_of(slice(0, half))
    for tile in range(2):
        sent_columns = slice(tile * half, (tile + 1) * half)
        own = product[2 * tile * tokens : (2 * tile + 1) * tokens]
        other = product[(2 * tile + 1) * tokens : (2 * tile + 2) * tokens]
        mine = rows_ref[:, columns].astype(jnp.float32) if tile == 0 else None
        sent, kept = combined(own, other, mine, gates_ref, columns)
        across_out[:, sent_columns] = sent.astype(jnp.bfloat16)
        first_kept[tile] = kept
    product = product_of(slice(half, 2 * half))
    for branch in range(2):
        sent_columns = slice(branch * half, (branch + 1) * half)
        second_kept[branch] = product[branch * tokens : (branch + 1) * tokens]
        along_out[:, sent_columns] = product[(branch + 2) * tokens : (branch + 3) * tokens].astype(
            jnp.bfloat16
        )


def stage_kernel(*refs, parts, start, next_start, fresh, middle, final):
    named = dict(zip(parts, refs))
    if fresh:
        begin(
            next_start,
            [
                named[name]
                for name in (
                    "attended", "core_attended", "weights", "core_weights", "both", "rows", "gates"
                )
                if name in named
            ],
            named["across_out"],
            named["along_out"],
            named["first_kept_out"],
            named["second_kept_out"],
        )
    if middle:
        across, along = named["across"], named["along"]
        first_kept, second_kept = named["first_kept"], named["second_kept"]
        half = first_kept.shape[2]
        sent_columns = slice(named["across_out"].shape[1] - half, named["across_out"].shape[1])
        named["along_out"][:, sent_columns] = (
            first_kept[1] + across[:, half : 2 * half].astype(jnp.float32)
        ).astype(jnp.bfloat16)
        named["first_left_out"][...] = first_kept[0] + across[:, :half].astype(jnp.float32)
        columns = slice(start + half, start + 2 * half)
        sent, kept = combined(
            second_kept[0] + along[:, :half].astype(jnp.float32),
            second_kept[1] + along[:, half : 2 * half].astype(jnp.float32),
            named["rows"][:, columns].astype(jnp.float32),
            named["gates"],
            columns,
        )
        named["across_out"][:, sent_columns] = sent.astype(jnp.bfloat16)
        named["second_left_out"][...] = kept
    if final:
        across, along = named["across"], named["along"]
        first_left, second_left = named["first_left"], named["second_left"]
        half = first_left.shape[1]
        columns = slice(across.shape[1] - half, across.shape[1])
        named["done_out"][:, :half] = (
            first_left[...] + along[:, columns].astype(jnp.float32)
        ).astype(jnp.bfloat16)
        named["done_out"][:, half:] = (
            second_left[...] + across[:, columns].astype(jnp.float32)
        ).astype(jnp.bfloat16)


def stage(operands, earlier, chunks, index, fresh, middle, final):
    tokens = operands["rows"].shape[0]
    next_start, next_chunk = chunks[index + 2] if fresh else (0, 0)
    start, chunk = chunks[index] if middle else (0, 0)
    outs = {}
    if fresh or middle:
        columns = next_chunk + chunk // 2
        outs["across_out"] = jax.ShapeDtypeStruct((tokens, columns), jnp.bfloat16)
        outs["along_out"] = outs["across_out"]
    if fresh:
        outs["first_kept_out"] = jax.ShapeDtypeStruct((2, tokens, next_chunk // 2), jnp.float32)
        outs["second_kept_out"] = outs["first_kept_out"]
    if middle:
        outs["first_left_out"] = jax.ShapeDtypeStruct((tokens, chunk // 2), jnp.float32)
        outs["second_left_out"] = outs["first_left_out"]
    if final:
        outs["done_out"] = jax.ShapeDtypeStruct((tokens, chunks[index - 2][1]), jnp.bfloat16)
    parts = list(operands) + ["earlier"] * len(earlier) + list(outs)
    results = pl.pallas_call(
        functools.partial(
            stage_kernel,
            parts=parts,
            start=start,
            next_start=next_start,
            fresh=fresh,
            middle=middle,
            final=final,
        ),
        grid=(1,),
        in_specs=[
            pl.BlockSpec((array.shape[0], next_chunk), lambda step: (0, next_start // next_chunk))
            if name in ("weights", "core_weights")
            else pl.BlockSpec(memory_space=pltpu.VMEM)
            for name, array in operands.items()
        ]
        + [pl.BlockSpec(memory_space=pl.ANY)] * len(earlier),
        out_specs=[pl.BlockSpec(memory_space=pltpu.VMEM)] * len(outs),
        out_shape=list(outs.values()),
        name="sum_stage",
        cost_estimate=SHORT,
        compiler_params=pltpu.CompilerParams(vmem_limit_bytes=16 * MIB),
    )(*operands.values(), *earlier)
    return dict(zip(outs, results))


def per_device(flight, modulation, project_in, project_out, stale_cache, visible):
    current = flight[0, 0]
    modulate = modulation[0, 0]
    token_rows, features = current.shape
    devices = lax.axis_size("sp") * lax.axis_size("cfg")

    context_rows = stale_cache.shape[2]
    width = project_in.shape[3]
    unpacked = stale_cache[0, 0].reshape(context_rows, 2, devices, width)
    packed = unpacked.transpose(2, 0, 1, 3).reshape(devices, context_rows, 2 * width)

    upper, lower = current[: token_rows // 2], current[token_rows // 2 :]
    across_upper, along_lower = from_partner(upper, "cfg", 1), from_partner(lower, "sp", 2)
    across_lower, along_upper = from_partner(lower, "cfg", 1), from_partner(upper, "sp", 2)
    other_modulate = from_partner(modulation, "cfg", 1)[0, 0]
    across_upper, along_lower = after(across_upper, (unpacked,)), after(along_lower, (unpacked,))
    first, second = from_partner(across_upper, "sp", 2), from_partner(along_lower, "cfg", 1)
    core_weights = from_partner(project_out[0], "sp", 1)
    near = [
        modulated_norm([current], modulate),
        modulated_norm([across_upper, across_lower], other_modulate),
        modulated_norm([along_upper, along_lower], modulate),
        modulated_norm([first, second], other_modulate),
    ]
    far = [from_partner(rows, "sp", 1) for rows in near]

    packed = after(packed, (across_lower, along_upper), limit=60)
    context = lax.all_to_all(packed, ("sp", "cfg"), split_axis=0, concat_axis=0, tiled=True)
    context = context.reshape(devices * context_rows, 2 * width)

    heads = project(near + far, project_in[0])
    gates = jnp.concatenate([modulate[2:3], other_modulate[2:3]], axis=0)
    count = len(CHUNK_SHARES)
    unit = features // sum(CHUNK_SHARES)
    chunks = [
        (sum(CHUNK_SHARES[:index]) * unit, share * unit) for index, share in enumerate(CHUNK_SHARES)
    ]
    for_core, queries, pool = attend_first(heads, context, visible[0])
    core_attended = from_partner(for_core, "sp", 1)
    attended, first_weights = attend_second(
        queries, pool, visible[0], project_out[0], core_weights, chunks[0][1], (for_core, gates)
    )

    kept, left, flights, arrivals, earlier = {}, {}, {}, [], []
    for index in range(-2, count + 2):
        fresh, middle, final = index + 2 < count, 0 <= index < count, index >= 2
        operands = {"rows": current, "gates": gates}
        if fresh:
            operands.update(attended=attended, core_attended=core_attended)
            if index == -2:
                operands["both"] = first_weights
            else:
                operands.update(weights=project_out[0], core_weights=core_weights)
        if index >= 0:
            operands["across"], operands["along"] = flights.pop(index)
        if middle:
            operands["first_kept"], operands["second_kept"] = kept.pop(index)
        if final:
            last = {name: operands[name] for name in ("rows", "across", "along")}
            last["first_left"], last["second_left"] = left.pop(index - 2)
            outs = stage(last, earlier, chunks, index, False, False, True)
            arrivals.append(from_behind(outs["done_out"], "pipe", 1))
            earlier = [outs["done_out"]]
        if fresh or middle:
            outs = stage(operands, earlier, chunks, index, fresh, middle, False)
        if "across_out" in outs:
            flights[index + 2] = (
                from_partner(outs["across_out"], "cfg", 1),
                from_partner(outs["along_out"], "sp", 2),
            )
        if fresh:
            kept[index + 2] = (outs["first_kept_out"], outs["second_kept_out"])
        if middle:
            left[index] = (outs["first_left_out"], outs["second_left_out"])
        earlier = [list(outs.values())[-1]] + (arrivals[-2:-1] if 3 <= index < count else [])
    return jnp.concatenate(arrivals, axis=1)[None, None]


def solution(mesh):
    placed = (
        P("pipe", "cfg", "sp", None),
        P("pipe", "cfg", None, None),
        P("pipe", None, None, ("sp", "cfg")),
        P("pipe", ("sp", "cfg"), None),
        P("pipe", "cfg", "sp", None, None),
        P("pipe", None, None),
    )
    return jax.shard_map(
        per_device,
        mesh=mesh,
        in_specs=placed,
        out_specs=P("pipe", "cfg", "sp", None),
        check_vma=False,
    )
```

```python
import functools

import jax
import jax.numpy as jnp
from jax import lax
from jax.experimental import pallas as pl
from jax.experimental.pallas import tpu as pltpu
from jax.sharding import PartitionSpec as P

HD = 128
TILE = 128
MIB = 2**20
SPARE = 39
LOG2E = 1.4426950408889634
CHUNK_SHARES = (5, 5, 2, 3, 3, 2)

guidance_scale = 5.0
SHORT = pl.CostEstimate(flops=1, bytes_accessed=1, transcendentals=0)


def from_behind(x, axis, by):
    count = lax.axis_size(axis)
    return lax.ppermute(x, axis, [(i, (i + by) % count) for i in range(count)])


def from_partner(value, axis, mask):
    pairs = [(source, source ^ mask) for source in range(lax.axis_size(axis))]
    return lax.ppermute(value, axis, pairs)


def norm_kernel(*refs):
    *parts, modulation_ref, out_ref = refs
    step = 16
    start = 0
    for part in parts:

        def body(index, carry, part=part, start=start):
            rows = pl.ds(pl.multiple_of(index * step, step), step)
            out_rows = pl.ds(pl.multiple_of(start + index * step, step), step)
            values = part[rows, :].astype(jnp.float32)
            centre = values - jnp.mean(values, axis=-1, keepdims=True)
            spread = jnp.mean(centre * centre, axis=-1, keepdims=True)
            normed = centre * lax.rsqrt(spread + 1e-06)
            out_ref[out_rows, :] = (
                normed * (1.0 + modulation_ref[1:2, :]) + modulation_ref[0:1, :]
            ).astype(jnp.bfloat16)
            return carry

        lax.fori_loop(0, part.shape[0] // step, body, 0, unroll=2)
        start += part.shape[0]


def modulated_norm(parts, modulation):
    rows, features = sum(part.shape[0] for part in parts), modulation.shape[1]
    return pl.pallas_call(
        norm_kernel,
        in_specs=[pl.BlockSpec(memory_space=pltpu.VMEM)] * (len(parts) + 1),
        out_shape=jax.ShapeDtypeStruct((rows, features), jnp.bfloat16),
        name="modulated_norm",
        cost_estimate=SHORT,
        compiler_params=pltpu.CompilerParams(vmem_limit_bytes=8 * MIB),
    )(*parts, modulation)


def halves_kernel(rows_ref, upper_ref, lower_ref, held, sems):
    half = upper_ref.shape[0]
    places = pl.ds(0, half), pl.ds(half, half)
    copies_in = [
        pltpu.make_async_copy(rows_ref.at[place], held.at[place], sems.at[0, index])
        for index, place in enumerate(places)
    ]
    copies_out = [
        pltpu.make_async_copy(held.at[place], ref, sems.at[1, index])
        for index, (place, ref) in enumerate(zip(places, (upper_ref, lower_ref)))
    ]
    for copy in copies_in:
        copy.start()
    for copy_in, copy_out in zip(copies_in, copies_out):
        copy_in.wait()
        copy_out.start()
    for copy in copies_out:
        copy.wait()


def halves_of(rows):
    count, features = rows.shape
    return pl.pallas_call(
        halves_kernel,
        in_specs=[pl.BlockSpec(memory_space=pl.ANY)],
        out_specs=[pl.BlockSpec(memory_space=pltpu.HBM)] * 2,
        out_shape=[jax.ShapeDtypeStruct((count // 2, features), rows.dtype)] * 2,
        scratch_shapes=[
            pltpu.VMEM((count, features), rows.dtype),
            pltpu.SemaphoreType.DMA((2, 2)),
        ],
        name="halves_of",
        cost_estimate=SHORT,
        compiler_params=pltpu.CompilerParams(vmem_limit_bytes=60 * MIB),
    )(rows)


def gate_kernel(value_ref, *refs):
    pass


def after(value, earlier, limit=1):
    return pl.pallas_call(
        gate_kernel,
        in_specs=[pl.BlockSpec(memory_space=pl.ANY)] * (1 + len(earlier)),
        out_specs=pl.BlockSpec(memory_space=pl.ANY),
        out_shape=jax.ShapeDtypeStruct(value.shape, value.dtype),
        input_output_aliases={0: 0},
        name="after",
        cost_estimate=SHORT,
        compiler_params=pltpu.CompilerParams(vmem_limit_bytes=limit * MIB),
    )(value, *earlier)


def project_kernel(*refs, blocks):
    block_refs, (weights_ref, out_ref, total_ref, heads_ref, sems) = refs[:blocks], refs[blocks:]
    step, steps = pl.program_id(0), pl.num_programs(0)
    weights = jnp.concatenate([weights_ref[0], weights_ref[1], weights_ref[2]], axis=1)
    block = weights.shape[0]
    columns = pl.ds(pl.multiple_of(step * block, block), block)
    rows = jnp.concatenate([ref[:, columns] for ref in block_refs], axis=0)
    product = jnp.dot(rows, weights, preferred_element_type=jnp.float32)

    @pl.when(step == 0)
    def _():
        total_ref[...] = product

    @pl.when((step > 0) & (step < steps - 1))
    def _():
        total_ref[...] += product

    @pl.when(step == steps - 1)
    def _():
        heads = heads_ref.shape[0]
        copies = []
        for head in range(heads):
            columns = slice(head * HD, (head + 1) * HD)
            values = total_ref[:, columns] + product[:, columns]
            if head < 2 * heads // 3:
                square = jnp.mean(values * values, axis=-1, keepdims=True)
                values = values * lax.rsqrt(square + 1e-06)
            heads_ref[head] = values.astype(jnp.bfloat16)
            copies.append(
                pltpu.make_async_copy(heads_ref.at[head], out_ref.at[head], sems.at[head])
            )
            copies[-1].start()
        for copy in copies:
            copy.wait()


def project(blocks, weights):
    _, depth, width = weights.shape
    steps = 2
    block = depth // steps
    count = sum(rows.shape[0] for rows in blocks)
    heads = 3 * width // HD
    return pl.pallas_call(
        functools.partial(project_kernel, blocks=len(blocks)),
        grid=(steps,),
        in_specs=[pl.BlockSpec(memory_space=pltpu.VMEM)] * len(blocks)
        + [pl.BlockSpec((3, block, width), lambda k: (0, k, 0))],
        out_specs=pl.BlockSpec(memory_space=pltpu.HBM),
        out_shape=jax.ShapeDtypeStruct((heads + SPARE, count, HD), jnp.bfloat16),
        scratch_shapes=[
            pltpu.VMEM((count, 3 * width), jnp.float32),
            pltpu.VMEM((heads, count, HD), jnp.bfloat16),
            pltpu.SemaphoreType.DMA((heads,)),
        ],
        name="project_heads",
        cost_estimate=pl.CostEstimate(
            flops=2 * count * depth * 3 * width,
            bytes_accessed=2 * (count * depth + weights.size),
            transcendentals=0,
        ),
        compiler_params=pltpu.CompilerParams(vmem_limit_bytes=42 * MIB),
    )(*blocks, weights)


def attend_units(visible_ref, queries_ref, pool_ref, out_ref, first_block, before_head):
    heads, fresh_rows, _ = queries_ref.shape
    tiles_seen = visible_ref.shape[1]
    tiles_fresh = visible_ref.shape[0]
    mine_high, mine_low = lax.axis_index("sp") // 2, lax.axis_index("sp") % 2
    mine_branch = lax.axis_index("cfg")
    blocks = out_ref.shape[0] // TILE
    places = []
    for block in range(blocks):
        index = first_block + block
        high, low = mine_high ^ ((index // 2) % 2), mine_low ^ (index // 4)
        tile, branch = high * 2 + low, mine_branch ^ (index % 2)
        seen = []
        for number in range(tiles_seen):
            number = visible_ref[tile, number]
            older = number - tiles_fresh
            fresh = (mine_low ^ (number % 2)) * 4 + (mine_high ^ ((number // 2) % 2)) * 2
            fresh = (fresh + index % 2) * TILE
            stale = fresh_rows + ((older // 2) * 2 + branch) * 2 * TILE + (older % 2) * TILE
            start = jnp.where(number < tiles_fresh, fresh, stale)
            seen.append(pl.ds(pl.multiple_of(start, TILE), TILE))
        places.append(seen)

    def scores_of(head, block):
        rows = pl.ds((first_block + block) * TILE, TILE)
        keys = jnp.concatenate([pool_ref[head, place, :] for place in places[block]], axis=0)
        return lax.dot_general(
            queries_ref[head, rows, :],
            keys,
            (((1,), (1,)), ((), ())),
            preferred_element_type=jnp.float32,
        )

    def finish(head, block, scores):
        values = [pool_ref[heads + head, place, :] for place in places[block]]
        values = jnp.concatenate(values, axis=0)
        exponent = jnp.exp2(scores * (HD ** (-0.5) * LOG2E)).astype(jnp.bfloat16)
        ones = jnp.ones(values.shape, jnp.bfloat16)
        mixed = jnp.dot(
            exponent, jnp.concatenate([values, ones], axis=1), preferred_element_type=jnp.float32
        )
        out_ref[block * TILE : (block + 1) * TILE, head * HD : (head + 1) * HD] = (
            mixed[:, :HD] / mixed[:, HD:]
        ).astype(jnp.bfloat16)

    waiting = []
    for head in range(heads):
        before_head(head)
        for block in range(blocks):
            waiting.append((head, block, scores_of(head, block)))
            if len(waiting) > 2:
                finish(*waiting.pop(0))
    for unit in waiting:
        finish(*unit)


def attend_first_kernel(
    visible_ref, heads_in, context_in, out_ref, queries_ref, pool_ref, sems
):
    heads, fresh_rows, _ = queries_ref.shape
    fresh, stale = pl.ds(0, fresh_rows), pl.ds(fresh_rows, context_in.shape[0])
    copies = []
    for head in range(heads):
        pairs = [(heads_in.at[head], queries_ref.at[head])]
        for kind in range(2):
            place = kind * heads + head
            columns = pl.ds(place * HD, HD)
            pairs.append((heads_in.at[heads + place], pool_ref.at[place, fresh]))
            pairs.append((context_in.at[:, columns], pool_ref.at[place, stale]))
        of_head = [
            pltpu.make_async_copy(source, target, sems.at[head, number])
            for number, (source, target) in enumerate(pairs)
        ]
        for copy in of_head:
            copy.start()
        copies.append(of_head)

    def before_head(head):
        for copy in copies[head]:
            copy.wait()

    first_block = out_ref.shape[0] // TILE
    attend_units(visible_ref, queries_ref, pool_ref, out_ref, first_block, before_head)


def attend_first(heads, context, visible):
    number, rows = (heads.shape[0] - SPARE) // 3, heads.shape[1]
    return pl.pallas_call(
        attend_first_kernel,
        in_specs=[
            pl.BlockSpec(memory_space=pltpu.SMEM),
            pl.BlockSpec(memory_space=pltpu.HBM),
            pl.BlockSpec(memory_space=pl.ANY),
        ],
        out_specs=[pl.BlockSpec(memory_space=pltpu.VMEM)] * 3,
        out_shape=[
            jax.ShapeDtypeStruct((rows // 2, number * HD), jnp.bfloat16),
            jax.ShapeDtypeStruct((number, rows, HD), heads.dtype),
            jax.ShapeDtypeStruct((2 * number, rows + context.shape[0], HD), heads.dtype),
        ],
        scratch_shapes=[pltpu.SemaphoreType.DMA((number, 5))],
        name="attend_first",
        cost_estimate=SHORT,
        compiler_params=pltpu.CompilerParams(vmem_limit_bytes=44 * MIB),
    )(visible, heads, context)


def attend_second_kernel(visible_ref, queries_ref, pool_ref, *refs):
    weights_ref, core_weights_ref = refs[:2]
    out_ref, both_ref, sems = refs[-3:]
    depth, columns = weights_ref.shape[0], pl.ds(0, both_ref.shape[1])
    copies = [
        pltpu.make_async_copy(
            ref.at[:, columns], both_ref.at[pl.ds(core * depth, depth)], sems.at[core]
        )
        for core, ref in enumerate((weights_ref, core_weights_ref))
    ]
    for copy in copies:
        copy.start()
    attend_units(visible_ref, queries_ref, pool_ref, out_ref, 0, lambda head: None)
    for copy in copies:
        copy.wait()


def attend_second(queries, pool, visible, weights, core_weights, columns, earlier):
    number, rows, _ = queries.shape
    return pl.pallas_call(
        attend_second_kernel,
        in_specs=[pl.BlockSpec(memory_space=pltpu.SMEM)]
        + [pl.BlockSpec(memory_space=pltpu.VMEM)] * 2
        + [pl.BlockSpec(memory_space=pl.ANY)] * (2 + len(earlier)),
        out_specs=[pl.BlockSpec(memory_space=pltpu.VMEM)] * 2,
        out_shape=[
            jax.ShapeDtypeStruct((rows // 2, number * HD), jnp.bfloat16),
            jax.ShapeDtypeStruct((2 * weights.shape[0], columns), weights.dtype),
        ],
        scratch_shapes=[pltpu.SemaphoreType.DMA((2,))],
        name="attend_second",
        cost_estimate=SHORT,
        compiler_params=pltpu.CompilerParams(vmem_limit_bytes=12 * MIB),
    )(visible, queries, pool, weights, core_weights, *earlier)


def combined(own, other, mine, gates_ref, columns):
    conditional = lax.axis_index("cfg") == 1
    last = lax.axis_index("pipe") == lax.axis_size("pipe") - 1
    weight = jnp.where(conditional, guidance_scale, 1.0 - guidance_scale).astype(jnp.float32)
    other_weight = jnp.where(conditional, 1.0 - guidance_scale, guidance_scale).astype(jnp.float32)
    own = own * gates_ref[0:1, columns]
    other = other * gates_ref[1:2, columns]
    if mine is not None:
        own = own + mine
    guided = weight * own + other_weight * other
    return jnp.where(last, guided, other), jnp.where(last, guided, own)


def begin(start, refs, across_out, along_out, first_kept, second_kept):
    attended_ref, core_attended_ref, *weights_refs, rows_ref, gates_ref = refs
    tokens, half = rows_ref.shape[0], first_kept.shape[2]
    attended = jnp.concatenate([attended_ref[...], core_attended_ref[...]], axis=1)

    def product_of(columns):
        weights = jnp.concatenate([ref[:, columns] for ref in weights_refs], axis=0)
        return jnp.dot(attended, weights, preferred_element_type=jnp.float32)

    columns = slice(start, start + half)
    product = product_of(slice(0, half))
    for tile in range(2):
        sent_columns = slice(tile * half, (tile + 1) * half)
        own = product[2 * tile * tokens : (2 * tile + 1) * tokens]
        other = product[(2 * tile + 1) * tokens : (2 * tile + 2) * tokens]
        mine = rows_ref[:, columns].astype(jnp.float32) if tile == 0 else None
        sent, kept = combined(own, other, mine, gates_ref, columns)
        across_out[:, sent_columns] = sent.astype(jnp.bfloat16)
        first_kept[tile] = kept
    product = product_of(slice(half, 2 * half))
    for branch in range(2):
        sent_columns = slice(branch * half, (branch + 1) * half)
        second_kept[branch] = product[branch * tokens : (branch + 1) * tokens]
        along_out[:, sent_columns] = product[(branch + 2) * tokens : (branch + 3) * tokens].astype(
            jnp.bfloat16
        )


def stage_kernel(*refs, parts, start, next_start, fresh, middle, final):
    named = dict(zip(parts, refs))
    if fresh:
        begin(
            next_start,
            [
                named[name]
                for name in (
                    "attended", "core_attended", "weights", "core_weights", "both", "rows", "gates"
                )
                if name in named
            ],
            named["across_out"],
            named["along_out"],
            named["first_kept_out"],
            named["second_kept_out"],
        )
    if middle:
        across, along = named["across"], named["along"]
        first_kept, second_kept = named["first_kept"], named["second_kept"]
        half = first_kept.shape[2]
        sent_columns = slice(named["across_out"].shape[1] - half, named["across_out"].shape[1])
        named["along_out"][:, sent_columns] = (
            first_kept[1] + across[:, half : 2 * half].astype(jnp.float32)
        ).astype(jnp.bfloat16)
        named["first_left_out"][...] = first_kept[0] + across[:, :half].astype(jnp.float32)
        columns = slice(start + half, start + 2 * half)
        sent, kept = combined(
            second_kept[0] + along[:, :half].astype(jnp.float32),
            second_kept[1] + along[:, half : 2 * half].astype(jnp.float32),
            named["rows"][:, columns].astype(jnp.float32),
            named["gates"],
            columns,
        )
        named["across_out"][:, sent_columns] = sent.astype(jnp.bfloat16)
        named["second_left_out"][...] = kept
    if final:
        across, along = named["across"], named["along"]
        first_left, second_left = named["first_left"], named["second_left"]
        half = first_left.shape[1]
        columns = slice(across.shape[1] - half, across.shape[1])
        named["done_out"][:, :half] = (
            first_left[...] + along[:, columns].astype(jnp.float32)
        ).astype(jnp.bfloat16)
        named["done_out"][:, half:] = (
            second_left[...] + across[:, columns].astype(jnp.float32)
        ).astype(jnp.bfloat16)


def stage(operands, earlier, chunks, index, fresh, middle, final):
    tokens = operands["rows"].shape[0]
    next_start, next_chunk = chunks[index + 2] if fresh else (0, 0)
    start, chunk = chunks[index] if middle else (0, 0)
    outs = {}
    if fresh or middle:
        columns = next_chunk + chunk // 2
        outs["across_out"] = jax.ShapeDtypeStruct((tokens, columns), jnp.bfloat16)
        outs["along_out"] = outs["across_out"]
    if fresh:
        outs["first_kept_out"] = jax.ShapeDtypeStruct((2, tokens, next_chunk // 2), jnp.float32)
        outs["second_kept_out"] = outs["first_kept_out"]
    if middle:
        outs["first_left_out"] = jax.ShapeDtypeStruct((tokens, chunk // 2), jnp.float32)
        outs["second_left_out"] = outs["first_left_out"]
    if final:
        outs["done_out"] = jax.ShapeDtypeStruct((tokens, chunks[index - 2][1]), jnp.bfloat16)
    parts = list(operands) + ["earlier"] * len(earlier) + list(outs)
    results = pl.pallas_call(
        functools.partial(
            stage_kernel,
            parts=parts,
            start=start,
            next_start=next_start,
            fresh=fresh,
            middle=middle,
            final=final,
        ),
        grid=(1,),
        in_specs=[
            pl.BlockSpec((array.shape[0], next_chunk), lambda step: (0, next_start // next_chunk))
            if name in ("weights", "core_weights")
            else pl.BlockSpec(memory_space=pltpu.VMEM)
            for name, array in operands.items()
        ]
        + [pl.BlockSpec(memory_space=pl.ANY)] * len(earlier),
        out_specs=[pl.BlockSpec(memory_space=pltpu.VMEM)] * len(outs),
        out_shape=list(outs.values()),
        name="sum_stage",
        cost_estimate=SHORT,
        compiler_params=pltpu.CompilerParams(vmem_limit_bytes=16 * MIB),
    )(*operands.values(), *earlier)
    return dict(zip(outs, results))


def per_device(flight, modulation, project_in, project_out, stale_cache, visible):
    current = flight[0, 0]
    modulate = modulation[0, 0]
    token_rows, features = current.shape
    devices = lax.axis_size("sp") * lax.axis_size("cfg")

    context_rows = stale_cache.shape[2]
    width = project_in.shape[3]
    unpacked = stale_cache[0, 0].reshape(context_rows, 2, devices, width)
    packed = unpacked.transpose(2, 0, 1, 3).reshape(devices, context_rows, 2 * width)

    upper, lower = halves_of(current)
    across_upper, along_lower = from_partner(upper, "cfg", 1), from_partner(lower, "sp", 2)
    across_lower, along_upper = from_partner(lower, "cfg", 1), from_partner(upper, "sp", 2)
    other_modulate = from_partner(modulation, "cfg", 1)[0, 0]
    across_upper, along_lower = after(across_upper, (unpacked,)), after(along_lower, (unpacked,))
    first, second = from_partner(across_upper, "sp", 2), from_partner(along_lower, "cfg", 1)
    core_weights = from_partner(project_out[0], "sp", 1)
    near = [
        modulated_norm([current], modulate),
        modulated_norm([across_upper, across_lower], other_modulate),
        modulated_norm([along_upper, along_lower], modulate),
        modulated_norm([first, second], other_modulate),
    ]
    far = [from_partner(rows, "sp", 1) for rows in near]

    packed = after(packed, (across_lower, along_upper), limit=60)
    context = lax.all_to_all(packed, ("sp", "cfg"), split_axis=0, concat_axis=0, tiled=True)
    context = context.reshape(devices * context_rows, 2 * width)

    heads = project(near + far, project_in[0])
    gates = jnp.concatenate([modulate[2:3], other_modulate[2:3]], axis=0)
    count = len(CHUNK_SHARES)
    unit = features // sum(CHUNK_SHARES)
    chunks = [
        (sum(CHUNK_SHARES[:index]) * unit, share * unit) for index, share in enumerate(CHUNK_SHARES)
    ]
    for_core, queries, pool = attend_first(heads, context, visible[0])
    core_attended = from_partner(for_core, "sp", 1)
    attended, first_weights = attend_second(
        queries, pool, visible[0], project_out[0], core_weights, chunks[0][1], (for_core, gates)
    )

    kept, left, flights, arrivals, earlier = {}, {}, {}, [], []
    for index in range(-2, count + 2):
        fresh, middle, final = index + 2 < count, 0 <= index < count, index >= 2
        operands = {"rows": current, "gates": gates}
        if fresh:
            operands.update(attended=attended, core_attended=core_attended)
            if index == -2:
                operands["both"] = first_weights
            else:
                operands.update(weights=project_out[0], core_weights=core_weights)
        if index >= 0:
            operands["across"], operands["along"] = flights.pop(index)
        if middle:
            operands["first_kept"], operands["second_kept"] = kept.pop(index)
        if final:
            last = {name: operands[name] for name in ("rows", "across", "along")}
            last["first_left"], last["second_left"] = left.pop(index - 2)
            outs = stage(last, earlier, chunks, index, False, False, True)
            arrivals.append(from_behind(outs["done_out"], "pipe", 1))
            earlier = [outs["done_out"]]
        if fresh or middle:
            outs = stage(operands, earlier, chunks, index, fresh, middle, False)
        if "across_out" in outs:
            flights[index + 2] = (
                from_partner(outs["across_out"], "cfg", 1),
                from_partner(outs["along_out"], "sp", 2),
            )
        if fresh:
            kept[index + 2] = (outs["first_kept_out"], outs["second_kept_out"])
        if middle:
            left[index] = (outs["first_left_out"], outs["second_left_out"])
        earlier = [list(outs.values())[-1]] + (arrivals[-2:-1] if 3 <= index < count else [])
    return jnp.concatenate(arrivals, axis=1)[None, None]


def solution(mesh):
    placed = (
        P("pipe", "cfg", "sp", None),
        P("pipe", "cfg", None, None),
        P("pipe", None, None, ("sp", "cfg")),
        P("pipe", ("sp", "cfg"), None),
        P("pipe", "cfg", "sp", None, None),
        P("pipe", None, None),
    )
    return jax.shard_map(
        per_device,
        mesh=mesh,
        in_specs=placed,
        out_specs=P("pipe", "cfg", "sp", None),
        check_vma=False,
    )
```

```python
import functools

import jax
import jax.numpy as jnp
from jax import lax
from jax.experimental import pallas as pl
from jax.experimental.pallas import tpu as pltpu
from jax.sharding import PartitionSpec as P

HD = 128
TILE = 128
MIB = 2**20
SPARE = 39
LOG2E = 1.4426950408889634
CHUNKS = ((8, 4), (15, 5), (0, 3), (3, 3), (12, 3), (6, 2))

guidance_scale = 5.0
SHORT = pl.CostEstimate(flops=1, bytes_accessed=1, transcendentals=0)


def from_behind(x, axis, by):
    count = lax.axis_size(axis)
    return lax.ppermute(x, axis, [(i, (i + by) % count) for i in range(count)])


def from_partner(value, axis, mask):
    pairs = [(source, source ^ mask) for source in range(lax.axis_size(axis))]
    return lax.ppermute(value, axis, pairs)


def norm_kernel(*refs):
    *parts, modulation_ref, out_ref = refs
    step = 16
    start = 0
    for part in parts:

        def body(index, carry, part=part, start=start):
            rows = pl.ds(pl.multiple_of(index * step, step), step)
            out_rows = pl.ds(pl.multiple_of(start + index * step, step), step)
            values = part[rows, :].astype(jnp.float32)
            centre = values - jnp.mean(values, axis=-1, keepdims=True)
            spread = jnp.mean(centre * centre, axis=-1, keepdims=True)
            normed = centre * lax.rsqrt(spread + 1e-06)
            out_ref[out_rows, :] = (
                normed * (1.0 + modulation_ref[1:2, :]) + modulation_ref[0:1, :]
            ).astype(jnp.bfloat16)
            return carry

        lax.fori_loop(0, part.shape[0] // step, body, 0, unroll=2)
        start += part.shape[0]


def modulated_norm(parts, modulation):
    rows, features = sum(part.shape[0] for part in parts), modulation.shape[1]
    return pl.pallas_call(
        norm_kernel,
        in_specs=[pl.BlockSpec(memory_space=pltpu.VMEM)] * (len(parts) + 1),
        out_shape=jax.ShapeDtypeStruct((rows, features), jnp.bfloat16),
        name="modulated_norm",
        cost_estimate=SHORT,
        compiler_params=pltpu.CompilerParams(vmem_limit_bytes=8 * MIB),
    )(*parts, modulation)


def halves_kernel(rows_ref, upper_ref, lower_ref, held, sems):
    half = upper_ref.shape[0]
    places = pl.ds(0, half), pl.ds(half, half)
    copies_in = [
        pltpu.make_async_copy(rows_ref.at[place], held.at[place], sems.at[0, index])
        for index, place in enumerate(places)
    ]
    copies_out = [
        pltpu.make_async_copy(held.at[place], ref, sems.at[1, index])
        for index, (place, ref) in enumerate(zip(places, (upper_ref, lower_ref)))
    ]
    for copy in copies_in:
        copy.start()
    for copy_in, copy_out in zip(copies_in, copies_out):
        copy_in.wait()
        copy_out.start()
    for copy in copies_out:
        copy.wait()


def halves_of(rows):
    count, features = rows.shape
    return pl.pallas_call(
        halves_kernel,
        in_specs=[pl.BlockSpec(memory_space=pl.ANY)],
        out_specs=[pl.BlockSpec(memory_space=pltpu.HBM)] * 2,
        out_shape=[jax.ShapeDtypeStruct((count // 2, features), rows.dtype)] * 2,
        scratch_shapes=[
            pltpu.VMEM((count, features), rows.dtype),
            pltpu.SemaphoreType.DMA((2, 2)),
        ],
        name="halves_of",
        cost_estimate=SHORT,
        compiler_params=pltpu.CompilerParams(vmem_limit_bytes=60 * MIB),
    )(rows)


def gate_kernel(value_ref, *refs):
    pass


def after(value, earlier, limit=1):
    return pl.pallas_call(
        gate_kernel,
        in_specs=[pl.BlockSpec(memory_space=pl.ANY)] * (1 + len(earlier)),
        out_specs=pl.BlockSpec(memory_space=pl.ANY),
        out_shape=jax.ShapeDtypeStruct(value.shape, value.dtype),
        input_output_aliases={0: 0},
        name="after",
        cost_estimate=SHORT,
        compiler_params=pltpu.CompilerParams(vmem_limit_bytes=limit * MIB),
    )(value, *earlier)


def project_kernel(*refs, blocks):
    block_refs, (weights_ref, out_ref, total_ref, heads_ref, sems) = refs[:blocks], refs[blocks:]
    step, steps = pl.program_id(0), pl.num_programs(0)
    weights = jnp.concatenate([weights_ref[0], weights_ref[1], weights_ref[2]], axis=1)
    block = weights.shape[0]
    columns = pl.ds(pl.multiple_of(step * block, block), block)
    rows = jnp.concatenate([ref[:, columns] for ref in block_refs], axis=0)
    product = jnp.dot(rows, weights, preferred_element_type=jnp.float32)

    @pl.when(step == 0)
    def _():
        total_ref[...] = product

    @pl.when((step > 0) & (step < steps - 1))
    def _():
        total_ref[...] += product

    @pl.when(step == steps - 1)
    def _():
        heads = heads_ref.shape[0]
        copies = []
        for head in range(heads):
            columns = slice(head * HD, (head + 1) * HD)
            values = total_ref[:, columns] + product[:, columns]
            if head < 2 * heads // 3:
                square = jnp.mean(values * values, axis=-1, keepdims=True)
                values = values * lax.rsqrt(square + 1e-06)
            heads_ref[head] = values.astype(jnp.bfloat16)
            copies.append(
                pltpu.make_async_copy(heads_ref.at[head], out_ref.at[head], sems.at[head])
            )
            copies[-1].start()
        for copy in copies:
            copy.wait()


def project(blocks, weights):
    _, depth, width = weights.shape
    steps = 2
    block = depth // steps
    count = sum(rows.shape[0] for rows in blocks)
    heads = 3 * width // HD
    return pl.pallas_call(
        functools.partial(project_kernel, blocks=len(blocks)),
        grid=(steps,),
        in_specs=[pl.BlockSpec(memory_space=pltpu.VMEM)] * len(blocks)
        + [pl.BlockSpec((3, block, width), lambda k: (0, k, 0))],
        out_specs=pl.BlockSpec(memory_space=pltpu.HBM),
        out_shape=jax.ShapeDtypeStruct((heads + SPARE, count, HD), jnp.bfloat16),
        scratch_shapes=[
            pltpu.VMEM((count, 3 * width), jnp.float32),
            pltpu.VMEM((heads, count, HD), jnp.bfloat16),
            pltpu.SemaphoreType.DMA((heads,)),
        ],
        name="project_heads",
        cost_estimate=pl.CostEstimate(
            flops=2 * count * depth * 3 * width,
            bytes_accessed=2 * (count * depth + weights.size),
            transcendentals=0,
        ),
        compiler_params=pltpu.CompilerParams(vmem_limit_bytes=42 * MIB),
    )(*blocks, weights)


def attend_units(visible_ref, queries_ref, pool_ref, out_ref, first_block, before_head):
    heads, fresh_rows, _ = queries_ref.shape
    tiles_seen = visible_ref.shape[1]
    tiles_fresh = visible_ref.shape[0]
    mine_high, mine_low = lax.axis_index("sp") // 2, lax.axis_index("sp") % 2
    mine_branch = lax.axis_index("cfg")
    blocks = out_ref.shape[0] // TILE
    places = []
    for block in range(blocks):
        index = first_block + block
        high, low = mine_high ^ ((index // 2) % 2), mine_low ^ (index // 4)
        tile, branch = high * 2 + low, mine_branch ^ (index % 2)
        seen = []
        for number in range(tiles_seen):
            number = visible_ref[tile, number]
            older = number - tiles_fresh
            fresh = (mine_low ^ (number % 2)) * 4 + (mine_high ^ ((number // 2) % 2)) * 2
            fresh = (fresh + index % 2) * TILE
            stale = fresh_rows + ((older // 2) * 2 + branch) * 2 * TILE + (older % 2) * TILE
            start = jnp.where(number < tiles_fresh, fresh, stale)
            seen.append(pl.ds(pl.multiple_of(start, TILE), TILE))
        places.append(seen)

    def scores_of(head, block):
        rows = pl.ds((first_block + block) * TILE, TILE)
        keys = jnp.concatenate([pool_ref[head, place, :] for place in places[block]], axis=0)
        return lax.dot_general(
            queries_ref[head, rows, :],
            keys,
            (((1,), (1,)), ((), ())),
            preferred_element_type=jnp.float32,
        )

    def finish(head, block, scores):
        values = [pool_ref[heads + head, place, :] for place in places[block]]
        values = jnp.concatenate(values, axis=0)
        exponent = jnp.exp2(scores * (HD ** (-0.5) * LOG2E)).astype(jnp.bfloat16)
        ones = jnp.ones(values.shape, jnp.bfloat16)
        mixed = jnp.dot(
            exponent, jnp.concatenate([values, ones], axis=1), preferred_element_type=jnp.float32
        )
        out_ref[block * TILE : (block + 1) * TILE, head * HD : (head + 1) * HD] = (
            mixed[:, :HD] / mixed[:, HD:]
        ).astype(jnp.bfloat16)

    waiting = []
    for head in range(heads):
        before_head(head)
        for block in range(blocks):
            waiting.append((head, block, scores_of(head, block)))
            if len(waiting) > 2:
                finish(*waiting.pop(0))
    for unit in waiting:
        finish(*unit)


def attend_first_kernel(
    visible_ref, heads_in, context_in, out_ref, queries_ref, pool_ref, sems
):
    heads, fresh_rows, _ = queries_ref.shape
    fresh, stale = pl.ds(0, fresh_rows), pl.ds(fresh_rows, context_in.shape[0])
    copies = []
    for head in range(heads):
        pairs = [(heads_in.at[head], queries_ref.at[head])]
        for kind in range(2):
            place = kind * heads + head
            columns = pl.ds(place * HD, HD)
            pairs.append((heads_in.at[heads + place], pool_ref.at[place, fresh]))
            pairs.append((context_in.at[:, columns], pool_ref.at[place, stale]))
        of_head = [
            pltpu.make_async_copy(source, target, sems.at[head, number])
            for number, (source, target) in enumerate(pairs)
        ]
        for copy in of_head:
            copy.start()
        copies.append(of_head)

    def before_head(head):
        for copy in copies[head]:
            copy.wait()

    first_block = out_ref.shape[0] // TILE
    attend_units(visible_ref, queries_ref, pool_ref, out_ref, first_block, before_head)


def attend_first(heads, context, visible):
    number, rows = (heads.shape[0] - SPARE) // 3, heads.shape[1]
    return pl.pallas_call(
        attend_first_kernel,
        in_specs=[
            pl.BlockSpec(memory_space=pltpu.SMEM),
            pl.BlockSpec(memory_space=pltpu.HBM),
            pl.BlockSpec(memory_space=pl.ANY),
        ],
        out_specs=[pl.BlockSpec(memory_space=pltpu.VMEM)] * 3,
        out_shape=[
            jax.ShapeDtypeStruct((rows // 2, number * HD), jnp.bfloat16),
            jax.ShapeDtypeStruct((number, rows, HD), heads.dtype),
            jax.ShapeDtypeStruct((2 * number, rows + context.shape[0], HD), heads.dtype),
        ],
        scratch_shapes=[pltpu.SemaphoreType.DMA((number, 5))],
        name="attend_first",
        cost_estimate=SHORT,
        compiler_params=pltpu.CompilerParams(vmem_limit_bytes=44 * MIB),
    )(visible, heads, context)


def attend_second_kernel(visible_ref, queries_ref, pool_ref, *refs, start):
    weights_ref, core_weights_ref = refs[:2]
    out_ref, both_ref, sems = refs[-3:]
    depth, columns = weights_ref.shape[0], pl.ds(start, both_ref.shape[1])
    copies = [
        pltpu.make_async_copy(
            ref.at[:, columns], both_ref.at[pl.ds(core * depth, depth)], sems.at[core]
        )
        for core, ref in enumerate((weights_ref, core_weights_ref))
    ]
    for copy in copies:
        copy.start()
    attend_units(visible_ref, queries_ref, pool_ref, out_ref, 0, lambda head: None)
    for copy in copies:
        copy.wait()


def attend_second(queries, pool, visible, weights, core_weights, chunk, earlier):
    number, rows, _ = queries.shape
    return pl.pallas_call(
        functools.partial(attend_second_kernel, start=chunk[0]),
        in_specs=[pl.BlockSpec(memory_space=pltpu.SMEM)]
        + [pl.BlockSpec(memory_space=pltpu.VMEM)] * 2
        + [pl.BlockSpec(memory_space=pl.ANY)] * (2 + len(earlier)),
        out_specs=[pl.BlockSpec(memory_space=pltpu.VMEM)] * 2,
        out_shape=[
            jax.ShapeDtypeStruct((rows // 2, number * HD), jnp.bfloat16),
            jax.ShapeDtypeStruct((2 * weights.shape[0], chunk[1]), weights.dtype),
        ],
        scratch_shapes=[pltpu.SemaphoreType.DMA((2,))],
        name="attend_second",
        cost_estimate=SHORT,
        compiler_params=pltpu.CompilerParams(vmem_limit_bytes=12 * MIB),
    )(visible, queries, pool, weights, core_weights, *earlier)


def combined(own, other, mine, gates_ref, columns):
    conditional = lax.axis_index("cfg") == 1
    last = lax.axis_index("pipe") == lax.axis_size("pipe") - 1
    weight = jnp.where(conditional, guidance_scale, 1.0 - guidance_scale).astype(jnp.float32)
    other_weight = jnp.where(conditional, 1.0 - guidance_scale, guidance_scale).astype(jnp.float32)
    own = own * gates_ref[0:1, columns]
    other = other * gates_ref[1:2, columns]
    if mine is not None:
        own = own + mine
    guided = weight * own + other_weight * other
    return jnp.where(last, guided, other), jnp.where(last, guided, own)


def begin(start, refs, across_out, along_out, first_kept, second_kept):
    attended_ref, core_attended_ref, *weights_refs, rows_ref, gates_ref = refs
    tokens, half = rows_ref.shape[0], first_kept.shape[2]
    attended = jnp.concatenate([attended_ref[...], core_attended_ref[...]], axis=1)

    def product_of(columns):
        weights = jnp.concatenate([ref[:, columns] for ref in weights_refs], axis=0)
        return jnp.dot(attended, weights, preferred_element_type=jnp.float32)

    columns = slice(start, start + half)
    product = product_of(slice(0, half))
    for tile in range(2):
        sent_columns = slice(tile * half, (tile + 1) * half)
        own = product[2 * tile * tokens : (2 * tile + 1) * tokens]
        other = product[(2 * tile + 1) * tokens : (2 * tile + 2) * tokens]
        mine = rows_ref[:, columns].astype(jnp.float32) if tile == 0 else None
        sent, kept = combined(own, other, mine, gates_ref, columns)
        across_out[:, sent_columns] = sent.astype(jnp.bfloat16)
        first_kept[tile] = kept
    product = product_of(slice(half, 2 * half))
    for branch in range(2):
        sent_columns = slice(branch * half, (branch + 1) * half)
        second_kept[branch] = product[branch * tokens : (branch + 1) * tokens]
        along_out[:, sent_columns] = product[(branch + 2) * tokens : (branch + 3) * tokens].astype(
            jnp.bfloat16
        )


def stage_kernel(*refs, parts, start, next_start, fresh, middle, final):
    named = dict(zip(parts, refs))
    if fresh:
        begin(
            next_start,
            [
                named[name]
                for name in (
                    "attended", "core_attended", "weights", "core_weights", "both", "rows", "gates"
                )
                if name in named
            ],
            named["across_out"],
            named["along_out"],
            named["first_kept_out"],
            named["second_kept_out"],
        )
    if middle:
        across, along = named["across"], named["along"]
        first_kept, second_kept = named["first_kept"], named["second_kept"]
        half = first_kept.shape[2]
        sent_columns = slice(named["across_out"].shape[1] - half, named["across_out"].shape[1])
        named["along_out"][:, sent_columns] = (
            first_kept[1] + across[:, half : 2 * half].astype(jnp.float32)
        ).astype(jnp.bfloat16)
        named["first_left_out"][...] = first_kept[0] + across[:, :half].astype(jnp.float32)
        columns = slice(start + half, start + 2 * half)
        sent, kept = combined(
            second_kept[0] + along[:, :half].astype(jnp.float32),
            second_kept[1] + along[:, half : 2 * half].astype(jnp.float32),
            named["rows"][:, columns].astype(jnp.float32),
            named["gates"],
            columns,
        )
        named["across_out"][:, sent_columns] = sent.astype(jnp.bfloat16)
        named["second_left_out"][...] = kept
    if final:
        across, along = named["across"], named["along"]
        first_left, second_left = named["first_left"], named["second_left"]
        half = first_left.shape[1]
        columns = slice(across.shape[1] - half, across.shape[1])
        named["done_out"][:, :half] = (
            first_left[...] + along[:, columns].astype(jnp.float32)
        ).astype(jnp.bfloat16)
        named["done_out"][:, half:] = (
            second_left[...] + across[:, columns].astype(jnp.float32)
        ).astype(jnp.bfloat16)


def stage(operands, earlier, chunks, index, fresh, middle, final):
    tokens = operands["rows"].shape[0]
    next_start, next_chunk = chunks[index + 2] if fresh else (0, 0)
    start, chunk = chunks[index] if middle else (0, 0)
    outs = {}
    if fresh or middle:
        columns = next_chunk + chunk // 2
        outs["across_out"] = jax.ShapeDtypeStruct((tokens, columns), jnp.bfloat16)
        outs["along_out"] = outs["across_out"]
    if fresh:
        outs["first_kept_out"] = jax.ShapeDtypeStruct((2, tokens, next_chunk // 2), jnp.float32)
        outs["second_kept_out"] = outs["first_kept_out"]
    if middle:
        outs["first_left_out"] = jax.ShapeDtypeStruct((tokens, chunk // 2), jnp.float32)
        outs["second_left_out"] = outs["first_left_out"]
    if final:
        outs["done_out"] = jax.ShapeDtypeStruct((tokens, chunks[index - 2][1]), jnp.bfloat16)
    parts = list(operands) + ["earlier"] * len(earlier) + list(outs)
    results = pl.pallas_call(
        functools.partial(
            stage_kernel,
            parts=parts,
            start=start,
            next_start=next_start,
            fresh=fresh,
            middle=middle,
            final=final,
        ),
        grid=(1,),
        in_specs=[
            pl.BlockSpec((array.shape[0], next_chunk), lambda step: (0, next_start // next_chunk))
            if name in ("weights", "core_weights")
            else pl.BlockSpec(memory_space=pltpu.VMEM)
            for name, array in operands.items()
        ]
        + [pl.BlockSpec(memory_space=pl.ANY)] * len(earlier),
        out_specs=[pl.BlockSpec(memory_space=pltpu.VMEM)] * len(outs),
        out_shape=list(outs.values()),
        name="sum_stage",
        cost_estimate=SHORT,
        compiler_params=pltpu.CompilerParams(vmem_limit_bytes=16 * MIB),
    )(*operands.values(), *earlier)
    return dict(zip(outs, results))


def per_device(flight, modulation, project_in, project_out, stale_cache, visible):
    current = flight[0, 0]
    modulate = modulation[0, 0]
    token_rows, features = current.shape
    devices = lax.axis_size("sp") * lax.axis_size("cfg")

    context_rows = stale_cache.shape[2]
    width = project_in.shape[3]
    unpacked = stale_cache[0, 0].reshape(context_rows, 2, devices, width)
    packed = unpacked.transpose(2, 0, 1, 3).reshape(devices, context_rows, 2 * width)

    upper, lower = halves_of(current)
    across_upper, along_lower = from_partner(upper, "cfg", 1), from_partner(lower, "sp", 2)
    across_lower, along_upper = from_partner(lower, "cfg", 1), from_partner(upper, "sp", 2)
    other_modulate = from_partner(modulation, "cfg", 1)[0, 0]
    across_upper, along_lower = after(across_upper, (unpacked,)), after(along_lower, (unpacked,))
    first, second = from_partner(across_upper, "sp", 2), from_partner(along_lower, "cfg", 1)
    core_weights = from_partner(project_out[0], "sp", 1)
    near = [
        modulated_norm([current], modulate),
        modulated_norm([across_upper, across_lower], other_modulate),
        modulated_norm([along_upper, along_lower], modulate),
        modulated_norm([first, second], other_modulate),
    ]
    far = [from_partner(rows, "sp", 1) for rows in near]

    packed = after(packed, (across_lower, along_upper), limit=60)
    context = lax.all_to_all(packed, ("sp", "cfg"), split_axis=0, concat_axis=0, tiled=True)
    context = context.reshape(devices * context_rows, 2 * width)

    heads = project(near + far, project_in[0])
    gates = jnp.concatenate([modulate[2:3], other_modulate[2:3]], axis=0)
    count = len(CHUNKS)
    unit = features // 20
    chunks = [(start * unit, width * unit) for start, width in CHUNKS]
    for_core, queries, pool = attend_first(heads, context, visible[0])
    core_attended = from_partner(for_core, "sp", 1)
    attended, first_weights = attend_second(
        queries, pool, visible[0], project_out[0], core_weights, chunks[0], (for_core, gates)
    )

    kept, left, flights, arrivals, earlier = {}, {}, {}, [], []
    for index in range(-2, count + 2):
        fresh, middle, final = index + 2 < count, 0 <= index < count, index >= 2
        operands = {"rows": current, "gates": gates}
        if fresh:
            operands.update(attended=attended, core_attended=core_attended)
            if index == -2:
                operands["both"] = first_weights
            else:
                operands.update(weights=project_out[0], core_weights=core_weights)
        if index >= 0:
            operands["across"], operands["along"] = flights.pop(index)
        if middle:
            operands["first_kept"], operands["second_kept"] = kept.pop(index)
        if final:
            last = {name: operands[name] for name in ("rows", "across", "along")}
            last["first_left"], last["second_left"] = left.pop(index - 2)
            outs = stage(last, earlier, chunks, index, False, False, True)
            arrivals.append(from_behind(outs["done_out"], "pipe", 1))
            earlier = [outs["done_out"]]
        if fresh or middle:
            outs = stage(operands, earlier, chunks, index, fresh, middle, False)
        if "across_out" in outs:
            flights[index + 2] = (
                from_partner(outs["across_out"], "cfg", 1),
                from_partner(outs["along_out"], "sp", 2),
            )
        if fresh:
            kept[index + 2] = (outs["first_kept_out"], outs["second_kept_out"])
        if middle:
            left[index] = (outs["first_left_out"], outs["second_left_out"])
        earlier = [list(outs.values())[-1]] + (arrivals[-2:-1] if 3 <= index < count else [])
    in_order = sorted(range(count), key=lambda index: chunks[index][0])
    return jnp.concatenate([arrivals[index] for index in in_order], axis=1)[None, None]


def solution(mesh):
    placed = (
        P("pipe", "cfg", "sp", None),
        P("pipe", "cfg", None, None),
        P("pipe", None, None, ("sp", "cfg")),
        P("pipe", ("sp", "cfg"), None),
        P("pipe", "cfg", "sp", None, None),
        P("pipe", None, None),
    )
    return jax.shard_map(
        per_device,
        mesh=mesh,
        in_specs=placed,
        out_specs=P("pipe", "cfg", "sp", None),
        check_vma=False,
    )
```

```python
import functools

import jax
import jax.numpy as jnp
from jax import lax
from jax.experimental import pallas as pl
from jax.experimental.pallas import tpu as pltpu
from jax.sharding import PartitionSpec as P

HD = 128
TILE = 128
MIB = 2**20
SPARE = 39
LOG2E = 1.4426950408889634
CHUNKS = ((8, 4), (15, 5), (0, 3), (3, 3), (12, 3), (6, 2))

guidance_scale = 5.0
SHORT = pl.CostEstimate(flops=1, bytes_accessed=1, transcendentals=0)


def from_behind(x, axis, by):
    count = lax.axis_size(axis)
    return lax.ppermute(x, axis, [(i, (i + by) % count) for i in range(count)])


def from_partner(value, axis, mask):
    pairs = [(source, source ^ mask) for source in range(lax.axis_size(axis))]
    return lax.ppermute(value, axis, pairs)


def norm_kernel(*refs):
    *parts, modulation_ref, out_ref = refs
    step = 16
    start = 0
    for part in parts:

        def body(index, carry, part=part, start=start):
            rows = pl.ds(pl.multiple_of(index * step, step), step)
            out_rows = pl.ds(pl.multiple_of(start + index * step, step), step)
            values = part[rows, :].astype(jnp.float32)
            centre = values - jnp.mean(values, axis=-1, keepdims=True)
            spread = jnp.mean(centre * centre, axis=-1, keepdims=True)
            normed = centre * lax.rsqrt(spread + 1e-06)
            out_ref[out_rows, :] = (
                normed * (1.0 + modulation_ref[1:2, :]) + modulation_ref[0:1, :]
            ).astype(jnp.bfloat16)
            return carry

        lax.fori_loop(0, part.shape[0] // step, body, 0, unroll=2)
        start += part.shape[0]


def modulated_norm(parts, modulation):
    rows, features = sum(part.shape[0] for part in parts), modulation.shape[1]
    return pl.pallas_call(
        norm_kernel,
        in_specs=[pl.BlockSpec(memory_space=pltpu.VMEM)] * (len(parts) + 1),
        out_shape=jax.ShapeDtypeStruct((rows, features), jnp.bfloat16),
        name="modulated_norm",
        cost_estimate=SHORT,
        compiler_params=pltpu.CompilerParams(vmem_limit_bytes=8 * MIB),
    )(*parts, modulation)


def halves_kernel(rows_ref, upper_ref, lower_ref, held, sems):
    half = upper_ref.shape[0]
    places = pl.ds(0, half), pl.ds(half, half)
    copies_in = [
        pltpu.make_async_copy(rows_ref.at[place], held.at[place], sems.at[0, index])
        for index, place in enumerate(places)
    ]
    copies_out = [
        pltpu.make_async_copy(held.at[place], ref, sems.at[1, index])
        for index, (place, ref) in enumerate(zip(places, (upper_ref, lower_ref)))
    ]
    for copy in copies_in:
        copy.start()
    for copy_in, copy_out in zip(copies_in, copies_out):
        copy_in.wait()
        copy_out.start()
    for copy in copies_out:
        copy.wait()


def halves_of(rows):
    count, features = rows.shape
    return pl.pallas_call(
        halves_kernel,
        in_specs=[pl.BlockSpec(memory_space=pl.ANY)],
        out_specs=[pl.BlockSpec(memory_space=pltpu.HBM)] * 2,
        out_shape=[jax.ShapeDtypeStruct((count // 2, features), rows.dtype)] * 2,
        scratch_shapes=[
            pltpu.VMEM((count, features), rows.dtype),
            pltpu.SemaphoreType.DMA((2, 2)),
        ],
        name="halves_of",
        cost_estimate=SHORT,
        compiler_params=pltpu.CompilerParams(vmem_limit_bytes=60 * MIB),
    )(rows)


def gate_kernel(value_ref, *refs):
    pass


def after(value, earlier, limit=1):
    return pl.pallas_call(
        gate_kernel,
        in_specs=[pl.BlockSpec(memory_space=pl.ANY)] * (1 + len(earlier)),
        out_specs=pl.BlockSpec(memory_space=pl.ANY),
        out_shape=jax.ShapeDtypeStruct(value.shape, value.dtype),
        input_output_aliases={0: 0},
        name="after",
        cost_estimate=SHORT,
        compiler_params=pltpu.CompilerParams(vmem_limit_bytes=limit * MIB),
    )(value, *earlier)


def project_kernel(*refs, blocks):
    block_refs, (weights_ref, out_ref, total_ref, heads_ref, sems) = refs[:blocks], refs[blocks:]
    step, steps = pl.program_id(0), pl.num_programs(0)
    weights = jnp.concatenate([weights_ref[0], weights_ref[1], weights_ref[2]], axis=1)
    block = weights.shape[0]
    columns = pl.ds(pl.multiple_of(step * block, block), block)
    rows = jnp.concatenate([ref[:, columns] for ref in block_refs], axis=0)
    product = jnp.dot(rows, weights, preferred_element_type=jnp.float32)

    @pl.when(step == 0)
    def _():
        total_ref[...] = product

    @pl.when((step > 0) & (step < steps - 1))
    def _():
        total_ref[...] += product

    @pl.when(step == steps - 1)
    def _():
        heads = heads_ref.shape[0]
        copies = []
        for head in range(heads):
            columns = slice(head * HD, (head + 1) * HD)
            values = total_ref[:, columns] + product[:, columns]
            if head < 2 * heads // 3:
                square = jnp.mean(values * values, axis=-1, keepdims=True)
                values = values * lax.rsqrt(square + 1e-06)
            heads_ref[head] = values.astype(jnp.bfloat16)
            copies.append(
                pltpu.make_async_copy(heads_ref.at[head], out_ref.at[head], sems.at[head])
            )
            copies[-1].start()
        for copy in copies:
            copy.wait()


def project(blocks, weights):
    _, depth, width = weights.shape
    steps = 2
    block = depth // steps
    count = sum(rows.shape[0] for rows in blocks)
    heads = 3 * width // HD
    return pl.pallas_call(
        functools.partial(project_kernel, blocks=len(blocks)),
        grid=(steps,),
        in_specs=[pl.BlockSpec(memory_space=pltpu.VMEM)] * len(blocks)
        + [pl.BlockSpec((3, block, width), lambda k: (0, k, 0))],
        out_specs=pl.BlockSpec(memory_space=pltpu.HBM),
        out_shape=jax.ShapeDtypeStruct((heads + SPARE, count, HD), jnp.bfloat16),
        scratch_shapes=[
            pltpu.VMEM((count, 3 * width), jnp.float32),
            pltpu.VMEM((heads, count, HD), jnp.bfloat16),
            pltpu.SemaphoreType.DMA((heads,)),
        ],
        name="project_heads",
        cost_estimate=pl.CostEstimate(
            flops=2 * count * depth * 3 * width,
            bytes_accessed=2 * (count * depth + weights.size),
            transcendentals=0,
        ),
        compiler_params=pltpu.CompilerParams(vmem_limit_bytes=42 * MIB),
    )(*blocks, weights)


def attend_units(visible_ref, queries_ref, pool_ref, out_ref, first_block, before):
    heads, fresh_rows, _ = queries_ref.shape
    tiles_seen = visible_ref.shape[1]
    tiles_fresh = visible_ref.shape[0]
    mine_high, mine_low = lax.axis_index("sp") // 2, lax.axis_index("sp") % 2
    mine_branch = lax.axis_index("cfg")
    blocks = out_ref.shape[0] // TILE
    places = []
    for block in range(blocks):
        index = first_block + block
        high, low = mine_high ^ ((index // 2) % 2), mine_low ^ (index // 4)
        tile, branch = high * 2 + low, mine_branch ^ (index % 2)
        seen = []
        for number in range(tiles_seen):
            number = visible_ref[tile, number]
            older = number - tiles_fresh
            fresh = (mine_low ^ (number % 2)) * 4 + (mine_high ^ ((number // 2) % 2)) * 2
            fresh = (fresh + index % 2) * TILE
            stale = fresh_rows + ((older // 2) * 2 + branch) * 2 * TILE + (older % 2) * TILE
            start = jnp.where(number < tiles_fresh, fresh, stale)
            seen.append(pl.ds(pl.multiple_of(start, TILE), TILE))
        places.append(seen)

    def scores_of(head, block):
        rows = pl.ds((first_block + block) * TILE, TILE)
        keys = jnp.concatenate([pool_ref[head, place, :] for place in places[block]], axis=0)
        return lax.dot_general(
            queries_ref[head, rows, :],
            keys,
            (((1,), (1,)), ((), ())),
            preferred_element_type=jnp.float32,
        )

    def finish(head, block, scores):
        if block == 0:
            before(head, "values")
        values = [pool_ref[heads + head, place, :] for place in places[block]]
        values = jnp.concatenate(values, axis=0)
        exponent = jnp.exp2(scores * (HD ** (-0.5) * LOG2E)).astype(jnp.bfloat16)
        ones = jnp.ones(values.shape, jnp.bfloat16)
        mixed = jnp.dot(
            exponent, jnp.concatenate([values, ones], axis=1), preferred_element_type=jnp.float32
        )
        out_ref[block * TILE : (block + 1) * TILE, head * HD : (head + 1) * HD] = (
            mixed[:, :HD] / mixed[:, HD:]
        ).astype(jnp.bfloat16)

    waiting = []
    for head in range(heads):
        before(head, "scores")
        for block in range(blocks):
            waiting.append((head, block, scores_of(head, block)))
            if len(waiting) > 2:
                finish(*waiting.pop(0))
    for unit in waiting:
        finish(*unit)


def attend_first_kernel(
    visible_ref, heads_in, context_in, out_ref, queries_ref, pool_ref, sems
):
    heads, fresh_rows, _ = queries_ref.shape
    fresh, stale = pl.ds(0, fresh_rows), pl.ds(fresh_rows, context_in.shape[0])
    copies = []
    for head in range(heads):
        pairs = [(heads_in.at[head], queries_ref.at[head])]
        for kind in range(2):
            place = kind * heads + head
            columns = pl.ds(place * HD, HD)
            pairs.append((heads_in.at[heads + place], pool_ref.at[place, fresh]))
            pairs.append((context_in.at[:, columns], pool_ref.at[place, stale]))
        of_head = [
            pltpu.make_async_copy(source, target, sems.at[head, number])
            for number, (source, target) in enumerate(pairs)
        ]
        for copy in of_head:
            copy.start()
        copies.append(of_head)

    def before(head, step):
        for copy in copies[head][:3] if step == "scores" else copies[head][3:]:
            copy.wait()

    first_block = out_ref.shape[0] // TILE
    attend_units(visible_ref, queries_ref, pool_ref, out_ref, first_block, before)


def attend_first(heads, context, visible):
    number, rows = (heads.shape[0] - SPARE) // 3, heads.shape[1]
    return pl.pallas_call(
        attend_first_kernel,
        in_specs=[
            pl.BlockSpec(memory_space=pltpu.SMEM),
            pl.BlockSpec(memory_space=pltpu.HBM),
            pl.BlockSpec(memory_space=pl.ANY),
        ],
        out_specs=[pl.BlockSpec(memory_space=pltpu.VMEM)] * 3,
        out_shape=[
            jax.ShapeDtypeStruct((rows // 2, number * HD), jnp.bfloat16),
            jax.ShapeDtypeStruct((number, rows, HD), heads.dtype),
            jax.ShapeDtypeStruct((2 * number, rows + context.shape[0], HD), heads.dtype),
        ],
        scratch_shapes=[pltpu.SemaphoreType.DMA((number, 5))],
        name="attend_first",
        cost_estimate=SHORT,
        compiler_params=pltpu.CompilerParams(vmem_limit_bytes=44 * MIB),
    )(visible, heads, context)


def attend_second_kernel(visible_ref, queries_ref, pool_ref, *refs, start):
    weights_ref, core_weights_ref = refs[:2]
    out_ref, both_ref, sems = refs[-3:]
    depth, columns = weights_ref.shape[0], pl.ds(start, both_ref.shape[1])
    copies = [
        pltpu.make_async_copy(
            ref.at[:, columns], both_ref.at[pl.ds(core * depth, depth)], sems.at[core]
        )
        for core, ref in enumerate((weights_ref, core_weights_ref))
    ]
    for copy in copies:
        copy.start()
    attend_units(visible_ref, queries_ref, pool_ref, out_ref, 0, lambda head, step: None)
    for copy in copies:
        copy.wait()


def attend_second(queries, pool, visible, weights, core_weights, chunk, earlier):
    number, rows, _ = queries.shape
    return pl.pallas_call(
        functools.partial(attend_second_kernel, start=chunk[0]),
        in_specs=[pl.BlockSpec(memory_space=pltpu.SMEM)]
        + [pl.BlockSpec(memory_space=pltpu.VMEM)] * 2
        + [pl.BlockSpec(memory_space=pl.ANY)] * (2 + len(earlier)),
        out_specs=[pl.BlockSpec(memory_space=pltpu.VMEM)] * 2,
        out_shape=[
            jax.ShapeDtypeStruct((rows // 2, number * HD), jnp.bfloat16),
            jax.ShapeDtypeStruct((2 * weights.shape[0], chunk[1]), weights.dtype),
        ],
        scratch_shapes=[pltpu.SemaphoreType.DMA((2,))],
        name="attend_second",
        cost_estimate=SHORT,
        compiler_params=pltpu.CompilerParams(vmem_limit_bytes=12 * MIB),
    )(visible, queries, pool, weights, core_weights, *earlier)


def combined(own, other, mine, gates_ref, columns):
    conditional = lax.axis_index("cfg") == 1
    last = lax.axis_index("pipe") == lax.axis_size("pipe") - 1
    weight = jnp.where(conditional, guidance_scale, 1.0 - guidance_scale).astype(jnp.float32)
    other_weight = jnp.where(conditional, 1.0 - guidance_scale, guidance_scale).astype(jnp.float32)
    own = own * gates_ref[0:1, columns]
    other = other * gates_ref[1:2, columns]
    if mine is not None:
        own = own + mine
    guided = weight * own + other_weight * other
    return jnp.where(last, guided, other), jnp.where(last, guided, own)


def begin(start, refs, across_out, along_out, first_kept, second_kept):
    attended_ref, core_attended_ref, *weights_refs, rows_ref, gates_ref = refs
    tokens, half = rows_ref.shape[0], first_kept.shape[2]
    attended = jnp.concatenate([attended_ref[...], core_attended_ref[...]], axis=1)

    def product_of(columns):
        weights = jnp.concatenate([ref[:, columns] for ref in weights_refs], axis=0)
        return jnp.dot(attended, weights, preferred_element_type=jnp.float32)

    columns = slice(start, start + half)
    product = product_of(slice(0, half))
    for tile in range(2):
        sent_columns = slice(tile * half, (tile + 1) * half)
        own = product[2 * tile * tokens : (2 * tile + 1) * tokens]
        other = product[(2 * tile + 1) * tokens : (2 * tile + 2) * tokens]
        mine = rows_ref[:, columns].astype(jnp.float32) if tile == 0 else None
        sent, kept = combined(own, other, mine, gates_ref, columns)
        across_out[:, sent_columns] = sent.astype(jnp.bfloat16)
        first_kept[tile] = kept
    product = product_of(slice(half, 2 * half))
    for branch in range(2):
        sent_columns = slice(branch * half, (branch + 1) * half)
        second_kept[branch] = product[branch * tokens : (branch + 1) * tokens]
        along_out[:, sent_columns] = product[(branch + 2) * tokens : (branch + 3) * tokens].astype(
            jnp.bfloat16
        )


def stage_kernel(*refs, parts, start, next_start, fresh, middle, final):
    named = dict(zip(parts, refs))
    if fresh:
        begin(
            next_start,
            [
                named[name]
                for name in (
                    "attended", "core_attended", "weights", "core_weights", "both", "rows", "gates"
                )
                if name in named
            ],
            named["across_out"],
            named["along_out"],
            named["first_kept_out"],
            named["second_kept_out"],
        )
    if middle:
        across, along = named["across"], named["along"]
        first_kept, second_kept = named["first_kept"], named["second_kept"]
        half = first_kept.shape[2]
        sent_columns = slice(named["across_out"].shape[1] - half, named["across_out"].shape[1])
        named["along_out"][:, sent_columns] = (
            first_kept[1] + across[:, half : 2 * half].astype(jnp.float32)
        ).astype(jnp.bfloat16)
        named["first_left_out"][...] = first_kept[0] + across[:, :half].astype(jnp.float32)
        columns = slice(start + half, start + 2 * half)
        sent, kept = combined(
            second_kept[0] + along[:, :half].astype(jnp.float32),
            second_kept[1] + along[:, half : 2 * half].astype(jnp.float32),
            named["rows"][:, columns].astype(jnp.float32),
            named["gates"],
            columns,
        )
        named["across_out"][:, sent_columns] = sent.astype(jnp.bfloat16)
        named["second_left_out"][...] = kept
    if final:
        across, along = named["across"], named["along"]
        first_left, second_left = named["first_left"], named["second_left"]
        half = first_left.shape[1]
        columns = slice(across.shape[1] - half, across.shape[1])
        named["done_out"][:, :half] = (
            first_left[...] + along[:, columns].astype(jnp.float32)
        ).astype(jnp.bfloat16)
        named["done_out"][:, half:] = (
            second_left[...] + across[:, columns].astype(jnp.float32)
        ).astype(jnp.bfloat16)


def stage(operands, earlier, chunks, index, fresh, middle, final):
    tokens = operands["rows"].shape[0]
    next_start, next_chunk = chunks[index + 2] if fresh else (0, 0)
    start, chunk = chunks[index] if middle else (0, 0)
    outs = {}
    if fresh or middle:
        columns = next_chunk + chunk // 2
        outs["across_out"] = jax.ShapeDtypeStruct((tokens, columns), jnp.bfloat16)
        outs["along_out"] = outs["across_out"]
    if fresh:
        outs["first_kept_out"] = jax.ShapeDtypeStruct((2, tokens, next_chunk // 2), jnp.float32)
        outs["second_kept_out"] = outs["first_kept_out"]
    if middle:
        outs["first_left_out"] = jax.ShapeDtypeStruct((tokens, chunk // 2), jnp.float32)
        outs["second_left_out"] = outs["first_left_out"]
    if final:
        outs["done_out"] = jax.ShapeDtypeStruct((tokens, chunks[index - 2][1]), jnp.bfloat16)
    parts = list(operands) + ["earlier"] * len(earlier) + list(outs)
    results = pl.pallas_call(
        functools.partial(
            stage_kernel,
            parts=parts,
            start=start,
            next_start=next_start,
            fresh=fresh,
            middle=middle,
            final=final,
        ),
        grid=(1,),
        in_specs=[
            pl.BlockSpec((array.shape[0], next_chunk), lambda step: (0, next_start // next_chunk))
            if name in ("weights", "core_weights")
            else pl.BlockSpec(memory_space=pltpu.VMEM)
            for name, array in operands.items()
        ]
        + [pl.BlockSpec(memory_space=pl.ANY)] * len(earlier),
        out_specs=[pl.BlockSpec(memory_space=pltpu.VMEM)] * len(outs),
        out_shape=list(outs.values()),
        name="sum_stage",
        cost_estimate=SHORT,
        compiler_params=pltpu.CompilerParams(vmem_limit_bytes=16 * MIB),
    )(*operands.values(), *earlier)
    return dict(zip(outs, results))


def per_device(flight, modulation, project_in, project_out, stale_cache, visible):
    current = flight[0, 0]
    modulate = modulation[0, 0]
    token_rows, features = current.shape
    devices = lax.axis_size("sp") * lax.axis_size("cfg")

    context_rows = stale_cache.shape[2]
    width = project_in.shape[3]
    unpacked = stale_cache[0, 0].reshape(context_rows, 2, devices, width)
    packed = unpacked.transpose(2, 0, 1, 3).reshape(devices, context_rows, 2 * width)

    upper, lower = halves_of(current)
    across_upper, along_lower = from_partner(upper, "cfg", 1), from_partner(lower, "sp", 2)
    across_lower, along_upper = from_partner(lower, "cfg", 1), from_partner(upper, "sp", 2)
    other_modulate = from_partner(modulation, "cfg", 1)[0, 0]
    across_upper, along_lower = after(across_upper, (unpacked,)), after(along_lower, (unpacked,))
    first, second = from_partner(across_upper, "sp", 2), from_partner(along_lower, "cfg", 1)
    core_weights = from_partner(project_out[0], "sp", 1)
    near = [
        modulated_norm([current], modulate),
        modulated_norm([across_upper, across_lower], other_modulate),
        modulated_norm([along_upper, along_lower], modulate),
        modulated_norm([first, second], other_modulate),
    ]
    far = [from_partner(rows, "sp", 1) for rows in near]

    packed = after(packed, (across_lower, along_upper), limit=60)
    context = lax.all_to_all(packed, ("sp", "cfg"), split_axis=0, concat_axis=0, tiled=True)
    context = context.reshape(devices * context_rows, 2 * width)

    heads = project(near + far, project_in[0])
    gates = jnp.concatenate([modulate[2:3], other_modulate[2:3]], axis=0)
    count = len(CHUNKS)
    unit = features // 20
    chunks = [(start * unit, width * unit) for start, width in CHUNKS]
    for_core, queries, pool = attend_first(heads, context, visible[0])
    core_attended = from_partner(for_core, "sp", 1)
    attended, first_weights = attend_second(
        queries, pool, visible[0], project_out[0], core_weights, chunks[0], (for_core, gates)
    )

    kept, left, flights, arrivals, earlier = {}, {}, {}, [], []
    for index in range(-2, count + 2):
        fresh, middle, final = index + 2 < count, 0 <= index < count, index >= 2
        operands = {"rows": current, "gates": gates}
        if fresh:
            operands.update(attended=attended, core_attended=core_attended)
            if index == -2:
                operands["both"] = first_weights
            else:
                operands.update(weights=project_out[0], core_weights=core_weights)
        if index >= 0:
            operands["across"], operands["along"] = flights.pop(index)
        if middle:
            operands["first_kept"], operands["second_kept"] = kept.pop(index)
        if final:
            last = {name: operands[name] for name in ("rows", "across", "along")}
            last["first_left"], last["second_left"] = left.pop(index - 2)
            outs = stage(last, earlier, chunks, index, False, False, True)
            arrivals.append(from_behind(outs["done_out"], "pipe", 1))
            earlier = [outs["done_out"]]
        if fresh or middle:
            outs = stage(operands, earlier, chunks, index, fresh, middle, False)
        if "across_out" in outs:
            flights[index + 2] = (
                from_partner(outs["across_out"], "cfg", 1),
                from_partner(outs["along_out"], "sp", 2),
            )
        if fresh:
            kept[index + 2] = (outs["first_kept_out"], outs["second_kept_out"])
        if middle:
            left[index] = (outs["first_left_out"], outs["second_left_out"])
        earlier = [list(outs.values())[-1]] + (arrivals[-2:-1] if 3 <= index < count else [])
    in_order = sorted(range(count), key=lambda index: chunks[index][0])
    return jnp.concatenate([arrivals[index] for index in in_order], axis=1)[None, None]


def solution(mesh):
    placed = (
        P("pipe", "cfg", "sp", None),
        P("pipe", "cfg", None, None),
        P("pipe", None, None, ("sp", "cfg")),
        P("pipe", ("sp", "cfg"), None),
        P("pipe", "cfg", "sp", None, None),
        P("pipe", None, None),
    )
    return jax.shard_map(
        per_device,
        mesh=mesh,
        in_specs=placed,
        out_specs=P("pipe", "cfg", "sp", None),
        check_vma=False,
    )
```

```python
import functools

import jax
import jax.numpy as jnp
from jax import lax
from jax.experimental import pallas as pl
from jax.experimental.pallas import tpu as pltpu
from jax.sharding import PartitionSpec as P

HD = 128
TILE = 128
MIB = 2**20
SPARE = 39
LOG2E = 1.4426950408889634
CHUNKS = ((8, 4), (15, 5), (0, 3), (3, 3), (12, 3), (6, 2))

guidance_scale = 5.0
SHORT = pl.CostEstimate(flops=1, bytes_accessed=1, transcendentals=0)


def from_behind(x, axis, by):
    count = lax.axis_size(axis)
    return lax.ppermute(x, axis, [(i, (i + by) % count) for i in range(count)])


def from_partner(value, axis, mask):
    pairs = [(source, source ^ mask) for source in range(lax.axis_size(axis))]
    return lax.ppermute(value, axis, pairs)


def norm_kernel(*refs):
    *parts, modulation_ref, out_ref = refs
    step = 16
    start = 0
    for part in parts:

        def body(index, carry, part=part, start=start):
            rows = pl.ds(pl.multiple_of(index * step, step), step)
            out_rows = pl.ds(pl.multiple_of(start + index * step, step), step)
            values = part[rows, :].astype(jnp.float32)
            centre = values - jnp.mean(values, axis=-1, keepdims=True)
            spread = jnp.mean(centre * centre, axis=-1, keepdims=True)
            normed = centre * lax.rsqrt(spread + 1e-06)
            out_ref[out_rows, :] = (
                normed * (1.0 + modulation_ref[1:2, :]) + modulation_ref[0:1, :]
            ).astype(jnp.bfloat16)
            return carry

        lax.fori_loop(0, part.shape[0] // step, body, 0, unroll=2)
        start += part.shape[0]


def modulated_norm(parts, modulation):
    rows, features = sum(part.shape[0] for part in parts), modulation.shape[1]
    return pl.pallas_call(
        norm_kernel,
        in_specs=[pl.BlockSpec(memory_space=pltpu.VMEM)] * (len(parts) + 1),
        out_shape=jax.ShapeDtypeStruct((rows, features), jnp.bfloat16),
        name="modulated_norm",
        cost_estimate=SHORT,
        compiler_params=pltpu.CompilerParams(vmem_limit_bytes=8 * MIB),
    )(*parts, modulation)


def halves_kernel(rows_ref, upper_ref, lower_ref, held, sems):
    half, pieces = upper_ref.shape[0], sems.shape[1]
    size = rows_ref.shape[0] // pieces
    copies_in, copies_out = [], []
    for piece in range(pieces):
        start = piece * size
        place = held.at[pl.ds(start, size)]
        target = (upper_ref, lower_ref)[start // half].at[pl.ds(start % half, size)]
        copies_in.append(
            pltpu.make_async_copy(rows_ref.at[pl.ds(start, size)], place, sems.at[0, piece])
        )
        copies_out.append(pltpu.make_async_copy(place, target, sems.at[1, piece]))
    for copy in copies_in:
        copy.start()
    for copy_in, copy_out in zip(copies_in, copies_out):
        copy_in.wait()
        copy_out.start()
    for copy in copies_out:
        copy.wait()


def halves_of(rows):
    count, features = rows.shape
    return pl.pallas_call(
        halves_kernel,
        in_specs=[pl.BlockSpec(memory_space=pl.ANY)],
        out_specs=[pl.BlockSpec(memory_space=pltpu.HBM)] * 2,
        out_shape=[jax.ShapeDtypeStruct((count // 2, features), rows.dtype)] * 2,
        scratch_shapes=[
            pltpu.VMEM((count, features), rows.dtype),
            pltpu.SemaphoreType.DMA((2, 4)),
        ],
        name="halves_of",
        cost_estimate=SHORT,
        compiler_params=pltpu.CompilerParams(vmem_limit_bytes=60 * MIB),
    )(rows)


def gate_kernel(value_ref, *refs):
    pass


def after(value, earlier, limit=1):
    return pl.pallas_call(
        gate_kernel,
        in_specs=[pl.BlockSpec(memory_space=pl.ANY)] * (1 + len(earlier)),
        out_specs=pl.BlockSpec(memory_space=pl.ANY),
        out_shape=jax.ShapeDtypeStruct(value.shape, value.dtype),
        input_output_aliases={0: 0},
        name="after",
        cost_estimate=SHORT,
        compiler_params=pltpu.CompilerParams(vmem_limit_bytes=limit * MIB),
    )(value, *earlier)


def project_kernel(*refs, blocks):
    block_refs, (weights_ref, out_ref, total_ref, heads_ref, sems) = refs[:blocks], refs[blocks:]
    step, steps = pl.program_id(0), pl.num_programs(0)
    weights = jnp.concatenate([weights_ref[0], weights_ref[1], weights_ref[2]], axis=1)
    block = weights.shape[0]
    columns = pl.ds(pl.multiple_of(step * block, block), block)
    rows = jnp.concatenate([ref[:, columns] for ref in block_refs], axis=0)
    product = jnp.dot(rows, weights, preferred_element_type=jnp.float32)

    @pl.when(step == 0)
    def _():
        total_ref[...] = product

    @pl.when((step > 0) & (step < steps - 1))
    def _():
        total_ref[...] += product

    @pl.when(step == steps - 1)
    def _():
        heads = heads_ref.shape[0]
        copies = []
        for head in range(heads):
            columns = slice(head * HD, (head + 1) * HD)
            values = total_ref[:, columns] + product[:, columns]
            if head < 2 * heads // 3:
                square = jnp.mean(values * values, axis=-1, keepdims=True)
                values = values * lax.rsqrt(square + 1e-06)
            heads_ref[head] = values.astype(jnp.bfloat16)
            copies.append(
                pltpu.make_async_copy(heads_ref.at[head], out_ref.at[head], sems.at[head])
            )
            copies[-1].start()
        for copy in copies:
            copy.wait()


def project(blocks, weights):
    _, depth, width = weights.shape
    steps = 2
    block = depth // steps
    count = sum(rows.shape[0] for rows in blocks)
    heads = 3 * width // HD
    return pl.pallas_call(
        functools.partial(project_kernel, blocks=len(blocks)),
        grid=(steps,),
        in_specs=[pl.BlockSpec(memory_space=pltpu.VMEM)] * len(blocks)
        + [pl.BlockSpec((3, block, width), lambda k: (0, k, 0))],
        out_specs=pl.BlockSpec(memory_space=pltpu.HBM),
        out_shape=jax.ShapeDtypeStruct((heads + SPARE, count, HD), jnp.bfloat16),
        scratch_shapes=[
            pltpu.VMEM((count, 3 * width), jnp.float32),
            pltpu.VMEM((heads, count, HD), jnp.bfloat16),
            pltpu.SemaphoreType.DMA((heads,)),
        ],
        name="project_heads",
        cost_estimate=pl.CostEstimate(
            flops=2 * count * depth * 3 * width,
            bytes_accessed=2 * (count * depth + weights.size),
            transcendentals=0,
        ),
        compiler_params=pltpu.CompilerParams(vmem_limit_bytes=42 * MIB),
    )(*blocks, weights)


def attend_units(visible_ref, queries_ref, pool_ref, out_ref, first_block, before_head):
    heads, fresh_rows, _ = queries_ref.shape
    tiles_seen = visible_ref.shape[1]
    tiles_fresh = visible_ref.shape[0]
    mine_high, mine_low = lax.axis_index("sp") // 2, lax.axis_index("sp") % 2
    mine_branch = lax.axis_index("cfg")
    blocks = out_ref.shape[0] // TILE
    places = []
    for block in range(blocks):
        index = first_block + block
        high, low = mine_high ^ ((index // 2) % 2), mine_low ^ (index // 4)
        tile, branch = high * 2 + low, mine_branch ^ (index % 2)
        seen = []
        for number in range(tiles_seen):
            number = visible_ref[tile, number]
            older = number - tiles_fresh
            fresh = (mine_low ^ (number % 2)) * 4 + (mine_high ^ ((number // 2) % 2)) * 2
            fresh = (fresh + index % 2) * TILE
            stale = fresh_rows + ((older // 2) * 2 + branch) * 2 * TILE + (older % 2) * TILE
            start = jnp.where(number < tiles_fresh, fresh, stale)
            seen.append(pl.ds(pl.multiple_of(start, TILE), TILE))
        places.append(seen)

    def scores_of(head, block):
        rows = pl.ds((first_block + block) * TILE, TILE)
        keys = jnp.concatenate([pool_ref[head, place, :] for place in places[block]], axis=0)
        return lax.dot_general(
            queries_ref[head, rows, :],
            keys,
            (((1,), (1,)), ((), ())),
            preferred_element_type=jnp.float32,
        )

    def finish(head, block, scores):
        values = [pool_ref[heads + head, place, :] for place in places[block]]
        values = jnp.concatenate(values, axis=0)
        exponent = jnp.exp2(scores * (HD ** (-0.5) * LOG2E)).astype(jnp.bfloat16)
        ones = jnp.ones(values.shape, jnp.bfloat16)
        mixed = jnp.dot(
            exponent, jnp.concatenate([values, ones], axis=1), preferred_element_type=jnp.float32
        )
        out_ref[block * TILE : (block + 1) * TILE, head * HD : (head + 1) * HD] = (
            mixed[:, :HD] / mixed[:, HD:]
        ).astype(jnp.bfloat16)

    waiting = []
    for head in range(heads):
        before_head(head)
        for block in range(blocks):
            waiting.append((head, block, scores_of(head, block)))
            if len(waiting) > 3:
                finish(*waiting.pop(0))
    for unit in waiting:
        finish(*unit)


def attend_first_kernel(
    visible_ref, heads_in, context_in, out_ref, queries_ref, pool_ref, sems
):
    heads, fresh_rows, _ = queries_ref.shape
    fresh, stale = pl.ds(0, fresh_rows), pl.ds(fresh_rows, context_in.shape[0])
    copies = []
    for head in range(heads):
        pairs = [(heads_in.at[head], queries_ref.at[head])]
        for kind in range(2):
            place = kind * heads + head
            columns = pl.ds(place * HD, HD)
            pairs.append((heads_in.at[heads + place], pool_ref.at[place, fresh]))
            pairs.append((context_in.at[:, columns], pool_ref.at[place, stale]))
        of_head = [
            pltpu.make_async_copy(source, target, sems.at[head, number])
            for number, (source, target) in enumerate(pairs)
        ]
        for copy in of_head:
            copy.start()
        copies.append(of_head)

    def before_head(head):
        for copy in copies[head]:
            copy.wait()

    first_block = out_ref.shape[0] // TILE
    attend_units(visible_ref, queries_ref, pool_ref, out_ref, first_block, before_head)


def attend_first(heads, context, visible):
    number, rows = (heads.shape[0] - SPARE) // 3, heads.shape[1]
    return pl.pallas_call(
        attend_first_kernel,
        in_specs=[
            pl.BlockSpec(memory_space=pltpu.SMEM),
            pl.BlockSpec(memory_space=pltpu.HBM),
            pl.BlockSpec(memory_space=pl.ANY),
        ],
        out_specs=[pl.BlockSpec(memory_space=pltpu.VMEM)] * 3,
        out_shape=[
            jax.ShapeDtypeStruct((rows // 2, number * HD), jnp.bfloat16),
            jax.ShapeDtypeStruct((number, rows, HD), heads.dtype),
            jax.ShapeDtypeStruct((2 * number, rows + context.shape[0], HD), heads.dtype),
        ],
        scratch_shapes=[pltpu.SemaphoreType.DMA((number, 5))],
        name="attend_first",
        cost_estimate=SHORT,
        compiler_params=pltpu.CompilerParams(vmem_limit_bytes=44 * MIB),
    )(visible, heads, context)


def attend_second_kernel(visible_ref, queries_ref, pool_ref, *refs, start):
    weights_ref, core_weights_ref = refs[:2]
    out_ref, both_ref, sems = refs[-3:]
    depth, columns = weights_ref.shape[0], pl.ds(start, both_ref.shape[1])
    copies = [
        pltpu.make_async_copy(
            ref.at[:, columns], both_ref.at[pl.ds(core * depth, depth)], sems.at[core]
        )
        for core, ref in enumerate((weights_ref, core_weights_ref))
    ]
    for copy in copies:
        copy.start()
    attend_units(visible_ref, queries_ref, pool_ref, out_ref, 0, lambda head: None)
    for copy in copies:
        copy.wait()


def attend_second(queries, pool, visible, weights, core_weights, chunk, earlier):
    number, rows, _ = queries.shape
    return pl.pallas_call(
        functools.partial(attend_second_kernel, start=chunk[0]),
        in_specs=[pl.BlockSpec(memory_space=pltpu.SMEM)]
        + [pl.BlockSpec(memory_space=pltpu.VMEM)] * 2
        + [pl.BlockSpec(memory_space=pl.ANY)] * (2 + len(earlier)),
        out_specs=[pl.BlockSpec(memory_space=pltpu.VMEM)] * 2,
        out_shape=[
            jax.ShapeDtypeStruct((rows // 2, number * HD), jnp.bfloat16),
            jax.ShapeDtypeStruct((2 * weights.shape[0], chunk[1]), weights.dtype),
        ],
        scratch_shapes=[pltpu.SemaphoreType.DMA((2,))],
        name="attend_second",
        cost_estimate=SHORT,
        compiler_params=pltpu.CompilerParams(vmem_limit_bytes=12 * MIB),
    )(visible, queries, pool, weights, core_weights, *earlier)


def combined(own, other, mine, gates_ref, columns):
    conditional = lax.axis_index("cfg") == 1
    last = lax.axis_index("pipe") == lax.axis_size("pipe") - 1
    weight = jnp.where(conditional, guidance_scale, 1.0 - guidance_scale).astype(jnp.float32)
    other_weight = jnp.where(conditional, 1.0 - guidance_scale, guidance_scale).astype(jnp.float32)
    own = own * gates_ref[0:1, columns]
    other = other * gates_ref[1:2, columns]
    if mine is not None:
        own = own + mine
    guided = weight * own + other_weight * other
    return jnp.where(last, guided, other), jnp.where(last, guided, own)


def begin(start, refs, across_out, along_out, first_kept, second_kept):
    attended_ref, core_attended_ref, *weights_refs, rows_ref, gates_ref = refs
    tokens, half = rows_ref.shape[0], first_kept.shape[2]
    attended = jnp.concatenate([attended_ref[...], core_attended_ref[...]], axis=1)

    def product_of(columns):
        weights = jnp.concatenate([ref[:, columns] for ref in weights_refs], axis=0)
        return jnp.dot(attended, weights, preferred_element_type=jnp.float32)

    columns = slice(start, start + half)
    product = product_of(slice(0, half))
    for tile in range(2):
        sent_columns = slice(tile * half, (tile + 1) * half)
        own = product[2 * tile * tokens : (2 * tile + 1) * tokens]
        other = product[(2 * tile + 1) * tokens : (2 * tile + 2) * tokens]
        mine = rows_ref[:, columns].astype(jnp.float32) if tile == 0 else None
        sent, kept = combined(own, other, mine, gates_ref, columns)
        across_out[:, sent_columns] = sent.astype(jnp.bfloat16)
        first_kept[tile] = kept
    product = product_of(slice(half, 2 * half))
    for branch in range(2):
        sent_columns = slice(branch * half, (branch + 1) * half)
        second_kept[branch] = product[branch * tokens : (branch + 1) * tokens]
        along_out[:, sent_columns] = product[(branch + 2) * tokens : (branch + 3) * tokens].astype(
            jnp.bfloat16
        )


def stage_kernel(*refs, parts, start, next_start, fresh, middle, final):
    named = dict(zip(parts, refs))
    if fresh:
        begin(
            next_start,
            [
                named[name]
                for name in (
                    "attended", "core_attended", "weights", "core_weights", "both", "rows", "gates"
                )
                if name in named
            ],
            named["across_out"],
            named["along_out"],
            named["first_kept_out"],
            named["second_kept_out"],
        )
    if middle:
        across, along = named["across"], named["along"]
        first_kept, second_kept = named["first_kept"], named["second_kept"]
        half = first_kept.shape[2]
        sent_columns = slice(named["across_out"].shape[1] - half, named["across_out"].shape[1])
        named["along_out"][:, sent_columns] = (
            first_kept[1] + across[:, half : 2 * half].astype(jnp.float32)
        ).astype(jnp.bfloat16)
        named["first_left_out"][...] = first_kept[0] + across[:, :half].astype(jnp.float32)
        columns = slice(start + half, start + 2 * half)
        sent, kept = combined(
            second_kept[0] + along[:, :half].astype(jnp.float32),
            second_kept[1] + along[:, half : 2 * half].astype(jnp.float32),
            named["rows"][:, columns].astype(jnp.float32),
            named["gates"],
            columns,
        )
        named["across_out"][:, sent_columns] = sent.astype(jnp.bfloat16)
        named["second_left_out"][...] = kept
    if final:
        across, along = named["across"], named["along"]
        first_left, second_left = named["first_left"], named["second_left"]
        half = first_left.shape[1]
        columns = slice(across.shape[1] - half, across.shape[1])
        named["done_out"][:, :half] = (
            first_left[...] + along[:, columns].astype(jnp.float32)
        ).astype(jnp.bfloat16)
        named["done_out"][:, half:] = (
            second_left[...] + across[:, columns].astype(jnp.float32)
        ).astype(jnp.bfloat16)


def stage(operands, earlier, chunks, index, fresh, middle, final):
    tokens = operands["rows"].shape[0]
    next_start, next_chunk = chunks[index + 2] if fresh else (0, 0)
    start, chunk = chunks[index] if middle else (0, 0)
    outs = {}
    if fresh or middle:
        columns = next_chunk + chunk // 2
        outs["across_out"] = jax.ShapeDtypeStruct((tokens, columns), jnp.bfloat16)
        outs["along_out"] = outs["across_out"]
    if fresh:
        outs["first_kept_out"] = jax.ShapeDtypeStruct((2, tokens, next_chunk // 2), jnp.float32)
        outs["second_kept_out"] = outs["first_kept_out"]
    if middle:
        outs["first_left_out"] = jax.ShapeDtypeStruct((tokens, chunk // 2), jnp.float32)
        outs["second_left_out"] = outs["first_left_out"]
    if final:
        outs["done_out"] = jax.ShapeDtypeStruct((tokens, chunks[index - 2][1]), jnp.bfloat16)
    parts = list(operands) + ["earlier"] * len(earlier) + list(outs)
    results = pl.pallas_call(
        functools.partial(
            stage_kernel,
            parts=parts,
            start=start,
            next_start=next_start,
            fresh=fresh,
            middle=middle,
            final=final,
        ),
        grid=(1,),
        in_specs=[
            pl.BlockSpec((array.shape[0], next_chunk), lambda step: (0, next_start // next_chunk))
            if name in ("weights", "core_weights")
            else pl.BlockSpec(memory_space=pltpu.VMEM)
            for name, array in operands.items()
        ]
        + [pl.BlockSpec(memory_space=pl.ANY)] * len(earlier),
        out_specs=[pl.BlockSpec(memory_space=pltpu.VMEM)] * len(outs),
        out_shape=list(outs.values()),
        name="sum_stage",
        cost_estimate=SHORT,
        compiler_params=pltpu.CompilerParams(vmem_limit_bytes=16 * MIB),
    )(*operands.values(), *earlier)
    return dict(zip(outs, results))


def per_device(flight, modulation, project_in, project_out, stale_cache, visible):
    current = flight[0, 0]
    modulate = modulation[0, 0]
    token_rows, features = current.shape
    devices = lax.axis_size("sp") * lax.axis_size("cfg")

    context_rows = stale_cache.shape[2]
    width = project_in.shape[3]
    unpacked = stale_cache[0, 0].reshape(context_rows, 2, devices, width)
    packed = unpacked.transpose(2, 0, 1, 3).reshape(devices, context_rows, 2 * width)

    upper, lower = halves_of(current)
    across_upper, along_lower = from_partner(upper, "cfg", 1), from_partner(lower, "sp", 2)
    across_lower, along_upper = from_partner(lower, "cfg", 1), from_partner(upper, "sp", 2)
    other_modulate = from_partner(modulation, "cfg", 1)[0, 0]
    across_upper, along_lower = after(across_upper, (unpacked,)), after(along_lower, (unpacked,))
    first, second = from_partner(across_upper, "sp", 2), from_partner(along_lower, "cfg", 1)
    core_weights = from_partner(project_out[0], "sp", 1)
    near = [
        modulated_norm([current], modulate),
        modulated_norm([across_upper, across_lower], other_modulate),
        modulated_norm([along_upper, along_lower], modulate),
        modulated_norm([first, second], other_modulate),
    ]
    far = [from_partner(rows, "sp", 1) for rows in near]

    packed = after(packed, (across_lower, along_upper), limit=60)
    context = lax.all_to_all(packed, ("sp", "cfg"), split_axis=0, concat_axis=0, tiled=True)
    context = context.reshape(devices * context_rows, 2 * width)

    heads = project(near + far, project_in[0])
    gates = jnp.concatenate([modulate[2:3], other_modulate[2:3]], axis=0)
    count = len(CHUNKS)
    unit = features // 20
    chunks = [(start * unit, width * unit) for start, width in CHUNKS]
    for_core, queries, pool = attend_first(heads, context, visible[0])
    core_attended = from_partner(for_core, "sp", 1)
    attended, first_weights = attend_second(
        queries, pool, visible[0], project_out[0], core_weights, chunks[0], (for_core, gates)
    )

    kept, left, flights, arrivals, earlier = {}, {}, {}, [], []
    for index in range(-2, count + 2):
        fresh, middle, final = index + 2 < count, 0 <= index < count, index >= 2
        operands = {"rows": current, "gates": gates}
        if fresh:
            operands.update(attended=attended, core_attended=core_attended)
            if index == -2:
                operands["both"] = first_weights
            else:
                operands.update(weights=project_out[0], core_weights=core_weights)
        if index >= 0:
            operands["across"], operands["along"] = flights.pop(index)
        if middle:
            operands["first_kept"], operands["second_kept"] = kept.pop(index)
        if final:
            last = {name: operands[name] for name in ("rows", "across", "along")}
            last["first_left"], last["second_left"] = left.pop(index - 2)
            outs = stage(last, earlier, chunks, index, False, False, True)
            arrivals.append(from_behind(outs["done_out"], "pipe", 1))
            earlier = [outs["done_out"]]
        if fresh or middle:
            outs = stage(operands, earlier, chunks, index, fresh, middle, False)
        if "across_out" in outs:
            flights[index + 2] = (
                from_partner(outs["across_out"], "cfg", 1),
                from_partner(outs["along_out"], "sp", 2),
            )
        if fresh:
            kept[index + 2] = (outs["first_kept_out"], outs["second_kept_out"])
        if middle:
            left[index] = (outs["first_left_out"], outs["second_left_out"])
        earlier = [list(outs.values())[-1]] + (arrivals[-2:-1] if 3 <= index < count else [])
    in_order = sorted(range(count), key=lambda index: chunks[index][0])
    return jnp.concatenate([arrivals[index] for index in in_order], axis=1)[None, None]


def solution(mesh):
    placed = (
        P("pipe", "cfg", "sp", None),
        P("pipe", "cfg", None, None),
        P("pipe", None, None, ("sp", "cfg")),
        P("pipe", ("sp", "cfg"), None),
        P("pipe", "cfg", "sp", None, None),
        P("pipe", None, None),
    )
    return jax.shard_map(
        per_device,
        mesh=mesh,
        in_specs=placed,
        out_specs=P("pipe", "cfg", "sp", None),
        check_vma=False,
    )
```
